32 devices in a mesh: song: 4 (over y, x), seq: 8 (over z, core).
Axes of the slice: x: 2, y: 2, z: 4, core: 2. Of those that a mesh axis runs over, the one named last changes fastest.
Arguments:
- queries: bfloat16 [4, 1024, 2048], P('song', 'seq'), may hold values from -64 to 64
- keys: bfloat16 [4, 1024, 2048], P('song', 'seq'), may hold values from -64 to 64
- values: bfloat16 [4, 1024, 2048], P('song', 'seq'), may hold values from -6 to 6
- lyric_keys: bfloat16 [4, 384, 2048], P('song', 'seq'), may hold values from -64 to 64
- lyric_values: bfloat16 [4, 384, 2048], P('song', 'seq'), may hold values from -6 to 6
- q_gain: float32 [128], replicated, may hold values from 0.5 to 1.5
- k_gain: float32 [128], replicated, may hold values from 0.5 to 1.5
- cotangent: bfloat16 [4, 1024, 2048], P('song', 'seq'), may hold values from -12 to 12
- alignment: int32 [4, 8, 2], P('song', 'seq'), may hold values from -1 to 2, as said below
- lyric_len: int32 [4], P('song'), may hold values from 192 to 384
Outputs:
- attn_out: bfloat16 [4, 1024, 2048], P('song', 'seq')
- grad_queries: bfloat16 [4, 1024, 2048], P('song', 'seq')
- grad_keys: bfloat16 [4, 1024, 2048], P('song', 'seq')
- grad_values: bfloat16 [4, 1024, 2048], P('song', 'seq')
- grad_lyric_keys: bfloat16 [4, 384, 2048], P('song', 'seq')
- grad_lyric_values: bfloat16 [4, 384, 2048], P('song', 'seq')
- grad_q_gain: float32 [128], replicated
- grad_k_gain: float32 [128], replicated
The draws below stay inside these ranges and needn't reach their ends.
Inputs may be any that keep to these rules, and one draw needn't show every extreme that they name: `alignment`: in each row the entries that are not -1 are distinct.
All inputs are finite; a program needn't handle non-finite values.
Results may differ from the reference program's by a relative error of at most 0.01.
Values may be sent and summed in bfloat16 or wider, within the bound.
No kernel may reach another device: no remote copies, remote signals or barrier semaphores. Data moves between devices by JAX's collectives and lax.ppermute only.
A program may use at most 128 MiB of HBM per device.

```python
import jax
import jax.numpy as jnp
from jax import lax

H = 16
HD = 128
MODEL_DIM = 2048
BLK = 128
WIN = 1
TILES = 2
LYRIC_TOKENS = 384
SONGS = 4
AUDIO_FRAMES = 1024
NAB = 8
NLB = 3


def scaled_draw(key, song_count, row_count):
    first_key, second_key, third_key = jax.random.split(key, 3)
    shape = (song_count, row_count, H, HD)
    base = jnp.clip(jax.random.normal(first_key, shape, jnp.float32), -6.0, 6.0)
    row_scale = 10.0 ** jax.random.uniform(second_key, (song_count, row_count, H, 1), jnp.float32, -0.5, 0.5)
    col_scale = 10.0 ** jax.random.uniform(third_key, (HD,), jnp.float32, -0.5, 0.5)
    return (base * row_scale * col_scale).reshape(song_count, row_count, H * HD).astype(jnp.bfloat16)


def draw_queries(key, part):
    return scaled_draw(jax.random.fold_in(key, 11), SONGS, AUDIO_FRAMES)


def draw_keys(key, part):
    return scaled_draw(jax.random.fold_in(key, 12), SONGS, AUDIO_FRAMES)


def draw_lyric_keys(key, part):
    return scaled_draw(jax.random.fold_in(key, 13), SONGS, LYRIC_TOKENS)


def draw_cotangent(key, part):
    first_key = jax.random.fold_in(jax.random.fold_in(key, 14), 0)
    shape = (SONGS, AUDIO_FRAMES, H * HD)
    ramp = 0.5 + lax.broadcasted_iota(jnp.float32, (1, AUDIO_FRAMES, 1), 1) / AUDIO_FRAMES
    noise = jnp.clip(jax.random.normal(first_key, shape, jnp.float32), -6.0, 6.0)
    return (noise * ramp).astype(jnp.bfloat16)


def draw_alignment(key, part):
    first_key, second_key = jax.random.split(jax.random.fold_in(key, 15))
    grid = (SONGS, NAB, NLB)
    ranking = jax.random.randint(first_key, grid, 0, 1 << 20) * NLB + lax.broadcasted_iota(jnp.int32, grid, 2)
    order = jnp.argsort(ranking, axis=-1)
    picked = order[..., :TILES].astype(jnp.int32)
    dropped = jax.random.randint(second_key, (SONGS, NAB, TILES), 0, 4) == 0
    return jnp.where(dropped, -1, picked).astype(jnp.int32)


def set_ends(result, stream_key, smallest, largest):
    dims = result.shape
    spot = [jax.random.randint(jax.random.fold_in(stream_key, axis), (), 0, dims[axis]) for axis in range(len(dims))]
    result = result.at[tuple(spot)].set(smallest)
    longest = dims.index(max(dims))
    spot[longest] = (spot[longest] + 1) % dims[longest]
    return result.at[tuple(spot)].set(largest)


def level_of(stream_key, shape, cuts, smallest, top_value):
    def one(dim, parts):
        heights = jax.random.uniform(jax.random.fold_in(jax.random.fold_in(stream_key, 6), dim), (parts,), jnp.float32, smallest / len(cuts), top_value / len(cuts))
        return jnp.repeat(jnp.exp(heights), shape[dim] // parts).reshape((-1,) + (1,) * (len(shape) - dim - 1))

    gain = one(*cuts[0])
    for cut in cuts[1:]:
        gain = gain * one(*cut)
    return gain


def scatter_about(own_key, shape, width, limit, shards=(), kind=jnp.bfloat16):
    loudness = level_of(own_key, shape, shards, -0.22, 0.18) if shards else 1.0
    entries = jax.random.normal(own_key, shape, jnp.float32) * width * loudness
    return jnp.minimum(jnp.maximum(entries, -limit), limit).astype(kind)


def setup_inputs(seed: int = 0) -> dict:
    arg_keys = jax.random.split(jax.random.key(seed), 11)
    queries = draw_queries(jax.random.fold_in(arg_keys[10], 71), 0)
    keys = draw_keys(jax.random.fold_in(arg_keys[10], 71), 0)
    values = scatter_about(arg_keys[2], (SONGS, AUDIO_FRAMES, MODEL_DIM), 1.0, 6.0, ((0, 4), (1, 8)))
    lyric_keys = draw_lyric_keys(jax.random.fold_in(arg_keys[10], 71), 0)
    lyric_values = scatter_about(arg_keys[4], (SONGS, LYRIC_TOKENS, MODEL_DIM), 1.0, 6.0, ((0, 4), (1, 8)))
    q_gain = jnp.clip(1.0 + 0.1 * jax.random.normal(arg_keys[5], (HD,), jnp.float32), 0.5, 1.5)
    k_gain = jnp.clip(1.0 + 0.1 * jax.random.normal(arg_keys[6], (HD,), jnp.float32), 0.5, 1.5)
    cotangent = draw_cotangent(jax.random.fold_in(arg_keys[10], 71), 0)
    alignment = draw_alignment(jax.random.fold_in(arg_keys[10], 71), 0)
    lyric_len = set_ends(jax.random.randint(arg_keys[9], (SONGS,), LYRIC_TOKENS // 2, LYRIC_TOKENS + 1), jax.random.fold_in(arg_keys[9], 1), LYRIC_TOKENS // 2, LYRIC_TOKENS).astype(jnp.int32)
    return dict(queries=queries, keys=keys, values=values, lyric_keys=lyric_keys, lyric_values=lyric_values, q_gain=q_gain, k_gain=k_gain, cotangent=cotangent, alignment=alignment, lyric_len=lyric_len)


NORM_EPS = 1e-06

def norm_heads(inputs, norm_gain):
    row_values = inputs.astype(jnp.float32).reshape(inputs.shape[0], -1, norm_gain.shape[0])
    inverse = lax.rsqrt(lax.optimization_barrier(jnp.mean(row_values * row_values, axis=-1, keepdims=True)) + NORM_EPS)
    return (row_values * inverse * norm_gain, inverse)

def norm_back(inputs, inverse, norm_gain, grad_out):
    row_values = inputs.astype(jnp.float32).reshape(grad_out.shape)
    scaled = grad_out * norm_gain
    grad_input = inverse * scaled - row_values * inverse * inverse * inverse * lax.optimization_barrier(jnp.mean(scaled * row_values, axis=-1, keepdims=True))
    grad_gain = lax.optimization_barrier(jnp.sum(grad_out * row_values * inverse, axis=(0, 1)))
    return (grad_input.reshape(inputs.shape), grad_gain)

def block_pass(query_rows, key_rows, value_rows, keep_mask, grad_rows, score_scale):
    query_f = query_rows.astype(jnp.float32)
    key_f = key_rows.astype(jnp.float32)
    value_f = value_rows.astype(jnp.float32)
    grad_f = grad_rows.astype(jnp.float32)
    scores = jnp.einsum('qhd,khd->hqk', query_f, key_f) * score_scale
    exp_scores = jnp.where(keep_mask[None, None, :], jnp.exp(scores), jnp.float32(0.0))
    totals = lax.optimization_barrier(jnp.sum(exp_scores, axis=2))
    prob_full = exp_scores / totals[:, :, None]
    prob_low = prob_full.astype(jnp.bfloat16)
    block_output = jnp.einsum('hqk,khd->qhd', prob_low.astype(jnp.float32), value_f).astype(jnp.bfloat16)
    delta_rows = lax.optimization_barrier(jnp.sum(grad_f * block_output.astype(jnp.float32), axis=2))
    grad_prob = jnp.einsum('qhd,khd->hqk', grad_f, value_f)
    grad_score = (prob_full * (grad_prob - delta_rows.T[:, :, None])).astype(jnp.bfloat16).astype(jnp.float32)
    query_gradient = jnp.einsum('hqk,khd->qhd', grad_score, key_f) * score_scale
    grad_key = jnp.einsum('hqk,qhd->khd', grad_score, query_f) * score_scale
    value_gradient = jnp.einsum('hqk,qhd->khd', prob_low.astype(jnp.float32), grad_f)
    return (block_output, query_gradient, grad_key, value_gradient)

def reference(queries, keys, values, lyric_keys, lyric_values, q_gain, k_gain, cotangent, alignment, lyric_len):
    score_scale = HD ** (-0.5)
    border_rows = WIN * BLK
    window_extent = (2 * WIN + 1) * BLK

    def one_song(song_args):
        query_raw, key_raw, value_raw, lyric_raw, lyric_vals, grad_raw, align_rows, length = song_args
        query_full, query_inv = norm_heads(query_raw, q_gain)
        key_full, key_inv = norm_heads(key_raw, k_gain)
        lyric_full, lyric_inv = norm_heads(lyric_raw, k_gain)
        query_norm = query_full.astype(jnp.bfloat16)
        key_norm = key_full.astype(jnp.bfloat16)
        lyric_norm = lyric_full.astype(jnp.bfloat16)
        lyric_vh = lyric_vals.reshape(LYRIC_TOKENS, H, HD)
        padding = ((border_rows, border_rows), (0, 0), (0, 0))
        key_pad = jnp.pad(key_norm, padding)
        value_pad = jnp.pad(value_raw.reshape(AUDIO_FRAMES, H, HD), padding)
        grad_heads = grad_raw.reshape(AUDIO_FRAMES, H, HD)

        def scan_step(carried_state, block_id):
            padded_key_gradient, padded_value_gradient, lyric_key_gradient, lyric_value_gradient = carried_state
            start_offset = block_id * BLK
            query_rows = lax.dynamic_slice_in_dim(query_norm, start_offset, BLK, 0)
            grad_rows = lax.dynamic_slice_in_dim(grad_heads, start_offset, BLK, 0)
            audio_keys = lax.dynamic_slice_in_dim(key_pad, start_offset, window_extent, 0)
            audio_vals = lax.dynamic_slice_in_dim(value_pad, start_offset, window_extent, 0)
            position = start_offset - border_rows + jnp.arange(window_extent, dtype=jnp.int32)
            audio_mask = (position >= 0) & (position < AUDIO_FRAMES)
            tile_ids = align_rows[block_id]
            row_grid = (jnp.maximum(tile_ids, 0) * BLK)[:, None] + jnp.arange(BLK, dtype=jnp.int32)[None, :]
            lyric_mask = ((tile_ids >= 0)[:, None] & (row_grid < length)).reshape(-1)
            row_index = row_grid.reshape(-1)
            all_keys = jnp.concatenate([audio_keys, lyric_norm[row_index]], axis=0)
            all_vals = jnp.concatenate([audio_vals, lyric_vh[row_index]], axis=0)
            keep_mask = jnp.concatenate([audio_mask, lyric_mask], axis=0)
            block_output, query_gradient, grad_key, value_gradient = block_pass(query_rows, all_keys, all_vals, keep_mask, grad_rows, score_scale)
            padded_key_gradient = lax.dynamic_update_slice_in_dim(padded_key_gradient, lax.dynamic_slice_in_dim(padded_key_gradient, start_offset, window_extent, 0) + grad_key[:window_extent], start_offset, 0)
            padded_value_gradient = lax.dynamic_update_slice_in_dim(padded_value_gradient, lax.dynamic_slice_in_dim(padded_value_gradient, start_offset, window_extent, 0) + value_gradient[:window_extent], start_offset, 0)
            lyric_key_gradient = lyric_key_gradient.at[row_index].add(grad_key[window_extent:])
            lyric_value_gradient = lyric_value_gradient.at[row_index].add(value_gradient[window_extent:])
            return ((padded_key_gradient, padded_value_gradient, lyric_key_gradient, lyric_value_gradient), (block_output, query_gradient))
        zeros_pad = jnp.zeros((AUDIO_FRAMES + 2 * border_rows, H, HD), jnp.float32)
        zeros_lyric = jnp.zeros((LYRIC_TOKENS, H, HD), jnp.float32)
        carried_state, stacked = lax.scan(scan_step, (zeros_pad, zeros_pad, zeros_lyric, zeros_lyric), jnp.arange(NAB, dtype=jnp.int32))
        padded_key_gradient, padded_value_gradient, lyric_key_gradient, lyric_value_gradient = carried_state
        output_list, grad_qn = stacked
        unnormed_query_gradient, query_gain_vector = norm_back(query_raw, query_inv, q_gain, grad_qn.reshape(AUDIO_FRAMES, H, HD))
        unnormed_key_gradient, key_gain_vector = norm_back(key_raw, key_inv, k_gain, padded_key_gradient[border_rows:border_rows + AUDIO_FRAMES])
        unnormed_lyric_gradient, lyric_gain_vector = norm_back(lyric_raw, lyric_inv, k_gain, lyric_key_gradient)
        return (output_list.reshape(AUDIO_FRAMES, MODEL_DIM), unnormed_query_gradient.astype(jnp.bfloat16), unnormed_key_gradient.astype(jnp.bfloat16), padded_value_gradient[border_rows:border_rows + AUDIO_FRAMES].reshape(AUDIO_FRAMES, MODEL_DIM).astype(jnp.bfloat16), unnormed_lyric_gradient.astype(jnp.bfloat16), lyric_value_gradient.reshape(LYRIC_TOKENS, MODEL_DIM).astype(jnp.bfloat16), query_gain_vector, key_gain_vector + lyric_gain_vector)
    results = lax.map(one_song, (queries, keys, values, lyric_keys, lyric_values, cotangent, alignment, lyric_len))
    return (results[0], results[1], results[2], results[3], results[4], results[5], lax.optimization_barrier(jnp.sum(results[6], axis=0)), lax.optimization_barrier(jnp.sum(results[7], axis=0)))
```

```python
import functools

import jax
import jax.numpy as jnp
from jax import lax
from jax.experimental import pallas as pl
from jax.experimental.pallas import tpu as pltpu
from jax.sharding import PartitionSpec as P

BLK = 128
TILES = 2
NORM_EPS = 1e-06
HEADS_PER_STEP = 2
VMEM_LIMIT = 48 * 1024 * 1024


def dot(lhs, rhs, lhs_dim, rhs_dim):
    return lax.dot_general(
        lhs, rhs, (((lhs_dim,), (rhs_dim,)), ((), ())), preferred_element_type=jnp.float32
    )


def attention_kernel(
    piece_rows, head_size, score_scale, meta_ref, gain_ref, query_ref, grad_ref, key_ref,
    value_ref, left_ref, right_ref, *refs
):
    pieces = len(piece_rows)
    piece_refs = refs[:pieces]
    out_ref, grad_query_ref, own_key_ref, own_value_ref, to_left_ref, to_right_ref = refs[
        pieces : pieces + 6
    ]
    lyric_refs = refs[pieces + 6 : 2 * pieces + 6]
    gain_grad_ref, mask_ref = refs[2 * pieces + 6 :]
    frames = query_ref.shape[0]

    @pl.when(pl.program_id(0) == 0)
    def _():
        gain_grad_ref[...] = jnp.zeros_like(gain_grad_ref)
        mask_ref[0:frames, :] = jnp.full((frames, frames), meta_ref[3], jnp.int32).astype(
            jnp.float32
        )
        mask_ref[frames : 2 * frames, :] = jnp.ones((frames, frames), jnp.float32)
        mask_ref[2 * frames : 3 * frames, :] = jnp.full(
            (frames, frames), meta_ref[4], jnp.int32
        ).astype(jnp.float32)
        start = 3 * frames
        for index, rows in enumerate(piece_rows):
            row = lax.broadcasted_iota(jnp.int32, (rows, frames), 0) + meta_ref[5 + index]
            keep = jnp.zeros((rows, frames), jnp.float32)
            for slot in range(TILES):
                tile = meta_ref[slot]
                lower = tile * BLK
                upper = jnp.minimum(lower + BLK, meta_ref[2])
                inside = (row >= lower) & (row < upper) & (lower >= 0)
                keep = jnp.where(inside, 1.0, keep)
            mask_ref[start : start + rows, :] = keep
            start += rows

    q_gain = gain_ref[0:1, :]
    k_gain = gain_ref[1:2, :]
    for head in range(query_ref.shape[1] // head_size):
        cols = slice(head * head_size, (head + 1) * head_size)
        query = query_ref[:, cols].astype(jnp.float32)
        cot = grad_ref[:, cols]
        raw_keys = jnp.concatenate(
            [left_ref[0:frames, cols], key_ref[:, cols], right_ref[0:frames, cols]]
            + [ref[0:rows, cols] for ref, rows in zip(piece_refs, piece_rows)],
            axis=0,
        ).astype(jnp.float32)
        value = jnp.concatenate(
            [left_ref[frames:, cols], value_ref[:, cols], right_ref[frames:, cols]]
            + [ref[rows:, cols] for ref, rows in zip(piece_refs, piece_rows)],
            axis=0,
        )
        query_inv = lax.rsqrt(jnp.mean(query * query, axis=1, keepdims=True) + NORM_EPS)
        key_inv = lax.rsqrt(jnp.mean(raw_keys * raw_keys, axis=1, keepdims=True) + NORM_EPS)
        query_hat = query * query_inv
        query_low = (query_hat * (q_gain * score_scale)).astype(jnp.bfloat16)
        key_hat = raw_keys * key_inv
        key_low = (key_hat * k_gain).astype(jnp.bfloat16)
        scores = dot(key_low, query_low, 1, 1)
        grad_prob = dot(value, cot, 1, 1)
        exp_scores = jnp.exp(scores) * mask_ref[...]
        prob = exp_scores * (1.0 / jnp.sum(exp_scores, axis=0, keepdims=True))
        prob_low = prob.astype(jnp.bfloat16)
        weighted = prob * grad_prob
        delta = jnp.sum(weighted, axis=0, keepdims=True)
        grad_score = (weighted - prob * delta).astype(jnp.bfloat16)
        out_ref[:, cols] = dot(prob_low, value, 0, 0).astype(jnp.bfloat16)
        grad_qn = dot(grad_score, key_low, 0, 0) * score_scale
        grad_keys = dot(grad_score, query_low, 1, 0)
        grad_values = dot(prob_low, cot, 1, 0)
        scaled = grad_qn * q_gain
        grad_query_ref[:, cols] = (
            query_inv * scaled
            - query_hat
            * (query_inv * query_inv)
            * jnp.mean(scaled * query, axis=1, keepdims=True)
        ).astype(jnp.bfloat16)
        gain_grad_ref[0:1, :] += jnp.sum(grad_qn * query_hat, axis=0, keepdims=True)
        gain_grad_ref[1:2, :] += jnp.sum(grad_keys * key_hat, axis=0, keepdims=True)
        own = slice(frames, 2 * frames)
        own_key_ref[:, cols] = grad_keys[own]
        own_value_ref[:, cols] = grad_values[own]
        for ref, rows in ((to_left_ref, slice(0, frames)), (to_right_ref, slice(2 * frames, 3 * frames))):
            ref[0:frames, cols] = grad_keys[rows].astype(jnp.bfloat16)
            ref[frames:, cols] = grad_values[rows].astype(jnp.bfloat16)
        start = 3 * frames
        for ref, rows in zip(lyric_refs, piece_rows):
            ref[0:rows, cols] = grad_keys[start : start + rows].astype(jnp.bfloat16)
            ref[rows:, cols] = grad_values[start : start + rows].astype(jnp.bfloat16)
            start += rows


def attention(meta, gains, query, cot, key, value, left, right, lyric_pieces):
    frames, width = query.shape
    head_size = gains.shape[1]
    step = HEADS_PER_STEP * head_size
    piece_rows = tuple(piece.shape[0] // 2 for piece in lyric_pieces)
    key_rows = 3 * frames + sum(piece_rows)

    def columns(rows):
        return pl.BlockSpec((rows, step), lambda i: (0, i))

    def rows_out(rows, dtype):
        return jax.ShapeDtypeStruct((rows, width), dtype)

    bf16, f32 = jnp.bfloat16, jnp.float32
    out_shape = (
        [rows_out(frames, bf16)] * 2
        + [rows_out(frames, f32)] * 2
        + [rows_out(2 * frames, bf16)] * 2
        + [rows_out(2 * rows, bf16) for rows in piece_rows]
        + [jax.ShapeDtypeStruct((8, head_size), f32)]
    )
    return pl.pallas_call(
        functools.partial(attention_kernel, piece_rows, head_size, head_size ** (-0.5)),
        grid=(width // step,),
        in_specs=[
            pl.BlockSpec(memory_space=pltpu.SMEM),
            pl.BlockSpec(gains.shape, lambda i: (0, 0)),
        ]
        + [columns(frames)] * 4
        + [columns(2 * frames)] * 2
        + [columns(2 * rows) for rows in piece_rows],
        out_specs=[columns(frames)] * 4
        + [columns(2 * frames)] * 2
        + [columns(2 * rows) for rows in piece_rows]
        + [pl.BlockSpec((8, head_size), lambda i: (0, 0))],
        out_shape=out_shape,
        scratch_shapes=[pltpu.VMEM((key_rows, frames), f32)],
        compiler_params=pltpu.CompilerParams(
            dimension_semantics=("arbitrary",), vmem_limit_bytes=VMEM_LIMIT
        ),
        cost_estimate=pl.CostEstimate(
            flops=12 * key_rows * frames * width,
            bytes_accessed=16 * 1024 * 1024,
            transcendentals=key_rows * frames * (width // head_size),
        ),
        name="attention",
    )(meta, gains, query, cot, key, value, left, right, *lyric_pieces)


def finish_kernel(terms, head_size, gain_ref, raw_ref, *refs):
    rows = raw_ref.shape[0]
    key_parts, value_parts = refs[:terms], refs[terms : 2 * terms]
    grad_key_ref, grad_value_ref = refs[2 * terms :]
    k_gain = gain_ref[1:2, :]
    total = value_parts[0][...].astype(jnp.float32)
    for part in value_parts[1:]:
        total = total + part[...].astype(jnp.float32)
    grad_value_ref[...] = total.astype(jnp.bfloat16)
    for head in range(raw_ref.shape[1] // head_size):
        cols = slice(head * head_size, (head + 1) * head_size)
        raw = raw_ref[:, cols].astype(jnp.float32)
        inverse = lax.rsqrt(jnp.mean(raw * raw, axis=1, keepdims=True) + NORM_EPS)
        grad = key_parts[0][:, cols].astype(jnp.float32)
        for part in key_parts[1:]:
            grad = grad + part[:, cols].astype(jnp.float32)
        scaled = grad * k_gain
        grad_key_ref[:, cols] = (
            inverse * scaled
            - raw
            * (inverse * inverse * inverse)
            * jnp.mean(scaled * raw, axis=1, keepdims=True)
        ).astype(jnp.bfloat16)


def finish(gains, raw, key_parts, value_parts, name):
    rows, width = raw.shape
    head_size = gains.shape[1]
    step = min(width, 4 * head_size)

    def columns(block):
        return pl.BlockSpec((rows, step), lambda i: (block, i))

    parts = list(key_parts) + list(value_parts)
    return pl.pallas_call(
        functools.partial(finish_kernel, len(key_parts), head_size),
        grid=(width // step,),
        in_specs=[pl.BlockSpec(gains.shape, lambda i: (0, 0)), columns(0)]
        + [columns(block) for _, block in parts],
        out_specs=[columns(0)] * 2,
        out_shape=[jax.ShapeDtypeStruct((rows, width), jnp.bfloat16)] * 2,
        compiler_params=pltpu.CompilerParams(
            dimension_semantics=("arbitrary",), vmem_limit_bytes=VMEM_LIMIT
        ),
        cost_estimate=pl.CostEstimate(
            flops=20 * rows * width,
            bytes_accessed=2 * rows * width * (3 + len(parts)),
            transcendentals=rows * (width // head_size),
        ),
        name=name,
    )(gains, raw, *[array for array, _ in parts])


def add_kernel(*refs):
    half = len(refs) // 3
    for first, second, total in zip(refs[:half], refs[half : 2 * half], refs[2 * half :]):
        total[...] = (
            first[...].astype(jnp.float32) + second[...].astype(jnp.float32)
        ).astype(total.dtype)


def add_pieces(first, second):
    rows, width = first[0].shape
    step = width // 4
    spec = pl.BlockSpec((rows, step), lambda i: (0, i))
    count = len(first)
    return pl.pallas_call(
        add_kernel,
        grid=(width // step,),
        in_specs=[spec] * (2 * count),
        out_specs=[spec] * count,
        out_shape=[jax.ShapeDtypeStruct((rows, width), jnp.bfloat16)] * count,
        compiler_params=pltpu.CompilerParams(
            dimension_semantics=("arbitrary",), vmem_limit_bytes=VMEM_LIMIT
        ),
        cost_estimate=pl.CostEstimate(
            flops=count * rows * width,
            bytes_accessed=6 * count * rows * width,
            transcendentals=0,
        ),
        name="add_pieces",
    )(*first, *second)


def sum_over(total, axis):
    count = lax.axis_size(axis)
    if count & (count - 1):
        return lax.psum(total, axis)
    bit = 1
    while bit < count:
        total = total + lax.ppermute(total, axis, [(i, i ^ bit) for i in range(count)])
        bit *= 2
    return total


def shift_chips(block, count, chips):
    return lax.ppermute(block, "seq", [(i, (i + 2 * chips) % count) for i in range(count)])


def swap_cores(block, count):
    return lax.ppermute(block, "seq", [(i, i ^ 1) for i in range(count)])


def body(
    queries, keys, values, lyric_keys, lyric_values, q_gain, k_gain, cotangent, alignment, lyric_len
):
    frames = queries.shape[1]
    lyric_local = lyric_keys.shape[1]
    count = lax.axis_size("seq")
    me = lax.axis_index("seq")
    forward = [(i, i + 1) for i in range(count - 1)]
    backward = [(i + 1, i) for i in range(count - 1)]
    gains = jnp.stack([q_gain, k_gain])

    paired = count % 2 == 0 and count <= 8 and lyric_local % 16 == 0
    own_lyric = jnp.concatenate([lyric_keys[0], lyric_values[0]], axis=0)
    own_window = jnp.concatenate([keys[0], values[0]], axis=0)
    left = lax.ppermute(own_window, "seq", forward)
    right = lax.ppermute(own_window, "seq", backward)
    if paired:
        chips = count // 2
        same = [own_lyric] + [shift_chips(own_lyric, count, -j) for j in range(1, chips)]
        other = [swap_cores(piece, count) for piece in same]
        pieces = same + other
        owners = [(me + 2 * j) % count for j in range(chips)]
        owners = owners + [owner ^ 1 for owner in owners]
        first_rows = [owner * lyric_local for owner in owners]
    else:
        pieces = [
            jnp.concatenate(
                [
                    lax.all_gather(lyric_keys[0], "seq", axis=0, tiled=True),
                    lax.all_gather(lyric_values[0], "seq", axis=0, tiled=True),
                ],
                axis=0,
            )
        ]
        first_rows = [jnp.int32(0)]
    meta = jnp.stack(
        [alignment[0, 0, slot] for slot in range(TILES)]
        + [lyric_len[0], (me > 0).astype(jnp.int32), (me < count - 1).astype(jnp.int32)]
        + [row.astype(jnp.int32) for row in first_rows]
    )
    results = attention(
        meta, gains, queries[0], cotangent[0], keys[0], values[0], left, right, pieces
    )
    output, grad_queries, own_key, own_value, to_left, to_right = results[:6]
    lyric_parts, gain_part = results[6:-1], results[-1]

    if paired:
        from_other = [swap_cores(part, count) for part in lyric_parts[chips:]]
        sums = add_pieces(lyric_parts[:chips], from_other)
        arrived = [sums[0]] + [shift_chips(sums[j], count, j) for j in range(1, chips)]
        lyric_key_parts = [(part, 0) for part in arrived]
        lyric_value_parts = [(part, 1) for part in arrived]
    else:
        total_rows = lyric_local * count
        scattered = [
            lax.psum_scatter(
                half.astype(jnp.float32), "seq", scatter_dimension=0, tiled=True
            )
            for half in (lyric_parts[0][:total_rows], lyric_parts[0][total_rows:])
        ]
        lyric_key_parts = [(scattered[0], 0)]
        lyric_value_parts = [(scattered[1], 0)]
    from_right = lax.ppermute(to_left, "seq", backward)
    from_left = lax.ppermute(to_right, "seq", forward)
    gain_total = sum_over(sum_over(gain_part, "seq"), "song")
    grad_keys, grad_values = finish(
        gains,
        keys[0],
        [(own_key, 0), (from_left, 0), (from_right, 0)],
        [(own_value, 0), (from_left, 1), (from_right, 1)],
        "finish_audio",
    )
    grad_lyric_keys, grad_lyric_values = finish(
        gains, lyric_keys[0], lyric_key_parts, lyric_value_parts, "finish_lyric"
    )
    return (
        output[None],
        grad_queries[None],
        grad_keys[None],
        grad_values[None],
        grad_lyric_keys[None],
        grad_lyric_values[None],
        gain_total[0],
        gain_total[1],
    )


def solution(mesh):
    split = P("song", "seq", None)
    return jax.shard_map(
        body,
        mesh=mesh,
        in_specs=(split, split, split, split, split, P(), P(), split, split, P("song")),
        out_specs=(split, split, split, split, split, split, P(), P()),
        check_vma=False,
    )
```

```python
import functools

import jax
import jax.numpy as jnp
from jax import lax
from jax.experimental import pallas as pl
from jax.experimental.pallas import tpu as pltpu
from jax.sharding import PartitionSpec as P

BLK = 128
TILES = 2
NORM_EPS = 1e-06
HEADS_PER_STEP = 1
VMEM_LIMIT = 32 * 1024 * 1024


def dot(lhs, rhs, lhs_dim, rhs_dim):
    return lax.dot_general(
        lhs, rhs, (((lhs_dim,), (rhs_dim,)), ((), ())), preferred_element_type=jnp.float32
    )


def params():
    return pltpu.CompilerParams(
        dimension_semantics=("arbitrary",), vmem_limit_bytes=VMEM_LIMIT
    )


def pack_kernel(
    core_ref, query, cot, key_other, value_other, key_own, value_own, lkey_other, lvalue_other,
    lkey_own, lvalue_own, mate_ref, near_ref, far_ref, lyric_ref,
):
    frames, lyric = query.shape[0], lkey_own.shape[0]
    start = 0
    for ref in (query, cot, key_other, value_other, lkey_other, lvalue_other):
        mate_ref[start : start + ref.shape[0], :] = ref[...]
        start += ref.shape[0]
    near_ref[0:frames, :] = key_other[...]
    near_ref[frames:, :] = value_other[...]
    far_ref[0:frames, :] = key_own[...]
    far_ref[frames:, :] = value_own[...]
    lyric_ref[0:lyric, :] = lkey_own[...]
    lyric_ref[lyric:, :] = lvalue_own[...]


def pack(core, query, cot, key, value, lyric_key, lyric_value):
    frames, width = query.shape
    lyric = lyric_key.shape[0]
    half = width // 2
    step = half // 4

    def other(rows):
        return pl.BlockSpec((rows, step), lambda i, core: (0, (1 - core[0]) * 4 + i))

    def own(rows):
        return pl.BlockSpec((rows, step), lambda i, core: (0, core[0] * 4 + i))

    out_rows = (4 * frames + 2 * lyric, 2 * frames, 2 * frames, 2 * lyric)
    return pl.pallas_call(
        pack_kernel,
        grid_spec=pltpu.PrefetchScalarGridSpec(
            num_scalar_prefetch=1,
            grid=(4,),
            in_specs=[other(frames)] * 4
            + [own(frames)] * 2
            + [other(lyric)] * 2
            + [own(lyric)] * 2,
            out_specs=[pl.BlockSpec((rows, step), lambda i, core: (0, i)) for rows in out_rows],
        ),
        out_shape=[jax.ShapeDtypeStruct((rows, half), jnp.bfloat16) for rows in out_rows],
        compiler_params=params(),
        cost_estimate=pl.CostEstimate(flops=0, bytes_accessed=5 * 1024 * 1024, transcendentals=0),
        name="pack",
    )(core, query, cot, key, value, key, value, lyric_key, lyric_value, lyric_key, lyric_value)


def attention_kernel(
    groups, head_size, score_scale, meta_ref, gain_ref, query_ref, grad_ref, key_ref, value_ref,
    mate_ref, near_ref, far_ref, *refs
):
    frames = query_ref.shape[0]
    arrays = len(groups)
    lyric_in = refs[:arrays]
    out_ref, grad_query_ref, own_key_ref, own_value_ref, to_mate_ref, to_near_ref, to_far_ref = (
        refs[arrays : arrays + 7]
    )
    lyric_out = refs[arrays + 7 : 2 * arrays + 7]
    gain_grad_ref, mask_ref = refs[2 * arrays + 7 :]
    runs = [(index, run) for index, group in enumerate(groups) for run in group]
    main = 2 * frames + sum(run[2] for _, run in runs)
    lanes = 2 * frames

    @pl.when(pl.program_id(0) == 0)
    def _():
        gain_grad_ref[...] = jnp.zeros_like(gain_grad_ref)
        start = 0
        for number, (_, (_, _, rows)) in enumerate(runs):
            row = lax.broadcasted_iota(jnp.int32, (rows, lanes), 0) + meta_ref[8 + number]
            lane = lax.broadcasted_iota(jnp.int32, (rows, lanes), 1)
            keep = jnp.zeros((rows, lanes), jnp.float32)
            for slot in range(TILES):
                lower = jnp.where(lane < frames, meta_ref[1 + slot], meta_ref[3 + slot]) * BLK
                upper = jnp.minimum(lower + BLK, meta_ref[5])
                inside = (row >= lower) & (row < upper) & (lower >= 0)
                keep = jnp.where(inside, 1.0, keep)
            mask_ref[start : start + rows, :] = keep
            start += rows
        lane = lax.broadcasted_iota(jnp.int32, (frames, lanes), 1)
        mask_ref[start : start + frames, :] = jnp.where(
            lane < frames, meta_ref[6], meta_ref[7]
        ).astype(jnp.float32)

    q_gain = gain_ref[0:1, :]
    k_gain = gain_ref[1:2, :]
    for head in range(query_ref.shape[1] // head_size):
        cols = slice(head * head_size, (head + 1) * head_size)
        query = jnp.concatenate([query_ref[:, cols], mate_ref[0:frames, cols]], axis=0)
        query = query.astype(jnp.float32)
        cot = jnp.concatenate([grad_ref[:, cols], mate_ref[frames : 2 * frames, cols]], axis=0)
        raw_keys = jnp.concatenate(
            [key_ref[:, cols], mate_ref[2 * frames : 3 * frames, cols]]
            + [lyric_in[index][run[0] : run[0] + run[2], cols] for index, run in runs]
            + [near_ref[0:frames, cols], far_ref[0:frames, cols]],
            axis=0,
        ).astype(jnp.float32)
        value = jnp.concatenate(
            [value_ref[:, cols], mate_ref[3 * frames : 4 * frames, cols]]
            + [lyric_in[index][run[1] : run[1] + run[2], cols] for index, run in runs]
            + [near_ref[frames:, cols], far_ref[frames:, cols]],
            axis=0,
        )
        query_inv = lax.rsqrt(jnp.mean(query * query, axis=1, keepdims=True) + NORM_EPS)
        key_inv = lax.rsqrt(jnp.mean(raw_keys * raw_keys, axis=1, keepdims=True) + NORM_EPS)
        query_hat = query * query_inv
        query_low = (query_hat * (q_gain * score_scale)).astype(jnp.bfloat16)
        key_hat = raw_keys * key_inv
        key_low = (key_hat * k_gain).astype(jnp.bfloat16)

        near, far = slice(main, main + frames), slice(main + frames, main + 2 * frames)

        def against(rows, columns):
            return jnp.concatenate(
                [
                    dot(rows[:main], columns, 1, 1),
                    jnp.concatenate(
                        [
                            dot(rows[near], columns[:frames], 1, 1),
                            dot(rows[far], columns[frames:], 1, 1),
                        ],
                        axis=1,
                    ),
                ],
                axis=0,
            )

        def over_keys(weights, rows):
            return dot(weights[:main], rows[:main], 0, 0) + jnp.concatenate(
                [
                    dot(weights[main:, :frames], rows[near], 0, 0),
                    dot(weights[main:, frames:], rows[far], 0, 0),
                ],
                axis=0,
            )

        def over_queries(weights, columns):
            return jnp.concatenate(
                [
                    dot(weights[:main], columns, 1, 0),
                    dot(weights[main:, :frames], columns[:frames], 1, 0),
                    dot(weights[main:, frames:], columns[frames:], 1, 0),
                ],
                axis=0,
            )

        exp_scores = jnp.exp(against(key_low, query_low))
        exp_scores = jnp.concatenate(
            [exp_scores[: 2 * frames], exp_scores[2 * frames :] * mask_ref[...]], axis=0
        )
        grad_prob = against(value, cot)
        prob = exp_scores * (1.0 / jnp.sum(exp_scores, axis=0, keepdims=True))
        prob_low = prob.astype(jnp.bfloat16)
        weighted = prob * grad_prob
        delta = jnp.sum(weighted, axis=0, keepdims=True)
        grad_score = (weighted - prob * delta).astype(jnp.bfloat16)
        output = over_keys(prob_low, value).astype(jnp.bfloat16)
        grad_qn = over_keys(grad_score, key_low) * score_scale
        grad_keys = over_queries(grad_score, query_low)
        grad_values = over_queries(prob_low, cot)
        scaled = grad_qn * q_gain
        grad_query = (
            query_inv * scaled
            - query_hat
            * (query_inv * query_inv)
            * jnp.mean(scaled * query, axis=1, keepdims=True)
        ).astype(jnp.bfloat16)
        gain_grad_ref[0:1, :] += jnp.sum(grad_qn * query_hat, axis=0, keepdims=True)
        gain_grad_ref[1:2, :] += jnp.sum(grad_keys * key_hat, axis=0, keepdims=True)

        out_ref[:, cols] = output[:frames]
        grad_query_ref[:, cols] = grad_query[:frames]
        own_key_ref[:, cols] = grad_keys[:frames]
        own_value_ref[:, cols] = grad_values[:frames]
        to_mate_ref[0:frames, cols] = output[frames:]
        to_mate_ref[frames : 2 * frames, cols] = grad_query[frames:]
        mate = slice(frames, 2 * frames)
        to_mate_ref[2 * frames : 3 * frames, cols] = grad_keys[mate].astype(jnp.bfloat16)
        to_mate_ref[3 * frames :, cols] = grad_values[mate].astype(jnp.bfloat16)
        for ref, rows in ((to_near_ref, near), (to_far_ref, far)):
            ref[0:frames, cols] = grad_keys[rows].astype(jnp.bfloat16)
            ref[frames:, cols] = grad_values[rows].astype(jnp.bfloat16)
        start = 2 * frames
        for index, (key_row, value_row, rows) in runs:
            part = slice(start, start + rows)
            lyric_out[index][key_row : key_row + rows, cols] = grad_keys[part].astype(jnp.bfloat16)
            lyric_out[index][value_row : value_row + rows, cols] = grad_values[part].astype(
                jnp.bfloat16
            )
            start += rows


def attention(meta, gains, query, cot, key, value, mate, near, far, lyrics, groups):
    frames, width = query.shape
    head_size = gains.shape[1]
    half = width // 2
    step = HEADS_PER_STEP * head_size
    steps = half // step
    lyric_rows = sum(run[2] for group in groups for run in group)
    lanes = 2 * frames
    key_rows = 3 * frames + lyric_rows

    def own(rows):
        return pl.BlockSpec((rows, step), lambda i, meta: (0, meta[0] * steps + i))

    def columns(rows):
        return pl.BlockSpec((rows, step), lambda i, meta: (0, i))

    def either(array):
        return own(array.shape[0]) if array.shape[1] == width else columns(array.shape[0])

    whole = lambda i, meta: (0, 0)
    bf16, f32 = jnp.bfloat16, jnp.float32
    return pl.pallas_call(
        functools.partial(attention_kernel, groups, head_size, head_size ** (-0.5)),
        grid_spec=pltpu.PrefetchScalarGridSpec(
            num_scalar_prefetch=1,
            grid=(steps,),
            in_specs=[pl.BlockSpec(gains.shape, whole)]
            + [own(frames)] * 4
            + [columns(mate.shape[0]), columns(2 * frames), columns(2 * frames)]
            + [either(array) for array in lyrics],
            out_specs=[own(frames)] * 2
            + [columns(frames)] * 2
            + [columns(4 * frames), columns(2 * frames), columns(2 * frames)]
            + [columns(array.shape[0]) for array in lyrics]
            + [pl.BlockSpec((8, head_size), whole)],
            scratch_shapes=[pltpu.VMEM((frames + lyric_rows, lanes), f32)],
        ),
        out_shape=[jax.ShapeDtypeStruct((frames, width), bf16)] * 2
        + [jax.ShapeDtypeStruct((frames, half), f32)] * 2
        + [
            jax.ShapeDtypeStruct((4 * frames, half), bf16),
            jax.ShapeDtypeStruct((2 * frames, half), bf16),
            jax.ShapeDtypeStruct((2 * frames, half), bf16),
        ]
        + [jax.ShapeDtypeStruct((array.shape[0], half), bf16) for array in lyrics]
        + [jax.ShapeDtypeStruct((8, head_size), f32)],
        compiler_params=params(),
        cost_estimate=pl.CostEstimate(
            flops=12 * key_rows * lanes * half,
            bytes_accessed=16 * 1024 * 1024,
            transcendentals=key_rows * lanes * (half // head_size),
        ),
        name="attention",
    )(meta, gains, query, cot, key, value, mate, near, far, *lyrics)


def fill_kernel(core_ref, first_ref, second_ref, *refs):
    refs[-2][...] = first_ref[...]
    refs[-1][...] = second_ref[...]


def fill_other(core, output, grad_query, mate):
    frames, width = output.shape
    step = width // 8
    spec = pl.BlockSpec((frames, step), lambda i, core: (0, (1 - core[0]) * 4 + i))
    return pl.pallas_call(
        fill_kernel,
        grid_spec=pltpu.PrefetchScalarGridSpec(
            num_scalar_prefetch=1,
            grid=(4,),
            in_specs=[
                pl.BlockSpec((frames, step), lambda i, core: (0, i)),
                pl.BlockSpec((frames, step), lambda i, core: (1, i)),
                pl.BlockSpec(memory_space=pl.ANY),
                pl.BlockSpec(memory_space=pl.ANY),
            ],
            out_specs=[spec] * 2,
        ),
        out_shape=[jax.ShapeDtypeStruct(output.shape, output.dtype)] * 2,
        input_output_aliases={3: 0, 4: 1},
        compiler_params=params(),
        name="fill_other",
    )(core, mate, mate, output, grad_query)


def through_norm(raw, grad, k_gain):
    raw = raw.astype(jnp.float32)
    inverse = lax.rsqrt(jnp.mean(raw * raw, axis=1, keepdims=True) + NORM_EPS)
    scaled = grad * k_gain
    return (
        inverse * scaled
        - raw * (inverse * inverse * inverse) * jnp.mean(scaled * raw, axis=1, keepdims=True)
    ).astype(jnp.bfloat16)


def finish_audio_kernel(
    head_size, core_ref, gain_ref, raw_ref, own_key, own_value, far_key, far_value, mate_key,
    mate_value, near_key, near_value, grad_key_ref, grad_value_ref,
):
    k_gain = gain_ref[1:2, :]

    def finish(keys, values):
        total = values[0][...].astype(jnp.float32) + values[1][...].astype(jnp.float32)
        grad_value_ref[...] = total.astype(jnp.bfloat16)
        for head in range(raw_ref.shape[1] // head_size):
            cols = slice(head * head_size, (head + 1) * head_size)
            grad = keys[0][:, cols].astype(jnp.float32) + keys[1][:, cols].astype(jnp.float32)
            grad_key_ref[:, cols] = through_norm(raw_ref[:, cols], grad, k_gain)

    @pl.when(pl.program_id(0) == 0)
    def _():
        finish((own_key, far_key), (own_value, far_value))

    @pl.when(pl.program_id(0) == 1)
    def _():
        finish((mate_key, near_key), (mate_value, near_value))


def finish_audio(core, gains, raw, own_key, own_value, from_far, mate, from_near):
    frames, width = raw.shape
    head_size = gains.shape[1]
    parts = 2
    step = width // 2 // parts

    def first(block):
        return pl.BlockSpec(
            (frames, step), lambda h, i, core: (block, jnp.where(h == 0, i, parts - 1))
        )

    def second(block):
        return pl.BlockSpec((frames, step), lambda h, i, core: (block, jnp.where(h == 0, 0, i)))

    both = pl.BlockSpec(
        (frames, step),
        lambda h, i, core: (0, jnp.where(h == 0, core[0], 1 - core[0]) * parts + i),
    )
    return pl.pallas_call(
        functools.partial(finish_audio_kernel, head_size),
        grid_spec=pltpu.PrefetchScalarGridSpec(
            num_scalar_prefetch=1,
            grid=(2, parts),
            in_specs=[pl.BlockSpec(gains.shape, lambda h, i, core: (0, 0)), both]
            + [first(0), first(0), first(0), first(1)]
            + [second(2), second(3), second(0), second(1)],
            out_specs=[both] * 2,
        ),
        out_shape=[jax.ShapeDtypeStruct((frames, width), jnp.bfloat16)] * 2,
        compiler_params=pltpu.CompilerParams(
            dimension_semantics=("arbitrary", "arbitrary"), vmem_limit_bytes=VMEM_LIMIT
        ),
        name="finish_audio",
    )(core, gains, raw, own_key, own_value, from_far, from_far, mate, mate, from_near, from_near)


def finish_lyric_kernel(head_size, gain_ref, raw_ref, *refs):
    rows = raw_ref.shape[0] // 4
    parts, out_refs = refs[:-2], refs[-2:]
    k_gain = gain_ref[1:2, :]
    for head in range(raw_ref.shape[1] // head_size):
        cols = slice(head * head_size, (head + 1) * head_size)
        total = parts[0][:, cols].astype(jnp.float32)
        for part in parts[1:]:
            total = total + part[:, cols].astype(jnp.float32)
        for index, ref in enumerate(out_refs):
            base = 2 * rows * index
            ref[0:rows, cols] = through_norm(
                raw_ref[base : base + rows, cols], total[base : base + rows], k_gain
            )
            ref[rows:, cols] = total[base + rows : base + 2 * rows].astype(jnp.bfloat16)


def finish_lyric(gains, raw, parts):
    rows, half = raw.shape
    head_size = gains.shape[1]
    step = half // 2
    spec = pl.BlockSpec((rows, step), lambda i: (0, i))
    out = pl.BlockSpec((rows // 2, step), lambda i: (0, i))
    return pl.pallas_call(
        functools.partial(finish_lyric_kernel, head_size),
        grid=(2,),
        in_specs=[pl.BlockSpec(gains.shape, lambda i: (0, 0)), spec] + [spec] * len(parts),
        out_specs=[out] * 2,
        out_shape=[jax.ShapeDtypeStruct((rows // 2, half), jnp.bfloat16)] * 2,
        compiler_params=params(),
        name="finish_lyric",
    )(gains, raw, *parts)


def join_kernel(core_ref, own_ref, mate_ref, grad_key_ref, grad_value_ref):
    rows, half = grad_key_ref.shape[0], own_ref.shape[1]
    for part, ref in ((core_ref[0], own_ref), (1 - core_ref[0], mate_ref)):
        cols = pl.ds(pl.multiple_of(part * half, half), half)
        grad_key_ref[:, cols] = ref[0:rows, :]
        grad_value_ref[:, cols] = ref[rows:, :]


def join_lyric(core, own, mate):
    rows, half = own.shape
    return pl.pallas_call(
        join_kernel,
        grid_spec=pltpu.PrefetchScalarGridSpec(
            num_scalar_prefetch=1,
            grid=(1,),
            in_specs=[pl.BlockSpec((rows, half), lambda i, core: (0, 0))] * 2,
            out_specs=[pl.BlockSpec((rows // 2, 2 * half), lambda i, core: (0, 0))] * 2,
        ),
        out_shape=[jax.ShapeDtypeStruct((rows // 2, 2 * half), jnp.bfloat16)] * 2,
        compiler_params=params(),
        name="join_lyric",
    )(core, own, mate)


def norm_lyric_kernel(head_size, gain_ref, raw_ref, grad_ref, out_ref):
    for head in range(raw_ref.shape[1] // head_size):
        cols = slice(head * head_size, (head + 1) * head_size)
        out_ref[:, cols] = through_norm(raw_ref[:, cols], grad_ref[:, cols], gain_ref[1:2, :])


def norm_lyric(gains, raw, grad):
    return pl.pallas_call(
        functools.partial(norm_lyric_kernel, gains.shape[1]),
        out_shape=jax.ShapeDtypeStruct(raw.shape, jnp.bfloat16),
        name="norm_lyric",
    )(gains, raw, grad)


def body(
    queries, keys, values, lyric_keys, lyric_values, q_gain, k_gain, cotangent, alignment, lyric_len
):
    frames = queries.shape[1]
    lyric_local, width = lyric_keys.shape[1:]
    count = lax.axis_size("seq")
    me = lax.axis_index("seq")
    core = me % 2
    chips = count // 2
    chip = me // 2
    core_array = core.astype(jnp.int32).reshape(1)
    gains = jnp.stack([q_gain, k_gain])

    swap = [(i, i ^ 1) for i in range(count)]
    near_pairs = [(i, i + 1) for i in range(1, count - 1, 2)]
    near_pairs += [(i, i - 1) for i in range(2, count, 2)]
    far_pairs = [(i, i + 2) for i in range(1, count - 2, 2)]
    far_pairs += [(i, i - 2) for i in range(2, count, 2)]

    def shift(block, steps):
        return lax.ppermute(
            block, "seq", [(i, (i + 2 * steps) % count) for i in range(count)]
        )

    def back(pairs):
        return [(target, source) for source, target in pairs]

    mate_align = lax.ppermute(alignment, "seq", swap)
    to_mate, to_near, to_far, own_lyric = pack(
        core_array, queries[0], cotangent[0], keys[0], values[0], lyric_keys[0], lyric_values[0]
    )
    near = lax.ppermute(to_near, "seq", near_pairs)
    far = lax.ppermute(to_far, "seq", far_pairs)
    mate = lax.ppermute(to_mate, "seq", swap)

    paired = chips <= 4 and lyric_local % 16 == 0
    if paired:
        pair_lyric = jnp.concatenate([own_lyric, mate[4 * frames :]], axis=0)
        lyrics = [pair_lyric] + [shift(pair_lyric, -j) for j in range(1, chips)]
        run = ((0, lyric_local, lyric_local), (2 * lyric_local, 3 * lyric_local, lyric_local))
        groups = (run,) * chips
        first_rows = []
        for j in range(chips):
            owner = 2 * ((chip + j) % chips)
            first_rows += [(owner + core) * lyric_local, (owner + 1 - core) * lyric_local]
    else:
        total_rows = lyric_local * count
        lyrics = [
            jnp.concatenate(
                [
                    lax.all_gather(lyric_keys[0], "seq", axis=0, tiled=True),
                    lax.all_gather(lyric_values[0], "seq", axis=0, tiled=True),
                ],
                axis=0,
            )
        ]
        groups = (((0, total_rows, total_rows),),)
        first_rows = [0]

    has_near = jnp.where(core == 0, me > 0, me < count - 1)
    has_far = jnp.where(core == 0, me + 1 < count - 1, me - 1 > 0)
    meta = jnp.stack(
        [
            jnp.asarray(value, jnp.int32)
            for value in [core]
            + [alignment[0, 0, slot] for slot in range(TILES)]
            + [mate_align[0, 0, slot] for slot in range(TILES)]
            + [lyric_len[0], has_near, has_far]
            + first_rows
        ]
    )
    results = attention(
        meta, gains, queries[0], cotangent[0], keys[0], values[0], mate, near, far, lyrics, groups
    )
    output, grad_queries, own_key, own_value, for_mate, for_near, for_far = results[:7]
    lyric_parts, gain_part = results[7:-1], results[-1]

    from_mate = lax.ppermute(for_mate, "seq", swap)
    if paired:
        lyric_sums = [lyric_parts[0]] + [shift(lyric_parts[j], j) for j in range(1, chips)]
        own_half, mate_half = finish_lyric(gains, pair_lyric, lyric_sums)
        grad_lyric_keys, grad_lyric_values = join_lyric(
            core_array, own_half, lax.ppermute(mate_half, "seq", swap)
        )
    else:
        spread = lax.dynamic_update_slice(
            jnp.zeros((2 * total_rows, width), jnp.float32),
            lyric_parts[0].astype(jnp.float32),
            (0, core * (width // 2)),
        )
        lyric_key_sum, grad_lyric_values = [
            lax.psum_scatter(part, "seq", scatter_dimension=0, tiled=True)
            for part in (spread[:total_rows], spread[total_rows:])
        ]
        grad_lyric_keys = norm_lyric(gains, lyric_keys[0], lyric_key_sum)
        grad_lyric_values = grad_lyric_values.astype(jnp.bfloat16)
    from_near = lax.ppermute(for_near, "seq", back(near_pairs))
    from_far = lax.ppermute(for_far, "seq", back(far_pairs))
    gain_total = jnp.sum(lax.all_gather(gain_part, ("song", "seq")), axis=0)
    output, grad_queries = fill_other(core_array, output, grad_queries, from_mate)
    grad_keys, grad_values = finish_audio(
        core_array, gains, keys[0], own_key, own_value, from_far, from_mate, from_near
    )
    return (
        output[None],
        grad_queries[None],
        grad_keys[None],
        grad_values[None],
        grad_lyric_keys[None],
        grad_lyric_values[None],
        gain_total[0],
        gain_total[1],
    )


def solution(mesh):
    split = P("song", "seq", None)
    return jax.shard_map(
        body,
        mesh=mesh,
        in_specs=(split, split, split, split, split, P(), P(), split, split, P("song")),
        out_specs=(split, split, split, split, split, split, P(), P()),
        check_vma=False,
    )
```

```python
import functools

import jax
import jax.numpy as jnp
from jax import lax
from jax.experimental import pallas as pl
from jax.experimental.pallas import tpu as pltpu
from jax.sharding import PartitionSpec as P

BLK = 128
TILES = 2
NORM_EPS = 1e-06
HEADS_PER_STEP = 1
CHUNKS = 2
VMEM_LIMIT = 32 * 1024 * 1024


def dot(lhs, rhs, lhs_dim, rhs_dim):
    return lax.dot_general(
        lhs, rhs, (((lhs_dim,), (rhs_dim,)), ((), ())), preferred_element_type=jnp.float32
    )


def params():
    return pltpu.CompilerParams(
        dimension_semantics=("arbitrary",), vmem_limit_bytes=VMEM_LIMIT
    )


def pack_kernel(core_ref, *refs):
    out_ref = refs[-1]
    start = 0
    for ref in refs[:-1]:
        out_ref[start : start + ref.shape[0], :] = ref[...]
        start += ref.shape[0]


def pack(core, chunk, arrays):
    width = arrays[0].shape[1]
    size = width // 2 // CHUNKS
    step = size // 2
    rows = sum(array.shape[0] for array in arrays)
    return pl.pallas_call(
        pack_kernel,
        grid_spec=pltpu.PrefetchScalarGridSpec(
            num_scalar_prefetch=1,
            grid=(2,),
            in_specs=[
                pl.BlockSpec(
                    (array.shape[0], step),
                    lambda i, core: (0, ((1 - core[0]) * CHUNKS + chunk) * 2 + i),
                )
                for array in arrays
            ],
            out_specs=pl.BlockSpec((rows, step), lambda i, core: (0, i)),
        ),
        out_shape=jax.ShapeDtypeStruct((rows, size), jnp.bfloat16),
        compiler_params=params(),
        cost_estimate=pl.CostEstimate(
            flops=0, bytes_accessed=4 * rows * size, transcendentals=0
        ),
        name="pack",
    )(core, *arrays)


def merge_kernel(lyric, core_ref, key_ref, value_ref, lkey_ref, lvalue_ref, mate_ref, *refs):
    up_ref, down_ref = refs[-2:]
    frames = key_ref.shape[0]
    first = mate_ref.shape[0] - 2 * frames
    for ref, owner in ((up_ref, 1), (down_ref, 0)):
        if lyric:
            ref[0:lyric, :] = lkey_ref[...]
            ref[lyric : 2 * lyric, :] = lvalue_ref[...]
            ref[2 * lyric : 4 * lyric, :] = mate_ref[0 : 2 * lyric, :]
        mine = core_ref[0] == owner
        ref[4 * lyric : 4 * lyric + frames, :] = jnp.where(
            mine, key_ref[...], mate_ref[first : first + frames, :]
        )
        ref[4 * lyric + frames :, :] = jnp.where(
            mine, value_ref[...], mate_ref[first + frames :, :]
        )


def merge(core, chunk, key, value, lyric_key, lyric_value, mate, with_lyric, after):
    frames, width = key.shape
    lyric = lyric_key.shape[0]
    size = width // 2 // CHUNKS
    step = size // 2
    rows = 2 * frames + (4 * lyric if with_lyric else 0)

    def own(array):
        return pl.BlockSpec(
            (array.shape[0], step), lambda i, core: (0, (core[0] * CHUNKS + chunk) * 2 + i)
        )

    def columns(count):
        return pl.BlockSpec((count, step), lambda i, core: (0, i))

    return pl.pallas_call(
        functools.partial(merge_kernel, lyric if with_lyric else 0),
        grid_spec=pltpu.PrefetchScalarGridSpec(
            num_scalar_prefetch=1,
            grid=(2,),
            in_specs=[own(key), own(value), own(lyric_key), own(lyric_value)]
            + [columns(mate.shape[0])]
            + [pl.BlockSpec(memory_space=pl.ANY)] * len(after),
            out_specs=[columns(rows)] * 2,
        ),
        out_shape=[jax.ShapeDtypeStruct((rows, size), jnp.bfloat16)] * 2,
        compiler_params=params(),
        cost_estimate=pl.CostEstimate(
            flops=0, bytes_accessed=8 * rows * size, transcendentals=0
        ),
        name="merge",
    )(core, key, value, lyric_key, lyric_value, mate, *after)


def attention_kernel(
    groups, chained, head_size, score_scale, meta_ref, gain_ref, query_ref, grad_ref, key_ref, value_ref,
    mate_ref, up_ref, down_ref, *refs
):
    frames = query_ref.shape[0]
    arrays = len(groups)
    inputs = 4 if arrays == 4 else arrays
    lyric_in, refs = refs[:inputs], refs[inputs + 2 * chained :]
    window = up_ref.shape[0] - 2 * frames
    out_ref, grad_query_ref, to_mate_ref, key_grad_ref, value_grad_ref = refs[:5]
    to_left_ref, to_right_ref = refs[5:7]
    lyric_out = refs[7 : arrays + 7]
    gain_grad_ref, mask_ref = refs[arrays + 7 :]
    runs = [(index, run) for index, group in enumerate(groups) for run in group]
    main = 2 * frames + sum(run[2] for _, run in runs)
    lanes = 2 * frames

    @pl.when(pl.program_id(0) == 0)
    def _():
        gain_grad_ref[...] = jnp.zeros_like(gain_grad_ref)
        start = 0
        for number, (_, (_, _, rows)) in enumerate(runs):
            row = lax.broadcasted_iota(jnp.int32, (rows, lanes), 0) + meta_ref[9 + number]
            lane = lax.broadcasted_iota(jnp.int32, (rows, lanes), 1)
            keep = jnp.zeros((rows, lanes), jnp.float32)
            for slot in range(TILES):
                lower = jnp.where(lane < frames, meta_ref[1 + slot], meta_ref[3 + slot]) * BLK
                upper = jnp.minimum(lower + BLK, meta_ref[5])
                inside = (row >= lower) & (row < upper) & (lower >= 0)
                keep = jnp.where(inside, 1.0, keep)
            mask_ref[start : start + rows, :] = keep
            start += rows
        lane = lax.broadcasted_iota(jnp.int32, (frames, lanes), 1)
        mask_ref[start : start + frames, :] = jnp.where(
            lane < frames, meta_ref[6], meta_ref[7]
        ).astype(jnp.float32)

    q_gain = gain_ref[0:1, :]
    k_gain = gain_ref[1:2, :]
    for head in range(query_ref.shape[1] // head_size):
        cols = slice(head * head_size, (head + 1) * head_size)
        if arrays == 4:
            pair, up_two, down_two, far_end = [ref[:, cols] for ref in lyric_in]
            up_one, down_one = up_ref[0:window, cols], down_ref[0:window, cols]
            chip = meta_ref[8]
            lyric = [
                pair,
                jnp.where(chip == 0, far_end, up_one),
                jnp.where(chip == 3, far_end, down_one),
                jnp.where(chip <= 1, down_two, up_two),
            ]
        else:
            lyric = [ref[:, cols] for ref in lyric_in]
        left, right = up_ref[window:, cols], down_ref[window:, cols]
        near_rows = jnp.where(meta_ref[0] == 0, left, right)
        far_rows = jnp.where(meta_ref[0] == 0, right, left)
        first = mate_ref.shape[0] - 4 * frames

        def from_mate(number):
            return mate_ref[first + number * frames : first + (number + 1) * frames, cols]

        query = jnp.concatenate([query_ref[:, cols], from_mate(0)], axis=0)
        query = query.astype(jnp.float32)
        cot = jnp.concatenate([grad_ref[:, cols], from_mate(1)], axis=0)
        raw_keys = jnp.concatenate(
            [key_ref[:, cols], from_mate(2)]
            + [lyric[index][run[0] : run[0] + run[2]] for index, run in runs]
            + [near_rows[:frames], far_rows[:frames]],
            axis=0,
        ).astype(jnp.float32)
        value = jnp.concatenate(
            [value_ref[:, cols], from_mate(3)]
            + [lyric[index][run[1] : run[1] + run[2]] for index, run in runs]
            + [near_rows[frames:], far_rows[frames:]],
            axis=0,
        )
        query_inv = lax.rsqrt(jnp.mean(query * query, axis=1, keepdims=True) + NORM_EPS)
        key_inv = lax.rsqrt(jnp.mean(raw_keys * raw_keys, axis=1, keepdims=True) + NORM_EPS)
        query_hat = query * query_inv
        query_low = (query_hat * (q_gain * score_scale)).astype(jnp.bfloat16)
        key_hat = raw_keys * key_inv
        key_low = (key_hat * k_gain).astype(jnp.bfloat16)

        near, far = slice(main, main + frames), slice(main + frames, main + 2 * frames)

        def against(rows, columns):
            return jnp.concatenate(
                [
                    dot(rows[:main], columns, 1, 1),
                    jnp.concatenate(
                        [
                            dot(rows[near], columns[:frames], 1, 1),
                            dot(rows[far], columns[frames:], 1, 1),
                        ],
                        axis=1,
                    ),
                ],
                axis=0,
            )

        def over_keys(weights, rows):
            return dot(weights[:main], rows[:main], 0, 0) + jnp.concatenate(
                [
                    dot(weights[main:, :frames], rows[near], 0, 0),
                    dot(weights[main:, frames:], rows[far], 0, 0),
                ],
                axis=0,
            )

        def over_queries(weights, columns):
            return jnp.concatenate(
                [
                    dot(weights[:main], columns, 1, 0),
                    dot(weights[main:, :frames], columns[:frames], 1, 0),
                    dot(weights[main:, frames:], columns[frames:], 1, 0),
                ],
                axis=0,
            )

        exp_scores = jnp.exp(against(key_low, query_low))
        exp_scores = jnp.concatenate(
            [exp_scores[: 2 * frames], exp_scores[2 * frames :] * mask_ref[...]], axis=0
        )
        grad_prob = against(value, cot)
        prob = exp_scores * (1.0 / jnp.sum(exp_scores, axis=0, keepdims=True))
        prob_low = prob.astype(jnp.bfloat16)
        weighted = prob * grad_prob
        delta = jnp.sum(weighted, axis=0, keepdims=True)
        grad_score = (weighted - prob * delta).astype(jnp.bfloat16)
        output = over_keys(prob_low, value).astype(jnp.bfloat16)
        grad_qn = over_keys(grad_score, key_low) * score_scale
        grad_keys = over_queries(grad_score, query_low)
        grad_values = over_queries(prob_low, cot)
        scaled = grad_qn * q_gain
        grad_query = (
            query_inv * scaled
            - query_hat
            * (query_inv * query_inv)
            * jnp.mean(scaled * query, axis=1, keepdims=True)
        ).astype(jnp.bfloat16)
        gain_grad_ref[0:1, :] += jnp.sum(grad_qn * query_hat, axis=0, keepdims=True)
        gain_grad_ref[1:2, :] += jnp.sum(grad_keys * key_hat, axis=0, keepdims=True)

        out_ref[:, cols] = output[:frames]
        grad_query_ref[:, cols] = grad_query[:frames]
        to_mate_ref[0:frames, cols] = output[frames:]
        to_mate_ref[frames:, cols] = grad_query[frames:]
        key_grad_ref[:, cols] = grad_keys[: 2 * frames]
        value_grad_ref[:, cols] = grad_values[: 2 * frames]
        for grads, part in (
            (grad_keys.astype(jnp.bfloat16), slice(0, frames)),
            (grad_values.astype(jnp.bfloat16), slice(frames, 2 * frames)),
        ):
            to_left_ref[part, cols] = jnp.where(meta_ref[0] == 0, grads[near], grads[far])
            to_right_ref[part, cols] = jnp.where(meta_ref[0] == 0, grads[far], grads[near])
        start = 2 * frames
        for index, (key_row, value_row, rows) in runs:
            part = slice(start, start + rows)
            lyric_out[index][key_row : key_row + rows, cols] = grad_keys[part].astype(jnp.bfloat16)
            lyric_out[index][value_row : value_row + rows, cols] = grad_values[part].astype(
                jnp.bfloat16
            )
            start += rows


def attention(chunk, meta, gains, query, cot, key, value, mate, up, down, lyrics, groups, carried):
    frames, width = query.shape
    head_size = gains.shape[1]
    size = width // 2 // CHUNKS
    step = HEADS_PER_STEP * head_size
    steps = size // step
    lyric_rows = sum(run[2] for group in groups for run in group)
    lanes = 2 * frames
    key_rows = 3 * frames + lyric_rows

    def own(rows):
        return pl.BlockSpec(
            (rows, step), lambda i, meta: (0, (meta[0] * CHUNKS + chunk) * steps + i)
        )

    def columns(rows):
        return pl.BlockSpec((rows, step), lambda i, meta: (0, i))

    slot = sum(2 * run[2] for run in groups[0])

    def either(array):
        return own(slot) if array.shape[1] == width else columns(slot)

    whole = lambda i, meta: (0, 0)
    bf16, f32 = jnp.bfloat16, jnp.float32
    slot_rows = [slot] * len(groups)
    return pl.pallas_call(
        functools.partial(
            attention_kernel, groups, len(carried) // 2, head_size, head_size ** (-0.5)
        ),
        grid_spec=pltpu.PrefetchScalarGridSpec(
            num_scalar_prefetch=1,
            grid=(steps,),
            in_specs=[pl.BlockSpec(gains.shape, whole)]
            + [own(frames)] * 4
            + [columns(mate.shape[0]), columns(up.shape[0]), columns(down.shape[0])]
            + [either(array) for array in lyrics]
            + [pl.BlockSpec(memory_space=pl.ANY)] * len(carried),
            out_specs=[own(frames)] * 2
            + [columns(2 * frames)] * 5
            + [columns(rows) for rows in slot_rows]
            + [pl.BlockSpec((8, head_size), whole)],
            scratch_shapes=[pltpu.VMEM((frames + lyric_rows, lanes), f32)],
        ),
        out_shape=[jax.ShapeDtypeStruct((frames, width), bf16)] * 2
        + [jax.ShapeDtypeStruct((2 * frames, size), dtype) for dtype in (bf16, f32, f32, bf16, bf16)]
        + [jax.ShapeDtypeStruct((rows, size), bf16) for rows in slot_rows]
        + [jax.ShapeDtypeStruct((8, head_size), f32)],
        input_output_aliases={9 + len(lyrics) + i: i for i in range(len(carried))},
        compiler_params=params(),
        cost_estimate=pl.CostEstimate(
            flops=12 * key_rows * lanes * size,
            bytes_accessed=16 * 1024 * 1024 // CHUNKS,
            transcendentals=key_rows * lanes * (size // head_size),
        ),
        name="attention",
    )(meta, gains, query, cot, key, value, mate, up, down, *lyrics, *carried)


def fill_kernel(count, core_ref, mate_ref, *refs):
    rows = mate_ref.shape[0] // count
    for index, ref in enumerate(refs[-count:]):
        ref[...] = mate_ref[index * rows : (index + 1) * rows, :]


def fill_other(core, chunk, arrays, mate):
    frames, width = arrays[0].shape
    count = len(arrays)
    size = width // 2 // CHUNKS
    step = size // 2
    spec = pl.BlockSpec(
        (frames, step), lambda i, core: (0, ((1 - core[0]) * CHUNKS + chunk) * 2 + i)
    )
    return pl.pallas_call(
        functools.partial(fill_kernel, count),
        grid_spec=pltpu.PrefetchScalarGridSpec(
            num_scalar_prefetch=1,
            grid=(2,),
            in_specs=[pl.BlockSpec((count * frames, step), lambda i, core: (0, i))]
            + [pl.BlockSpec(memory_space=pl.ANY)] * count,
            out_specs=[spec] * count,
        ),
        out_shape=[jax.ShapeDtypeStruct(array.shape, array.dtype) for array in arrays],
        input_output_aliases={2 + i: i for i in range(count)},
        compiler_params=params(),
        cost_estimate=pl.CostEstimate(
            flops=0, bytes_accessed=4 * count * frames * size, transcendentals=0
        ),
        name="fill_other",
    )(core, mate, *arrays)


def through_norm(raw, grad, k_gain):
    raw = raw.astype(jnp.float32)
    inverse = lax.rsqrt(jnp.mean(raw * raw, axis=1, keepdims=True) + NORM_EPS)
    scaled = grad * k_gain
    return (
        inverse * scaled
        - raw * (inverse * inverse * inverse) * jnp.mean(scaled * raw, axis=1, keepdims=True)
    ).astype(jnp.bfloat16)


def finish_audio_kernel(
    head_size, core_ref, gain_ref, raw_ref, mate_ref, key_grad_ref, value_grad_ref, up_ref,
    down_ref, ready_ref, *refs,
):
    k_gain = gain_ref[1:2, :]
    grad_key_ref, grad_value_ref, to_mate_ref = refs[-3:]
    frames = raw_ref.shape[0]
    own, mate = slice(0, frames), slice(frames, 2 * frames)
    first = up_ref.shape[0] - 2 * frames
    mate_keys = mate_ref.shape[0] - 2 * frames
    to_mate_ref[0 : 2 * frames, :] = ready_ref[...]
    for head in range(raw_ref.shape[1] // head_size):
        cols = slice(head * head_size, (head + 1) * head_size)
        up = up_ref[first:, cols].astype(jnp.float32)
        down = down_ref[first:, cols].astype(jnp.float32)
        for_own = jnp.where(core_ref[0] == 0, up, down)
        for_mate = jnp.where(core_ref[0] == 0, down, up)
        grad_key_ref[:, cols] = through_norm(
            raw_ref[:, cols], key_grad_ref[own, cols] + for_own[:frames], k_gain
        )
        grad_value_ref[:, cols] = (value_grad_ref[own, cols] + for_own[frames:]).astype(
            jnp.bfloat16
        )
        to_mate_ref[2 * frames : 3 * frames, cols] = through_norm(
            mate_ref[mate_keys : mate_keys + frames, cols],
            key_grad_ref[mate, cols] + for_mate[:frames],
            k_gain,
        )
        to_mate_ref[3 * frames :, cols] = (
            value_grad_ref[mate, cols] + for_mate[frames:]
        ).astype(jnp.bfloat16)


def finish_audio(core, chunk, gains, raw, mate, key_grad, value_grad, up, down, ready, carried):
    frames, width = raw.shape
    head_size = gains.shape[1]
    size = width // 2 // CHUNKS
    step = size // 2

    def columns(array):
        return pl.BlockSpec((array.shape[0], step), lambda i, core: (0, i))

    own = pl.BlockSpec((frames, step), lambda i, core: (0, (core[0] * CHUNKS + chunk) * 2 + i))
    arrays = (mate, key_grad, value_grad, up, down, ready)
    return pl.pallas_call(
        functools.partial(finish_audio_kernel, head_size),
        grid_spec=pltpu.PrefetchScalarGridSpec(
            num_scalar_prefetch=1,
            grid=(2,),
            in_specs=[pl.BlockSpec(gains.shape, lambda i, core: (0, 0)), own]
            + [columns(array) for array in arrays]
            + [pl.BlockSpec(memory_space=pl.ANY)] * len(carried),
            out_specs=[own] * 2 + [pl.BlockSpec((4 * frames, step), lambda i, core: (0, i))],
        ),
        out_shape=[jax.ShapeDtypeStruct((frames, width), jnp.bfloat16)] * 2
        + [jax.ShapeDtypeStruct((4 * frames, size), jnp.bfloat16)],
        input_output_aliases={9 + i: i for i in range(len(carried))},
        compiler_params=params(),
        cost_estimate=pl.CostEstimate(
            flops=40 * frames * size, bytes_accessed=40 * frames * size, transcendentals=0
        ),
        name="finish_audio",
    )(core, gains, raw, *arrays, *carried)


def relay_kernel(third_ref, sum_ref, left_ref, right_ref, up_ref, down_ref):
    rows = third_ref.shape[0]
    total = (third_ref[...].astype(jnp.float32) + sum_ref[...].astype(jnp.float32)).astype(
        jnp.bfloat16
    )
    up_ref[0:rows, :] = total
    up_ref[rows:, :] = right_ref[...]
    down_ref[0:rows, :] = total
    down_ref[rows:, :] = left_ref[...]


def relay(third, far_sum, to_left, to_right):
    rows, size = third.shape
    step = size // 2
    out_rows = rows + to_left.shape[0]

    def columns(count):
        return pl.BlockSpec((count, step), lambda i: (0, i))

    return pl.pallas_call(
        relay_kernel,
        grid=(2,),
        in_specs=[columns(rows)] * 2 + [columns(to_left.shape[0])] * 2,
        out_specs=[columns(out_rows)] * 2,
        out_shape=[jax.ShapeDtypeStruct((out_rows, size), jnp.bfloat16)] * 2,
        compiler_params=params(),
        cost_estimate=pl.CostEstimate(
            flops=rows * size, bytes_accessed=8 * out_rows * size, transcendentals=0
        ),
        name="relay",
    )(third, far_sum, to_left, to_right)


def finish_lyric_kernel(head_size, gain_ref, raw_ref, *refs):
    rows = raw_ref.shape[0] // 4
    parts, out_refs = refs[:-2], refs[-2:]
    k_gain = gain_ref[1:2, :]
    for head in range(raw_ref.shape[1] // head_size):
        cols = slice(head * head_size, (head + 1) * head_size)
        total = parts[0][:, cols].astype(jnp.float32)
        for part in parts[1:]:
            total = total + part[:, cols].astype(jnp.float32)
        for index, ref in enumerate(out_refs):
            base = 2 * rows * index
            ref[0:rows, cols] = through_norm(
                raw_ref[base : base + rows, cols], total[base : base + rows], k_gain
            )
            ref[rows:, cols] = total[base + rows : base + 2 * rows].astype(jnp.bfloat16)


def finish_lyric(gains, raw, parts):
    rows, size = parts[0].shape
    head_size = gains.shape[1]
    step = size // 2
    spec = pl.BlockSpec((rows, step), lambda i: (0, i))
    out = pl.BlockSpec((rows // 2, step), lambda i: (0, i))
    return pl.pallas_call(
        functools.partial(finish_lyric_kernel, head_size),
        grid=(2,),
        in_specs=[pl.BlockSpec(gains.shape, lambda i: (0, 0)), spec] + [spec] * len(parts),
        out_specs=[out] * 2,
        out_shape=[jax.ShapeDtypeStruct((rows // 2, size), jnp.bfloat16)] * 2,
        compiler_params=params(),
        cost_estimate=pl.CostEstimate(
            flops=20 * rows * size, bytes_accessed=10 * rows * size, transcendentals=0
        ),
        name="finish_lyric",
    )(gains, raw, *parts)


def join_kernel(core_ref, *refs):
    grad_key_ref, grad_value_ref = refs[-2:]
    chunks = len(refs) // 2 - 1
    rows, size = grad_key_ref.shape[0], refs[0].shape[1]
    for part, parts in ((core_ref[0], refs[:chunks]), (1 - core_ref[0], refs[chunks:-2])):
        for chunk, ref in enumerate(parts):
            cols = pl.ds(pl.multiple_of((part * chunks + chunk) * size, size), size)
            grad_key_ref[:, cols] = ref[0:rows, :]
            grad_value_ref[:, cols] = ref[rows:, :]


def join_lyric(core, own, mate):
    rows, size = own[0].shape
    width = 2 * len(own) * size
    return pl.pallas_call(
        join_kernel,
        grid_spec=pltpu.PrefetchScalarGridSpec(
            num_scalar_prefetch=1,
            grid=(1,),
            in_specs=[pl.BlockSpec((rows, size), lambda i, core: (0, 0))] * (2 * len(own)),
            out_specs=[pl.BlockSpec((rows // 2, width), lambda i, core: (0, 0))] * 2,
        ),
        out_shape=[jax.ShapeDtypeStruct((rows // 2, width), jnp.bfloat16)] * 2,
        compiler_params=params(),
        name="join_lyric",
    )(core, *own, *mate)


def norm_lyric_kernel(head_size, gain_ref, raw_ref, grad_ref, out_ref):
    for head in range(raw_ref.shape[1] // head_size):
        cols = slice(head * head_size, (head + 1) * head_size)
        out_ref[:, cols] = through_norm(raw_ref[:, cols], grad_ref[:, cols], gain_ref[1:2, :])


def norm_lyric(gains, raw, grad):
    return pl.pallas_call(
        functools.partial(norm_lyric_kernel, gains.shape[1]),
        out_shape=jax.ShapeDtypeStruct(raw.shape, jnp.bfloat16),
        name="norm_lyric",
    )(gains, raw, grad)


def sum_over(total, axis, bits):
    count = lax.axis_size(axis)
    for bit in bits:
        total = total + lax.ppermute(total, axis, [(i, i ^ bit) for i in range(count)])
    return total


def tie_kernel(block_ref, *refs):
    refs[-1][...] = block_ref[...]


def tie(block, after):
    return pl.pallas_call(
        tie_kernel,
        in_specs=[pl.BlockSpec(memory_space=pltpu.VMEM)]
        + [pl.BlockSpec(memory_space=pl.ANY)] * len(after),
        out_shape=jax.ShapeDtypeStruct(block.shape, block.dtype),
        name="tie",
    )(block, *after)


def bits_of(count):
    return [1 << bit for bit in range(count.bit_length() - 1)]


def body(
    queries, keys, values, lyric_keys, lyric_values, q_gain, k_gain, cotangent, alignment, lyric_len
):
    frames = queries.shape[1]
    lyric_local, width = lyric_keys.shape[1:]
    count = lax.axis_size("seq")
    songs = lax.axis_size("song")
    me = lax.axis_index("seq")
    core = me % 2
    chips = count // 2
    chip = me // 2
    core_array = core.astype(jnp.int32).reshape(1)
    gains = jnp.stack([q_gain, k_gain])

    swap = [(i, i ^ 1) for i in range(count)]
    above = [(a, a + 1) for a in range(chips - 1)]
    below = [(a + 1, a) for a in range(chips - 1)]

    def hop(block, moves):
        pairs = [(2 * a + c, 2 * b + c) for a, b in moves for c in (0, 1)]
        return lax.ppermute(block, "seq", pairs)

    hops = chips == 4 and lyric_local % 16 == 0
    total_rows = lyric_local * count
    mate_align = lax.ppermute(alignment, "seq", swap)
    if hops:
        run = ((0, lyric_local, lyric_local), (2 * lyric_local, 3 * lyric_local, lyric_local))
        groups = (run,) * 4
        owners = [
            chip,
            jnp.where(chip == 0, 3, chip - 1),
            jnp.where(chip == 3, 0, chip + 1),
            jnp.where(chip <= 1, chip + 2, chip - 2),
        ]
        first_rows = []
        for owner in owners:
            first_rows += [
                (2 * owner + core) * lyric_local,
                (2 * owner + 1 - core) * lyric_local,
            ]
    else:
        gathered = jnp.concatenate(
            [
                lax.all_gather(lyric_keys[0], "seq", axis=0, tiled=True),
                lax.all_gather(lyric_values[0], "seq", axis=0, tiled=True),
            ],
            axis=0,
        )
        groups = (((0, total_rows, total_rows),),)
        first_rows = [0]
    has_left, has_right = chip > 0, chip < chips - 1
    has_near = jnp.where(core == 0, has_left, has_right)
    has_far = jnp.where(core == 0, has_right, has_left)
    meta = jnp.stack(
        [
            jnp.asarray(value, jnp.int32)
            for value in [core]
            + [alignment[0, 0, slot] for slot in range(TILES)]
            + [mate_align[0, 0, slot] for slot in range(TILES)]
            + [lyric_len[0], has_near, has_far, chip]
            + first_rows
        ]
    )

    rows = 4 * lyric_local
    attended = []
    carried = []
    after = []
    for chunk in range(CHUNKS):
        to_mate = pack(
            core_array,
            chunk,
            [lyric_keys[0], lyric_values[0], queries[0], cotangent[0], keys[0], values[0]],
        )
        mate = lax.ppermute(to_mate, "seq", swap)
        up, down = merge(
            core_array, chunk, keys[0], values[0], lyric_keys[0], lyric_values[0], mate, hops,
            after,
        )
        up_one, down_one = hop(up, above), hop(down, below)
        after = [up_one, down_one]
        if hops:
            up_two = hop(up_one[:rows], [(1, 2), (2, 3)])
            down_two = hop(down_one[:rows], [(1, 0), (2, 1)])
            far_end = hop(jnp.where(chip == 2, up_two, down_two), [(2, 3), (1, 0)])
            lyrics = [up, up_two, down_two, far_end]
        else:
            lyrics = [gathered]
        results = attention(
            chunk, meta, gains, queries[0], cotangent[0], keys[0], values[0], mate, up_one,
            down_one, lyrics, groups, carried,
        )
        carried = results[:2]
        attended.append((results[2:], lyrics, mate))
    output, grad_queries = carried

    grads = []
    own_halves, mate_halves, lyric_cols, from_mates = [], [], [], []
    for chunk, (results, lyrics, mate) in enumerate(attended):
        for_mate, key_grad, value_grad, to_left, to_right = results[:5]
        parts = results[5:-1]
        if hops:
            held, first, second, third = parts
            far_sum = hop(jnp.where(chip == 0, first, second), [(0, 1), (3, 2)])
            to_up, to_down = relay(third, far_sum, to_left, to_right)
        else:
            to_up, to_down = to_right, to_left
        up_two, down_two = hop(to_up, above), hop(to_down, below)
        sent = to_up
        if hops:
            to_up, to_down = second + up_two[:rows], first + down_two[:rows]
            up_one, down_one = hop(to_up, above), hop(to_down, below)
            own_half, mate_half = finish_lyric(gains, lyrics[0], [held, up_one, down_one])
            own_halves.append(own_half)
            mate_halves.append(lax.ppermute(mate_half, "seq", swap))
        else:
            lyric_cols.append(parts[0])
        *grads, for_mate = finish_audio(
            core_array, chunk, gains, keys[0], mate, key_grad, value_grad, up_two, down_two,
            for_mate, grads,
        )
        from_mates.append(lax.ppermute(for_mate, "seq", swap))
    filled = [output, grad_queries, *grads]
    for chunk, from_mate in enumerate(from_mates):
        filled = fill_other(core_array, chunk, filled, from_mate)
    output, grad_queries, grad_keys, grad_values = filled
    gain_total = sum(results[-1] for results, _, _ in attended)
    if (count & (count - 1)) or (songs & (songs - 1)):
        gain_total = lax.psum(gain_total, ("song", "seq"))
    else:
        gain_total = sum_over(tie(gain_total, [sent]), "song", bits_of(songs))
        gain_total = sum_over(tie(gain_total, [to_up, to_down]), "seq", bits_of(count))
    if hops:
        grad_lyric_keys, grad_lyric_values = join_lyric(core_array, own_halves, mate_halves)
    else:
        spread = lax.dynamic_update_slice(
            jnp.zeros((2 * total_rows, width), jnp.float32),
            jnp.concatenate(lyric_cols, axis=1).astype(jnp.float32),
            (0, core * (width // 2)),
        )
        lyric_key_sum, grad_lyric_values = [
            lax.psum_scatter(part, "seq", scatter_dimension=0, tiled=True)
            for part in (spread[:total_rows], spread[total_rows:])
        ]
        grad_lyric_keys = norm_lyric(gains, lyric_keys[0], lyric_key_sum)
        grad_lyric_values = grad_lyric_values.astype(jnp.bfloat16)
    return (
        output[None],
        grad_queries[None],
        grad_keys[None],
        grad_values[None],
        grad_lyric_keys[None],
        grad_lyric_values[None],
        gain_total[0],
        gain_total[1],
    )


def solution(mesh):
    split = P("song", "seq", None)
    return jax.shard_map(
        body,
        mesh=mesh,
        in_specs=(split, split, split, split, split, P(), P(), split, split, P("song")),
        out_specs=(split, split, split, split, split, split, P(), P()),
        check_vma=False,
    )
```

```python
import functools

import jax
import jax.numpy as jnp
from jax import lax
from jax.experimental import pallas as pl
from jax.experimental.pallas import tpu as pltpu
from jax.sharding import PartitionSpec as P

BLK = 128
TILES = 2
NORM_EPS = 1e-06
HEADS_PER_STEP = 1
CHUNKS = 1
VMEM_LIMIT = 8 * 1024 * 1024
ATTENTION_VMEM_LIMIT = 24 * 1024 * 1024
GAIN_ROWS = 32
SMALL = pl.CostEstimate(flops=1, bytes_accessed=1, transcendentals=0)


def dot(lhs, rhs, lhs_dim, rhs_dim):
    return lax.dot_general(
        lhs, rhs, (((lhs_dim,), (rhs_dim,)), ((), ())), preferred_element_type=jnp.float32
    )


def params(limit=VMEM_LIMIT):
    return pltpu.CompilerParams(dimension_semantics=("arbitrary",), vmem_limit_bytes=limit)


def split_rows(sums):
    high = sums.astype(jnp.bfloat16).astype(jnp.float32)
    rest = sums - high
    middle = rest.astype(jnp.bfloat16).astype(jnp.float32)
    low = rest - middle
    return jnp.concatenate([high, middle, low, jnp.zeros_like(high)], axis=0).astype(jnp.bfloat16)


def joined_rows(rows):
    rows = rows.astype(jnp.float32)
    return (rows[16:24] + rows[8:16]) + rows[0:8]


def pack_kernel(state_ref, align_ref, *refs):
    ins, out_ref = refs[:-1], refs[-1]
    start = 0
    for ref in ins[:-4]:
        out_ref[start : start + ref.shape[0], :] = ref[...]
        start += ref.shape[0]
    row = lax.broadcasted_iota(jnp.int32, (16, out_ref.shape[1]), 0)
    tiles = jnp.zeros((16, out_ref.shape[1]), jnp.int32)
    for slot in range(TILES):
        tiles = jnp.where(row == slot, align_ref[slot], tiles)
    out_ref[start : start + 16, :] = tiles.astype(jnp.float32).astype(jnp.bfloat16)
    start += 16
    for ref in ins[-4:]:
        out_ref[start : start + ref.shape[0], :] = ref[...]
        start += ref.shape[0]


def pack(state, align, arrays):
    width = arrays[0].shape[1]
    half = width // 2
    step = half // 4
    rows = sum(array.shape[0] for array in arrays) + 16
    return pl.pallas_call(
        pack_kernel,
        grid_spec=pltpu.PrefetchScalarGridSpec(
            num_scalar_prefetch=2,
            grid=(4,),
            in_specs=[
                pl.BlockSpec(
                    (array.shape[0], step), lambda i, state, _: (0, (1 - state[0]) * 4 + i)
                )
                for array in arrays
            ],
            out_specs=pl.BlockSpec((rows, step), lambda i, state, _: (0, i)),
        ),
        out_shape=jax.ShapeDtypeStruct((rows, half), jnp.bfloat16),
        compiler_params=params(),
        cost_estimate=SMALL,
        name="pack",
    )(state, align, *arrays)


def merge_kernel(lyric, state_ref, key_ref, value_ref, lkey_ref, lvalue_ref, mate_ref, *refs):
    frames = key_ref.shape[0]
    first = mate_ref.shape[0] - 2 * frames
    one_ref, mid_ref = refs[-2:]
    if lyric:
        pair_ref = refs[-3]
        pair_ref[0:lyric, :] = lkey_ref[...]
        pair_ref[lyric : 2 * lyric, :] = lvalue_ref[...]
        pair_ref[2 * lyric :, :] = mate_ref[0 : 2 * lyric, :]
        one_ref[0 : 4 * lyric, :] = pair_ref[...]
    for ref, start, touching in ((one_ref, 4 * lyric, 1), (mid_ref, 0, 0)):
        mine = state_ref[1] == touching
        ref[start : start + frames, :] = jnp.where(
            mine, key_ref[...], mate_ref[first : first + frames, :]
        )
        ref[start + frames :, :] = jnp.where(
            mine, value_ref[...], mate_ref[first + frames :, :]
        )


def merge(state, chunk, key, value, lyric_key, lyric_value, mate, with_lyric, after):
    frames, width = key.shape
    lyric = lyric_key.shape[0] if with_lyric else 0
    size = width // 2 // CHUNKS
    step = size // 2
    out_rows = ([4 * lyric] if lyric else []) + [2 * frames + 4 * lyric, 2 * frames]

    def own(array):
        return pl.BlockSpec(
            (array.shape[0], step), lambda i, state: (0, (state[0] * CHUNKS + chunk) * 2 + i)
        )

    return pl.pallas_call(
        functools.partial(merge_kernel, lyric),
        grid_spec=pltpu.PrefetchScalarGridSpec(
            num_scalar_prefetch=1,
            grid=(2,),
            in_specs=[own(key), own(value), own(lyric_key), own(lyric_value)]
            + [pl.BlockSpec((mate.shape[0], step), lambda i, state: (0, chunk * 2 + i))]
            + [pl.BlockSpec(memory_space=pl.ANY)] * len(after),
            out_specs=[pl.BlockSpec((rows, step), lambda i, state: (0, i)) for rows in out_rows],
        ),
        out_shape=[jax.ShapeDtypeStruct((rows, size), jnp.bfloat16) for rows in out_rows],
        compiler_params=params(),
        cost_estimate=SMALL,
        name="merge",
    )(state, key, value, lyric_key, lyric_value, mate, *after)


def attention_kernel(
    groups, chained, head_size, score_scale, meta_ref, gain_ref, query_ref, grad_ref, key_ref,
    value_ref, mate_ref, one_ref, mid_ref, *refs
):
    frames = query_ref.shape[0]
    exchanged = len(groups) == 4
    inputs = 3 if exchanged else 1
    lyric_in, refs = refs[:inputs], refs[inputs:]
    window = one_ref.shape[0] - 2 * frames
    if chained:
        gain_before_ref, refs = refs[0], refs[3:]
    out_ref, grad_query_ref, to_mate_ref, key_grad_ref, value_grad_ref = refs[:5]
    to_one_ref, to_mid_ref, gain_grad_ref = refs[5:8]
    lyric_out, mask_ref = refs[8:-1], refs[-1]
    runs = [(index, run) for index, group in enumerate(groups) for run in group]
    main = 2 * frames + sum(run[2] for _, run in runs)
    lanes = 2 * frames
    first = mate_ref.shape[0] - 4 * frames
    touching = meta_ref[1] == 1

    @pl.when(pl.program_id(0) == 0)
    def _():
        if chained:
            gain_grad_ref[...] = gain_before_ref[...]
        else:
            gain_grad_ref[...] = jnp.zeros_like(gain_grad_ref)
        mate_tiles = mate_ref[first - 16 : first, 0:frames].astype(jnp.float32).astype(jnp.int32)
        start = 0
        for number, (_, (_, _, rows)) in enumerate(runs):
            row = lax.broadcasted_iota(jnp.int32, (rows, lanes), 0) + meta_ref[7 + number]
            keep = jnp.zeros((rows, lanes), jnp.float32)
            for slot in range(TILES):
                tile = jnp.concatenate(
                    [
                        jnp.full((1, frames), meta_ref[2 + slot], jnp.int32),
                        mate_tiles[slot : slot + 1],
                    ],
                    axis=1,
                )
                lower = tile * BLK
                upper = jnp.minimum(lower + BLK, meta_ref[4])
                inside = (row >= lower) & (row < upper) & (lower >= 0)
                keep = jnp.where(inside, 1.0, keep)
            mask_ref[start : start + rows, :] = keep
            start += rows
        lane = lax.broadcasted_iota(jnp.int32, (frames, lanes), 1)
        mask_ref[start : start + frames, :] = jnp.where(
            lane < frames, meta_ref[5], meta_ref[6]
        ).astype(jnp.float32)

    q_gain = gain_ref[0:1, :]
    k_gain = gain_ref[1:2, :]
    for head in range(query_ref.shape[1] // head_size):
        cols = slice(head * head_size, (head + 1) * head_size)
        lyric = [ref[:, cols] for ref in lyric_in]
        if exchanged:
            lyric = [lyric[0], lyric[1], one_ref[0:window, cols], lyric[2]]
        one_rows, mid_rows = one_ref[window:, cols], mid_ref[:, cols]
        near_rows = jnp.where(touching, one_rows, mid_rows)
        far_rows = jnp.where(touching, mid_rows, one_rows)

        def from_mate(number):
            return mate_ref[first + number * frames : first + (number + 1) * frames, cols]

        query = jnp.concatenate([query_ref[:, cols], from_mate(0)], axis=0)
        query = query.astype(jnp.float32)
        cot = jnp.concatenate([grad_ref[:, cols], from_mate(1)], axis=0)
        raw_keys = jnp.concatenate(
            [key_ref[:, cols], from_mate(2)]
            + [lyric[index][run[0] : run[0] + run[2]] for index, run in runs]
            + [near_rows[:frames], far_rows[:frames]],
            axis=0,
        ).astype(jnp.float32)
        value = jnp.concatenate(
            [value_ref[:, cols], from_mate(3)]
            + [lyric[index][run[1] : run[1] + run[2]] for index, run in runs]
            + [near_rows[frames:], far_rows[frames:]],
            axis=0,
        )
        query_inv = lax.rsqrt(jnp.mean(query * query, axis=1, keepdims=True) + NORM_EPS)
        key_inv = lax.rsqrt(jnp.mean(raw_keys * raw_keys, axis=1, keepdims=True) + NORM_EPS)
        query_hat = query * query_inv
        query_low = (query_hat * (q_gain * score_scale)).astype(jnp.bfloat16)
        key_hat = raw_keys * key_inv
        key_low = (key_hat * k_gain).astype(jnp.bfloat16)

        near, far = slice(main, main + frames), slice(main + frames, main + 2 * frames)

        def against(rows, columns):
            return jnp.concatenate(
                [
                    dot(rows[:main], columns, 1, 1),
                    jnp.concatenate(
                        [
                            dot(rows[near], columns[:frames], 1, 1),
                            dot(rows[far], columns[frames:], 1, 1),
                        ],
                        axis=1,
                    ),
                ],
                axis=0,
            )

        def over_keys(weights, rows):
            return dot(weights[:main], rows[:main], 0, 0) + jnp.concatenate(
                [
                    dot(weights[main:, :frames], rows[near], 0, 0),
                    dot(weights[main:, frames:], rows[far], 0, 0),
                ],
                axis=0,
            )

        def over_queries(weights, columns):
            return jnp.concatenate(
                [
                    dot(weights[:main], columns, 1, 0),
                    dot(weights[main:, :frames], columns[:frames], 1, 0),
                    dot(weights[main:, frames:], columns[frames:], 1, 0),
                ],
                axis=0,
            )

        exp_scores = jnp.exp(against(key_low, query_low))
        exp_scores = jnp.concatenate(
            [exp_scores[: 2 * frames], exp_scores[2 * frames :] * mask_ref[...]], axis=0
        )
        grad_prob = against(value, cot)
        prob = exp_scores * (1.0 / jnp.sum(exp_scores, axis=0, keepdims=True))
        prob_low = prob.astype(jnp.bfloat16)
        weighted = prob * grad_prob
        delta = jnp.sum(weighted, axis=0, keepdims=True)
        grad_score = (weighted - prob * delta).astype(jnp.bfloat16)
        output = over_keys(prob_low, value).astype(jnp.bfloat16)
        grad_qn = over_keys(grad_score, key_low) * score_scale
        grad_keys = over_queries(grad_score, query_low)
        grad_values = over_queries(prob_low, cot)
        scaled = grad_qn * q_gain
        grad_query = (
            query_inv * scaled
            - query_hat
            * (query_inv * query_inv)
            * jnp.mean(scaled * query, axis=1, keepdims=True)
        ).astype(jnp.bfloat16)
        gain_grad_ref[0:1, :] += jnp.sum(grad_qn * query_hat, axis=0, keepdims=True)
        gain_grad_ref[1:2, :] += jnp.sum(grad_keys * key_hat, axis=0, keepdims=True)

        out_ref[:, cols] = output[:frames]
        grad_query_ref[:, cols] = grad_query[:frames]
        to_mate_ref[0:frames, cols] = output[frames:]
        to_mate_ref[frames:, cols] = grad_query[frames:]
        key_grad_ref[:, cols] = grad_keys[: 2 * frames]
        value_grad_ref[:, cols] = grad_values[: 2 * frames]
        for grads, part in (
            (grad_keys.astype(jnp.bfloat16), 0),
            (grad_values.astype(jnp.bfloat16), frames),
        ):
            to_one_ref[window + part : window + part + frames, cols] = jnp.where(
                touching, grads[near], grads[far]
            )
            to_mid_ref[part : part + frames, cols] = jnp.where(touching, grads[far], grads[near])
        if exchanged:
            held_ref, two_ref, to_two_ref = lyric_out
            outs = (held_ref, two_ref, to_one_ref, to_two_ref)
        else:
            outs = lyric_out
        start = 2 * frames
        for index, (key_row, value_row, rows) in runs:
            part = slice(start, start + rows)
            outs[index][key_row : key_row + rows, cols] = grad_keys[part].astype(jnp.bfloat16)
            outs[index][value_row : value_row + rows, cols] = grad_values[part].astype(
                jnp.bfloat16
            )
            start += rows


def attention(chunk, meta, gains, query, cot, key, value, mate, one, mid, lyrics, groups, carried):
    frames, width = query.shape
    head_size = gains.shape[1]
    size = width // 2 // CHUNKS
    step = HEADS_PER_STEP * head_size
    steps = size // step
    lyric_rows = sum(run[2] for group in groups for run in group)
    lanes = 2 * frames
    key_rows = 3 * frames + lyric_rows
    exchanged = len(groups) == 4

    def own(rows):
        return pl.BlockSpec(
            (rows, step), lambda i, meta: (0, (meta[0] * CHUNKS + chunk) * steps + i)
        )

    def columns(rows):
        return pl.BlockSpec((rows, step), lambda i, meta: (0, i))

    def either(array):
        return own(array.shape[0]) if array.shape[1] == width else columns(array.shape[0])

    whole = lambda i, meta: (0, 0)
    bf16, f32 = jnp.bfloat16, jnp.float32
    out_rows = [(2 * frames, bf16), (2 * frames, f32), (2 * frames, f32)]
    out_rows += [(one.shape[0], bf16), (2 * frames, bf16)]
    slot = sum(2 * run[2] for run in groups[0])
    extra_rows = [slot] * (3 if exchanged else 1)
    return pl.pallas_call(
        functools.partial(
            attention_kernel, groups, bool(carried), head_size, head_size ** (-0.5)
        ),
        grid_spec=pltpu.PrefetchScalarGridSpec(
            num_scalar_prefetch=1,
            grid=(steps,),
            in_specs=[pl.BlockSpec(gains.shape, whole)]
            + [own(frames)] * 4
            + [
                pl.BlockSpec((mate.shape[0], step), lambda i, meta: (0, chunk * steps + i)),
                columns(one.shape[0]),
                columns(mid.shape[0]),
            ]
            + [either(array) for array in lyrics]
            + [pl.BlockSpec((8, head_size), whole)] * bool(carried)
            + [pl.BlockSpec(memory_space=pl.ANY)] * len(carried[1:]),
            out_specs=[own(frames)] * 2
            + [columns(rows) for rows, _ in out_rows]
            + [pl.BlockSpec((8, head_size), whole)]
            + [columns(rows) for rows in extra_rows],
            scratch_shapes=[pltpu.VMEM((frames + lyric_rows, lanes), f32)],
        ),
        out_shape=[jax.ShapeDtypeStruct((frames, width), bf16)] * 2
        + [jax.ShapeDtypeStruct((rows, size), dtype) for rows, dtype in out_rows]
        + [jax.ShapeDtypeStruct((8, head_size), f32)]
        + [jax.ShapeDtypeStruct((rows, size), bf16) for rows in extra_rows],
        input_output_aliases={10 + len(lyrics) + i: i for i in range(len(carried[1:]))},
        compiler_params=params(ATTENTION_VMEM_LIMIT),
        cost_estimate=pl.CostEstimate(
            flops=12 * key_rows * lanes * size,
            bytes_accessed=16 * 1024 * 1024 // CHUNKS,
            transcendentals=key_rows * lanes * (size // head_size),
        ),
        name="attention",
    )(meta, gains, query, cot, key, value, mate, one, mid, *lyrics, *carried)


def fill_kernel(count, core_ref, mate_ref, *refs):
    for index, ref in enumerate(refs[-count:]):
        rows = ref.shape[0]
        ref[...] = mate_ref[index * rows : (index + 1) * rows, :]


def fill_other(core, chunk, arrays, mate):
    frames, width = arrays[0].shape
    count = len(arrays)
    size = width // 2 // CHUNKS
    step = size // 2
    spec = pl.BlockSpec(
        (frames, step), lambda i, core: (0, ((1 - core[0]) * CHUNKS + chunk) * 2 + i)
    )
    return pl.pallas_call(
        functools.partial(fill_kernel, count),
        grid_spec=pltpu.PrefetchScalarGridSpec(
            num_scalar_prefetch=1,
            grid=(2,),
            in_specs=[pl.BlockSpec((mate.shape[0], step), lambda i, core: (0, i))]
            + [pl.BlockSpec(memory_space=pl.ANY)] * count,
            out_specs=[spec] * count,
        ),
        out_shape=[jax.ShapeDtypeStruct(array.shape, array.dtype) for array in arrays],
        input_output_aliases={2 + i: i for i in range(count)},
        compiler_params=params(),
        cost_estimate=SMALL,
        name="fill_other",
    )(core, mate, *arrays)


def through_norm(raw, grad, k_gain):
    raw = raw.astype(jnp.float32)
    inverse = lax.rsqrt(jnp.mean(raw * raw, axis=1, keepdims=True) + NORM_EPS)
    scaled = grad * k_gain
    return (
        inverse * scaled
        - raw * (inverse * inverse * inverse) * jnp.mean(scaled * raw, axis=1, keepdims=True)
    ).astype(jnp.bfloat16)


def finish_audio_kernel(
    head_size, state_ref, gain_ref, raw_ref, mate_ref, key_grad_ref, value_grad_ref, one_ref,
    mid_ref, ready_ref, *refs,
):
    k_gain = gain_ref[1:2, :]
    grad_key_ref, grad_value_ref, to_mate_ref = refs[-3:]
    frames = raw_ref.shape[0]
    own, mate = slice(0, frames), slice(frames, 2 * frames)
    first = one_ref.shape[0] - 2 * frames
    touching = state_ref[1] == 1
    mate_keys = mate_ref.shape[0] - 2 * frames
    to_mate_ref[0 : 2 * frames, :] = ready_ref[...]
    for head in range(raw_ref.shape[1] // head_size):
        cols = slice(head * head_size, (head + 1) * head_size)
        one = one_ref[first:, cols].astype(jnp.float32)
        mid = mid_ref[:, cols].astype(jnp.float32)
        for_own = jnp.where(touching, one, mid)
        for_mate = jnp.where(touching, mid, one)
        grad_key_ref[:, cols] = through_norm(
            raw_ref[:, cols], key_grad_ref[own, cols] + for_own[:frames], k_gain
        )
        grad_value_ref[:, cols] = (value_grad_ref[own, cols] + for_own[frames:]).astype(
            jnp.bfloat16
        )
        to_mate_ref[2 * frames : 3 * frames, cols] = through_norm(
            mate_ref[mate_keys : mate_keys + frames, cols],
            key_grad_ref[mate, cols] + for_mate[:frames],
            k_gain,
        )
        to_mate_ref[3 * frames : 4 * frames, cols] = (
            value_grad_ref[mate, cols] + for_mate[frames:]
        ).astype(jnp.bfloat16)


def finish_audio(state, chunk, gains, raw, mate, key_grad, value_grad, one, mid, ready, carried):
    frames, width = raw.shape
    head_size = gains.shape[1]
    size = width // 2 // CHUNKS
    step = size // 2

    def columns(array):
        return pl.BlockSpec((array.shape[0], step), lambda i, core: (0, i))

    own = pl.BlockSpec((frames, step), lambda i, core: (0, (core[0] * CHUNKS + chunk) * 2 + i))
    arrays = (key_grad, value_grad, one, mid, ready)
    return pl.pallas_call(
        functools.partial(finish_audio_kernel, head_size),
        grid_spec=pltpu.PrefetchScalarGridSpec(
            num_scalar_prefetch=1,
            grid=(2,),
            in_specs=[pl.BlockSpec(gains.shape, lambda i, core: (0, 0)), own]
            + [pl.BlockSpec((mate.shape[0], step), lambda i, core: (0, chunk * 2 + i))]
            + [columns(array) for array in arrays]
            + [pl.BlockSpec(memory_space=pl.ANY)] * len(carried),
            out_specs=[own] * 2 + [pl.BlockSpec((4 * frames, step), lambda i, core: (0, i))],
        ),
        out_shape=[jax.ShapeDtypeStruct((frames, width), jnp.bfloat16)] * 2
        + [jax.ShapeDtypeStruct((5 * frames, size), jnp.bfloat16)],
        input_output_aliases={9 + i: i for i in range(len(carried))},
        compiler_params=params(),
        cost_estimate=SMALL,
        name="finish_audio",
    )(state, gains, raw, mate, *arrays, *carried)


def relay_kernel(head_size, part_ref, arrived_ref, *refs):
    out_ref = refs[-1]
    rows = part_ref.shape[0]
    out_ref[0:rows, :] = (
        part_ref[...].astype(jnp.float32) + arrived_ref[...].astype(jnp.float32)
    ).astype(jnp.bfloat16)
    if len(refs) == 2:
        out_ref[rows:, 0:head_size] = split_rows(refs[0][...])
        out_ref[rows:, head_size:] = jnp.zeros_like(out_ref[rows:, head_size:])


def relay(part, arrived, sums):
    rows, size = part.shape
    step = size // 2
    out_rows = rows + GAIN_ROWS * len(sums)
    spec = pl.BlockSpec((rows, step), lambda i: (0, i))
    return pl.pallas_call(
        functools.partial(relay_kernel, sums[0].shape[1] if sums else 0),
        grid=(2,),
        in_specs=[spec] * 2 + [pl.BlockSpec(total.shape, lambda i: (0, 0)) for total in sums],
        out_specs=pl.BlockSpec((out_rows, step), lambda i: (0, i)),
        out_shape=jax.ShapeDtypeStruct((out_rows, size), jnp.bfloat16),
        compiler_params=params(),
        cost_estimate=SMALL,
        name="relay",
    )(part, arrived, *sums)


def finish_lyric_kernel(head_size, gain_ref, raw_ref, held_ref, one_ref, two_ref, *refs):
    lyric_rows = raw_ref.shape[0]
    rows = lyric_rows // 4
    own_ref, to_mate_ref, total_ref = refs[-3:]
    k_gain = gain_ref[1:2, :]
    if len(refs) == 5:
        total_ref[...] = refs[0][...] + joined_rows(two_ref[lyric_rows:, 0:head_size])
    else:
        total_ref[...] = jnp.zeros_like(total_ref)
    for head in range(raw_ref.shape[1] // head_size):
        cols = slice(head * head_size, (head + 1) * head_size)
        total = held_ref[:, cols].astype(jnp.float32)
        for part in (one_ref, two_ref):
            total = total + part[0:lyric_rows, cols].astype(jnp.float32)
        for index, ref in enumerate((own_ref, to_mate_ref)):
            base = 2 * rows * index
            ref[0:rows, cols] = through_norm(
                raw_ref[base : base + rows, cols], total[base : base + rows], k_gain
            )
            ref[rows : 2 * rows, cols] = total[base + rows : base + 2 * rows].astype(jnp.bfloat16)
        to_mate_ref[2 * rows :, cols] = split_rows(total_ref[...])


def finish_lyric(gains, raw, held, one, two, sums, to_mate):
    rows, size = raw.shape
    head_size = gains.shape[1]
    step = size // 2
    tail = rows // 2 + GAIN_ROWS
    last = to_mate.shape[0] // tail - 1
    spec = pl.BlockSpec((rows, step), lambda i: (0, i))
    whole = pl.BlockSpec((8, head_size), lambda i: (0, 0))
    return pl.pallas_call(
        functools.partial(finish_lyric_kernel, head_size),
        grid=(2,),
        in_specs=[pl.BlockSpec(gains.shape, lambda i: (0, 0)), spec, spec, spec]
        + [pl.BlockSpec((two.shape[0], step), lambda i: (0, i))]
        + [whole] * len(sums)
        + [pl.BlockSpec(memory_space=pl.ANY)],
        out_specs=[
            pl.BlockSpec((rows // 2, step), lambda i: (0, i)),
            pl.BlockSpec((tail, step), lambda i: (last, i)),
            whole,
        ],
        out_shape=[
            jax.ShapeDtypeStruct((rows // 2, size), jnp.bfloat16),
            jax.ShapeDtypeStruct(to_mate.shape, jnp.bfloat16),
            jax.ShapeDtypeStruct((8, head_size), jnp.float32),
        ],
        input_output_aliases={5 + len(sums): 1},
        compiler_params=params(),
        cost_estimate=SMALL,
        name="finish_lyric",
    )(gains, raw, held, one, two, *sums, to_mate)


def join_kernel(count, chunks, state_ref, gain_ref, *refs):
    owns, mates, outs = refs[:chunks], refs[chunks : 2 * chunks], refs[-count - 3 :]
    grad_key_ref, grad_value_ref, total_ref = outs[count:]
    rows, size = grad_key_ref.shape[0], owns[0].shape[1]
    frames = outs[0].shape[0]
    for index, ref in enumerate(outs[:count]):
        ref[...] = mates[-1][index * frames : (index + 1) * frames, :]
    for part, parts, first in (
        (state_ref[0], owns, 0),
        (1 - state_ref[0], mates, count * frames),
    ):
        for chunk, ref in enumerate(parts):
            cols = pl.ds(pl.multiple_of((part * chunks + chunk) * size, size), size)
            grad_key_ref[:, cols] = ref[first : first + rows, :]
            grad_value_ref[:, cols] = ref[first + rows : first + 2 * rows, :]
    sums = mates[-1][mates[-1].shape[0] - GAIN_ROWS :, 0 : gain_ref.shape[1]]
    total_ref[...] = gain_ref[...] + joined_rows(sums)


def join(state, gain, arrays, own, mate):
    rows, size = own[0].shape
    frames, width = arrays[0].shape
    count, chunks = len(arrays), len(own)
    whole = lambda i, state: (0, 0)
    other = pl.BlockSpec(
        (frames, size), lambda i, state: (0, (1 - state[0]) * chunks + chunks - 1)
    )
    return pl.pallas_call(
        functools.partial(join_kernel, count, chunks),
        grid_spec=pltpu.PrefetchScalarGridSpec(
            num_scalar_prefetch=1,
            grid=(1,),
            in_specs=[pl.BlockSpec(array.shape, whole) for array in [gain, *own, *mate]]
            + [pl.BlockSpec(memory_space=pl.ANY)] * count,
            out_specs=[other] * count
            + [pl.BlockSpec((rows // 2, width), whole)] * 2
            + [pl.BlockSpec(gain.shape, whole)],
        ),
        out_shape=[jax.ShapeDtypeStruct(array.shape, array.dtype) for array in arrays]
        + [jax.ShapeDtypeStruct((rows // 2, width), jnp.bfloat16)] * 2
        + [jax.ShapeDtypeStruct(gain.shape, jnp.float32)],
        input_output_aliases={2 + 2 * chunks + i: i for i in range(count)},
        compiler_params=params(),
        cost_estimate=SMALL,
        name="join",
    )(state, gain, *own, *mate, *arrays)


def norm_lyric_kernel(head_size, gain_ref, raw_ref, grad_ref, out_ref):
    for head in range(raw_ref.shape[1] // head_size):
        cols = slice(head * head_size, (head + 1) * head_size)
        out_ref[:, cols] = through_norm(raw_ref[:, cols], grad_ref[:, cols], gain_ref[1:2, :])


def norm_lyric(gains, raw, grad):
    return pl.pallas_call(
        functools.partial(norm_lyric_kernel, gains.shape[1]),
        out_shape=jax.ShapeDtypeStruct(raw.shape, jnp.bfloat16),
        name="norm_lyric",
    )(gains, raw, grad)


def sum_over(total, axis, bits):
    count = lax.axis_size(axis)
    for bit in bits:
        total = total + lax.ppermute(total, axis, [(i, i ^ bit) for i in range(count)])
    return total


def bits_of(count):
    return [1 << bit for bit in range(count.bit_length() - 1)]


def body(
    queries, keys, values, lyric_keys, lyric_values, q_gain, k_gain, cotangent, alignment, lyric_len
):
    frames = queries.shape[1]
    lyric_local, width = lyric_keys.shape[1:]
    count = lax.axis_size("seq")
    songs = lax.axis_size("song")
    me = lax.axis_index("seq")
    core = me % 2
    chips = count // 2
    chip = me // 2
    touching = (chip % 2) ^ core
    state = jnp.stack([core, touching]).astype(jnp.int32)
    gains = jnp.stack([q_gain, k_gain])

    swap = [(i, i ^ 1) for i in range(count)]
    partners = [(a, a ^ 1) for a in range(chips)]
    across = [(a, a ^ 2) for a in range(chips)]
    between = [(a, a + 1) for a in range(1, chips - 1, 2)]
    between += [(b, a) for a, b in between]

    def hop(block, moves):
        pairs = [(2 * a + c, 2 * b + c) for a, b in moves for c in (0, 1)]
        return lax.ppermute(block, "seq", pairs)

    hops = chips == 4 and lyric_local % 16 == 0 and 2 * lyric_local + GAIN_ROWS == frames
    total_rows = lyric_local * count
    if hops:
        run = ((0, lyric_local, lyric_local), (2 * lyric_local, 3 * lyric_local, lyric_local))
        groups = (run,) * 4
        owners = [chip, chip ^ 2, chip ^ 1, chip ^ 3]
        first_rows = []
        for owner in owners:
            first_rows += [
                (2 * owner + core) * lyric_local,
                (2 * owner + 1 - core) * lyric_local,
            ]
    else:
        gathered = jnp.concatenate(
            [
                lax.all_gather(lyric_keys[0], "seq", axis=0, tiled=True),
                lax.all_gather(lyric_values[0], "seq", axis=0, tiled=True),
            ],
            axis=0,
        )
        groups = (((0, total_rows, total_rows),),)
        first_rows = [0]
    has_left, has_right = chip > 0, chip < chips - 1
    has_near = jnp.where(core == 0, has_left, has_right)
    has_far = jnp.where(core == 0, has_right, has_left)
    meta = jnp.stack(
        [
            jnp.asarray(value, jnp.int32)
            for value in [core, touching]
            + [alignment[0, 0, slot] for slot in range(TILES)]
            + [lyric_len[0], has_near, has_far]
            + first_rows
        ]
    )

    rows = 4 * lyric_local
    to_mate = pack(
        state,
        alignment[0, 0],
        ([lyric_keys[0], lyric_values[0]] if hops else [])
        + [queries[0], cotangent[0], keys[0], values[0]],
    )
    mate = lax.ppermute(to_mate, "seq", swap)
    attended = []
    carried = []
    after = []
    for chunk in range(CHUNKS):
        *pair, to_one, to_mid = merge(
            state, chunk, keys[0], values[0], lyric_keys[0], lyric_values[0], mate, hops, after
        )
        if hops:
            two = hop(pair[0], across)
        one = hop(to_one, partners)
        mid = hop(to_mid, between)
        if hops:
            lyrics = [pair[0], two, hop(two, partners)]
            after = [two]
        else:
            lyrics = [gathered]
        results = attention(
            chunk, meta, gains, queries[0], cotangent[0], keys[0], values[0], mate, one, mid,
            lyrics, groups, carried,
        )
        carried = [results[7], *results[:2]]
        attended.append((results[2:], lyrics))
    gain_total, output, grad_queries = carried

    grads = []
    own_halves, lyric_cols, from_mates = [], [], []
    if hops:
        gain_total = sum_over(sum_over(gain_total, "song", bits_of(songs)), "seq", [2])
    for chunk, (results, lyrics) in enumerate(attended):
        for_mate, key_grad, value_grad, to_one, to_mid, _, *parts = results
        one = hop(to_one, partners)
        mid = hop(to_mid, between)
        *grads, for_mate = finish_audio(
            state, chunk, gains, keys[0], mate, key_grad, value_grad, one, mid, for_mate, grads
        )
        if hops:
            held, for_two, to_two = parts
            sums = [gain_total] if chunk == CHUNKS - 1 else []
            two = hop(relay(for_two, hop(to_two, partners), sums), across)
            own_half, for_mate, total = finish_lyric(
                gains, lyrics[0], held, one, two, sums, for_mate
            )
            own_halves.append(own_half)
        else:
            lyric_cols.append(parts[0])
        from_mates.append(lax.ppermute(for_mate, "seq", swap))
    filled = [output, grad_queries, *grads]
    for chunk, from_mate in enumerate(from_mates[: CHUNKS - hops]):
        filled = fill_other(state, chunk, filled, from_mate)
    if hops:
        *filled, grad_lyric_keys, grad_lyric_values, gain_total = join(
            state, total, filled, own_halves, from_mates
        )
    else:
        gain_total = lax.psum(gain_total, ("song", "seq"))
        spread = lax.dynamic_update_slice(
            jnp.zeros((2 * total_rows, width), jnp.float32),
            jnp.concatenate(lyric_cols, axis=1).astype(jnp.float32),
            (0, core * (width // 2)),
        )
        lyric_key_sum, grad_lyric_values = [
            lax.psum_scatter(part, "seq", scatter_dimension=0, tiled=True)
            for part in (spread[:total_rows], spread[total_rows:])
        ]
        grad_lyric_keys = norm_lyric(gains, lyric_keys[0], lyric_key_sum)
        grad_lyric_values = grad_lyric_values.astype(jnp.bfloat16)
    output, grad_queries, grad_keys, grad_values = filled
    return (
        output[None],
        grad_queries[None],
        grad_keys[None],
        grad_values[None],
        grad_lyric_keys[None],
        grad_lyric_values[None],
        gain_total[0],
        gain_total[1],
    )


def solution(mesh):
    split = P("song", "seq", None)
    return jax.shard_map(
        body,
        mesh=mesh,
        in_specs=(split, split, split, split, split, P(), P(), split, split, P("song")),
        out_specs=(split, split, split, split, split, split, P(), P()),
        check_vma=False,
    )
```

```python
import functools

import jax
import jax.numpy as jnp
from jax import lax
from jax.experimental import pallas as pl
from jax.experimental.pallas import tpu as pltpu
from jax.sharding import PartitionSpec as P

BLK = 128
TILES = 2
NORM_EPS = 1e-06
HEADS_PER_STEP = 1
CHUNKS = 1
VMEM_LIMIT = 8 * 1024 * 1024
ATTENTION_VMEM_LIMIT = 24 * 1024 * 1024
PACK_VMEM_LIMIT = 60 * 1024 * 1024
GAIN_ROWS = 32
ALIGN_ROWS = 32
SMALL = pl.CostEstimate(flops=1, bytes_accessed=1, transcendentals=0)


def dot(lhs, rhs, lhs_dim, rhs_dim):
    return lax.dot_general(
        lhs, rhs, (((lhs_dim,), (rhs_dim,)), ((), ())), preferred_element_type=jnp.float32
    )


def params(limit=VMEM_LIMIT):
    return pltpu.CompilerParams(dimension_semantics=("arbitrary",), vmem_limit_bytes=limit)


def split_rows(sums):
    high = sums.astype(jnp.bfloat16).astype(jnp.float32)
    rest = sums - high
    middle = rest.astype(jnp.bfloat16).astype(jnp.float32)
    low = rest - middle
    return jnp.concatenate([high, middle, low, jnp.zeros_like(high)], axis=0).astype(jnp.bfloat16)


def joined_rows(rows):
    rows = rows.astype(jnp.float32)
    return (rows[16:24] + rows[8:16]) + rows[0:8]


def pack_kernel(state_ref, align_ref, *refs):
    out_ref = refs[-1]
    start = 0
    for ref in refs[:-1]:
        out_ref[start : start + ref.shape[0], :] = ref[...]
        start += ref.shape[0]
    row = lax.broadcasted_iota(jnp.int32, (ALIGN_ROWS, out_ref.shape[1]), 0)
    tiles = jnp.zeros((ALIGN_ROWS, out_ref.shape[1]), jnp.int32)
    for slot in range(TILES):
        tiles = jnp.where(row == slot, align_ref[slot], tiles)
    out_ref[start:, :] = tiles.astype(jnp.float32).astype(jnp.bfloat16)


def pack(state, align, arrays):
    width = arrays[0].shape[1]
    half = width // 2
    step = half // 4
    rows = sum(array.shape[0] for array in arrays) + ALIGN_ROWS
    return pl.pallas_call(
        pack_kernel,
        grid_spec=pltpu.PrefetchScalarGridSpec(
            num_scalar_prefetch=2,
            grid=(4,),
            in_specs=[
                pl.BlockSpec(
                    (array.shape[0], step), lambda i, state, _: (0, (1 - state[0]) * 4 + i)
                )
                for array in arrays
            ],
            out_specs=pl.BlockSpec((rows, step), lambda i, state, _: (0, i)),
        ),
        out_shape=jax.ShapeDtypeStruct((rows, half), jnp.bfloat16),
        compiler_params=params(PACK_VMEM_LIMIT),
        cost_estimate=SMALL,
        name="pack",
    )(state, align, *arrays)


def pair_kernel(state_ref, lkey_ref, lvalue_ref, mate_ref, pair_ref):
    lyric = lkey_ref.shape[0]
    pair_ref[0:lyric, :] = lkey_ref[...]
    pair_ref[lyric : 2 * lyric, :] = lvalue_ref[...]
    pair_ref[2 * lyric :, :] = mate_ref[0 : 2 * lyric, :]


def pair_lyrics(state, chunk, lyric_key, lyric_value, mate):
    rows, width = lyric_key.shape
    size = width // 2 // CHUNKS
    step = size // 2
    last = mate.shape[0] // BLK - 1
    own = pl.BlockSpec((rows, step), lambda i, state: (0, (state[0] * CHUNKS + chunk) * 2 + i))
    return pl.pallas_call(
        pair_kernel,
        grid_spec=pltpu.PrefetchScalarGridSpec(
            num_scalar_prefetch=1,
            grid=(2,),
            in_specs=[own, own, pl.BlockSpec((BLK, step), lambda i, state: (last, chunk * 2 + i))],
            out_specs=pl.BlockSpec((4 * rows, step), lambda i, state: (0, i)),
        ),
        out_shape=jax.ShapeDtypeStruct((4 * rows, size), jnp.bfloat16),
        compiler_params=params(),
        cost_estimate=SMALL,
        name="pair_lyrics",
    )(state, lyric_key, lyric_value, mate)


def edge_kernel(touching, state_ref, key_ref, value_ref, mate_key_ref, mate_value_ref, *refs):
    out_ref = refs[-1]
    frames = key_ref.shape[0]
    first = out_ref.shape[0] - 2 * frames
    if first:
        out_ref[0:first, :] = refs[0][...]
    mine = state_ref[1] == touching
    out_ref[first : first + frames, :] = jnp.where(mine, key_ref[...], mate_key_ref[...])
    out_ref[first + frames :, :] = jnp.where(mine, value_ref[...], mate_value_ref[...])


def edge(state, chunk, touching, key, value, mate, lead, after):
    frames, width = key.shape
    size = width // 2 // CHUNKS
    step = size // 2
    rows = sum(array.shape[0] for array in lead) + 2 * frames
    own = pl.BlockSpec((frames, step), lambda i, state: (0, (state[0] * CHUNKS + chunk) * 2 + i))
    return pl.pallas_call(
        functools.partial(edge_kernel, touching),
        grid_spec=pltpu.PrefetchScalarGridSpec(
            num_scalar_prefetch=1,
            grid=(2,),
            in_specs=[own, own]
            + [pl.BlockSpec((frames, step), lambda i, state: (2, chunk * 2 + i))]
            + [pl.BlockSpec((frames, step), lambda i, state: (3, chunk * 2 + i))]
            + [pl.BlockSpec((array.shape[0], step), lambda i, state: (0, i)) for array in lead]
            + [pl.BlockSpec(memory_space=pl.ANY)] * len(after),
            out_specs=pl.BlockSpec((rows, step), lambda i, state: (0, i)),
        ),
        out_shape=jax.ShapeDtypeStruct((rows, size), jnp.bfloat16),
        compiler_params=params(),
        cost_estimate=SMALL,
        name="edge",
    )(state, key, value, mate, mate, *lead, *after)


def attention_kernel(
    groups, chained, head_size, score_scale, meta_ref, gain_ref, query_ref, grad_ref, key_ref,
    value_ref, mate_ref, one_ref, mid_ref, *refs
):
    frames = query_ref.shape[0]
    exchanged = len(groups) == 4
    inputs = 3 if exchanged else 1
    lyric_in, refs = refs[:inputs], refs[inputs:]
    window = one_ref.shape[0] - 2 * frames
    if chained:
        gain_before_ref, refs = refs[0], refs[3:]
    out_ref, grad_query_ref, to_mate_ref, key_grad_ref, value_grad_ref = refs[:5]
    to_one_ref, to_mid_ref, gain_grad_ref = refs[5:8]
    lyric_out, mask_ref = refs[8:-1], refs[-1]
    runs = [(index, run) for index, group in enumerate(groups) for run in group]
    main = 2 * frames + sum(run[2] for _, run in runs)
    lanes = 2 * frames
    align = mate_ref.shape[0] - ALIGN_ROWS
    touching = meta_ref[1] == 1

    @pl.when(pl.program_id(0) == 0)
    def _():
        if chained:
            gain_grad_ref[...] = gain_before_ref[...]
        else:
            gain_grad_ref[...] = jnp.zeros_like(gain_grad_ref)
        mate_tiles = mate_ref[align:, 0:frames].astype(jnp.float32).astype(jnp.int32)
        start = 0
        for number, (_, (_, _, rows)) in enumerate(runs):
            row = lax.broadcasted_iota(jnp.int32, (rows, lanes), 0) + meta_ref[7 + number]
            keep = jnp.zeros((rows, lanes), jnp.float32)
            for slot in range(TILES):
                tile = jnp.concatenate(
                    [
                        jnp.full((1, frames), meta_ref[2 + slot], jnp.int32),
                        mate_tiles[slot : slot + 1],
                    ],
                    axis=1,
                )
                lower = tile * BLK
                upper = jnp.minimum(lower + BLK, meta_ref[4])
                inside = (row >= lower) & (row < upper) & (lower >= 0)
                keep = jnp.where(inside, 1.0, keep)
            mask_ref[start : start + rows, :] = keep
            start += rows
        lane = lax.broadcasted_iota(jnp.int32, (frames, lanes), 1)
        mask_ref[start : start + frames, :] = jnp.where(
            lane < frames, meta_ref[5], meta_ref[6]
        ).astype(jnp.float32)

    q_gain = gain_ref[0:1, :]
    k_gain = gain_ref[1:2, :]
    for head in range(query_ref.shape[1] // head_size):
        cols = slice(head * head_size, (head + 1) * head_size)
        lyric = [ref[:, cols] for ref in lyric_in]
        if exchanged:
            lyric = [lyric[0], lyric[1], one_ref[0:window, cols], lyric[2]]
        one_rows, mid_rows = one_ref[window:, cols], mid_ref[:, cols]
        near_rows = jnp.where(touching, one_rows, mid_rows)
        far_rows = jnp.where(touching, mid_rows, one_rows)

        def from_mate(number):
            return mate_ref[number * frames : (number + 1) * frames, cols]

        query = jnp.concatenate([query_ref[:, cols], from_mate(0)], axis=0)
        query = query.astype(jnp.float32)
        cot = jnp.concatenate([grad_ref[:, cols], from_mate(1)], axis=0)
        raw_keys = jnp.concatenate(
            [key_ref[:, cols], from_mate(2)]
            + [lyric[index][run[0] : run[0] + run[2]] for index, run in runs]
            + [near_rows[:frames], far_rows[:frames]],
            axis=0,
        ).astype(jnp.float32)
        value = jnp.concatenate(
            [value_ref[:, cols], from_mate(3)]
            + [lyric[index][run[1] : run[1] + run[2]] for index, run in runs]
            + [near_rows[frames:], far_rows[frames:]],
            axis=0,
        )
        query_inv = lax.rsqrt(jnp.mean(query * query, axis=1, keepdims=True) + NORM_EPS)
        key_inv = lax.rsqrt(jnp.mean(raw_keys * raw_keys, axis=1, keepdims=True) + NORM_EPS)
        query_hat = query * query_inv
        query_low = (query_hat * (q_gain * score_scale)).astype(jnp.bfloat16)
        key_hat = raw_keys * key_inv
        key_low = (key_hat * k_gain).astype(jnp.bfloat16)

        near, far = slice(main, main + frames), slice(main + frames, main + 2 * frames)

        def against(rows, columns):
            return jnp.concatenate(
                [
                    dot(rows[:main], columns, 1, 1),
                    jnp.concatenate(
                        [
                            dot(rows[near], columns[:frames], 1, 1),
                            dot(rows[far], columns[frames:], 1, 1),
                        ],
                        axis=1,
                    ),
                ],
                axis=0,
            )

        def over_keys(weights, rows):
            return dot(weights[:main], rows[:main], 0, 0) + jnp.concatenate(
                [
                    dot(weights[main:, :frames], rows[near], 0, 0),
                    dot(weights[main:, frames:], rows[far], 0, 0),
                ],
                axis=0,
            )

        def over_queries(weights, columns):
            return jnp.concatenate(
                [
                    dot(weights[:main], columns, 1, 0),
                    dot(weights[main:, :frames], columns[:frames], 1, 0),
                    dot(weights[main:, frames:], columns[frames:], 1, 0),
                ],
                axis=0,
            )

        exp_scores = jnp.exp(against(key_low, query_low))
        exp_scores = jnp.concatenate(
            [exp_scores[: 2 * frames], exp_scores[2 * frames :] * mask_ref[...]], axis=0
        )
        grad_prob = against(value, cot)
        prob = exp_scores * (1.0 / jnp.sum(exp_scores, axis=0, keepdims=True))
        prob_low = prob.astype(jnp.bfloat16)
        weighted = prob * grad_prob
        delta = jnp.sum(weighted, axis=0, keepdims=True)
        grad_score = (weighted - prob * delta).astype(jnp.bfloat16)
        output = over_keys(prob_low, value).astype(jnp.bfloat16)
        grad_qn = over_keys(grad_score, key_low) * score_scale
        grad_keys = over_queries(grad_score, query_low)
        grad_values = over_queries(prob_low, cot)
        scaled = grad_qn * q_gain
        grad_query = (
            query_inv * scaled
            - query_hat
            * (query_inv * query_inv)
            * jnp.mean(scaled * query, axis=1, keepdims=True)
        ).astype(jnp.bfloat16)
        gain_grad_ref[0:1, :] += jnp.sum(grad_qn * query_hat, axis=0, keepdims=True)
        gain_grad_ref[1:2, :] += jnp.sum(grad_keys * key_hat, axis=0, keepdims=True)

        out_ref[:, cols] = output[:frames]
        grad_query_ref[:, cols] = grad_query[:frames]
        to_mate_ref[0:frames, cols] = output[frames:]
        to_mate_ref[frames:, cols] = grad_query[frames:]
        key_grad_ref[:, cols] = grad_keys[: 2 * frames]
        value_grad_ref[:, cols] = grad_values[: 2 * frames]
        for grads, part in (
            (grad_keys.astype(jnp.bfloat16), 0),
            (grad_values.astype(jnp.bfloat16), frames),
        ):
            to_one_ref[window + part : window + part + frames, cols] = jnp.where(
                touching, grads[near], grads[far]
            )
            to_mid_ref[part : part + frames, cols] = jnp.where(touching, grads[far], grads[near])
        if exchanged:
            held_ref, two_ref, to_two_ref = lyric_out
            outs = (held_ref, two_ref, to_one_ref, to_two_ref)
        else:
            outs = lyric_out
        start = 2 * frames
        for index, (key_row, value_row, rows) in runs:
            part = slice(start, start + rows)
            outs[index][key_row : key_row + rows, cols] = grad_keys[part].astype(jnp.bfloat16)
            outs[index][value_row : value_row + rows, cols] = grad_values[part].astype(
                jnp.bfloat16
            )
            start += rows


def attention(chunk, meta, gains, query, cot, key, value, mate, one, mid, lyrics, groups, carried):
    frames, width = query.shape
    head_size = gains.shape[1]
    size = width // 2 // CHUNKS
    step = HEADS_PER_STEP * head_size
    steps = size // step
    lyric_rows = sum(run[2] for group in groups for run in group)
    lanes = 2 * frames
    key_rows = 3 * frames + lyric_rows
    exchanged = len(groups) == 4

    def own(rows):
        return pl.BlockSpec(
            (rows, step), lambda i, meta: (0, (meta[0] * CHUNKS + chunk) * steps + i)
        )

    def columns(rows):
        return pl.BlockSpec((rows, step), lambda i, meta: (0, i))

    def either(array):
        return own(array.shape[0]) if array.shape[1] == width else columns(array.shape[0])

    whole = lambda i, meta: (0, 0)
    bf16, f32 = jnp.bfloat16, jnp.float32
    out_rows = [(2 * frames, bf16), (2 * frames, f32), (2 * frames, f32)]
    out_rows += [(one.shape[0], bf16), (2 * frames, bf16)]
    slot = sum(2 * run[2] for run in groups[0])
    extra_rows = [slot] * (3 if exchanged else 1)
    return pl.pallas_call(
        functools.partial(
            attention_kernel, groups, bool(carried), head_size, head_size ** (-0.5)
        ),
        grid_spec=pltpu.PrefetchScalarGridSpec(
            num_scalar_prefetch=1,
            grid=(steps,),
            in_specs=[pl.BlockSpec(gains.shape, whole)]
            + [own(frames)] * 4
            + [
                pl.BlockSpec((mate.shape[0], step), lambda i, meta: (0, chunk * steps + i)),
                columns(one.shape[0]),
                columns(mid.shape[0]),
            ]
            + [either(array) for array in lyrics]
            + [pl.BlockSpec((8, head_size), whole)] * bool(carried)
            + [pl.BlockSpec(memory_space=pl.ANY)] * len(carried[1:]),
            out_specs=[own(frames)] * 2
            + [columns(rows) for rows, _ in out_rows]
            + [pl.BlockSpec((8, head_size), whole)]
            + [columns(rows) for rows in extra_rows],
            scratch_shapes=[pltpu.VMEM((frames + lyric_rows, lanes), f32)],
        ),
        out_shape=[jax.ShapeDtypeStruct((frames, width), bf16)] * 2
        + [jax.ShapeDtypeStruct((rows, size), dtype) for rows, dtype in out_rows]
        + [jax.ShapeDtypeStruct((8, head_size), f32)]
        + [jax.ShapeDtypeStruct((rows, size), bf16) for rows in extra_rows],
        input_output_aliases={10 + len(lyrics) + i: i for i in range(len(carried[1:]))},
        compiler_params=params(ATTENTION_VMEM_LIMIT),
        cost_estimate=pl.CostEstimate(
            flops=12 * key_rows * lanes * size,
            bytes_accessed=16 * 1024 * 1024 // CHUNKS,
            transcendentals=key_rows * lanes * (size // head_size),
        ),
        name="attention",
    )(meta, gains, query, cot, key, value, mate, one, mid, *lyrics, *carried)


def fill_kernel(count, core_ref, mate_ref, *refs):
    for index, ref in enumerate(refs[-count:]):
        rows = ref.shape[0]
        ref[...] = mate_ref[index * rows : (index + 1) * rows, :]


def fill_other(core, chunk, arrays, mate):
    frames, width = arrays[0].shape
    count = len(arrays)
    size = width // 2 // CHUNKS
    step = size // 2
    spec = pl.BlockSpec(
        (frames, step), lambda i, core: (0, ((1 - core[0]) * CHUNKS + chunk) * 2 + i)
    )
    return pl.pallas_call(
        functools.partial(fill_kernel, count),
        grid_spec=pltpu.PrefetchScalarGridSpec(
            num_scalar_prefetch=1,
            grid=(2,),
            in_specs=[pl.BlockSpec((mate.shape[0], step), lambda i, core: (0, i))]
            + [pl.BlockSpec(memory_space=pl.ANY)] * count,
            out_specs=[spec] * count,
        ),
        out_shape=[jax.ShapeDtypeStruct(array.shape, array.dtype) for array in arrays],
        input_output_aliases={2 + i: i for i in range(count)},
        compiler_params=params(),
        cost_estimate=SMALL,
        name="fill_other",
    )(core, mate, *arrays)


def through_norm(raw, grad, k_gain):
    raw = raw.astype(jnp.float32)
    inverse = lax.rsqrt(jnp.mean(raw * raw, axis=1, keepdims=True) + NORM_EPS)
    scaled = grad * k_gain
    return (
        inverse * scaled
        - raw * (inverse * inverse * inverse) * jnp.mean(scaled * raw, axis=1, keepdims=True)
    ).astype(jnp.bfloat16)


def finish_audio_kernel(
    head_size, state_ref, gain_ref, raw_ref, mate_ref, key_grad_ref, value_grad_ref, one_ref,
    mid_ref, ready_ref, *refs,
):
    k_gain = gain_ref[1:2, :]
    grad_key_ref, grad_value_ref, to_mate_ref = refs[-3:]
    frames = raw_ref.shape[0]
    own, mate = slice(0, frames), slice(frames, 2 * frames)
    first = one_ref.shape[0] - 2 * frames
    touching = state_ref[1] == 1
    to_mate_ref[0 : 2 * frames, :] = ready_ref[...]
    for head in range(raw_ref.shape[1] // head_size):
        cols = slice(head * head_size, (head + 1) * head_size)
        one = one_ref[first:, cols].astype(jnp.float32)
        mid = mid_ref[:, cols].astype(jnp.float32)
        for_own = jnp.where(touching, one, mid)
        for_mate = jnp.where(touching, mid, one)
        grad_key_ref[:, cols] = through_norm(
            raw_ref[:, cols], key_grad_ref[own, cols] + for_own[:frames], k_gain
        )
        grad_value_ref[:, cols] = (value_grad_ref[own, cols] + for_own[frames:]).astype(
            jnp.bfloat16
        )
        to_mate_ref[2 * frames : 3 * frames, cols] = through_norm(
            mate_ref[:, cols], key_grad_ref[mate, cols] + for_mate[:frames], k_gain
        )
        to_mate_ref[3 * frames :, cols] = (
            value_grad_ref[mate, cols] + for_mate[frames:]
        ).astype(jnp.bfloat16)


def finish_audio(
    state, chunk, gains, raw, mate, key_grad, value_grad, one, mid, ready, carried, to_mate
):
    frames, width = raw.shape
    head_size = gains.shape[1]
    size = width // 2 // CHUNKS
    step = size // 2

    def columns(array):
        return pl.BlockSpec((array.shape[0], step), lambda i, core: (0, i))

    own = pl.BlockSpec((frames, step), lambda i, core: (0, (core[0] * CHUNKS + chunk) * 2 + i))
    arrays = (key_grad, value_grad, one, mid, ready)
    aliases = {9 + i: i for i in range(len(carried))}
    if to_mate:
        aliases[9 + len(carried)] = 2
    return pl.pallas_call(
        functools.partial(finish_audio_kernel, head_size),
        grid_spec=pltpu.PrefetchScalarGridSpec(
            num_scalar_prefetch=1,
            grid=(2,),
            in_specs=[pl.BlockSpec(gains.shape, lambda i, core: (0, 0)), own]
            + [pl.BlockSpec((frames, step), lambda i, core: (2, chunk * 2 + i))]
            + [columns(array) for array in arrays]
            + [pl.BlockSpec(memory_space=pl.ANY)] * len(carried + to_mate),
            out_specs=[own] * 2 + [pl.BlockSpec((4 * frames, step), lambda i, core: (0, i))],
        ),
        out_shape=[jax.ShapeDtypeStruct((frames, width), jnp.bfloat16)] * 2
        + [jax.ShapeDtypeStruct((5 * frames, size), jnp.bfloat16)],
        input_output_aliases=aliases,
        compiler_params=params(),
        cost_estimate=SMALL,
        name="finish_audio",
    )(state, gains, raw, mate, *arrays, *carried, *to_mate)


def relay_kernel(head_size, part_ref, arrived_ref, *refs):
    out_ref = refs[-2]
    rows = part_ref.shape[0]
    out_ref[0:rows, :] = (
        part_ref[...].astype(jnp.float32) + arrived_ref[...].astype(jnp.float32)
    ).astype(jnp.bfloat16)
    if head_size:
        out_ref[rows:, 0:head_size] = split_rows(refs[0][...])
        out_ref[rows:, head_size:] = jnp.zeros_like(out_ref[rows:, head_size:])


def relay(part, arrived, sums, later):
    rows, size = part.shape
    step = size // 2
    out_rows = rows + GAIN_ROWS * len(sums)
    spec = pl.BlockSpec((rows, step), lambda i: (0, i))
    return pl.pallas_call(
        functools.partial(relay_kernel, sums[0].shape[1] if sums else 0),
        grid=(2,),
        in_specs=[spec] * 2
        + [pl.BlockSpec(total.shape, lambda i: (0, 0)) for total in sums]
        + [pl.BlockSpec(memory_space=pl.ANY)],
        out_specs=[
            pl.BlockSpec((out_rows, step), lambda i: (0, i)),
            pl.BlockSpec(memory_space=pl.ANY),
        ],
        out_shape=[
            jax.ShapeDtypeStruct((out_rows, size), jnp.bfloat16),
            jax.ShapeDtypeStruct(later.shape, later.dtype),
        ],
        input_output_aliases={2 + len(sums): 1},
        compiler_params=params(),
        cost_estimate=SMALL,
        name="relay",
    )(part, arrived, *sums, later)


def finish_lyric_kernel(head_size, gain_ref, raw_ref, held_ref, one_ref, two_ref, *refs):
    lyric_rows = raw_ref.shape[0]
    rows = lyric_rows // 4
    own_ref, to_mate_ref, total_ref = refs[-3:]
    k_gain = gain_ref[1:2, :]
    if len(refs) == 4:
        total_ref[...] = refs[0][...] + joined_rows(two_ref[lyric_rows:, 0:head_size])
    else:
        total_ref[...] = jnp.zeros_like(total_ref)
    for head in range(raw_ref.shape[1] // head_size):
        cols = slice(head * head_size, (head + 1) * head_size)
        total = held_ref[:, cols].astype(jnp.float32)
        for part in (one_ref, two_ref):
            total = total + part[0:lyric_rows, cols].astype(jnp.float32)
        for index, ref in enumerate((own_ref, to_mate_ref)):
            base = 2 * rows * index
            ref[0:rows, cols] = through_norm(
                raw_ref[base : base + rows, cols], total[base : base + rows], k_gain
            )
            ref[rows : 2 * rows, cols] = total[base + rows : base + 2 * rows].astype(jnp.bfloat16)
        to_mate_ref[2 * rows :, cols] = split_rows(total_ref[...])


def finish_lyric(gains, raw, held, one, two, sums, frames):
    rows, size = raw.shape
    head_size = gains.shape[1]
    step = size // 2
    tail = rows // 2 + GAIN_ROWS
    spec = pl.BlockSpec((rows, step), lambda i: (0, i))
    whole = pl.BlockSpec((8, head_size), lambda i: (0, 0))
    return pl.pallas_call(
        functools.partial(finish_lyric_kernel, head_size),
        grid=(2,),
        in_specs=[pl.BlockSpec(gains.shape, lambda i: (0, 0)), spec, spec, spec]
        + [pl.BlockSpec((two.shape[0], step), lambda i: (0, i))]
        + [whole] * len(sums),
        out_specs=[
            pl.BlockSpec((rows // 2, step), lambda i: (0, i)),
            pl.BlockSpec((tail, step), lambda i: (4 * frames // tail, i)),
            whole,
        ],
        out_shape=[
            jax.ShapeDtypeStruct((rows // 2, size), jnp.bfloat16),
            jax.ShapeDtypeStruct((4 * frames + tail, size), jnp.bfloat16),
            jax.ShapeDtypeStruct((8, head_size), jnp.float32),
        ],
        compiler_params=params(),
        cost_estimate=SMALL,
        name="finish_lyric",
    )(gains, raw, held, one, two, *sums)


def join_kernel(count, chunks, state_ref, gain_ref, *refs):
    owns, mates, outs = refs[:chunks], refs[chunks : 2 * chunks], refs[-count - 4 :]
    grad_key_ref, grad_value_ref, q_total_ref, k_total_ref = outs[count:]
    rows, size = grad_key_ref.shape[0], owns[0].shape[1]
    frames = outs[0].shape[0]
    for index, ref in enumerate(outs[:count]):
        ref[...] = mates[-1][index * frames : (index + 1) * frames, :]
    for part, parts, first in (
        (state_ref[0], owns, 0),
        (1 - state_ref[0], mates, count * frames),
    ):
        for chunk, ref in enumerate(parts):
            cols = pl.ds(pl.multiple_of((part * chunks + chunk) * size, size), size)
            grad_key_ref[:, cols] = ref[first : first + rows, :]
            grad_value_ref[:, cols] = ref[first + rows : first + 2 * rows, :]
    sums = mates[-1][mates[-1].shape[0] - GAIN_ROWS :, 0 : gain_ref.shape[1]]
    total = gain_ref[...] + joined_rows(sums)
    q_total_ref[...] = total[0:1]
    k_total_ref[...] = total[1:2]


def join(state, gain, arrays, own, mate):
    rows, size = own[0].shape
    frames, width = arrays[0].shape
    count, chunks = len(arrays), len(own)
    whole = lambda i, state: (0, 0)
    other = pl.BlockSpec(
        (frames, size), lambda i, state: (0, (1 - state[0]) * chunks + chunks - 1)
    )
    return pl.pallas_call(
        functools.partial(join_kernel, count, chunks),
        grid_spec=pltpu.PrefetchScalarGridSpec(
            num_scalar_prefetch=1,
            grid=(1,),
            in_specs=[pl.BlockSpec(array.shape, whole) for array in [gain, *own, *mate]]
            + [pl.BlockSpec(memory_space=pl.ANY)] * count,
            out_specs=[other] * count
            + [pl.BlockSpec((rows // 2, width), whole)] * 2
            + [pl.BlockSpec((1, gain.shape[1]), whole)] * 2,
        ),
        out_shape=[jax.ShapeDtypeStruct(array.shape, array.dtype) for array in arrays]
        + [jax.ShapeDtypeStruct((rows // 2, width), jnp.bfloat16)] * 2
        + [jax.ShapeDtypeStruct((1, gain.shape[1]), jnp.float32)] * 2,
        input_output_aliases={2 + 2 * chunks + i: i for i in range(count)},
        compiler_params=params(),
        cost_estimate=SMALL,
        name="join",
    )(state, gain, *own, *mate, *arrays)


def norm_lyric_kernel(head_size, gain_ref, raw_ref, grad_ref, out_ref):
    for head in range(raw_ref.shape[1] // head_size):
        cols = slice(head * head_size, (head + 1) * head_size)
        out_ref[:, cols] = through_norm(raw_ref[:, cols], grad_ref[:, cols], gain_ref[1:2, :])


def norm_lyric(gains, raw, grad):
    return pl.pallas_call(
        functools.partial(norm_lyric_kernel, gains.shape[1]),
        out_shape=jax.ShapeDtypeStruct(raw.shape, jnp.bfloat16),
        name="norm_lyric",
    )(gains, raw, grad)


def sum_over(total, axis, bits):
    count = lax.axis_size(axis)
    for bit in bits:
        total = total + lax.ppermute(total, axis, [(i, i ^ bit) for i in range(count)])
    return total


def bits_of(count):
    return [1 << bit for bit in range(count.bit_length() - 1)]


def body(
    queries, keys, values, lyric_keys, lyric_values, q_gain, k_gain, cotangent, alignment, lyric_len
):
    frames = queries.shape[1]
    lyric_local, width = lyric_keys.shape[1:]
    count = lax.axis_size("seq")
    songs = lax.axis_size("song")
    me = lax.axis_index("seq")
    core = me % 2
    chips = count // 2
    chip = me // 2
    touching = (chip % 2) ^ core
    state = jnp.stack([core, touching]).astype(jnp.int32)
    gains = jnp.stack([q_gain, k_gain])

    swap = [(i, i ^ 1) for i in range(count)]
    partners = [(a, a ^ 1) for a in range(chips)]
    across = [(a, a ^ 2) for a in range(chips)]
    between = [(a, a + 1) for a in range(1, chips - 1, 2)]
    between += [(b, a) for a, b in between]

    def hop(block, moves):
        pairs = [(2 * a + c, 2 * b + c) for a, b in moves for c in (0, 1)]
        return lax.ppermute(block, "seq", pairs)

    hops = chips == 4 and lyric_local % 16 == 0 and 2 * lyric_local + GAIN_ROWS == frames
    total_rows = lyric_local * count
    if hops:
        run = ((0, lyric_local, lyric_local), (2 * lyric_local, 3 * lyric_local, lyric_local))
        groups = (run,) * 4
        owners = [chip, chip ^ 2, chip ^ 1, chip ^ 3]
        first_rows = []
        for owner in owners:
            first_rows += [
                (2 * owner + core) * lyric_local,
                (2 * owner + 1 - core) * lyric_local,
            ]
    else:
        gathered = jnp.concatenate(
            [
                lax.all_gather(lyric_keys[0], "seq", axis=0, tiled=True),
                lax.all_gather(lyric_values[0], "seq", axis=0, tiled=True),
            ],
            axis=0,
        )
        groups = (((0, total_rows, total_rows),),)
        first_rows = [0]
    has_left, has_right = chip > 0, chip < chips - 1
    has_near = jnp.where(core == 0, has_left, has_right)
    has_far = jnp.where(core == 0, has_right, has_left)
    meta = jnp.stack(
        [
            jnp.asarray(value, jnp.int32)
            for value in [core, touching]
            + [alignment[0, 0, slot] for slot in range(TILES)]
            + [lyric_len[0], has_near, has_far]
            + first_rows
        ]
    )

    to_mate = pack(
        state,
        alignment[0, 0],
        [queries[0], cotangent[0], keys[0], values[0]]
        + ([lyric_keys[0], lyric_values[0]] if hops else []),
    )
    mate = lax.ppermute(to_mate, "seq", swap)
    attended = []
    carried = []
    for chunk in range(CHUNKS):
        if hops:
            pair = pair_lyrics(state, chunk, lyric_keys[0], lyric_values[0], mate)
            two = hop(pair, across)
            lyrics = [pair, two, hop(two, partners)]
            lead, after = [pair], [two]
        else:
            lyrics, lead, after = [gathered], [], []
        one = hop(edge(state, chunk, 1, keys[0], values[0], mate, lead, []), partners)
        mid = hop(edge(state, chunk, 0, keys[0], values[0], mate, [], after), between)
        results = attention(
            chunk, meta, gains, queries[0], cotangent[0], keys[0], values[0], mate, one, mid,
            lyrics, groups, carried,
        )
        carried = [results[7], *results[:2]]
        attended.append((results[2:], lyrics))
    gain_total, output, grad_queries = carried

    grads = []
    own_halves, lyric_cols, from_mates = [], [], []
    if hops:
        gain_total = sum_over(sum_over(gain_total, "song", bits_of(songs)), "seq", [2])
    for chunk, (results, lyrics) in enumerate(attended):
        for_mate, key_grad, value_grad, to_one, to_mid, _, *parts = results
        to_mate = []
        mid = hop(to_mid, between)
        if hops:
            held, for_two, to_two = parts
            sums = [gain_total] if chunk == CHUNKS - 1 else []
            to_two, to_one = relay(for_two, hop(to_two, partners), sums, to_one)
            two, one = hop(to_two, across), hop(to_one, partners)
            own_half, to_mate, total = finish_lyric(
                gains, lyrics[0], held, one, two, sums, frames
            )
            own_halves.append(own_half)
            to_mate = [to_mate]
        else:
            one = hop(to_one, partners)
            lyric_cols.append(parts[0])
        *grads, for_mate = finish_audio(
            state, chunk, gains, keys[0], mate, key_grad, value_grad, one, mid, for_mate, grads,
            to_mate,
        )
        from_mates.append(lax.ppermute(for_mate, "seq", swap))
    filled = [output, grad_queries, *grads]
    for chunk, from_mate in enumerate(from_mates[: CHUNKS - hops]):
        filled = fill_other(state, chunk, filled, from_mate)
    if hops:
        *filled, grad_lyric_keys, grad_lyric_values, q_total, k_total = join(
            state, total, filled, own_halves, from_mates
        )
    else:
        gain_total = lax.psum(gain_total, ("song", "seq"))
        q_total, k_total = gain_total[0:1], gain_total[1:2]
        spread = lax.dynamic_update_slice(
            jnp.zeros((2 * total_rows, width), jnp.float32),
            jnp.concatenate(lyric_cols, axis=1).astype(jnp.float32),
            (0, core * (width // 2)),
        )
        lyric_key_sum, grad_lyric_values = [
            lax.psum_scatter(part, "seq", scatter_dimension=0, tiled=True)
            for part in (spread[:total_rows], spread[total_rows:])
        ]
        grad_lyric_keys = norm_lyric(gains, lyric_keys[0], lyric_key_sum)
        grad_lyric_values = grad_lyric_values.astype(jnp.bfloat16)
    output, grad_queries, grad_keys, grad_values = filled
    return (
        output[None],
        grad_queries[None],
        grad_keys[None],
        grad_values[None],
        grad_lyric_keys[None],
        grad_lyric_values[None],
        q_total[0],
        k_total[0],
    )


def solution(mesh):
    split = P("song", "seq", None)
    return jax.shard_map(
        body,
        mesh=mesh,
        in_specs=(split, split, split, split, split, P(), P(), split, split, P("song")),
        out_specs=(split, split, split, split, split, split, P(), P()),
        check_vma=False,
    )
```

```python
import functools

import jax
import jax.numpy as jnp
from jax import lax
from jax.experimental import pallas as pl
from jax.experimental.pallas import tpu as pltpu
from jax.sharding import PartitionSpec as P

BLK = 128
TILES = 2
NORM_EPS = 1e-06
HEADS_PER_STEP = 1
CHUNKS = 1
VMEM_LIMIT = 8 * 1024 * 1024
ATTENTION_VMEM_LIMIT = 24 * 1024 * 1024
PACK_VMEM_LIMIT = 60 * 1024 * 1024
GAIN_ROWS = 32
ALIGN_ROWS = 32
SMALL = pl.CostEstimate(flops=1, bytes_accessed=1, transcendentals=0)


def dot(lhs, rhs, lhs_dim, rhs_dim):
    return lax.dot_general(
        lhs, rhs, (((lhs_dim,), (rhs_dim,)), ((), ())), preferred_element_type=jnp.float32
    )


def params(limit=VMEM_LIMIT):
    return pltpu.CompilerParams(dimension_semantics=("arbitrary",), vmem_limit_bytes=limit)


def split_rows(sums):
    high = sums.astype(jnp.bfloat16).astype(jnp.float32)
    rest = sums - high
    middle = rest.astype(jnp.bfloat16).astype(jnp.float32)
    low = rest - middle
    return jnp.concatenate([high, middle, low, jnp.zeros_like(high)], axis=0).astype(jnp.bfloat16)


def joined_rows(rows):
    rows = rows.astype(jnp.float32)
    return (rows[16:24] + rows[8:16]) + rows[0:8]


def pack_kernel(state_ref, align_ref, *refs):
    ins, (out_ref, tile_ref, sems) = refs[:-3], refs[-3:]
    half = out_ref.shape[1]
    cols = pl.ds(pl.multiple_of((1 - state_ref[0]) * half, half), half)
    start = 0
    copies = []
    for index, ref in enumerate(ins):
        rows = ref.shape[0]
        copies.append(
            pltpu.make_async_copy(
                ref.at[:, cols], out_ref.at[start : start + rows, :], sems.at[index]
            )
        )
        copies[-1].start()
        start += rows
    row = lax.broadcasted_iota(jnp.int32, tile_ref.shape, 0)
    tiles = jnp.zeros(tile_ref.shape, jnp.int32)
    for slot in range(TILES):
        tiles = jnp.where(row == slot, align_ref[slot], tiles)
    tile_ref[...] = tiles.astype(jnp.float32).astype(jnp.bfloat16)
    copies.append(
        pltpu.make_async_copy(
            tile_ref, out_ref.at[start : start + ALIGN_ROWS, :], sems.at[len(ins)]
        )
    )
    copies[-1].start()
    for copy in copies:
        copy.wait()


def pack(state, align, arrays):
    width = arrays[0].shape[1]
    half = width // 2
    rows = sum(array.shape[0] for array in arrays) + ALIGN_ROWS
    return pl.pallas_call(
        pack_kernel,
        grid_spec=pltpu.PrefetchScalarGridSpec(
            num_scalar_prefetch=2,
            grid=(1,),
            in_specs=[pl.BlockSpec(memory_space=pl.ANY)] * len(arrays),
            out_specs=pl.BlockSpec(memory_space=pl.ANY),
            scratch_shapes=[
                pltpu.VMEM((ALIGN_ROWS, half), jnp.bfloat16),
                pltpu.SemaphoreType.DMA((len(arrays) + 1,)),
            ],
        ),
        out_shape=jax.ShapeDtypeStruct((rows, half), jnp.bfloat16),
        compiler_params=params(PACK_VMEM_LIMIT),
        cost_estimate=SMALL,
        name="pack",
    )(state, align, *arrays)


def pair_kernel(state_ref, gain_ref, key_ref, value_ref, mate_ref, pair_ref):
    rows = key_ref.shape[0]
    norm_columns(pair_ref, slice(0, rows), key_ref[...], gain_ref)
    pair_ref[rows : 2 * rows, :] = value_ref[...]
    norm_columns(pair_ref, slice(2 * rows, 3 * rows), mate_ref[0:rows, :], gain_ref)
    pair_ref[3 * rows :, :] = mate_ref[rows : 2 * rows, :]


def pair_lyrics(state, chunk, gains, lyric_key, lyric_value, mate):
    rows, width = lyric_key.shape
    size = width // 2 // CHUNKS
    step = size // 2
    last = mate.shape[0] // BLK - 1
    own = pl.BlockSpec((rows, step), lambda i, state: (0, (state[0] * CHUNKS + chunk) * 2 + i))
    return pl.pallas_call(
        pair_kernel,
        grid_spec=pltpu.PrefetchScalarGridSpec(
            num_scalar_prefetch=1,
            grid=(2,),
            in_specs=[
                pl.BlockSpec(gains.shape, lambda i, state: (0, 0)),
                own,
                own,
                pl.BlockSpec((BLK, step), lambda i, state: (last, chunk * 2 + i)),
            ],
            out_specs=pl.BlockSpec((4 * rows, step), lambda i, state: (0, i)),
        ),
        out_shape=jax.ShapeDtypeStruct((4 * rows, size), jnp.bfloat16),
        compiler_params=params(),
        cost_estimate=SMALL,
        name="pair_lyrics",
    )(state, gains, lyric_key, lyric_value, mate)


def edge_kernel(
    touching, state_ref, gain_ref, key_ref, value_ref, mate_key_ref, mate_value_ref, *refs
):
    out_ref = refs[-1]
    frames = key_ref.shape[0]
    first = out_ref.shape[0] - 2 * frames
    if first:
        out_ref[0:first, :] = refs[0][...]
    mine = state_ref[1] == touching
    keys = jnp.where(mine, key_ref[...], mate_key_ref[...])
    norm_columns(out_ref, slice(first, first + frames), keys, gain_ref)
    out_ref[first + frames :, :] = jnp.where(mine, value_ref[...], mate_value_ref[...])


def edge(state, chunk, touching, gains, key, value, mate, lead, after):
    frames, width = key.shape
    size = width // 2 // CHUNKS
    step = size // 2
    rows = sum(array.shape[0] for array in lead) + 2 * frames
    own = pl.BlockSpec((frames, step), lambda i, state: (0, (state[0] * CHUNKS + chunk) * 2 + i))
    return pl.pallas_call(
        functools.partial(edge_kernel, touching),
        grid_spec=pltpu.PrefetchScalarGridSpec(
            num_scalar_prefetch=1,
            grid=(2,),
            in_specs=[pl.BlockSpec(gains.shape, lambda i, state: (0, 0)), own, own]
            + [pl.BlockSpec((frames, step), lambda i, state: (2, chunk * 2 + i))]
            + [pl.BlockSpec((frames, step), lambda i, state: (3, chunk * 2 + i))]
            + [pl.BlockSpec((array.shape[0], step), lambda i, state: (0, i)) for array in lead]
            + [pl.BlockSpec(memory_space=pl.ANY)] * len(after),
            out_specs=pl.BlockSpec((rows, step), lambda i, state: (0, i)),
        ),
        out_shape=jax.ShapeDtypeStruct((rows, size), jnp.bfloat16),
        compiler_params=params(),
        cost_estimate=SMALL,
        name="edge",
    )(state, gains, key, value, mate, mate, *lead, *after)


def prepare_kernel(state_ref, gain_ref, key_ref, mate_ref, *refs):
    out_ref = refs[-1]
    frames = key_ref.shape[0]
    norm_columns(out_ref, slice(0, frames), key_ref[...], gain_ref)
    norm_columns(out_ref, slice(frames, 2 * frames), mate_ref[...], gain_ref)


def prepare_keys(state, gains, key, mate, after):
    frames, width = key.shape
    half = width // 2
    step = half // 2
    return pl.pallas_call(
        prepare_kernel,
        grid_spec=pltpu.PrefetchScalarGridSpec(
            num_scalar_prefetch=1,
            grid=(2,),
            in_specs=[
                pl.BlockSpec(gains.shape, lambda i, state: (0, 0)),
                pl.BlockSpec((frames, step), lambda i, state: (0, state[0] * 2 + i)),
                pl.BlockSpec((frames, step), lambda i, state: (2, i)),
            ]
            + [pl.BlockSpec(memory_space=pl.ANY)] * len(after),
            out_specs=pl.BlockSpec((2 * frames, step), lambda i, state: (0, i)),
        ),
        out_shape=jax.ShapeDtypeStruct((2 * frames, half), jnp.bfloat16),
        compiler_params=params(),
        cost_estimate=SMALL,
        name="prepare_keys",
    )(state, gains, key, mate, *after)


def attention_kernel(
    groups, chained, head_size, score_scale, meta_ref, gain_ref, query_ref, grad_ref, value_ref,
    key_ref, mate_ref, one_ref, mid_ref, *refs
):
    frames = query_ref.shape[0]
    exchanged = len(groups) == 4
    inputs = 3 if exchanged else 1
    lyric_in, refs = refs[:inputs], refs[inputs:]
    window = one_ref.shape[0] - 2 * frames
    if chained:
        gain_before_ref, refs = refs[0], refs[3:]
    out_ref, grad_query_ref, to_mate_ref, key_grad_ref, value_grad_ref = refs[:5]
    to_one_ref, to_mid_ref, gain_grad_ref = refs[5:8]
    lyric_out, mask_ref = refs[8:-1], refs[-1]
    runs = [(index, run) for index, group in enumerate(groups) for run in group]
    main = 2 * frames + sum(run[2] for _, run in runs)
    lanes = 2 * frames
    align = mate_ref.shape[0] - ALIGN_ROWS
    touching = meta_ref[1] == 1

    @pl.when(pl.program_id(0) == 0)
    def _():
        if chained:
            gain_grad_ref[...] = gain_before_ref[...]
        else:
            gain_grad_ref[...] = jnp.zeros_like(gain_grad_ref)
        mate_tiles = mate_ref[align:, 0:frames].astype(jnp.float32).astype(jnp.int32)
        start = 0
        for number, (_, (_, _, rows)) in enumerate(runs):
            row = lax.broadcasted_iota(jnp.int32, (rows, lanes), 0) + meta_ref[7 + number]
            keep = jnp.zeros((rows, lanes), jnp.float32)
            for slot in range(TILES):
                tile = jnp.concatenate(
                    [
                        jnp.full((1, frames), meta_ref[2 + slot], jnp.int32),
                        mate_tiles[slot : slot + 1],
                    ],
                    axis=1,
                )
                lower = tile * BLK
                upper = jnp.minimum(lower + BLK, meta_ref[4])
                inside = (row >= lower) & (row < upper) & (lower >= 0)
                keep = jnp.where(inside, 1.0, keep)
            mask_ref[start : start + rows, :] = keep
            start += rows
        lane = lax.broadcasted_iota(jnp.int32, (frames, lanes), 1)
        mask_ref[start : start + frames, :] = jnp.where(
            lane < frames, meta_ref[5], meta_ref[6]
        ).astype(jnp.float32)

    q_gain = gain_ref[0:1, :]
    k_gain = gain_ref[1:2, :]
    for head in range(query_ref.shape[1] // head_size):
        cols = slice(head * head_size, (head + 1) * head_size)
        lyric = [ref[:, cols] for ref in lyric_in]
        if exchanged:
            lyric = [lyric[0], lyric[1], one_ref[0:window, cols], lyric[2]]
        one_rows, mid_rows = one_ref[window:, cols], mid_ref[:, cols]
        near_rows = jnp.where(touching, one_rows, mid_rows)
        far_rows = jnp.where(touching, mid_rows, one_rows)

        def from_mate(number):
            return mate_ref[number * frames : (number + 1) * frames, cols]

        query = jnp.concatenate([query_ref[:, cols], from_mate(0)], axis=0)
        query = query.astype(jnp.float32)
        cot = jnp.concatenate([grad_ref[:, cols], from_mate(1)], axis=0)
        key_low = jnp.concatenate(
            [key_ref[:, cols]]
            + [lyric[index][run[0] : run[0] + run[2]] for index, run in runs]
            + [near_rows[:frames], far_rows[:frames]],
            axis=0,
        )
        value = jnp.concatenate(
            [value_ref[:, cols], from_mate(3)]
            + [lyric[index][run[1] : run[1] + run[2]] for index, run in runs]
            + [near_rows[frames:], far_rows[frames:]],
            axis=0,
        )
        query_inv = lax.rsqrt(jnp.mean(query * query, axis=1, keepdims=True) + NORM_EPS)
        query_hat = query * query_inv
        query_low = (query_hat * (q_gain * score_scale)).astype(jnp.bfloat16)

        near, far = slice(main, main + frames), slice(main + frames, main + 2 * frames)

        def against(rows, columns):
            return jnp.concatenate(
                [
                    dot(rows[:main], columns, 1, 1),
                    jnp.concatenate(
                        [
                            dot(rows[near], columns[:frames], 1, 1),
                            dot(rows[far], columns[frames:], 1, 1),
                        ],
                        axis=1,
                    ),
                ],
                axis=0,
            )

        def over_keys(weights, rows):
            return dot(weights[:main], rows[:main], 0, 0) + jnp.concatenate(
                [
                    dot(weights[main:, :frames], rows[near], 0, 0),
                    dot(weights[main:, frames:], rows[far], 0, 0),
                ],
                axis=0,
            )

        def over_queries(weights, columns):
            return jnp.concatenate(
                [
                    dot(weights[:main], columns, 1, 0),
                    dot(weights[main:, :frames], columns[:frames], 1, 0),
                    dot(weights[main:, frames:], columns[frames:], 1, 0),
                ],
                axis=0,
            )

        exp_scores = jnp.exp(against(key_low, query_low))
        exp_scores = jnp.concatenate(
            [exp_scores[: 2 * frames], exp_scores[2 * frames :] * mask_ref[...]], axis=0
        )
        grad_prob = against(value, cot)
        prob = exp_scores * (1.0 / jnp.sum(exp_scores, axis=0, keepdims=True))
        prob_low = prob.astype(jnp.bfloat16)
        weighted = prob * grad_prob
        delta = jnp.sum(weighted, axis=0, keepdims=True)
        grad_score = (weighted - prob * delta).astype(jnp.bfloat16)
        output = over_keys(prob_low, value).astype(jnp.bfloat16)
        grad_low = over_keys(grad_score, key_low)
        grad_qn = grad_low * score_scale
        grad_keys = over_queries(grad_score, query_low)
        grad_values = over_queries(prob_low, cot)
        scaled = grad_qn * q_gain
        grad_query = (
            query_inv * scaled
            - query_hat
            * (query_inv * query_inv)
            * jnp.mean(scaled * query, axis=1, keepdims=True)
        ).astype(jnp.bfloat16)
        gain_grad_ref[0:1, :] += jnp.sum(grad_qn * query_hat, axis=0, keepdims=True)
        gain_grad_ref[1:2, :] += (
            jnp.sum(grad_low * query_low.astype(jnp.float32), axis=0, keepdims=True) / k_gain
        )

        out_ref[:, cols] = output[:frames]
        grad_query_ref[:, cols] = grad_query[:frames]
        to_mate_ref[0:frames, cols] = output[frames:]
        to_mate_ref[frames:, cols] = grad_query[frames:]
        key_grad_ref[:, cols] = grad_keys[: 2 * frames]
        value_grad_ref[:, cols] = grad_values[: 2 * frames]
        for grads, part in (
            (grad_keys.astype(jnp.bfloat16), 0),
            (grad_values.astype(jnp.bfloat16), frames),
        ):
            to_one_ref[window + part : window + part + frames, cols] = jnp.where(
                touching, grads[near], grads[far]
            )
            to_mid_ref[part : part + frames, cols] = jnp.where(touching, grads[far], grads[near])
        if exchanged:
            held_ref, two_ref, to_two_ref = lyric_out
            outs = (held_ref, two_ref, to_one_ref, to_two_ref)
        else:
            outs = lyric_out
        start = 2 * frames
        for index, (key_row, value_row, rows) in runs:
            part = slice(start, start + rows)
            outs[index][key_row : key_row + rows, cols] = grad_keys[part].astype(jnp.bfloat16)
            outs[index][value_row : value_row + rows, cols] = grad_values[part].astype(
                jnp.bfloat16
            )
            start += rows


def attention(chunk, meta, gains, query, cot, value, key, mate, one, mid, lyrics, groups, carried):
    frames, width = query.shape
    head_size = gains.shape[1]
    size = width // 2 // CHUNKS
    step = HEADS_PER_STEP * head_size
    steps = size // step
    lyric_rows = sum(run[2] for group in groups for run in group)
    lanes = 2 * frames
    key_rows = 3 * frames + lyric_rows
    exchanged = len(groups) == 4

    def own(rows):
        return pl.BlockSpec(
            (rows, step), lambda i, meta: (0, (meta[0] * CHUNKS + chunk) * steps + i)
        )

    def columns(rows):
        return pl.BlockSpec((rows, step), lambda i, meta: (0, i))

    def either(array):
        return own(array.shape[0]) if array.shape[1] == width else columns(array.shape[0])

    whole = lambda i, meta: (0, 0)
    bf16, f32 = jnp.bfloat16, jnp.float32
    out_rows = [(2 * frames, bf16), (2 * frames, f32), (2 * frames, f32)]
    out_rows += [(one.shape[0], bf16), (2 * frames, bf16)]
    slot = sum(2 * run[2] for run in groups[0])
    extra_rows = [slot] * (3 if exchanged else 1)
    return pl.pallas_call(
        functools.partial(
            attention_kernel, groups, bool(carried), head_size, head_size ** (-0.5)
        ),
        grid_spec=pltpu.PrefetchScalarGridSpec(
            num_scalar_prefetch=1,
            grid=(steps,),
            in_specs=[pl.BlockSpec(gains.shape, whole)]
            + [own(frames)] * 3
            + [
                pl.BlockSpec((2 * frames, step), lambda i, meta: (0, chunk * steps + i)),
                pl.BlockSpec((mate.shape[0], step), lambda i, meta: (0, chunk * steps + i)),
                columns(one.shape[0]),
                columns(mid.shape[0]),
            ]
            + [either(array) for array in lyrics]
            + [pl.BlockSpec((8, head_size), whole)] * bool(carried)
            + [pl.BlockSpec(memory_space=pl.ANY)] * len(carried[1:]),
            out_specs=[own(frames)] * 2
            + [columns(rows) for rows, _ in out_rows]
            + [pl.BlockSpec((8, head_size), whole)]
            + [columns(rows) for rows in extra_rows],
            scratch_shapes=[pltpu.VMEM((frames + lyric_rows, lanes), f32)],
        ),
        out_shape=[jax.ShapeDtypeStruct((frames, width), bf16)] * 2
        + [jax.ShapeDtypeStruct((rows, size), dtype) for rows, dtype in out_rows]
        + [jax.ShapeDtypeStruct((8, head_size), f32)]
        + [jax.ShapeDtypeStruct((rows, size), bf16) for rows in extra_rows],
        input_output_aliases={10 + len(lyrics) + i: i for i in range(len(carried[1:]))},
        compiler_params=params(ATTENTION_VMEM_LIMIT),
        cost_estimate=pl.CostEstimate(
            flops=12 * key_rows * lanes * size,
            bytes_accessed=16 * 1024 * 1024 // CHUNKS,
            transcendentals=key_rows * lanes * (size // head_size),
        ),
        name="attention",
    )(meta, gains, query, cot, value, key, mate, one, mid, *lyrics, *carried)


def fill_kernel(count, core_ref, mate_ref, *refs):
    for index, ref in enumerate(refs[-count:]):
        rows = ref.shape[0]
        ref[...] = mate_ref[index * rows : (index + 1) * rows, :]


def fill_other(core, chunk, arrays, mate):
    frames, width = arrays[0].shape
    count = len(arrays)
    size = width // 2 // CHUNKS
    step = size // 2
    spec = pl.BlockSpec(
        (frames, step), lambda i, core: (0, ((1 - core[0]) * CHUNKS + chunk) * 2 + i)
    )
    return pl.pallas_call(
        functools.partial(fill_kernel, count),
        grid_spec=pltpu.PrefetchScalarGridSpec(
            num_scalar_prefetch=1,
            grid=(2,),
            in_specs=[pl.BlockSpec((mate.shape[0], step), lambda i, core: (0, i))]
            + [pl.BlockSpec(memory_space=pl.ANY)] * count,
            out_specs=[spec] * count,
        ),
        out_shape=[jax.ShapeDtypeStruct(array.shape, array.dtype) for array in arrays],
        input_output_aliases={2 + i: i for i in range(count)},
        compiler_params=params(),
        cost_estimate=SMALL,
        name="fill_other",
    )(core, mate, *arrays)


def normed(raw, k_gain):
    raw = raw.astype(jnp.float32)
    inverse = lax.rsqrt(jnp.mean(raw * raw, axis=1, keepdims=True) + NORM_EPS)
    return (raw * inverse * k_gain).astype(jnp.bfloat16)


def norm_columns(out_ref, rows, raw, gain_ref):
    head_size = gain_ref.shape[1]
    for head in range(raw.shape[1] // head_size):
        cols = slice(head * head_size, (head + 1) * head_size)
        out_ref[rows, cols] = normed(raw[:, cols], gain_ref[1:2, :])


def through_norm(raw, grad, k_gain):
    raw = raw.astype(jnp.float32)
    inverse = lax.rsqrt(jnp.mean(raw * raw, axis=1, keepdims=True) + NORM_EPS)
    scaled = grad * k_gain
    return (
        inverse * scaled
        - raw * (inverse * inverse * inverse) * jnp.mean(scaled * raw, axis=1, keepdims=True)
    ).astype(jnp.bfloat16)


def finish_audio_kernel(
    head_size, state_ref, gain_ref, raw_ref, mate_ref, key_grad_ref, value_grad_ref, one_ref,
    mid_ref, ready_ref, *refs,
):
    k_gain = gain_ref[1:2, :]
    grad_key_ref, grad_value_ref, to_mate_ref = refs[-3:]
    frames = raw_ref.shape[0]
    own, mate = slice(0, frames), slice(frames, 2 * frames)
    first = one_ref.shape[0] - 2 * frames
    touching = state_ref[1] == 1
    to_mate_ref[0 : 2 * frames, :] = ready_ref[...]
    for head in range(raw_ref.shape[1] // head_size):
        cols = slice(head * head_size, (head + 1) * head_size)
        one = one_ref[first:, cols].astype(jnp.float32)
        mid = mid_ref[:, cols].astype(jnp.float32)
        for_own = jnp.where(touching, one, mid)
        for_mate = jnp.where(touching, mid, one)
        grad_key_ref[:, cols] = through_norm(
            raw_ref[:, cols], key_grad_ref[own, cols] + for_own[:frames], k_gain
        )
        grad_value_ref[:, cols] = (value_grad_ref[own, cols] + for_own[frames:]).astype(
            jnp.bfloat16
        )
        to_mate_ref[2 * frames : 3 * frames, cols] = through_norm(
            mate_ref[:, cols], key_grad_ref[mate, cols] + for_mate[:frames], k_gain
        )
        to_mate_ref[3 * frames :, cols] = (
            value_grad_ref[mate, cols] + for_mate[frames:]
        ).astype(jnp.bfloat16)


def finish_audio(
    state, chunk, gains, raw, mate, key_grad, value_grad, one, mid, ready, carried, to_mate
):
    frames, width = raw.shape
    head_size = gains.shape[1]
    size = width // 2 // CHUNKS
    step = size // 2

    def columns(array):
        return pl.BlockSpec((array.shape[0], step), lambda i, core: (0, i))

    own = pl.BlockSpec((frames, step), lambda i, core: (0, (core[0] * CHUNKS + chunk) * 2 + i))
    arrays = (key_grad, value_grad, one, mid, ready)
    aliases = {9 + i: i for i in range(len(carried))}
    if to_mate:
        aliases[9 + len(carried)] = 2
    return pl.pallas_call(
        functools.partial(finish_audio_kernel, head_size),
        grid_spec=pltpu.PrefetchScalarGridSpec(
            num_scalar_prefetch=1,
            grid=(2,),
            in_specs=[pl.BlockSpec(gains.shape, lambda i, core: (0, 0)), own]
            + [pl.BlockSpec((frames, step), lambda i, core: (2, chunk * 2 + i))]
            + [columns(array) for array in arrays]
            + [pl.BlockSpec(memory_space=pl.ANY)] * len(carried + to_mate),
            out_specs=[own] * 2 + [pl.BlockSpec((4 * frames, step), lambda i, core: (0, i))],
        ),
        out_shape=[jax.ShapeDtypeStruct((frames, width), jnp.bfloat16)] * 2
        + [jax.ShapeDtypeStruct((5 * frames, size), jnp.bfloat16)],
        input_output_aliases=aliases,
        compiler_params=params(),
        cost_estimate=SMALL,
        name="finish_audio",
    )(state, gains, raw, mate, *arrays, *carried, *to_mate)


def relay_kernel(head_size, part_ref, arrived_ref, *refs):
    out_ref = refs[-2]
    rows = part_ref.shape[0]
    out_ref[0:rows, :] = (
        part_ref[...].astype(jnp.float32) + arrived_ref[...].astype(jnp.float32)
    ).astype(jnp.bfloat16)
    if head_size:
        out_ref[rows:, 0:head_size] = split_rows(refs[0][...])
        out_ref[rows:, head_size:] = jnp.zeros_like(out_ref[rows:, head_size:])


def relay(part, arrived, sums, later):
    rows, size = part.shape
    step = size // 2
    out_rows = rows + GAIN_ROWS * len(sums)
    spec = pl.BlockSpec((rows, step), lambda i: (0, i))
    return pl.pallas_call(
        functools.partial(relay_kernel, sums[0].shape[1] if sums else 0),
        grid=(2,),
        in_specs=[spec] * 2
        + [pl.BlockSpec(total.shape, lambda i: (0, 0)) for total in sums]
        + [pl.BlockSpec(memory_space=pl.ANY)],
        out_specs=[
            pl.BlockSpec((out_rows, step), lambda i: (0, i)),
            pl.BlockSpec(memory_space=pl.ANY),
        ],
        out_shape=[
            jax.ShapeDtypeStruct((out_rows, size), jnp.bfloat16),
            jax.ShapeDtypeStruct(later.shape, later.dtype),
        ],
        input_output_aliases={2 + len(sums): 1},
        compiler_params=params(),
        cost_estimate=SMALL,
        name="relay",
    )(part, arrived, *sums, later)


def finish_lyric_kernel(
    head_size, state_ref, gain_ref, raw_ref, mate_ref, held_ref, one_ref, two_ref, *refs
):
    rows = raw_ref.shape[0]
    lyric_rows = 4 * rows
    own_ref, to_mate_ref, total_ref = refs[-3:]
    k_gain = gain_ref[1:2, :]
    if len(refs) == 4:
        total_ref[...] = refs[0][...] + joined_rows(two_ref[lyric_rows:, 0:head_size])
    else:
        total_ref[...] = jnp.zeros_like(total_ref)
    for head in range(raw_ref.shape[1] // head_size):
        cols = slice(head * head_size, (head + 1) * head_size)
        total = held_ref[:, cols].astype(jnp.float32)
        for part in (one_ref, two_ref):
            total = total + part[0:lyric_rows, cols].astype(jnp.float32)
        for index, (ref, raw) in enumerate(((own_ref, raw_ref), (to_mate_ref, mate_ref))):
            base = 2 * rows * index
            ref[0:rows, cols] = through_norm(
                raw[0:rows, cols], total[base : base + rows], k_gain
            )
            ref[rows : 2 * rows, cols] = total[base + rows : base + 2 * rows].astype(jnp.bfloat16)
        to_mate_ref[2 * rows :, cols] = split_rows(total_ref[...])


def finish_lyric(state, chunk, gains, raw, mate, held, one, two, sums, frames):
    rows = raw.shape[0]
    size = held.shape[1]
    head_size = gains.shape[1]
    step = size // 2
    tail = 2 * rows + GAIN_ROWS
    last = mate.shape[0] // BLK - 1
    spec = pl.BlockSpec((4 * rows, step), lambda i, state: (0, i))
    whole = pl.BlockSpec((8, head_size), lambda i, state: (0, 0))
    return pl.pallas_call(
        functools.partial(finish_lyric_kernel, head_size),
        grid_spec=pltpu.PrefetchScalarGridSpec(
            num_scalar_prefetch=1,
            grid=(2,),
            in_specs=[
                pl.BlockSpec(gains.shape, lambda i, state: (0, 0)),
                pl.BlockSpec(
                    (rows, step), lambda i, state: (0, (state[0] * CHUNKS + chunk) * 2 + i)
                ),
                pl.BlockSpec((BLK, step), lambda i, state: (last, chunk * 2 + i)),
                spec,
                spec,
                pl.BlockSpec((two.shape[0], step), lambda i, state: (0, i)),
            ]
            + [whole] * len(sums),
            out_specs=[
                pl.BlockSpec((2 * rows, step), lambda i, state: (0, i)),
                pl.BlockSpec((tail, step), lambda i, state: (4 * frames // tail, i)),
                whole,
            ],
        ),
        out_shape=[
            jax.ShapeDtypeStruct((2 * rows, size), jnp.bfloat16),
            jax.ShapeDtypeStruct((4 * frames + tail, size), jnp.bfloat16),
            jax.ShapeDtypeStruct((8, head_size), jnp.float32),
        ],
        compiler_params=params(),
        cost_estimate=SMALL,
        name="finish_lyric",
    )(state, gains, raw, mate, held, one, two, *sums)


def join_kernel(count, chunks, state_ref, gain_ref, *refs):
    owns, mates, outs = refs[:chunks], refs[chunks : 2 * chunks], refs[-count - 4 :]
    grad_key_ref, grad_value_ref, q_total_ref, k_total_ref = outs[count:]
    rows, size = grad_key_ref.shape[0], owns[0].shape[1]
    frames = outs[0].shape[0]
    for index, ref in enumerate(outs[:count]):
        ref[...] = mates[-1][index * frames : (index + 1) * frames, :]
    for part, parts, first in (
        (state_ref[0], owns, 0),
        (1 - state_ref[0], mates, count * frames),
    ):
        for chunk, ref in enumerate(parts):
            cols = pl.ds(pl.multiple_of((part * chunks + chunk) * size, size), size)
            grad_key_ref[:, cols] = ref[first : first + rows, :]
            grad_value_ref[:, cols] = ref[first + rows : first + 2 * rows, :]
    sums = mates[-1][mates[-1].shape[0] - GAIN_ROWS :, 0 : gain_ref.shape[1]]
    total = gain_ref[...] + joined_rows(sums)
    q_total_ref[...] = total[0:1]
    k_total_ref[...] = total[1:2]


def join(state, gain, arrays, own, mate):
    rows, size = own[0].shape
    frames, width = arrays[0].shape
    count, chunks = len(arrays), len(own)
    whole = lambda i, state: (0, 0)
    other = pl.BlockSpec(
        (frames, size), lambda i, state: (0, (1 - state[0]) * chunks + chunks - 1)
    )
    return pl.pallas_call(
        functools.partial(join_kernel, count, chunks),
        grid_spec=pltpu.PrefetchScalarGridSpec(
            num_scalar_prefetch=1,
            grid=(1,),
            in_specs=[pl.BlockSpec(array.shape, whole) for array in [gain, *own, *mate]]
            + [pl.BlockSpec(memory_space=pl.ANY)] * count,
            out_specs=[other] * count
            + [pl.BlockSpec((rows // 2, width), whole)] * 2
            + [pl.BlockSpec((1, gain.shape[1]), whole)] * 2,
        ),
        out_shape=[jax.ShapeDtypeStruct(array.shape, array.dtype) for array in arrays]
        + [jax.ShapeDtypeStruct((rows // 2, width), jnp.bfloat16)] * 2
        + [jax.ShapeDtypeStruct((1, gain.shape[1]), jnp.float32)] * 2,
        input_output_aliases={2 + 2 * chunks + i: i for i in range(count)},
        compiler_params=params(),
        cost_estimate=SMALL,
        name="join",
    )(state, gain, *own, *mate, *arrays)


def norm_rows_kernel(gain_ref, raw_ref, out_ref):
    norm_columns(out_ref, slice(0, raw_ref.shape[0]), raw_ref[...], gain_ref)


def norm_rows(gains, raw):
    return pl.pallas_call(
        norm_rows_kernel,
        out_shape=jax.ShapeDtypeStruct(raw.shape, raw.dtype),
        name="norm_rows",
    )(gains, raw)


def norm_lyric_kernel(head_size, gain_ref, raw_ref, grad_ref, out_ref):
    for head in range(raw_ref.shape[1] // head_size):
        cols = slice(head * head_size, (head + 1) * head_size)
        out_ref[:, cols] = through_norm(raw_ref[:, cols], grad_ref[:, cols], gain_ref[1:2, :])


def norm_lyric(gains, raw, grad):
    return pl.pallas_call(
        functools.partial(norm_lyric_kernel, gains.shape[1]),
        out_shape=jax.ShapeDtypeStruct(raw.shape, jnp.bfloat16),
        name="norm_lyric",
    )(gains, raw, grad)


def sum_over(total, axis, bits):
    count = lax.axis_size(axis)
    for bit in bits:
        total = total + lax.ppermute(total, axis, [(i, i ^ bit) for i in range(count)])
    return total


def bits_of(count):
    return [1 << bit for bit in range(count.bit_length() - 1)]


def body(
    queries, keys, values, lyric_keys, lyric_values, q_gain, k_gain, cotangent, alignment, lyric_len
):
    frames = queries.shape[1]
    lyric_local, width = lyric_keys.shape[1:]
    count = lax.axis_size("seq")
    songs = lax.axis_size("song")
    me = lax.axis_index("seq")
    core = me % 2
    chips = count // 2
    chip = me // 2
    touching = (chip % 2) ^ core
    state = jnp.stack([core, touching]).astype(jnp.int32)
    gains = jnp.stack([q_gain, k_gain])

    swap = [(i, i ^ 1) for i in range(count)]
    partners = [(a, a ^ 1) for a in range(chips)]
    across = [(a, a ^ 2) for a in range(chips)]
    between = [(a, a + 1) for a in range(1, chips - 1, 2)]
    between += [(b, a) for a, b in between]

    def hop(block, moves):
        pairs = [(2 * a + c, 2 * b + c) for a, b in moves for c in (0, 1)]
        return lax.ppermute(block, "seq", pairs)

    hops = chips == 4 and lyric_local % 16 == 0 and 2 * lyric_local + GAIN_ROWS == frames
    total_rows = lyric_local * count
    if hops:
        run = ((0, lyric_local, lyric_local), (2 * lyric_local, 3 * lyric_local, lyric_local))
        groups = (run,) * 4
        owners = [chip, chip ^ 2, chip ^ 1, chip ^ 3]
        first_rows = []
        for owner in owners:
            first_rows += [
                (2 * owner + core) * lyric_local,
                (2 * owner + 1 - core) * lyric_local,
            ]
    else:
        gathered = jnp.concatenate(
            [
                lax.all_gather(
                    norm_rows(gains, lyric_keys[0]), "seq", axis=0, tiled=True
                ),
                lax.all_gather(lyric_values[0], "seq", axis=0, tiled=True),
            ],
            axis=0,
        )
        groups = (((0, total_rows, total_rows),),)
        first_rows = [0]
    has_left, has_right = chip > 0, chip < chips - 1
    has_near = jnp.where(core == 0, has_left, has_right)
    has_far = jnp.where(core == 0, has_right, has_left)
    meta = jnp.stack(
        [
            jnp.asarray(value, jnp.int32)
            for value in [core, touching]
            + [alignment[0, 0, slot] for slot in range(TILES)]
            + [lyric_len[0], has_near, has_far]
            + first_rows
        ]
    )

    to_mate = pack(
        state,
        alignment[0, 0],
        [queries[0], cotangent[0], keys[0], values[0]]
        + ([lyric_keys[0], lyric_values[0]] if hops else []),
    )
    mate = lax.ppermute(to_mate, "seq", swap)
    attended = []
    carried = []
    for chunk in range(CHUNKS):
        if hops:
            pair = pair_lyrics(state, chunk, gains, lyric_keys[0], lyric_values[0], mate)
            two = hop(pair, across)
            lyrics = [pair, two, hop(two, partners)]
            lead, after = [pair], [two]
        else:
            lyrics, lead, after = [gathered], [], []
        one = hop(edge(state, chunk, 1, gains, keys[0], values[0], mate, lead, []), partners)
        mid = hop(edge(state, chunk, 0, gains, keys[0], values[0], mate, [], after), between)
        if chunk == 0:
            key_low = prepare_keys(state, gains, keys[0], mate, after)
        results = attention(
            chunk, meta, gains, queries[0], cotangent[0], values[0], key_low, mate, one, mid,
            lyrics, groups, carried,
        )
        carried = [results[7], *results[:2]]
        attended.append((results[2:], lyrics))
    gain_total, output, grad_queries = carried

    grads = []
    own_halves, lyric_cols, from_mates = [], [], []
    if hops:
        gain_total = sum_over(sum_over(gain_total, "song", bits_of(songs)), "seq", [2])
    for chunk, (results, lyrics) in enumerate(attended):
        for_mate, key_grad, value_grad, to_one, to_mid, _, *parts = results
        to_mate = []
        mid = hop(to_mid, between)
        if hops:
            held, for_two, to_two = parts
            sums = [gain_total] if chunk == CHUNKS - 1 else []
            to_two, to_one = relay(for_two, hop(to_two, partners), sums, to_one)
            two, one = hop(to_two, across), hop(to_one, partners)
            own_half, to_mate, total = finish_lyric(
                state, chunk, gains, lyric_keys[0], mate, held, one, two, sums, frames
            )
            own_halves.append(own_half)
            to_mate = [to_mate]
        else:
            one = hop(to_one, partners)
            lyric_cols.append(parts[0])
        *grads, for_mate = finish_audio(
            state, chunk, gains, keys[0], mate, key_grad, value_grad, one, mid, for_mate, grads,
            to_mate,
        )
        from_mates.append(lax.ppermute(for_mate, "seq", swap))
    filled = [output, grad_queries, *grads]
    for chunk, from_mate in enumerate(from_mates[: CHUNKS - hops]):
        filled = fill_other(state, chunk, filled, from_mate)
    if hops:
        *filled, grad_lyric_keys, grad_lyric_values, q_total, k_total = join(
            state, total, filled, own_halves, from_mates
        )
    else:
        gain_total = lax.psum(gain_total, ("song", "seq"))
        q_total, k_total = gain_total[0:1], gain_total[1:2]
        spread = lax.dynamic_update_slice(
            jnp.zeros((2 * total_rows, width), jnp.float32),
            jnp.concatenate(lyric_cols, axis=1).astype(jnp.float32),
            (0, core * (width // 2)),
        )
        lyric_key_sum, grad_lyric_values = [
            lax.psum_scatter(part, "seq", scatter_dimension=0, tiled=True)
            for part in (spread[:total_rows], spread[total_rows:])
        ]
        grad_lyric_keys = norm_lyric(gains, lyric_keys[0], lyric_key_sum)
        grad_lyric_values = grad_lyric_values.astype(jnp.bfloat16)
    output, grad_queries, grad_keys, grad_values = filled
    return (
        output[None],
        grad_queries[None],
        grad_keys[None],
        grad_values[None],
        grad_lyric_keys[None],
        grad_lyric_values[None],
        q_total[0],
        k_total[0],
    )


def solution(mesh):
    split = P("song", "seq", None)
    return jax.shard_map(
        body,
        mesh=mesh,
        in_specs=(split, split, split, split, split, P(), P(), split, split, P("song")),
        out_specs=(split, split, split, split, split, split, P(), P()),
        check_vma=False,
    )
```

```python
import functools

import jax
import jax.numpy as jnp
from jax import lax
from jax.experimental import pallas as pl
from jax.experimental.pallas import tpu as pltpu
from jax.sharding import PartitionSpec as P

BLK = 128
TILES = 2
NORM_EPS = 1e-06
VMEM_LIMIT = 8 * 1024 * 1024
ATTENTION_VMEM_LIMIT = 24 * 1024 * 1024
PACK_VMEM_LIMIT = 60 * 1024 * 1024
VMEM = pl.BlockSpec(memory_space=pltpu.VMEM)
SMEM = pl.BlockSpec(memory_space=pltpu.SMEM)
HBM = pl.BlockSpec(memory_space=pltpu.HBM)
ANY = pl.BlockSpec(memory_space=pl.ANY)
GAIN_ROWS = 32
ALIGN_ROWS = 32
SMALL = pl.CostEstimate(flops=1, bytes_accessed=1, transcendentals=0)


def dot(lhs, rhs, lhs_dim, rhs_dim):
    return lax.dot_general(
        lhs, rhs, (((lhs_dim,), (rhs_dim,)), ((), ())), preferred_element_type=jnp.float32
    )


def call(kernel, name, in_specs, out_specs, out_shape, limit=VMEM_LIMIT, cost=SMALL, **options):
    return pl.pallas_call(
        kernel,
        in_specs=in_specs,
        out_specs=out_specs,
        out_shape=out_shape,
        compiler_params=pltpu.CompilerParams(vmem_limit_bytes=limit),
        cost_estimate=cost,
        name=name,
        **options,
    )


def shape(rows, cols, dtype=jnp.bfloat16):
    return jax.ShapeDtypeStruct((rows, cols), dtype)


def half_of(ref, core):
    half = ref.shape[1] // 2
    return pl.ds(pl.multiple_of(core * half, half), half)


def split_rows(sums):
    high = sums.astype(jnp.bfloat16).astype(jnp.float32)
    rest = sums - high
    middle = rest.astype(jnp.bfloat16).astype(jnp.float32)
    low = rest - middle
    return jnp.concatenate([high, middle, low, jnp.zeros_like(high)], axis=0).astype(jnp.bfloat16)


def joined_rows(rows):
    rows = rows.astype(jnp.float32)
    return (rows[16:24] + rows[8:16]) + rows[0:8]


def normed(raw, k_gain):
    raw = raw.astype(jnp.float32)
    inverse = lax.rsqrt(jnp.mean(raw * raw, axis=1, keepdims=True) + NORM_EPS)
    return (raw * inverse * k_gain).astype(jnp.bfloat16)


def norm_columns(out_ref, rows, raw, gain_ref):
    head_size = gain_ref.shape[1]
    for head in range(raw.shape[1] // head_size):
        cols = slice(head * head_size, (head + 1) * head_size)
        out_ref[rows, cols] = normed(raw[:, cols], gain_ref[1:2, :])


def through_norm(raw, grad, k_gain):
    raw = raw.astype(jnp.float32)
    inverse = lax.rsqrt(jnp.mean(raw * raw, axis=1, keepdims=True) + NORM_EPS)
    scaled = grad * k_gain
    return (
        inverse * scaled
        - raw * (inverse * inverse * inverse) * jnp.mean(scaled * raw, axis=1, keepdims=True)
    ).astype(jnp.bfloat16)


def pack_kernel(state_ref, align_ref, *refs):
    ins, (out_ref, sems) = refs[:-2], refs[-2:]
    start = 0
    copies = []
    for index, ref in enumerate(ins):
        rows = ref.shape[0]
        copies.append(
            pltpu.make_async_copy(
                ref.at[:, half_of(ref, 1 - state_ref[0])],
                out_ref.at[start : start + rows, :],
                sems.at[index],
            )
        )
        copies[-1].start()
        start += rows
    row = lax.broadcasted_iota(jnp.int32, (ALIGN_ROWS, out_ref.shape[1]), 0)
    tiles = jnp.zeros(row.shape, jnp.int32)
    for slot in range(TILES):
        tiles = jnp.where(row == slot, align_ref[slot], tiles)
    out_ref[start:, :] = tiles.astype(jnp.float32).astype(jnp.bfloat16)
    for copy in copies:
        copy.wait()


def pack(state, align, arrays):
    rows = sum(array.shape[0] for array in arrays) + ALIGN_ROWS
    return call(
        pack_kernel,
        "pack",
        [SMEM, SMEM] + [HBM] * len(arrays),
        VMEM,
        shape(rows, arrays[0].shape[1] // 2),
        scratch_shapes=[pltpu.SemaphoreType.DMA((len(arrays),))],
    )(state, align, *arrays)


def pair_kernel(state_ref, gain_ref, key_ref, value_ref, mate_ref, pair_ref):
    rows = key_ref.shape[0]
    first = mate_ref.shape[0] - ALIGN_ROWS - 2 * rows
    own = half_of(key_ref, state_ref[0])
    norm_columns(pair_ref, slice(0, rows), key_ref[:, own], gain_ref)
    pair_ref[rows : 2 * rows, :] = value_ref[:, own]
    norm_columns(
        pair_ref, slice(2 * rows, 3 * rows), mate_ref[first : first + rows, :], gain_ref
    )
    pair_ref[3 * rows :, :] = mate_ref[first + rows : first + 2 * rows, :]


def pair_lyrics(state, gains, lyric_key, lyric_value, mate):
    rows, width = lyric_key.shape
    return call(
        pair_kernel, "pair_lyrics", [SMEM] + [VMEM] * 4, VMEM, shape(4 * rows, width // 2)
    )(state, gains, lyric_key, lyric_value, mate)


def edge_kernel(touching, leading, state_ref, gain_ref, key_ref, value_ref, mate_ref, *refs):
    out_ref = refs[-1]
    frames = key_ref.shape[0]
    first = out_ref.shape[0] - 2 * frames
    if leading:
        out_ref[0:first, :] = refs[0][...]
    mine = state_ref[1] == touching
    own = half_of(key_ref, state_ref[0])
    keys = jnp.where(mine, key_ref[:, own], mate_ref[2 * frames : 3 * frames, :])
    norm_columns(out_ref, slice(first, first + frames), keys, gain_ref)
    out_ref[first + frames :, :] = jnp.where(
        mine, value_ref[:, own], mate_ref[3 * frames : 4 * frames, :]
    )


def edge(state, touching, gains, key, value, mate, lead, after):
    frames, width = key.shape
    rows = sum(array.shape[0] for array in lead) + 2 * frames
    return call(
        functools.partial(edge_kernel, touching, bool(lead)),
        "edge",
        [SMEM] + [VMEM] * (4 + len(lead)) + [ANY] * len(after),
        VMEM,
        shape(rows, width // 2),
    )(state, gains, key, value, mate, *lead, *after)


def prepare_kernel(state_ref, gain_ref, key_ref, mate_ref, *refs):
    out_ref = refs[-1]
    frames = key_ref.shape[0]
    own = half_of(key_ref, state_ref[0])
    norm_columns(out_ref, slice(0, frames), key_ref[:, own], gain_ref)
    norm_columns(
        out_ref, slice(frames, 2 * frames), mate_ref[2 * frames : 3 * frames, :], gain_ref
    )


def prepare_keys(state, gains, key, mate, after):
    frames, width = key.shape
    return call(
        prepare_kernel,
        "prepare_keys",
        [SMEM] + [VMEM] * 3 + [ANY] * len(after),
        VMEM,
        shape(2 * frames, width // 2),
    )(state, gains, key, mate, *after)


def attention_kernel(
    groups, head_size, score_scale, meta_ref, gain_ref, query_ref, grad_ref, value_ref, key_ref,
    mate_ref, one_ref, mid_ref, *refs
):
    frames = query_ref.shape[0]
    exchanged = len(groups) == 4
    inputs = 3 if exchanged else 1
    lyric_in, refs = refs[:inputs], refs[inputs:]
    window = one_ref.shape[0] - 2 * frames
    out_ref, grad_query_ref, to_mate_ref, key_grad_ref, value_grad_ref = refs[:5]
    to_one_ref, to_mid_ref, gain_grad_ref = refs[5:8]
    lyric_out, mask_ref = refs[8:-1], refs[-1]
    runs = [(index, run) for index, group in enumerate(groups) for run in group]
    main = 2 * frames + sum(run[2] for _, run in runs)
    lanes = 2 * frames
    align = mate_ref.shape[0] - ALIGN_ROWS
    touching = meta_ref[1] == 1

    gain_grad_ref[...] = jnp.zeros_like(gain_grad_ref)
    mate_tiles = mate_ref[align:, 0:frames].astype(jnp.float32).astype(jnp.int32)
    start = 0
    for number, (_, (_, _, rows)) in enumerate(runs):
        row = lax.broadcasted_iota(jnp.int32, (rows, lanes), 0) + meta_ref[7 + number]
        keep = jnp.zeros((rows, lanes), jnp.float32)
        for slot in range(TILES):
            tile = jnp.concatenate(
                [
                    jnp.full((1, frames), meta_ref[2 + slot], jnp.int32),
                    mate_tiles[slot : slot + 1],
                ],
                axis=1,
            )
            lower = tile * BLK
            upper = jnp.minimum(lower + BLK, meta_ref[4])
            inside = (row >= lower) & (row < upper) & (lower >= 0)
            keep = jnp.where(inside, 1.0, keep)
        mask_ref[start : start + rows, :] = keep
        start += rows
    lane = lax.broadcasted_iota(jnp.int32, (frames, lanes), 1)
    mask_ref[start : start + frames, :] = jnp.where(
        lane < frames, meta_ref[5], meta_ref[6]
    ).astype(jnp.float32)

    q_gain = gain_ref[0:1, :]
    k_gain = gain_ref[1:2, :]
    heads = key_ref.shape[1] // head_size

    @pl.loop(0, heads)
    def _(head):
        cols = pl.ds(pl.multiple_of(head * head_size, head_size), head_size)
        own_cols = pl.ds(
            pl.multiple_of((meta_ref[0] * heads + head) * head_size, head_size), head_size
        )
        lyric = [ref[:, cols if exchanged else own_cols] for ref in lyric_in]
        if exchanged:
            lyric = [lyric[0], lyric[1], one_ref[0:window, cols], lyric[2]]
        one_rows, mid_rows = one_ref[window:, cols], mid_ref[:, cols]
        near_rows = jnp.where(touching, one_rows, mid_rows)
        far_rows = jnp.where(touching, mid_rows, one_rows)

        def from_mate(number):
            return mate_ref[number * frames : (number + 1) * frames, cols]

        query = jnp.concatenate([query_ref[:, own_cols], from_mate(0)], axis=0)
        query = query.astype(jnp.float32)
        cot = jnp.concatenate([grad_ref[:, own_cols], from_mate(1)], axis=0)
        key_low = jnp.concatenate(
            [key_ref[:, cols]]
            + [lyric[index][run[0] : run[0] + run[2]] for index, run in runs]
            + [near_rows[:frames], far_rows[:frames]],
            axis=0,
        )
        value = jnp.concatenate(
            [value_ref[:, own_cols], from_mate(3)]
            + [lyric[index][run[1] : run[1] + run[2]] for index, run in runs]
            + [near_rows[frames:], far_rows[frames:]],
            axis=0,
        )
        query_inv = lax.rsqrt(jnp.mean(query * query, axis=1, keepdims=True) + NORM_EPS)
        query_hat = query * query_inv
        query_low = (query_hat * (q_gain * score_scale)).astype(jnp.bfloat16)

        near, far = slice(main, main + frames), slice(main + frames, main + 2 * frames)

        def against(rows, columns):
            return jnp.concatenate(
                [
                    dot(rows[:main], columns, 1, 1),
                    jnp.concatenate(
                        [
                            dot(rows[near], columns[:frames], 1, 1),
                            dot(rows[far], columns[frames:], 1, 1),
                        ],
                        axis=1,
                    ),
                ],
                axis=0,
            )

        def over_keys(weights, rows):
            return dot(weights[:main], rows[:main], 0, 0) + jnp.concatenate(
                [
                    dot(weights[main:, :frames], rows[near], 0, 0),
                    dot(weights[main:, frames:], rows[far], 0, 0),
                ],
                axis=0,
            )

        def over_queries(weights, columns):
            return jnp.concatenate(
                [
                    dot(weights[:main], columns, 1, 0),
                    dot(weights[main:, :frames], columns[:frames], 1, 0),
                    dot(weights[main:, frames:], columns[frames:], 1, 0),
                ],
                axis=0,
            )

        exp_scores = jnp.exp(against(key_low, query_low))
        exp_scores = jnp.concatenate(
            [exp_scores[: 2 * frames], exp_scores[2 * frames :] * mask_ref[...]], axis=0
        )
        grad_prob = against(value, cot)
        prob = exp_scores * (1.0 / jnp.sum(exp_scores, axis=0, keepdims=True))
        prob_low = prob.astype(jnp.bfloat16)
        weighted = prob * grad_prob
        delta = jnp.sum(weighted, axis=0, keepdims=True)
        grad_score = (weighted - prob * delta).astype(jnp.bfloat16)
        output = over_keys(prob_low, value).astype(jnp.bfloat16)
        grad_low = over_keys(grad_score, key_low)
        grad_qn = grad_low * score_scale
        grad_keys = over_queries(grad_score, query_low)
        grad_values = over_queries(prob_low, cot)
        scaled = grad_qn * q_gain
        grad_query = (
            query_inv * scaled
            - query_hat
            * (query_inv * query_inv)
            * jnp.mean(scaled * query, axis=1, keepdims=True)
        ).astype(jnp.bfloat16)
        gain_grad_ref[0:1, :] += jnp.sum(grad_qn * query_hat, axis=0, keepdims=True)
        gain_grad_ref[1:2, :] += (
            jnp.sum(grad_low * query_low.astype(jnp.float32), axis=0, keepdims=True) / k_gain
        )

        out_ref[:, cols] = output[:frames]
        grad_query_ref[:, cols] = grad_query[:frames]
        to_mate_ref[0:frames, cols] = output[frames:]
        to_mate_ref[frames:, cols] = grad_query[frames:]
        key_grad_ref[:, cols] = grad_keys[: 2 * frames]
        value_grad_ref[:, cols] = grad_values[: 2 * frames]
        for grads, part in (
            (grad_keys.astype(jnp.bfloat16), 0),
            (grad_values.astype(jnp.bfloat16), frames),
        ):
            to_one_ref[window + part : window + part + frames, cols] = jnp.where(
                touching, grads[near], grads[far]
            )
            to_mid_ref[part : part + frames, cols] = jnp.where(touching, grads[far], grads[near])
        if exchanged:
            held_ref, two_ref, to_two_ref = lyric_out
            outs = (held_ref, two_ref, to_one_ref, to_two_ref)
        else:
            outs = lyric_out
        start = 2 * frames
        for index, (key_row, value_row, rows) in runs:
            part = slice(start, start + rows)
            outs[index][key_row : key_row + rows, cols] = grad_keys[part].astype(jnp.bfloat16)
            outs[index][value_row : value_row + rows, cols] = grad_values[part].astype(
                jnp.bfloat16
            )
            start += rows


def attention(meta, gains, query, cot, value, key, mate, one, mid, lyrics, groups):
    frames, width = query.shape
    head_size = gains.shape[1]
    half = width // 2
    lyric_rows = sum(run[2] for group in groups for run in group)
    key_rows = 3 * frames + lyric_rows
    bf16, f32 = jnp.bfloat16, jnp.float32
    slot = sum(2 * run[2] for run in groups[0])
    out_shape = [shape(frames, half)] * 2
    out_shape += [shape(2 * frames, half, dtype) for dtype in (bf16, f32, f32)]
    out_shape += [shape(one.shape[0], half), shape(2 * frames, half), shape(8, head_size, f32)]
    out_shape += [shape(slot, half)] * len(lyrics)
    return call(
        functools.partial(attention_kernel, groups, head_size, head_size ** (-0.5)),
        "attention",
        [SMEM] + [VMEM] * (8 + len(lyrics)),
        [VMEM] * len(out_shape),
        out_shape,
        limit=ATTENTION_VMEM_LIMIT,
        cost=pl.CostEstimate(
            flops=24 * key_rows * frames * half,
            bytes_accessed=16 * 1024 * 1024,
            transcendentals=2 * key_rows * frames * (half // head_size),
        ),
        scratch_shapes=[pltpu.VMEM((frames + lyric_rows, 2 * frames), f32)],
    )(meta, gains, query, cot, value, key, mate, one, mid, *lyrics)


def finish_audio_kernel(
    aliased, state_ref, gain_ref, raw_ref, mate_ref, key_grad_ref, value_grad_ref, one_ref,
    mid_ref, ready_ref, out_own_ref, query_own_ref, *refs,
):
    refs = refs[aliased:]
    outs, to_mate_ref, key_ref, value_ref, sems = refs[:4], *refs[4:]
    head_size = gain_ref.shape[1]
    k_gain = gain_ref[1:2, :]
    frames = raw_ref.shape[0]
    own, mate = slice(0, frames), slice(frames, 2 * frames)
    first = one_ref.shape[0] - 2 * frames
    touching = state_ref[1] == 1
    copies = [
        pltpu.make_async_copy(source, out.at[:, half_of(out, state_ref[0])], sems.at[index])
        for index, (source, out) in enumerate(
            zip((out_own_ref, query_own_ref, key_ref, value_ref), outs)
        )
    ]
    copies[0].start()
    copies[1].start()
    to_mate_ref[0 : 2 * frames, :] = ready_ref[...]
    raw_keys = raw_ref[:, half_of(raw_ref, state_ref[0])]
    for head in range(key_ref.shape[1] // head_size):
        cols = slice(head * head_size, (head + 1) * head_size)
        one = one_ref[first:, cols].astype(jnp.float32)
        mid = mid_ref[:, cols].astype(jnp.float32)
        for_own = jnp.where(touching, one, mid)
        for_mate = jnp.where(touching, mid, one)
        key_ref[:, cols] = through_norm(
            raw_keys[:, cols], key_grad_ref[own, cols] + for_own[:frames], k_gain
        )
        value_ref[:, cols] = (value_grad_ref[own, cols] + for_own[frames:]).astype(jnp.bfloat16)
        to_mate_ref[2 * frames : 3 * frames, cols] = through_norm(
            mate_ref[2 * frames : 3 * frames, cols],
            key_grad_ref[mate, cols] + for_mate[:frames],
            k_gain,
        )
        to_mate_ref[3 * frames : 4 * frames, cols] = (
            value_grad_ref[mate, cols] + for_mate[frames:]
        ).astype(jnp.bfloat16)
    copies[2].start()
    copies[3].start()
    for copy in copies:
        copy.wait()


def finish_audio(state, gains, raw, mate, key_grad, value_grad, one, mid, ready, owns, to_mate):
    frames, width = raw.shape
    half = width // 2
    return call(
        functools.partial(finish_audio_kernel, len(to_mate)),
        "finish_audio",
        [SMEM] + [VMEM] * (10 + len(to_mate)),
        [HBM] * 4 + [VMEM],
        [shape(frames, width)] * 4 + [shape(5 * frames, half)],
        input_output_aliases={11: 4} if to_mate else {},
        scratch_shapes=[pltpu.VMEM((frames, half), jnp.bfloat16)] * 2
        + [pltpu.SemaphoreType.DMA((4,))],
    )(state, gains, raw, mate, key_grad, value_grad, one, mid, ready, *owns, *to_mate)


def relay_kernel(head_size, part_ref, arrived_ref, total_ref, later_ref, out_ref, handed_ref):
    rows = part_ref.shape[0]
    out_ref[0:rows, :] = (
        part_ref[...].astype(jnp.float32) + arrived_ref[...].astype(jnp.float32)
    ).astype(jnp.bfloat16)
    out_ref[rows:, 0:head_size] = split_rows(total_ref[...])
    out_ref[rows:, head_size:] = jnp.zeros_like(out_ref[rows:, head_size:])


def relay(part, arrived, total, later):
    rows, half = part.shape
    return call(
        functools.partial(relay_kernel, total.shape[1]),
        "relay",
        [VMEM] * 3 + [ANY],
        [VMEM, ANY],
        [shape(rows + GAIN_ROWS, half), shape(*later.shape)],
        input_output_aliases={3: 1},
    )(part, arrived, total, later)


def finish_lyric_kernel(
    state_ref, gain_ref, raw_ref, mate_ref, held_ref, one_ref, two_ref, sum_ref, own_ref,
    to_mate_ref, total_ref,
):
    rows = raw_ref.shape[0]
    head_size = gain_ref.shape[1]
    k_gain = gain_ref[1:2, :]
    first = mate_ref.shape[0] - ALIGN_ROWS - 2 * rows
    end = to_mate_ref.shape[0] - GAIN_ROWS
    total_ref[...] = sum_ref[...] + joined_rows(two_ref[4 * rows :, 0:head_size])
    to_mate_ref[end:, 0:head_size] = split_rows(total_ref[...])
    to_mate_ref[end:, head_size:] = jnp.zeros_like(to_mate_ref[end:, head_size:])
    raw_keys = raw_ref[:, half_of(raw_ref, state_ref[0])]
    for head in range(own_ref.shape[1] // head_size):
        cols = slice(head * head_size, (head + 1) * head_size)
        total = held_ref[:, cols].astype(jnp.float32)
        for part in (one_ref, two_ref):
            total = total + part[0 : 4 * rows, cols].astype(jnp.float32)
        mate_keys = mate_ref[first : first + rows, cols]
        for ref, start, base, raw in (
            (own_ref, 0, 0, raw_keys[:, cols]),
            (to_mate_ref, end - 2 * rows, 2 * rows, mate_keys),
        ):
            ref[start : start + rows, cols] = through_norm(raw, total[base : base + rows], k_gain)
            ref[start + rows : start + 2 * rows, cols] = total[
                base + rows : base + 2 * rows
            ].astype(jnp.bfloat16)


def finish_lyric(state, gains, raw, mate, held, one, two, total, frames):
    rows = raw.shape[0]
    half = held.shape[1]
    return call(
        finish_lyric_kernel,
        "finish_lyric",
        [SMEM] + [VMEM] * 7,
        [VMEM] * 3,
        [
            shape(2 * rows, half),
            shape(4 * frames + 2 * rows + GAIN_ROWS, half),
            shape(*total.shape, jnp.float32),
        ],
    )(state, gains, raw, mate, held, one, two, total)


def join_kernel(count, state_ref, gain_ref, own_ref, mate_ref, *refs):
    outs, (q_total_ref, k_total_ref, sems) = refs[count:-3], refs[-3:]
    frames = outs[0].shape[0]
    rows = own_ref.shape[0] // 2
    pieces = [
        (mate_ref.at[index * frames : (index + 1) * frames, :], out, 1 - state_ref[0])
        for index, out in enumerate(outs[:count])
    ]
    for ref, first, core in ((own_ref, 0, state_ref[0]), (mate_ref, count * frames, 1 - state_ref[0])):
        for index, out in enumerate(outs[count:]):
            start = first + index * rows
            pieces.append((ref.at[start : start + rows, :], out, core))
    copies = [
        pltpu.make_async_copy(source, out.at[:, half_of(out, core)], sems.at[index])
        for index, (source, out, core) in enumerate(pieces)
    ]
    for copy in copies:
        copy.start()
    sums = mate_ref[mate_ref.shape[0] - GAIN_ROWS :, 0 : gain_ref.shape[1]]
    total = gain_ref[...] + joined_rows(sums)
    q_total_ref[...] = total[0:1]
    k_total_ref[...] = total[1:2]
    for copy in copies:
        copy.wait()


def join(state, gain, arrays, own, mate):
    rows, half = own.shape
    count = len(arrays)
    return call(
        functools.partial(join_kernel, count),
        "join",
        [SMEM] + [VMEM] * 3 + [HBM] * count,
        [HBM] * (count + 2) + [VMEM] * 2,
        [shape(*array.shape) for array in arrays]
        + [shape(rows // 2, 2 * half)] * 2
        + [shape(1, gain.shape[1], jnp.float32)] * 2,
        input_output_aliases={4 + i: i for i in range(count)},
        scratch_shapes=[pltpu.SemaphoreType.DMA((count + 4,))],
    )(state, gain, own, mate, *arrays)


def fill_kernel(count, state_ref, mate_ref, *refs):
    outs, sems = refs[count:-1], refs[-1]
    frames = outs[0].shape[0]
    copies = [
        pltpu.make_async_copy(
            mate_ref.at[index * frames : (index + 1) * frames, :],
            out.at[:, half_of(out, 1 - state_ref[0])],
            sems.at[index],
        )
        for index, out in enumerate(outs)
    ]
    for copy in copies:
        copy.start()
    for copy in copies:
        copy.wait()


def fill_other(state, arrays, mate):
    count = len(arrays)
    return call(
        functools.partial(fill_kernel, count),
        "fill_other",
        [SMEM, VMEM] + [HBM] * count,
        [HBM] * count,
        [shape(*array.shape) for array in arrays],
        input_output_aliases={2 + i: i for i in range(count)},
        scratch_shapes=[pltpu.SemaphoreType.DMA((count,))],
    )(state, mate, *arrays)


def norm_rows_kernel(gain_ref, raw_ref, out_ref):
    norm_columns(out_ref, slice(0, raw_ref.shape[0]), raw_ref[...], gain_ref)


def norm_rows(gains, raw):
    return pl.pallas_call(
        norm_rows_kernel,
        out_shape=jax.ShapeDtypeStruct(raw.shape, raw.dtype),
        name="norm_rows",
    )(gains, raw)


def norm_lyric_kernel(head_size, gain_ref, raw_ref, grad_ref, out_ref):
    for head in range(raw_ref.shape[1] // head_size):
        cols = slice(head * head_size, (head + 1) * head_size)
        out_ref[:, cols] = through_norm(raw_ref[:, cols], grad_ref[:, cols], gain_ref[1:2, :])


def norm_lyric(gains, raw, grad):
    return pl.pallas_call(
        functools.partial(norm_lyric_kernel, gains.shape[1]),
        out_shape=jax.ShapeDtypeStruct(raw.shape, jnp.bfloat16),
        name="norm_lyric",
    )(gains, raw, grad)


def sum_over(total, axis, bits):
    count = lax.axis_size(axis)
    for bit in bits:
        total = total + lax.ppermute(total, axis, [(i, i ^ bit) for i in range(count)])
    return total


def bits_of(count):
    return [1 << bit for bit in range(count.bit_length() - 1)]


def body(
    queries, keys, values, lyric_keys, lyric_values, q_gain, k_gain, cotangent, alignment, lyric_len
):
    frames = queries.shape[1]
    lyric_local, width = lyric_keys.shape[1:]
    count = lax.axis_size("seq")
    songs = lax.axis_size("song")
    me = lax.axis_index("seq")
    core = me % 2
    chips = count // 2
    chip = me // 2
    touching = (chip % 2) ^ core
    state = jnp.stack([core, touching]).astype(jnp.int32)
    gains = jnp.stack([q_gain, k_gain])

    swap = [(i, i ^ 1) for i in range(count)]
    partners = [(a, a ^ 1) for a in range(chips)]
    across = [(a, a ^ 2) for a in range(chips)]
    between = [(a, a + 1) for a in range(1, chips - 1, 2)]
    between += [(b, a) for a, b in between]

    def hop(block, moves):
        pairs = [(2 * a + c, 2 * b + c) for a, b in moves for c in (0, 1)]
        return lax.ppermute(block, "seq", pairs)

    hops = chips == 4 and lyric_local % 16 == 0 and 2 * lyric_local + GAIN_ROWS == frames
    total_rows = lyric_local * count
    if hops:
        run = ((0, lyric_local, lyric_local), (2 * lyric_local, 3 * lyric_local, lyric_local))
        groups = (run,) * 4
        owners = [chip, chip ^ 2, chip ^ 1, chip ^ 3]
        first_rows = []
        for owner in owners:
            first_rows += [
                (2 * owner + core) * lyric_local,
                (2 * owner + 1 - core) * lyric_local,
            ]
    else:
        gathered = jnp.concatenate(
            [
                lax.all_gather(
                    norm_rows(gains, lyric_keys[0]), "seq", axis=0, tiled=True
                ),
                lax.all_gather(lyric_values[0], "seq", axis=0, tiled=True),
            ],
            axis=0,
        )
        groups = (((0, total_rows, total_rows),),)
        first_rows = [0]
    has_left, has_right = chip > 0, chip < chips - 1
    has_near = jnp.where(core == 0, has_left, has_right)
    has_far = jnp.where(core == 0, has_right, has_left)
    meta = jnp.stack(
        [
            jnp.asarray(value, jnp.int32)
            for value in [core, touching]
            + [alignment[0, 0, slot] for slot in range(TILES)]
            + [lyric_len[0], has_near, has_far]
            + first_rows
        ]
    )

    to_mate = pack(
        state,
        alignment[0, 0],
        [queries[0], cotangent[0], keys[0], values[0]]
        + ([lyric_keys[0], lyric_values[0]] if hops else []),
    )
    mate = lax.ppermute(to_mate, "seq", swap)
    if hops:
        pair = pair_lyrics(state, gains, lyric_keys[0], lyric_values[0], mate)
        two = hop(pair, across)
        lyrics = [pair, two, hop(two, partners)]
        lead, after = [pair], [two]
    else:
        lyrics, lead, after = [gathered], [], []
    one = hop(edge(state, 1, gains, keys[0], values[0], mate, lead, []), partners)
    mid = hop(edge(state, 0, gains, keys[0], values[0], mate, [], after), between)
    key_low = prepare_keys(state, gains, keys[0], mate, after)
    output, grad_queries, for_mate, key_grad, value_grad, to_one, to_mid, gain_part, *parts = (
        attention(
            meta, gains, queries[0], cotangent[0], values[0], key_low, mate, one, mid, lyrics,
            groups,
        )
    )

    to_mate = []
    mid = hop(to_mid, between)
    if hops:
        held, for_two, to_two = parts
        gain_total = sum_over(sum_over(gain_part, "song", bits_of(songs)), "seq", [2])
        to_two, to_one = relay(for_two, hop(to_two, partners), gain_total, to_one)
        two, one = hop(to_two, across), hop(to_one, partners)
        own_half, part_to_mate, gain_total = finish_lyric(
            state, gains, lyric_keys[0], mate, held, one, two, gain_total, frames
        )
        to_mate = [part_to_mate]
    else:
        one = hop(to_one, partners)
    *filled, to_mate = finish_audio(
        state, gains, keys[0], mate, key_grad, value_grad, one, mid, for_mate,
        [output, grad_queries], to_mate,
    )
    from_mate = lax.ppermute(to_mate, "seq", swap)
    if hops:
        *filled, grad_lyric_keys, grad_lyric_values, q_total, k_total = join(
            state, gain_total, filled, own_half, from_mate
        )
    else:
        filled = fill_other(state, filled, from_mate)
        gain_total = lax.psum(gain_part, ("song", "seq"))
        q_total, k_total = gain_total[0:1], gain_total[1:2]
        spread = lax.dynamic_update_slice(
            jnp.zeros((2 * total_rows, width), jnp.float32),
            parts[0].astype(jnp.float32),
            (0, core * (width // 2)),
        )
        lyric_key_sum, grad_lyric_values = [
            lax.psum_scatter(part, "seq", scatter_dimension=0, tiled=True)
            for part in (spread[:total_rows], spread[total_rows:])
        ]
        grad_lyric_keys = norm_lyric(gains, lyric_keys[0], lyric_key_sum)
        grad_lyric_values = grad_lyric_values.astype(jnp.bfloat16)
    output, grad_queries, grad_keys, grad_values = filled
    return (
        output[None],
        grad_queries[None],
        grad_keys[None],
        grad_values[None],
        grad_lyric_keys[None],
        grad_lyric_values[None],
        q_total[0],
        k_total[0],
    )


def solution(mesh):
    split = P("song", "seq", None)
    return jax.shard_map(
        body,
        mesh=mesh,
        in_specs=(split, split, split, split, split, P(), P(), split, split, P("song")),
        out_specs=(split, split, split, split, split, split, P(), P()),
        check_vma=False,
    )
```

```python
import functools

import jax
import jax.numpy as jnp
from jax import lax
from jax.experimental import pallas as pl
from jax.experimental.pallas import tpu as pltpu
from jax.sharding import PartitionSpec as P

BLK = 128
TILES = 2
NORM_EPS = 1e-06
VMEM_LIMIT = 8 * 1024 * 1024
ATTENTION_VMEM_LIMIT = 24 * 1024 * 1024
PACK_VMEM_LIMIT = 60 * 1024 * 1024
VMEM = pl.BlockSpec(memory_space=pltpu.VMEM)
SMEM = pl.BlockSpec(memory_space=pltpu.SMEM)
HBM = pl.BlockSpec(memory_space=pltpu.HBM)
ANY = pl.BlockSpec(memory_space=pl.ANY)
GAIN_ROWS = 16
HEADS_PER_STEP = 2
ALIGN_ROWS = 32
SMALL = pl.CostEstimate(flops=1, bytes_accessed=1, transcendentals=0)


def dot(lhs, rhs, lhs_dim, rhs_dim):
    return lax.dot_general(
        lhs, rhs, (((lhs_dim,), (rhs_dim,)), ((), ())), preferred_element_type=jnp.float32
    )


def call(kernel, name, in_specs, out_specs, out_shape, limit=VMEM_LIMIT, cost=SMALL, **options):
    return pl.pallas_call(
        kernel,
        in_specs=in_specs,
        out_specs=out_specs,
        out_shape=out_shape,
        compiler_params=pltpu.CompilerParams(vmem_limit_bytes=limit),
        cost_estimate=cost,
        name=name,
        **options,
    )


def shape(rows, cols, dtype=jnp.bfloat16):
    return jax.ShapeDtypeStruct((rows, cols), dtype)


def half_of(ref, core):
    half = ref.shape[1] // 2
    return pl.ds(pl.multiple_of(core * half, half), half)


def split_rows(sums, cols):
    high = sums.astype(jnp.bfloat16).astype(jnp.float32)
    rest = sums - high
    middle = rest.astype(jnp.bfloat16).astype(jnp.float32)
    low = rest - middle
    empty = jnp.zeros((sums.shape[0], cols - 3 * sums.shape[1]), jnp.float32)
    rows = jnp.concatenate([high, middle, low, empty], axis=1)
    return jnp.concatenate([rows, jnp.zeros_like(rows)], axis=0).astype(jnp.bfloat16)


def joined_rows(rows, size):
    rows = rows.astype(jnp.float32)[0:8]
    return (rows[:, 2 * size : 3 * size] + rows[:, size : 2 * size]) + rows[:, 0:size]


def normed(raw, k_gain):
    raw = raw.astype(jnp.float32)
    inverse = lax.rsqrt(jnp.mean(raw * raw, axis=1, keepdims=True) + NORM_EPS)
    return (raw * inverse * k_gain).astype(jnp.bfloat16)


def norm_columns(out_ref, rows, raw, gain_ref):
    head_size = gain_ref.shape[1]
    for head in range(raw.shape[1] // head_size):
        cols = slice(head * head_size, (head + 1) * head_size)
        out_ref[rows, cols] = normed(raw[:, cols], gain_ref[1:2, :])


def through_norm(raw, grad, k_gain):
    raw = raw.astype(jnp.float32)
    inverse = lax.rsqrt(jnp.mean(raw * raw, axis=1, keepdims=True) + NORM_EPS)
    scaled = grad * k_gain
    return (
        inverse * scaled
        - raw * (inverse * inverse * inverse) * jnp.mean(scaled * raw, axis=1, keepdims=True)
    ).astype(jnp.bfloat16)


def pack_kernel(state_ref, align_ref, *refs):
    ins, (out_ref, sems) = refs[:-2], refs[-2:]
    start = 0
    copies = []
    for index, ref in enumerate(ins):
        rows = ref.shape[0]
        copies.append(
            pltpu.make_async_copy(
                ref.at[:, half_of(ref, 1 - state_ref[0])],
                out_ref.at[start : start + rows, :],
                sems.at[index],
            )
        )
        copies[-1].start()
        start += rows
    row = lax.broadcasted_iota(jnp.int32, (ALIGN_ROWS, out_ref.shape[1]), 0)
    tiles = jnp.zeros(row.shape, jnp.int32)
    for slot in range(TILES):
        tiles = jnp.where(row == slot, align_ref[slot], tiles)
    out_ref[start:, :] = tiles.astype(jnp.float32).astype(jnp.bfloat16)
    for copy in copies:
        copy.wait()


def pack(state, align, arrays):
    rows = sum(array.shape[0] for array in arrays) + ALIGN_ROWS
    return call(
        pack_kernel,
        "pack",
        [SMEM, SMEM] + [HBM] * len(arrays),
        VMEM,
        shape(rows, arrays[0].shape[1] // 2),
        limit=PACK_VMEM_LIMIT,
        scratch_shapes=[pltpu.SemaphoreType.DMA((len(arrays),))],
    )(state, align, *arrays)


def pair_kernel(state_ref, gain_ref, key_ref, value_ref, mate_ref, pair_ref):
    rows = key_ref.shape[0]
    first = mate_ref.shape[0] - ALIGN_ROWS - 2 * rows
    own = half_of(key_ref, state_ref[0])
    norm_columns(pair_ref, slice(0, rows), key_ref[:, own], gain_ref)
    pair_ref[rows : 2 * rows, :] = value_ref[:, own]
    norm_columns(
        pair_ref, slice(2 * rows, 3 * rows), mate_ref[first : first + rows, :], gain_ref
    )
    pair_ref[3 * rows :, :] = mate_ref[first + rows : first + 2 * rows, :]


def pair_lyrics(state, gains, lyric_key, lyric_value, mate):
    rows, width = lyric_key.shape
    return call(
        pair_kernel, "pair_lyrics", [SMEM] + [VMEM] * 4, VMEM, shape(4 * rows, width // 2)
    )(state, gains, lyric_key, lyric_value, mate)


def edge_kernel(touching, leading, state_ref, gain_ref, key_ref, value_ref, mate_ref, *refs):
    out_ref = refs[-1]
    frames = key_ref.shape[0]
    first = out_ref.shape[0] - 2 * frames
    if leading:
        out_ref[0:first, :] = refs[0][...]
    mine = state_ref[1] == touching
    own = half_of(key_ref, state_ref[0])
    keys = jnp.where(mine, key_ref[:, own], mate_ref[2 * frames : 3 * frames, :])
    norm_columns(out_ref, slice(first, first + frames), keys, gain_ref)
    out_ref[first + frames :, :] = jnp.where(
        mine, value_ref[:, own], mate_ref[3 * frames : 4 * frames, :]
    )


def edge(state, touching, gains, key, value, mate, lead, after):
    frames, width = key.shape
    rows = sum(array.shape[0] for array in lead) + 2 * frames
    return call(
        functools.partial(edge_kernel, touching, bool(lead)),
        "edge",
        [SMEM] + [VMEM] * (4 + len(lead)) + [ANY] * len(after),
        VMEM,
        shape(rows, width // 2),
    )(state, gains, key, value, mate, *lead, *after)


def prepare_kernel(state_ref, gain_ref, key_ref, mate_ref, *refs):
    out_ref = refs[-1]
    frames = key_ref.shape[0]
    own = half_of(key_ref, state_ref[0])
    norm_columns(out_ref, slice(0, frames), key_ref[:, own], gain_ref)
    norm_columns(
        out_ref, slice(frames, 2 * frames), mate_ref[2 * frames : 3 * frames, :], gain_ref
    )


def prepare_keys(state, gains, key, mate, after):
    frames, width = key.shape
    return call(
        prepare_kernel,
        "prepare_keys",
        [SMEM] + [VMEM] * 3 + [ANY] * len(after),
        VMEM,
        shape(2 * frames, width // 2),
    )(state, gains, key, mate, *after)


def attention_kernel(
    groups, head_size, score_scale, meta_ref, gain_ref, query_ref, grad_ref, value_ref, key_ref,
    mate_ref, one_ref, mid_ref, *refs
):
    frames = query_ref.shape[0]
    exchanged = len(groups) == 4
    inputs = 3 if exchanged else 1
    lyric_in, refs = refs[:inputs], refs[inputs:]
    window = one_ref.shape[0] - 2 * frames
    out_ref, grad_query_ref, to_mate_ref, key_grad_ref, value_grad_ref = refs[:5]
    to_one_ref, to_mid_ref, gain_grad_ref = refs[5:8]
    lyric_out, mask_ref = refs[8:-1], refs[-1]
    runs = [(index, run) for index, group in enumerate(groups) for run in group]
    main = 2 * frames + sum(run[2] for _, run in runs)
    lanes = 2 * frames
    align = mate_ref.shape[0] - ALIGN_ROWS
    touching = meta_ref[1] == 1

    gain_grad_ref[...] = jnp.zeros_like(gain_grad_ref)
    mate_tiles = mate_ref[align:, 0:frames].astype(jnp.float32).astype(jnp.int32)
    start = 0
    for number, (_, (_, _, rows)) in enumerate(runs):
        row = lax.broadcasted_iota(jnp.int32, (rows, lanes), 0) + meta_ref[7 + number]
        keep = jnp.zeros((rows, lanes), jnp.float32)
        for slot in range(TILES):
            tile = jnp.concatenate(
                [
                    jnp.full((1, frames), meta_ref[2 + slot], jnp.int32),
                    mate_tiles[slot : slot + 1],
                ],
                axis=1,
            )
            lower = tile * BLK
            upper = jnp.minimum(lower + BLK, meta_ref[4])
            inside = (row >= lower) & (row < upper) & (lower >= 0)
            keep = jnp.where(inside, 1.0, keep)
        mask_ref[start : start + rows, :] = keep
        start += rows
    lane = lax.broadcasted_iota(jnp.int32, (frames, lanes), 1)
    mask_ref[start : start + frames, :] = jnp.where(
        lane < frames, meta_ref[5], meta_ref[6]
    ).astype(jnp.float32)

    q_gain = gain_ref[0:1, :]
    k_gain = gain_ref[1:2, :]
    heads = key_ref.shape[1] // head_size

    def one_head(head):
        cols = pl.ds(pl.multiple_of(head * head_size, head_size), head_size)
        own_cols = pl.ds(
            pl.multiple_of((meta_ref[0] * heads + head) * head_size, head_size), head_size
        )
        lyric = [ref[:, cols if exchanged else own_cols] for ref in lyric_in]
        if exchanged:
            lyric = [lyric[0], lyric[1], one_ref[0:window, cols], lyric[2]]
        one_rows, mid_rows = one_ref[window:, cols], mid_ref[:, cols]
        near_rows = jnp.where(touching, one_rows, mid_rows)
        far_rows = jnp.where(touching, mid_rows, one_rows)

        def from_mate(number):
            return mate_ref[number * frames : (number + 1) * frames, cols]

        query = jnp.concatenate([query_ref[:, own_cols], from_mate(0)], axis=0)
        query = query.astype(jnp.float32)
        cot = jnp.concatenate([grad_ref[:, own_cols], from_mate(1)], axis=0)
        key_low = jnp.concatenate(
            [key_ref[:, cols]]
            + [lyric[index][run[0] : run[0] + run[2]] for index, run in runs]
            + [near_rows[:frames], far_rows[:frames]],
            axis=0,
        )
        value = jnp.concatenate(
            [value_ref[:, own_cols], from_mate(3)]
            + [lyric[index][run[1] : run[1] + run[2]] for index, run in runs]
            + [near_rows[frames:], far_rows[frames:]],
            axis=0,
        )
        query_inv = lax.rsqrt(jnp.mean(query * query, axis=1, keepdims=True) + NORM_EPS)
        query_hat = query * query_inv
        query_low = (query_hat * (q_gain * score_scale)).astype(jnp.bfloat16)

        near, far = slice(main, main + frames), slice(main + frames, main + 2 * frames)

        def against(rows, columns):
            return jnp.concatenate(
                [
                    dot(rows[:main], columns, 1, 1),
                    jnp.concatenate(
                        [
                            dot(rows[near], columns[:frames], 1, 1),
                            dot(rows[far], columns[frames:], 1, 1),
                        ],
                        axis=1,
                    ),
                ],
                axis=0,
            )

        def over_keys(weights, rows):
            return dot(weights[:main], rows[:main], 0, 0) + jnp.concatenate(
                [
                    dot(weights[main:, :frames], rows[near], 0, 0),
                    dot(weights[main:, frames:], rows[far], 0, 0),
                ],
                axis=0,
            )

        def over_queries(weights, columns):
            return jnp.concatenate(
                [
                    dot(weights[:main], columns, 1, 0),
                    dot(weights[main:, :frames], columns[:frames], 1, 0),
                    dot(weights[main:, frames:], columns[frames:], 1, 0),
                ],
                axis=0,
            )

        exp_scores = jnp.exp(against(key_low, query_low))
        exp_scores = jnp.concatenate(
            [exp_scores[: 2 * frames], exp_scores[2 * frames :] * mask_ref[...]], axis=0
        )
        grad_prob = against(value, cot)
        prob = exp_scores * (1.0 / jnp.sum(exp_scores, axis=0, keepdims=True))
        prob_low = prob.astype(jnp.bfloat16)
        weighted = prob * grad_prob
        delta = jnp.sum(weighted, axis=0, keepdims=True)
        grad_score = (weighted - prob * delta).astype(jnp.bfloat16)
        output = over_keys(prob_low, value).astype(jnp.bfloat16)
        grad_low = over_keys(grad_score, key_low)
        grad_qn = grad_low * score_scale
        grad_keys = over_queries(grad_score, query_low)
        grad_values = over_queries(prob_low, cot)
        scaled = grad_qn * q_gain
        grad_query = (
            query_inv * scaled
            - query_hat
            * (query_inv * query_inv)
            * jnp.mean(scaled * query, axis=1, keepdims=True)
        ).astype(jnp.bfloat16)
        gain_grad_ref[0:1, :] += jnp.sum(grad_qn * query_hat, axis=0, keepdims=True)
        gain_grad_ref[1:2, :] += (
            jnp.sum(grad_low * query_low.astype(jnp.float32), axis=0, keepdims=True) / k_gain
        )

        out_ref[:, cols] = output[:frames]
        grad_query_ref[:, cols] = grad_query[:frames]
        to_mate_ref[0:frames, cols] = output[frames:]
        to_mate_ref[frames:, cols] = grad_query[frames:]
        key_grad_ref[:, cols] = grad_keys[: 2 * frames]
        value_grad_ref[:, cols] = grad_values[: 2 * frames]
        for grads, part in (
            (grad_keys.astype(jnp.bfloat16), 0),
            (grad_values.astype(jnp.bfloat16), frames),
        ):
            to_one_ref[window + part : window + part + frames, cols] = jnp.where(
                touching, grads[near], grads[far]
            )
            to_mid_ref[part : part + frames, cols] = jnp.where(touching, grads[far], grads[near])
        if exchanged:
            held_ref, two_ref, to_two_ref = lyric_out
            outs = (held_ref, two_ref, to_one_ref, to_two_ref)
        else:
            outs = lyric_out
        start = 2 * frames
        for index, (key_row, value_row, rows) in runs:
            part = slice(start, start + rows)
            outs[index][key_row : key_row + rows, cols] = grad_keys[part].astype(jnp.bfloat16)
            outs[index][value_row : value_row + rows, cols] = grad_values[part].astype(
                jnp.bfloat16
            )
            start += rows

    @pl.loop(0, heads // HEADS_PER_STEP)
    def _(step):
        for number in range(HEADS_PER_STEP):
            one_head(step * HEADS_PER_STEP + number)


def attention(meta, gains, query, cot, value, key, mate, one, mid, lyrics, groups):
    frames, width = query.shape
    head_size = gains.shape[1]
    half = width // 2
    lyric_rows = sum(run[2] for group in groups for run in group)
    key_rows = 3 * frames + lyric_rows
    bf16, f32 = jnp.bfloat16, jnp.float32
    slot = sum(2 * run[2] for run in groups[0])
    out_shape = [shape(frames, half)] * 2
    out_shape += [shape(2 * frames, half, dtype) for dtype in (bf16, f32, f32)]
    out_shape += [shape(one.shape[0], half), shape(2 * frames, half), shape(8, head_size, f32)]
    out_shape += [shape(slot, half)] * len(lyrics)
    return call(
        functools.partial(attention_kernel, groups, head_size, head_size ** (-0.5)),
        "attention",
        [SMEM] + [VMEM] * (8 + len(lyrics)),
        [VMEM] * len(out_shape),
        out_shape,
        limit=ATTENTION_VMEM_LIMIT,
        cost=pl.CostEstimate(
            flops=24 * key_rows * frames * half,
            bytes_accessed=16 * 1024 * 1024,
            transcendentals=2 * key_rows * frames * (half // head_size),
        ),
        scratch_shapes=[pltpu.VMEM((frames + lyric_rows, 2 * frames), f32)],
    )(meta, gains, query, cot, value, key, mate, one, mid, *lyrics)


def finish_audio_kernel(
    aliased, state_ref, gain_ref, raw_ref, mate_ref, key_grad_ref, value_grad_ref, one_ref,
    mid_ref, ready_ref, out_own_ref, query_own_ref, *refs,
):
    refs = refs[aliased:]
    outs, to_mate_ref, key_ref, value_ref, sems = refs[:4], *refs[4:]
    head_size = gain_ref.shape[1]
    k_gain = gain_ref[1:2, :]
    frames = raw_ref.shape[0]
    own, mate = slice(0, frames), slice(frames, 2 * frames)
    first = one_ref.shape[0] - 2 * frames
    touching = state_ref[1] == 1
    copies = [
        pltpu.make_async_copy(source, out.at[:, half_of(out, state_ref[0])], sems.at[index])
        for index, (source, out) in enumerate(
            zip((out_own_ref, query_own_ref, key_ref, value_ref), outs)
        )
    ]
    copies[0].start()
    copies[1].start()
    to_mate_ref[0 : 2 * frames, :] = ready_ref[...]
    raw_keys = raw_ref[:, half_of(raw_ref, state_ref[0])]
    for head in range(key_ref.shape[1] // head_size):
        cols = slice(head * head_size, (head + 1) * head_size)
        one = one_ref[first:, cols].astype(jnp.float32)
        mid = mid_ref[:, cols].astype(jnp.float32)
        for_own = jnp.where(touching, one, mid)
        for_mate = jnp.where(touching, mid, one)
        key_ref[:, cols] = through_norm(
            raw_keys[:, cols], key_grad_ref[own, cols] + for_own[:frames], k_gain
        )
        value_ref[:, cols] = (value_grad_ref[own, cols] + for_own[frames:]).astype(jnp.bfloat16)
        to_mate_ref[2 * frames : 3 * frames, cols] = through_norm(
            mate_ref[2 * frames : 3 * frames, cols],
            key_grad_ref[mate, cols] + for_mate[:frames],
            k_gain,
        )
        to_mate_ref[3 * frames : 4 * frames, cols] = (
            value_grad_ref[mate, cols] + for_mate[frames:]
        ).astype(jnp.bfloat16)
    copies[2].start()
    copies[3].start()
    for copy in copies:
        copy.wait()


def finish_audio(state, gains, raw, mate, key_grad, value_grad, one, mid, ready, owns, to_mate):
    frames, width = raw.shape
    half = width // 2
    return call(
        functools.partial(finish_audio_kernel, len(to_mate)),
        "finish_audio",
        [SMEM] + [VMEM] * (10 + len(to_mate)),
        [HBM] * 4 + [VMEM],
        [shape(frames, width)] * 4
        + [shape(*array.shape) for array in to_mate or [shape(4 * frames, half)]],
        input_output_aliases={11: 4} if to_mate else {},
        scratch_shapes=[pltpu.VMEM((frames, half), jnp.bfloat16)] * 2
        + [pltpu.SemaphoreType.DMA((4,))],
    )(state, gains, raw, mate, key_grad, value_grad, one, mid, ready, *owns, *to_mate)


def relay_kernel(part_ref, arrived_ref, total_ref, later_ref, out_ref, handed_ref):
    rows = part_ref.shape[0]
    out_ref[0:rows, :] = (
        part_ref[...].astype(jnp.float32) + arrived_ref[...].astype(jnp.float32)
    ).astype(jnp.bfloat16)
    out_ref[rows:, :] = split_rows(total_ref[...], out_ref.shape[1])


def relay(part, arrived, total, later):
    rows, half = part.shape
    return call(
        relay_kernel,
        "relay",
        [VMEM] * 3 + [ANY],
        [VMEM, ANY],
        [shape(rows + GAIN_ROWS, half), shape(*later.shape)],
        input_output_aliases={3: 1},
    )(part, arrived, total, later)


def finish_lyric_kernel(
    state_ref, gain_ref, raw_ref, mate_ref, held_ref, one_ref, two_ref, sum_ref, own_ref,
    to_mate_ref, total_ref,
):
    rows = raw_ref.shape[0]
    head_size = gain_ref.shape[1]
    k_gain = gain_ref[1:2, :]
    first = mate_ref.shape[0] - ALIGN_ROWS - 2 * rows
    end = to_mate_ref.shape[0] - GAIN_ROWS
    total_ref[...] = sum_ref[...] + joined_rows(two_ref[4 * rows :, :], head_size)
    to_mate_ref[end:, :] = split_rows(total_ref[...], to_mate_ref.shape[1])
    raw_keys = raw_ref[:, half_of(raw_ref, state_ref[0])]
    for head in range(own_ref.shape[1] // head_size):
        cols = slice(head * head_size, (head + 1) * head_size)
        total = held_ref[:, cols].astype(jnp.float32)
        for part in (one_ref, two_ref):
            total = total + part[0 : 4 * rows, cols].astype(jnp.float32)
        mate_keys = mate_ref[first : first + rows, cols]
        for ref, start, base, raw in (
            (own_ref, 0, 0, raw_keys[:, cols]),
            (to_mate_ref, end - 2 * rows, 2 * rows, mate_keys),
        ):
            ref[start : start + rows, cols] = through_norm(raw, total[base : base + rows], k_gain)
            ref[start + rows : start + 2 * rows, cols] = total[
                base + rows : base + 2 * rows
            ].astype(jnp.bfloat16)


def finish_lyric(state, gains, raw, mate, held, one, two, total, frames):
    rows = raw.shape[0]
    half = held.shape[1]
    return call(
        finish_lyric_kernel,
        "finish_lyric",
        [SMEM] + [VMEM] * 7,
        [VMEM] * 3,
        [
            shape(2 * rows, half),
            shape(4 * frames + 2 * rows + GAIN_ROWS, half),
            shape(*total.shape, jnp.float32),
        ],
    )(state, gains, raw, mate, held, one, two, total)


def join_kernel(count, state_ref, gain_ref, own_ref, mate_ref, *refs):
    outs, (q_total_ref, k_total_ref, sems) = refs[count:-3], refs[-3:]
    frames = outs[0].shape[0]
    rows = own_ref.shape[0] // 2
    pieces = [
        (mate_ref.at[index * frames : (index + 1) * frames, :], out, 1 - state_ref[0])
        for index, out in enumerate(outs[:count])
    ]
    for ref, first, core in ((own_ref, 0, state_ref[0]), (mate_ref, count * frames, 1 - state_ref[0])):
        for index, out in enumerate(outs[count:]):
            start = first + index * rows
            pieces.append((ref.at[start : start + rows, :], out, core))
    copies = [
        pltpu.make_async_copy(source, out.at[:, half_of(out, core)], sems.at[index])
        for index, (source, out, core) in enumerate(pieces)
    ]
    for copy in copies:
        copy.start()
    sums = mate_ref[mate_ref.shape[0] - GAIN_ROWS :, :]
    total = gain_ref[...] + joined_rows(sums, gain_ref.shape[1])
    q_total_ref[...] = total[0:1]
    k_total_ref[...] = total[1:2]
    for copy in copies:
        copy.wait()


def join(state, gain, arrays, own, mate):
    rows, half = own.shape
    count = len(arrays)
    return call(
        functools.partial(join_kernel, count),
        "join",
        [SMEM] + [VMEM] * 3 + [HBM] * count,
        [HBM] * (count + 2) + [VMEM] * 2,
        [shape(*array.shape) for array in arrays]
        + [shape(rows // 2, 2 * half)] * 2
        + [shape(1, gain.shape[1], jnp.float32)] * 2,
        input_output_aliases={4 + i: i for i in range(count)},
        scratch_shapes=[pltpu.SemaphoreType.DMA((count + 4,))],
    )(state, gain, own, mate, *arrays)


def fill_kernel(count, state_ref, mate_ref, *refs):
    outs, sems = refs[count:-1], refs[-1]
    frames = outs[0].shape[0]
    copies = [
        pltpu.make_async_copy(
            mate_ref.at[index * frames : (index + 1) * frames, :],
            out.at[:, half_of(out, 1 - state_ref[0])],
            sems.at[index],
        )
        for index, out in enumerate(outs)
    ]
    for copy in copies:
        copy.start()
    for copy in copies:
        copy.wait()


def fill_other(state, arrays, mate):
    count = len(arrays)
    return call(
        functools.partial(fill_kernel, count),
        "fill_other",
        [SMEM, VMEM] + [HBM] * count,
        [HBM] * count,
        [shape(*array.shape) for array in arrays],
        input_output_aliases={2 + i: i for i in range(count)},
        scratch_shapes=[pltpu.SemaphoreType.DMA((count,))],
    )(state, mate, *arrays)


def norm_rows_kernel(gain_ref, raw_ref, out_ref):
    norm_columns(out_ref, slice(0, raw_ref.shape[0]), raw_ref[...], gain_ref)


def norm_rows(gains, raw):
    return pl.pallas_call(
        norm_rows_kernel,
        out_shape=jax.ShapeDtypeStruct(raw.shape, raw.dtype),
        name="norm_rows",
    )(gains, raw)


def norm_lyric_kernel(head_size, gain_ref, raw_ref, grad_ref, out_ref):
    for head in range(raw_ref.shape[1] // head_size):
        cols = slice(head * head_size, (head + 1) * head_size)
        out_ref[:, cols] = through_norm(raw_ref[:, cols], grad_ref[:, cols], gain_ref[1:2, :])


def norm_lyric(gains, raw, grad):
    return pl.pallas_call(
        functools.partial(norm_lyric_kernel, gains.shape[1]),
        out_shape=jax.ShapeDtypeStruct(raw.shape, jnp.bfloat16),
        name="norm_lyric",
    )(gains, raw, grad)


def sum_over(total, axis, bits):
    count = lax.axis_size(axis)
    for bit in bits:
        total = total + lax.ppermute(total, axis, [(i, i ^ bit) for i in range(count)])
    return total


def bits_of(count):
    return [1 << bit for bit in range(count.bit_length() - 1)]


def body(
    queries, keys, values, lyric_keys, lyric_values, q_gain, k_gain, cotangent, alignment, lyric_len
):
    frames = queries.shape[1]
    lyric_local, width = lyric_keys.shape[1:]
    count = lax.axis_size("seq")
    songs = lax.axis_size("song")
    me = lax.axis_index("seq")
    core = me % 2
    chips = count // 2
    chip = me // 2
    touching = (chip % 2) ^ core
    state = jnp.stack([core, touching]).astype(jnp.int32)
    gains = jnp.stack([q_gain, k_gain])

    swap = [(i, i ^ 1) for i in range(count)]
    partners = [(a, a ^ 1) for a in range(chips)]
    across = [(a, a ^ 2) for a in range(chips)]
    between = [(a, a + 1) for a in range(1, chips - 1, 2)]
    between += [(b, a) for a, b in between]

    def hop(block, moves):
        pairs = [(2 * a + c, 2 * b + c) for a, b in moves for c in (0, 1)]
        return lax.ppermute(block, "seq", pairs)

    hops = chips == 4 and lyric_local % 16 == 0
    total_rows = lyric_local * count
    if hops:
        run = ((0, lyric_local, lyric_local), (2 * lyric_local, 3 * lyric_local, lyric_local))
        groups = (run,) * 4
        owners = [chip, chip ^ 2, chip ^ 1, chip ^ 3]
        first_rows = []
        for owner in owners:
            first_rows += [
                (2 * owner + core) * lyric_local,
                (2 * owner + 1 - core) * lyric_local,
            ]
    else:
        gathered = jnp.concatenate(
            [
                lax.all_gather(
                    norm_rows(gains, lyric_keys[0]), "seq", axis=0, tiled=True
                ),
                lax.all_gather(lyric_values[0], "seq", axis=0, tiled=True),
            ],
            axis=0,
        )
        groups = (((0, total_rows, total_rows),),)
        first_rows = [0]
    has_left, has_right = chip > 0, chip < chips - 1
    has_near = jnp.where(core == 0, has_left, has_right)
    has_far = jnp.where(core == 0, has_right, has_left)
    meta = jnp.stack(
        [
            jnp.asarray(value, jnp.int32)
            for value in [core, touching]
            + [alignment[0, 0, slot] for slot in range(TILES)]
            + [lyric_len[0], has_near, has_far]
            + first_rows
        ]
    )

    to_mate = pack(
        state,
        alignment[0, 0],
        [queries[0], cotangent[0], keys[0], values[0]]
        + ([lyric_keys[0], lyric_values[0]] if hops else []),
    )
    mate = lax.ppermute(to_mate, "seq", swap)
    if hops:
        pair = pair_lyrics(state, gains, lyric_keys[0], lyric_values[0], mate)
        two = hop(pair, across)
        lyrics = [pair, two, hop(two, partners)]
        lead, after = [pair], [two]
    else:
        lyrics, lead, after = [gathered], [], []
    one = hop(edge(state, 1, gains, keys[0], values[0], mate, lead, []), partners)
    mid = hop(edge(state, 0, gains, keys[0], values[0], mate, [], after), between)
    key_low = prepare_keys(state, gains, keys[0], mate, after)
    output, grad_queries, for_mate, key_grad, value_grad, to_one, to_mid, gain_part, *parts = (
        attention(
            meta, gains, queries[0], cotangent[0], values[0], key_low, mate, one, mid, lyrics,
            groups,
        )
    )

    to_mate = []
    mid = hop(to_mid, between)
    if hops:
        held, for_two, to_two = parts
        gain_total = sum_over(sum_over(gain_part, "song", bits_of(songs)), "seq", [2])
        to_two, to_one = relay(for_two, hop(to_two, partners), gain_total, to_one)
        two, one = hop(to_two, across), hop(to_one, partners)
        own_half, part_to_mate, gain_total = finish_lyric(
            state, gains, lyric_keys[0], mate, held, one, two, gain_total, frames
        )
        to_mate = [part_to_mate]
    else:
        one = hop(to_one, partners)
    *filled, to_mate = finish_audio(
        state, gains, keys[0], mate, key_grad, value_grad, one, mid, for_mate,
        [output, grad_queries], to_mate,
    )
    from_mate = lax.ppermute(to_mate, "seq", swap)
    if hops:
        *filled, grad_lyric_keys, grad_lyric_values, q_total, k_total = join(
            state, gain_total, filled, own_half, from_mate
        )
    else:
        filled = fill_other(state, filled, from_mate)
        gain_total = lax.psum(gain_part, ("song", "seq"))
        q_total, k_total = gain_total[0:1], gain_total[1:2]
        spread = lax.dynamic_update_slice(
            jnp.zeros((2 * total_rows, width), jnp.float32),
            parts[0].astype(jnp.float32),
            (0, core * (width // 2)),
        )
        lyric_key_sum, grad_lyric_values = [
            lax.psum_scatter(part, "seq", scatter_dimension=0, tiled=True)
            for part in (spread[:total_rows], spread[total_rows:])
        ]
        grad_lyric_keys = norm_lyric(gains, lyric_keys[0], lyric_key_sum)
        grad_lyric_values = grad_lyric_values.astype(jnp.bfloat16)
    output, grad_queries, grad_keys, grad_values = filled
    return (
        output[None],
        grad_queries[None],
        grad_keys[None],
        grad_values[None],
        grad_lyric_keys[None],
        grad_lyric_values[None],
        q_total[0],
        k_total[0],
    )


def solution(mesh):
    split = P("song", "seq", None)
    return jax.shard_map(
        body,
        mesh=mesh,
        in_specs=(split, split, split, split, split, P(), P(), split, split, P("song")),
        out_specs=(split, split, split, split, split, split, P(), P()),
        check_vma=False,
    )
```

```python
import functools

import jax
import jax.numpy as jnp
from jax import lax
from jax.experimental import pallas as pl
from jax.experimental.pallas import tpu as pltpu
from jax.sharding import PartitionSpec as P

BLK = 128
TILES = 2
NORM_EPS = 1e-06
VMEM_LIMIT = 8 * 1024 * 1024
ATTENTION_VMEM_LIMIT = 24 * 1024 * 1024
PACK_VMEM_LIMIT = 60 * 1024 * 1024
VMEM = pl.BlockSpec(memory_space=pltpu.VMEM)
SMEM = pl.BlockSpec(memory_space=pltpu.SMEM)
HBM = pl.BlockSpec(memory_space=pltpu.HBM)
ANY = pl.BlockSpec(memory_space=pl.ANY)
GAIN_ROWS = 16
HEADS_PER_STEP = 2
CHUNKS = 2
ALIGN_ROWS = 32
SMALL = pl.CostEstimate(flops=1, bytes_accessed=1, transcendentals=0)


def dot(lhs, rhs, lhs_dim, rhs_dim):
    return lax.dot_general(
        lhs, rhs, (((lhs_dim,), (rhs_dim,)), ((), ())), preferred_element_type=jnp.float32
    )


def call(kernel, name, in_specs, out_specs, out_shape, limit=VMEM_LIMIT, cost=SMALL, **options):
    return pl.pallas_call(
        kernel,
        in_specs=in_specs,
        out_specs=out_specs,
        out_shape=out_shape,
        compiler_params=pltpu.CompilerParams(vmem_limit_bytes=limit),
        cost_estimate=cost,
        name=name,
        **options,
    )


def shape(rows, cols, dtype=jnp.bfloat16):
    return jax.ShapeDtypeStruct((rows, cols), dtype)


def half_of(ref, core):
    half = ref.shape[1] // 2
    return pl.ds(pl.multiple_of(core * half, half), half)


def chunk_of(ref, core, chunk):
    size = ref.shape[1] // 2 // CHUNKS
    return pl.ds(pl.multiple_of((core * CHUNKS + chunk) * size, size), size)


def chunk_cols(chunk, size):
    return slice(chunk * size, (chunk + 1) * size)


def split_rows(sums, cols):
    high = sums.astype(jnp.bfloat16).astype(jnp.float32)
    rest = sums - high
    middle = rest.astype(jnp.bfloat16).astype(jnp.float32)
    low = rest - middle
    empty = jnp.zeros((sums.shape[0], cols - 3 * sums.shape[1]), jnp.float32)
    rows = jnp.concatenate([high, middle, low, empty], axis=1)
    return jnp.concatenate([rows, jnp.zeros_like(rows)], axis=0).astype(jnp.bfloat16)


def joined_rows(rows, size):
    rows = rows.astype(jnp.float32)[0:8]
    return (rows[:, 2 * size : 3 * size] + rows[:, size : 2 * size]) + rows[:, 0:size]


def normed(raw, k_gain):
    raw = raw.astype(jnp.float32)
    inverse = lax.rsqrt(jnp.mean(raw * raw, axis=1, keepdims=True) + NORM_EPS)
    return (raw * inverse * k_gain).astype(jnp.bfloat16)


def norm_columns(out_ref, rows, raw, gain_ref):
    head_size = gain_ref.shape[1]
    for head in range(raw.shape[1] // head_size):
        cols = slice(head * head_size, (head + 1) * head_size)
        out_ref[rows, cols] = normed(raw[:, cols], gain_ref[1:2, :])


def through_norm(raw, grad, k_gain):
    raw = raw.astype(jnp.float32)
    inverse = lax.rsqrt(jnp.mean(raw * raw, axis=1, keepdims=True) + NORM_EPS)
    scaled = grad * k_gain
    return (
        inverse * scaled
        - raw * (inverse * inverse * inverse) * jnp.mean(scaled * raw, axis=1, keepdims=True)
    ).astype(jnp.bfloat16)


def pack_kernel(state_ref, align_ref, *refs):
    ins, (out_ref, sems) = refs[:-2], refs[-2:]
    start = 0
    copies = []
    for index, ref in enumerate(ins):
        rows = ref.shape[0]
        copies.append(
            pltpu.make_async_copy(
                ref.at[:, half_of(ref, 1 - state_ref[0])],
                out_ref.at[start : start + rows, :],
                sems.at[index],
            )
        )
        copies[-1].start()
        start += rows
    row = lax.broadcasted_iota(jnp.int32, (ALIGN_ROWS, out_ref.shape[1]), 0)
    tiles = jnp.zeros(row.shape, jnp.int32)
    for slot in range(TILES):
        tiles = jnp.where(row == slot, align_ref[slot], tiles)
    out_ref[start:, :] = tiles.astype(jnp.float32).astype(jnp.bfloat16)
    for copy in copies:
        copy.wait()


def pack(state, align, arrays):
    rows = sum(array.shape[0] for array in arrays) + ALIGN_ROWS
    return call(
        pack_kernel,
        "pack",
        [SMEM, SMEM] + [HBM] * len(arrays),
        VMEM,
        shape(rows, arrays[0].shape[1] // 2),
        limit=PACK_VMEM_LIMIT,
        scratch_shapes=[pltpu.SemaphoreType.DMA((len(arrays),))],
    )(state, align, *arrays)


def pair_kernel(chunk, state_ref, gain_ref, key_ref, value_ref, mate_ref, pair_ref):
    rows = key_ref.shape[0]
    first = mate_ref.shape[0] - ALIGN_ROWS - 2 * rows
    own = chunk_of(key_ref, state_ref[0], chunk)
    cols = chunk_cols(chunk, pair_ref.shape[1])
    norm_columns(pair_ref, slice(0, rows), key_ref[:, own], gain_ref)
    pair_ref[rows : 2 * rows, :] = value_ref[:, own]
    norm_columns(
        pair_ref, slice(2 * rows, 3 * rows), mate_ref[first : first + rows, cols], gain_ref
    )
    pair_ref[3 * rows :, :] = mate_ref[first + rows : first + 2 * rows, cols]


def pair_lyrics(state, chunk, gains, lyric_key, lyric_value, mate):
    rows, width = lyric_key.shape
    return call(
        functools.partial(pair_kernel, chunk),
        "pair_lyrics",
        [SMEM] + [VMEM] * 4,
        VMEM,
        shape(4 * rows, width // 2 // CHUNKS),
    )(state, gains, lyric_key, lyric_value, mate)


def edge_kernel(
    chunk, touching, leading, state_ref, gain_ref, key_ref, value_ref, mate_ref, *refs
):
    out_ref = refs[-1]
    frames = key_ref.shape[0]
    first = out_ref.shape[0] - 2 * frames
    if leading:
        out_ref[0:first, :] = refs[0][...]
    mine = state_ref[1] == touching
    own = chunk_of(key_ref, state_ref[0], chunk)
    cols = chunk_cols(chunk, out_ref.shape[1])
    keys = jnp.where(mine, key_ref[:, own], mate_ref[2 * frames : 3 * frames, cols])
    norm_columns(out_ref, slice(first, first + frames), keys, gain_ref)
    out_ref[first + frames :, :] = jnp.where(
        mine, value_ref[:, own], mate_ref[3 * frames : 4 * frames, cols]
    )


def edge(state, chunk, touching, gains, key, value, mate, lead, after):
    frames, width = key.shape
    rows = sum(array.shape[0] for array in lead) + 2 * frames
    return call(
        functools.partial(edge_kernel, chunk, touching, bool(lead)),
        "edge",
        [SMEM] + [VMEM] * (4 + len(lead)) + [ANY] * len(after),
        VMEM,
        shape(rows, width // 2 // CHUNKS),
    )(state, gains, key, value, mate, *lead, *after)


def prepare_kernel(state_ref, gain_ref, key_ref, mate_ref, *refs):
    out_ref = refs[-1]
    frames = key_ref.shape[0]
    own = half_of(key_ref, state_ref[0])
    norm_columns(out_ref, slice(0, frames), key_ref[:, own], gain_ref)
    norm_columns(
        out_ref, slice(frames, 2 * frames), mate_ref[2 * frames : 3 * frames, :], gain_ref
    )


def prepare_keys(state, gains, key, mate, after):
    frames, width = key.shape
    return call(
        prepare_kernel,
        "prepare_keys",
        [SMEM] + [VMEM] * 3 + [ANY] * len(after),
        VMEM,
        shape(2 * frames, width // 2),
    )(state, gains, key, mate, *after)


def attention_kernel(
    chunk, groups, head_size, score_scale, meta_ref, gain_ref, query_ref, grad_ref, value_ref, key_ref,
    mate_ref, one_ref, mid_ref, *refs
):
    frames = query_ref.shape[0]
    exchanged = len(groups) == 4
    inputs = 3 if exchanged else 1
    lyric_in, refs = refs[:inputs], refs[inputs:]
    earlier, refs = refs[: 3 * chunk], refs[3 * chunk :]
    window = one_ref.shape[0] - 2 * frames
    out_ref, grad_query_ref, to_mate_ref, key_grad_ref, value_grad_ref = refs[:5]
    to_one_ref, to_mid_ref, gain_grad_ref = refs[5:8]
    lyric_out, mask_ref = refs[8:-1], refs[-1]
    runs = [(index, run) for index, group in enumerate(groups) for run in group]
    main = 2 * frames + sum(run[2] for _, run in runs)
    lanes = 2 * frames
    align = mate_ref.shape[0] - ALIGN_ROWS
    touching = meta_ref[1] == 1

    size = out_ref.shape[1]
    for index in range(chunk):
        for ref, part_ref in zip((to_one_ref, to_mid_ref), earlier[3 * index :]):
            if ref.shape[1] > size:
                ref[:, chunk_cols(index, size)] = part_ref[...]
    gain_grad_ref[...] = earlier[-1][...] if chunk else jnp.zeros_like(gain_grad_ref)
    mate_tiles = mate_ref[align:, 0:frames].astype(jnp.float32).astype(jnp.int32)
    start = 0
    for number, (_, (_, _, rows)) in enumerate(runs):
        row = lax.broadcasted_iota(jnp.int32, (rows, lanes), 0) + meta_ref[7 + number]
        keep = jnp.zeros((rows, lanes), jnp.float32)
        for slot in range(TILES):
            tile = jnp.concatenate(
                [
                    jnp.full((1, frames), meta_ref[2 + slot], jnp.int32),
                    mate_tiles[slot : slot + 1],
                ],
                axis=1,
            )
            lower = tile * BLK
            upper = jnp.minimum(lower + BLK, meta_ref[4])
            inside = (row >= lower) & (row < upper) & (lower >= 0)
            keep = jnp.where(inside, 1.0, keep)
        mask_ref[start : start + rows, :] = keep
        start += rows
    lane = lax.broadcasted_iota(jnp.int32, (frames, lanes), 1)
    mask_ref[start : start + frames, :] = jnp.where(
        lane < frames, meta_ref[5], meta_ref[6]
    ).astype(jnp.float32)

    q_gain = gain_ref[0:1, :]
    k_gain = gain_ref[1:2, :]
    heads = size // head_size
    sent = to_one_ref.shape[1] // size > 1

    def one_head(head):
        cols = pl.ds(pl.multiple_of(head * head_size, head_size), head_size)
        half_cols = pl.ds(
            pl.multiple_of((chunk * heads + head) * head_size, head_size), head_size
        )
        own_cols = pl.ds(
            pl.multiple_of(
                ((meta_ref[0] * CHUNKS + chunk) * heads + head) * head_size, head_size
            ),
            head_size,
        )
        sent_cols = half_cols if sent else cols
        lyric = [ref[:, cols if exchanged else own_cols] for ref in lyric_in]
        if exchanged:
            lyric = [lyric[0], lyric[1], one_ref[0:window, cols], lyric[2]]
        one_rows, mid_rows = one_ref[window:, cols], mid_ref[:, cols]
        near_rows = jnp.where(touching, one_rows, mid_rows)
        far_rows = jnp.where(touching, mid_rows, one_rows)

        def from_mate(number):
            return mate_ref[number * frames : (number + 1) * frames, half_cols]

        query = jnp.concatenate([query_ref[:, own_cols], from_mate(0)], axis=0)
        query = query.astype(jnp.float32)
        cot = jnp.concatenate([grad_ref[:, own_cols], from_mate(1)], axis=0)
        key_low = jnp.concatenate(
            [key_ref[:, half_cols]]
            + [lyric[index][run[0] : run[0] + run[2]] for index, run in runs]
            + [near_rows[:frames], far_rows[:frames]],
            axis=0,
        )
        value = jnp.concatenate(
            [value_ref[:, own_cols], from_mate(3)]
            + [lyric[index][run[1] : run[1] + run[2]] for index, run in runs]
            + [near_rows[frames:], far_rows[frames:]],
            axis=0,
        )
        query_inv = lax.rsqrt(jnp.mean(query * query, axis=1, keepdims=True) + NORM_EPS)
        query_hat = query * query_inv
        query_low = (query_hat * (q_gain * score_scale)).astype(jnp.bfloat16)

        near, far = slice(main, main + frames), slice(main + frames, main + 2 * frames)

        def against(rows, columns):
            return jnp.concatenate(
                [
                    dot(rows[:main], columns, 1, 1),
                    jnp.concatenate(
                        [
                            dot(rows[near], columns[:frames], 1, 1),
                            dot(rows[far], columns[frames:], 1, 1),
                        ],
                        axis=1,
                    ),
                ],
                axis=0,
            )

        def over_keys(weights, rows):
            return dot(weights[:main], rows[:main], 0, 0) + jnp.concatenate(
                [
                    dot(weights[main:, :frames], rows[near], 0, 0),
                    dot(weights[main:, frames:], rows[far], 0, 0),
                ],
                axis=0,
            )

        def over_queries(weights, columns):
            return jnp.concatenate(
                [
                    dot(weights[:main], columns, 1, 0),
                    dot(weights[main:, :frames], columns[:frames], 1, 0),
                    dot(weights[main:, frames:], columns[frames:], 1, 0),
                ],
                axis=0,
            )

        exp_scores = jnp.exp(against(key_low, query_low))
        exp_scores = jnp.concatenate(
            [exp_scores[: 2 * frames], exp_scores[2 * frames :] * mask_ref[...]], axis=0
        )
        grad_prob = against(value, cot)
        prob = exp_scores * (1.0 / jnp.sum(exp_scores, axis=0, keepdims=True))
        prob_low = prob.astype(jnp.bfloat16)
        weighted = prob * grad_prob
        delta = jnp.sum(weighted, axis=0, keepdims=True)
        grad_score = (weighted - prob * delta).astype(jnp.bfloat16)
        output = over_keys(prob_low, value).astype(jnp.bfloat16)
        grad_low = over_keys(grad_score, key_low)
        grad_qn = grad_low * score_scale
        grad_keys = over_queries(grad_score, query_low)
        grad_values = over_queries(prob_low, cot)
        scaled = grad_qn * q_gain
        grad_query = (
            query_inv * scaled
            - query_hat
            * (query_inv * query_inv)
            * jnp.mean(scaled * query, axis=1, keepdims=True)
        ).astype(jnp.bfloat16)
        gain_grad_ref[0:1, :] += jnp.sum(grad_qn * query_hat, axis=0, keepdims=True)
        gain_grad_ref[1:2, :] += (
            jnp.sum(grad_low * query_low.astype(jnp.float32), axis=0, keepdims=True) / k_gain
        )

        out_ref[:, cols] = output[:frames]
        grad_query_ref[:, cols] = grad_query[:frames]
        to_mate_ref[0:frames, cols] = output[frames:]
        to_mate_ref[frames:, cols] = grad_query[frames:]
        key_grad_ref[:, cols] = grad_keys[: 2 * frames]
        value_grad_ref[:, cols] = grad_values[: 2 * frames]
        for grads, part in (
            (grad_keys.astype(jnp.bfloat16), 0),
            (grad_values.astype(jnp.bfloat16), frames),
        ):
            to_one_ref[window + part : window + part + frames, sent_cols] = jnp.where(
                touching, grads[near], grads[far]
            )
            to_mid_ref[part : part + frames, sent_cols] = jnp.where(touching, grads[far], grads[near])
        if exchanged:
            held_ref, two_ref, to_two_ref = lyric_out
            outs = (held_ref, two_ref, to_one_ref, to_two_ref)
        else:
            outs = lyric_out
        start = 2 * frames
        for index, (key_row, value_row, rows) in runs:
            part = slice(start, start + rows)
            put = sent_cols if outs[index] is to_one_ref else cols
            outs[index][key_row : key_row + rows, put] = grad_keys[part].astype(jnp.bfloat16)
            outs[index][value_row : value_row + rows, put] = grad_values[part].astype(
                jnp.bfloat16
            )
            start += rows

    @pl.loop(0, heads // HEADS_PER_STEP)
    def _(step):
        for number in range(HEADS_PER_STEP):
            one_head(step * HEADS_PER_STEP + number)


def attention(
    chunk, meta, gains, query, cot, value, key, mate, one, mid, lyrics, groups, earlier
):
    frames, width = query.shape
    head_size = gains.shape[1]
    size = width // 2 // CHUNKS
    sent = size if chunk < CHUNKS - 1 else width // 2
    lyric_rows = sum(run[2] for group in groups for run in group)
    key_rows = 3 * frames + lyric_rows
    bf16, f32 = jnp.bfloat16, jnp.float32
    slot = sum(2 * run[2] for run in groups[0])
    out_shape = [shape(frames, size)] * 2
    out_shape += [shape(2 * frames, size, dtype) for dtype in (bf16, f32, f32)]
    out_shape += [shape(one.shape[0], sent), shape(2 * frames, sent), shape(8, head_size, f32)]
    out_shape += [shape(slot, size)] * len(lyrics)
    return call(
        functools.partial(attention_kernel, chunk, groups, head_size, head_size ** (-0.5)),
        "attention",
        [SMEM] + [VMEM] * (8 + len(lyrics) + len(earlier)),
        [VMEM] * len(out_shape),
        out_shape,
        limit=ATTENTION_VMEM_LIMIT,
        cost=pl.CostEstimate(
            flops=24 * key_rows * frames * size,
            bytes_accessed=8 * 1024 * 1024,
            transcendentals=2 * key_rows * frames * (size // head_size),
        ),
        scratch_shapes=[pltpu.VMEM((frames + lyric_rows, 2 * frames), f32)],
    )(meta, gains, query, cot, value, key, mate, one, mid, *lyrics, *earlier)


def finish_audio_kernel(
    state_ref, gain_ref, raw_ref, mate_ref, one_ref, mid_ref, *refs
):
    chunk_refs, refs = refs[: 5 * CHUNKS], refs[5 * CHUNKS :]
    *lyric, out, query_out, key_out, value_out, to_mate_ref, key_ref, value_ref, sems = refs
    head_size = gain_ref.shape[1]
    k_gain = gain_ref[1:2, :]
    frames, half = key_ref.shape
    size = half // CHUNKS
    own, mate = slice(0, frames), slice(frames, 2 * frames)
    first = one_ref.shape[0] - 2 * frames
    touching = state_ref[1] == 1
    copies = []
    for chunk in range(CHUNKS):
        out_own_ref, query_own_ref, ready_ref = chunk_refs[5 * chunk : 5 * chunk + 3]
        for source, target in ((out_own_ref, out), (query_own_ref, query_out)):
            copies.append(
                pltpu.make_async_copy(
                    source,
                    target.at[:, chunk_of(target, state_ref[0], chunk)],
                    sems.at[len(copies)],
                )
            )
            copies[-1].start()
        to_mate_ref[0 : 2 * frames, chunk_cols(chunk, size)] = ready_ref[...]
    for ref in lyric:
        to_mate_ref[4 * frames :, :] = ref[...]
    raw_keys = raw_ref[:, half_of(raw_ref, state_ref[0])]
    for head in range(half // head_size):
        cols = slice(head * head_size, (head + 1) * head_size)
        chunk = head * head_size // size
        part = slice(head * head_size - chunk * size, (head + 1) * head_size - chunk * size)
        key_grad_ref, value_grad_ref = chunk_refs[5 * chunk + 3 : 5 * chunk + 5]
        one = one_ref[first:, cols].astype(jnp.float32)
        mid = mid_ref[:, cols].astype(jnp.float32)
        for_own = jnp.where(touching, one, mid)
        for_mate = jnp.where(touching, mid, one)
        key_ref[:, cols] = through_norm(
            raw_keys[:, cols], key_grad_ref[own, part] + for_own[:frames], k_gain
        )
        value_ref[:, cols] = (value_grad_ref[own, part] + for_own[frames:]).astype(jnp.bfloat16)
        to_mate_ref[2 * frames : 3 * frames, cols] = through_norm(
            mate_ref[2 * frames : 3 * frames, cols],
            key_grad_ref[mate, part] + for_mate[:frames],
            k_gain,
        )
        to_mate_ref[3 * frames : 4 * frames, cols] = (
            value_grad_ref[mate, part] + for_mate[frames:]
        ).astype(jnp.bfloat16)
    for source, target in ((key_ref, key_out), (value_ref, value_out)):
        copies.append(
            pltpu.make_async_copy(
                source, target.at[:, half_of(target, state_ref[0])], sems.at[len(copies)]
            )
        )
        copies[-1].start()
    for copy in copies:
        copy.wait()


def finish_audio(state, gains, raw, mate, one, mid, chunks, lyric):
    frames, width = raw.shape
    half = width // 2
    rows = 4 * frames + sum(array.shape[0] for array in lyric)
    return call(
        finish_audio_kernel,
        "finish_audio",
        [SMEM] + [VMEM] * (5 + len(chunks) + len(lyric)),
        [HBM] * 4 + [VMEM],
        [shape(frames, width)] * 4 + [shape(rows, half)],
        scratch_shapes=[pltpu.VMEM((frames, half), jnp.bfloat16)] * 2
        + [pltpu.SemaphoreType.DMA((2 * CHUNKS + 2,))],
    )(state, gains, raw, mate, one, mid, *chunks, *lyric)


def relay_kernel(total_ref, later_ref, *refs):
    parts, arrived, (out_ref, _) = refs[:CHUNKS], refs[CHUNKS : 2 * CHUNKS], refs[2 * CHUNKS :]
    rows, size = parts[0].shape
    for chunk, (part_ref, arrived_ref) in enumerate(zip(parts, arrived)):
        out_ref[0:rows, chunk_cols(chunk, size)] = (
            part_ref[...].astype(jnp.float32) + arrived_ref[...].astype(jnp.float32)
        ).astype(jnp.bfloat16)
    out_ref[rows:, :] = split_rows(total_ref[...], out_ref.shape[1])


def relay(parts, arrived, total, later):
    rows, size = parts[0].shape
    return call(
        relay_kernel,
        "relay",
        [VMEM, ANY] + [VMEM] * (2 * CHUNKS),
        [VMEM, ANY],
        [shape(rows + GAIN_ROWS, CHUNKS * size), shape(*later.shape)],
        input_output_aliases={1: 1},
    )(total, later, *parts, *arrived)


def finish_lyric_kernel(
    state_ref, gain_ref, raw_ref, mate_ref, one_ref, two_ref, sum_ref, *refs
):
    held_refs, (own_ref, to_mate_ref, total_ref) = refs[:CHUNKS], refs[CHUNKS:]
    rows = raw_ref.shape[0]
    head_size = gain_ref.shape[1]
    k_gain = gain_ref[1:2, :]
    size = held_refs[0].shape[1]
    first = mate_ref.shape[0] - ALIGN_ROWS - 2 * rows
    total_ref[...] = sum_ref[...] + joined_rows(two_ref[4 * rows :, :], head_size)
    to_mate_ref[2 * rows :, :] = split_rows(total_ref[...], to_mate_ref.shape[1])
    raw_keys = raw_ref[:, half_of(raw_ref, state_ref[0])]
    for head in range(own_ref.shape[1] // head_size):
        cols = slice(head * head_size, (head + 1) * head_size)
        chunk = head * head_size // size
        part = slice(head * head_size - chunk * size, (head + 1) * head_size - chunk * size)
        total = held_refs[chunk][:, part].astype(jnp.float32)
        for ref in (one_ref, two_ref):
            total = total + ref[0 : 4 * rows, cols].astype(jnp.float32)
        mate_keys = mate_ref[first : first + rows, cols]
        for ref, base, raw in (
            (own_ref, 0, raw_keys[:, cols]),
            (to_mate_ref, 2 * rows, mate_keys),
        ):
            ref[0:rows, cols] = through_norm(raw, total[base : base + rows], k_gain)
            ref[rows : 2 * rows, cols] = total[base + rows : base + 2 * rows].astype(jnp.bfloat16)


def finish_lyric(state, gains, raw, mate, held, one, two, total):
    rows, width = raw.shape
    half = width // 2
    return call(
        finish_lyric_kernel,
        "finish_lyric",
        [SMEM] + [VMEM] * (6 + len(held)),
        [VMEM] * 3,
        [
            shape(2 * rows, half),
            shape(2 * rows + GAIN_ROWS, half),
            shape(*total.shape, jnp.float32),
        ],
    )(state, gains, raw, mate, one, two, total, *held)


def join_kernel(count, state_ref, gain_ref, own_ref, mate_ref, *refs):
    outs, (q_total_ref, k_total_ref, sems) = refs[count:-3], refs[-3:]
    frames = outs[0].shape[0]
    rows = own_ref.shape[0] // 2
    pieces = [
        (mate_ref.at[index * frames : (index + 1) * frames, :], out, 1 - state_ref[0])
        for index, out in enumerate(outs[:count])
    ]
    for ref, first, core in ((own_ref, 0, state_ref[0]), (mate_ref, count * frames, 1 - state_ref[0])):
        for index, out in enumerate(outs[count:]):
            start = first + index * rows
            pieces.append((ref.at[start : start + rows, :], out, core))
    copies = [
        pltpu.make_async_copy(source, out.at[:, half_of(out, core)], sems.at[index])
        for index, (source, out, core) in enumerate(pieces)
    ]
    for copy in copies:
        copy.start()
    sums = mate_ref[mate_ref.shape[0] - GAIN_ROWS :, :]
    total = gain_ref[...] + joined_rows(sums, gain_ref.shape[1])
    q_total_ref[...] = total[0:1]
    k_total_ref[...] = total[1:2]
    for copy in copies:
        copy.wait()


def join(state, gain, arrays, own, mate):
    rows, half = own.shape
    count = len(arrays)
    return call(
        functools.partial(join_kernel, count),
        "join",
        [SMEM] + [VMEM] * 3 + [HBM] * count,
        [HBM] * (count + 2) + [VMEM] * 2,
        [shape(*array.shape) for array in arrays]
        + [shape(rows // 2, 2 * half)] * 2
        + [shape(1, gain.shape[1], jnp.float32)] * 2,
        input_output_aliases={4 + i: i for i in range(count)},
        scratch_shapes=[pltpu.SemaphoreType.DMA((count + 4,))],
    )(state, gain, own, mate, *arrays)


def fill_kernel(count, state_ref, mate_ref, *refs):
    outs, sems = refs[count:-1], refs[-1]
    frames = outs[0].shape[0]
    copies = [
        pltpu.make_async_copy(
            mate_ref.at[index * frames : (index + 1) * frames, :],
            out.at[:, half_of(out, 1 - state_ref[0])],
            sems.at[index],
        )
        for index, out in enumerate(outs)
    ]
    for copy in copies:
        copy.start()
    for copy in copies:
        copy.wait()


def fill_other(state, arrays, mate):
    count = len(arrays)
    return call(
        functools.partial(fill_kernel, count),
        "fill_other",
        [SMEM, VMEM] + [HBM] * count,
        [HBM] * count,
        [shape(*array.shape) for array in arrays],
        input_output_aliases={2 + i: i for i in range(count)},
        scratch_shapes=[pltpu.SemaphoreType.DMA((count,))],
    )(state, mate, *arrays)


def norm_rows_kernel(gain_ref, raw_ref, out_ref):
    norm_columns(out_ref, slice(0, raw_ref.shape[0]), raw_ref[...], gain_ref)


def norm_rows(gains, raw):
    return pl.pallas_call(
        norm_rows_kernel,
        out_shape=jax.ShapeDtypeStruct(raw.shape, raw.dtype),
        name="norm_rows",
    )(gains, raw)


def norm_lyric_kernel(head_size, gain_ref, raw_ref, grad_ref, out_ref):
    for head in range(raw_ref.shape[1] // head_size):
        cols = slice(head * head_size, (head + 1) * head_size)
        out_ref[:, cols] = through_norm(raw_ref[:, cols], grad_ref[:, cols], gain_ref[1:2, :])


def norm_lyric(gains, raw, grad):
    return pl.pallas_call(
        functools.partial(norm_lyric_kernel, gains.shape[1]),
        out_shape=jax.ShapeDtypeStruct(raw.shape, jnp.bfloat16),
        name="norm_lyric",
    )(gains, raw, grad)


def sum_over(total, axis, bits):
    count = lax.axis_size(axis)
    for bit in bits:
        total = total + lax.ppermute(total, axis, [(i, i ^ bit) for i in range(count)])
    return total


def bits_of(count):
    return [1 << bit for bit in range(count.bit_length() - 1)]


def body(
    queries, keys, values, lyric_keys, lyric_values, q_gain, k_gain, cotangent, alignment, lyric_len
):
    frames = queries.shape[1]
    lyric_local, width = lyric_keys.shape[1:]
    count = lax.axis_size("seq")
    songs = lax.axis_size("song")
    me = lax.axis_index("seq")
    core = me % 2
    chips = count // 2
    chip = me // 2
    touching = (chip % 2) ^ core
    state = jnp.stack([core, touching]).astype(jnp.int32)
    gains = jnp.stack([q_gain, k_gain])

    swap = [(i, i ^ 1) for i in range(count)]
    partners = [(a, a ^ 1) for a in range(chips)]
    across = [(a, a ^ 2) for a in range(chips)]
    between = [(a, a + 1) for a in range(1, chips - 1, 2)]
    between += [(b, a) for a, b in between]

    def hop(block, moves):
        pairs = [(2 * a + c, 2 * b + c) for a, b in moves for c in (0, 1)]
        return lax.ppermute(block, "seq", pairs)

    hops = chips == 4 and lyric_local % 16 == 0
    total_rows = lyric_local * count
    if hops:
        run = ((0, lyric_local, lyric_local), (2 * lyric_local, 3 * lyric_local, lyric_local))
        groups = (run,) * 4
        owners = [chip, chip ^ 2, chip ^ 1, chip ^ 3]
        first_rows = []
        for owner in owners:
            first_rows += [
                (2 * owner + core) * lyric_local,
                (2 * owner + 1 - core) * lyric_local,
            ]
    else:
        gathered = jnp.concatenate(
            [
                lax.all_gather(
                    norm_rows(gains, lyric_keys[0]), "seq", axis=0, tiled=True
                ),
                lax.all_gather(lyric_values[0], "seq", axis=0, tiled=True),
            ],
            axis=0,
        )
        groups = (((0, total_rows, total_rows),),)
        first_rows = [0]
    has_left, has_right = chip > 0, chip < chips - 1
    has_near = jnp.where(core == 0, has_left, has_right)
    has_far = jnp.where(core == 0, has_right, has_left)
    meta = jnp.stack(
        [
            jnp.asarray(value, jnp.int32)
            for value in [core, touching]
            + [alignment[0, 0, slot] for slot in range(TILES)]
            + [lyric_len[0], has_near, has_far]
            + first_rows
        ]
    )

    to_mate = pack(
        state,
        alignment[0, 0],
        [queries[0], cotangent[0], keys[0], values[0]]
        + ([lyric_keys[0], lyric_values[0]] if hops else []),
    )
    mate = lax.ppermute(to_mate, "seq", swap)
    chunks, parts, earlier, arrived = [], [], [], []
    after = []
    for chunk in range(CHUNKS):
        before = after
        if hops:
            pair = pair_lyrics(state, chunk, gains, lyric_keys[0], lyric_values[0], mate)
            two = hop(pair, across)
            lyrics = [pair, two, hop(two, partners)]
            lead, after = [pair], [two]
        else:
            lyrics, lead = [gathered], []
        one = hop(edge(state, chunk, 1, gains, keys[0], values[0], mate, lead, before), partners)
        mid = hop(edge(state, chunk, 0, gains, keys[0], values[0], mate, [], after), between)
        if not chunk:
            key_low = prepare_keys(state, gains, keys[0], mate, after)
        results = attention(
            chunk, meta, gains, queries[0], cotangent[0], values[0], key_low, mate, one, mid,
            lyrics, groups, earlier,
        )
        chunks += results[:5]
        earlier = [*earlier, *results[5:8]]
        parts.append(results[8:])
        if hops:
            arrived.append(hop(results[-1], partners))
    to_one, to_mid, gain_part = earlier[-3:]

    mid = hop(to_mid, between)
    to_mate = []
    if hops:
        gain_total = sum_over(sum_over(gain_part, "song", bits_of(songs)), "seq", [2])
        to_two, to_one = relay([part[1] for part in parts], arrived, gain_total, to_one)
        two, one = hop(to_two, across), hop(to_one, partners)
        own_half, part_to_mate, gain_total = finish_lyric(
            state, gains, lyric_keys[0], mate, [part[0] for part in parts], one, two, gain_total
        )
        to_mate = [part_to_mate]
    else:
        one = hop(to_one, partners)
    *filled, to_mate = finish_audio(state, gains, keys[0], mate, one, mid, chunks, to_mate)
    from_mate = lax.ppermute(to_mate, "seq", swap)
    if hops:
        *filled, grad_lyric_keys, grad_lyric_values, q_total, k_total = join(
            state, gain_total, filled, own_half, from_mate
        )
    else:
        filled = fill_other(state, filled, from_mate)
        gain_total = lax.psum(gain_part, ("song", "seq"))
        q_total, k_total = gain_total[0:1], gain_total[1:2]
        spread = lax.dynamic_update_slice(
            jnp.zeros((2 * total_rows, width), jnp.float32),
            jnp.concatenate([part[0] for part in parts], axis=1).astype(jnp.float32),
            (0, core * (width // 2)),
        )
        lyric_key_sum, grad_lyric_values = [
            lax.psum_scatter(part, "seq", scatter_dimension=0, tiled=True)
            for part in (spread[:total_rows], spread[total_rows:])
        ]
        grad_lyric_keys = norm_lyric(gains, lyric_keys[0], lyric_key_sum)
        grad_lyric_values = grad_lyric_values.astype(jnp.bfloat16)
    output, grad_queries, grad_keys, grad_values = filled
    return (
        output[None],
        grad_queries[None],
        grad_keys[None],
        grad_values[None],
        grad_lyric_keys[None],
        grad_lyric_values[None],
        q_total[0],
        k_total[0],
    )


def solution(mesh):
    split = P("song", "seq", None)
    return jax.shard_map(
        body,
        mesh=mesh,
        in_specs=(split, split, split, split, split, P(), P(), split, split, P("song")),
        out_specs=(split, split, split, split, split, split, P(), P()),
        check_vma=False,
    )
```

```python
import functools

import jax
import jax.numpy as jnp
from jax import lax
from jax.experimental import pallas as pl
from jax.experimental.pallas import tpu as pltpu
from jax.sharding import PartitionSpec as P

BLK = 128
TILES = 2
NORM_EPS = 1e-06
VMEM_LIMIT = 8 * 1024 * 1024
ATTENTION_VMEM_LIMIT = 24 * 1024 * 1024
PACK_VMEM_LIMIT = 60 * 1024 * 1024
VMEM = pl.BlockSpec(memory_space=pltpu.VMEM)
SMEM = pl.BlockSpec(memory_space=pltpu.SMEM)
HBM = pl.BlockSpec(memory_space=pltpu.HBM)
ANY = pl.BlockSpec(memory_space=pl.ANY)
GAIN_ROWS = 16
HEADS_PER_STEP = 2
CHUNKS = 2
ALIGN_ROWS = 32
SMALL = pl.CostEstimate(flops=1, bytes_accessed=1, transcendentals=0)


def dot(lhs, rhs, lhs_dim, rhs_dim):
    return lax.dot_general(
        lhs, rhs, (((lhs_dim,), (rhs_dim,)), ((), ())), preferred_element_type=jnp.float32
    )


def call(kernel, name, in_specs, out_specs, out_shape, limit=VMEM_LIMIT, cost=SMALL, **options):
    return pl.pallas_call(
        kernel,
        in_specs=in_specs,
        out_specs=out_specs,
        out_shape=out_shape,
        compiler_params=pltpu.CompilerParams(vmem_limit_bytes=limit),
        cost_estimate=cost,
        name=name,
        **options,
    )


def shape(rows, cols, dtype=jnp.bfloat16):
    return jax.ShapeDtypeStruct((rows, cols), dtype)


def half_of(ref, core):
    half = ref.shape[1] // 2
    return pl.ds(pl.multiple_of(core * half, half), half)


def chunk_of(ref, core, chunk):
    size = ref.shape[1] // 2 // CHUNKS
    return pl.ds(pl.multiple_of((core * CHUNKS + chunk) * size, size), size)


def chunk_cols(chunk, size):
    return slice(chunk * size, (chunk + 1) * size)


def split_rows(sums, cols):
    high = sums.astype(jnp.bfloat16).astype(jnp.float32)
    rest = sums - high
    middle = rest.astype(jnp.bfloat16).astype(jnp.float32)
    low = rest - middle
    empty = jnp.zeros((sums.shape[0], cols - 3 * sums.shape[1]), jnp.float32)
    rows = jnp.concatenate([high, middle, low, empty], axis=1)
    return jnp.concatenate([rows, jnp.zeros_like(rows)], axis=0).astype(jnp.bfloat16)


def joined_rows(rows, size):
    rows = rows.astype(jnp.float32)[0:8]
    return (rows[:, 2 * size : 3 * size] + rows[:, size : 2 * size]) + rows[:, 0:size]


def normed(raw, k_gain):
    raw = raw.astype(jnp.float32)
    inverse = lax.rsqrt(jnp.mean(raw * raw, axis=1, keepdims=True) + NORM_EPS)
    return (raw * inverse * k_gain).astype(jnp.bfloat16)


def norm_columns(out_ref, rows, raw, gain_ref):
    head_size = gain_ref.shape[1]
    for head in range(raw.shape[1] // head_size):
        cols = slice(head * head_size, (head + 1) * head_size)
        out_ref[rows, cols] = normed(raw[:, cols], gain_ref[1:2, :])


def through_norm(raw, grad, k_gain):
    raw = raw.astype(jnp.float32)
    inverse = lax.rsqrt(jnp.mean(raw * raw, axis=1, keepdims=True) + NORM_EPS)
    scaled = grad * k_gain
    return (
        inverse * scaled
        - raw * (inverse * inverse * inverse) * jnp.mean(scaled * raw, axis=1, keepdims=True)
    ).astype(jnp.bfloat16)


def pack_kernel(state_ref, align_ref, *refs):
    ins, (out_ref, sems) = refs[:-2], refs[-2:]
    start = 0
    copies = []
    for index, ref in enumerate(ins):
        rows = ref.shape[0]
        copies.append(
            pltpu.make_async_copy(
                ref.at[:, half_of(ref, 1 - state_ref[0])],
                out_ref.at[start : start + rows, :],
                sems.at[index],
            )
        )
        copies[-1].start()
        start += rows
    row = lax.broadcasted_iota(jnp.int32, (ALIGN_ROWS, out_ref.shape[1]), 0)
    tiles = jnp.zeros(row.shape, jnp.int32)
    for slot in range(TILES):
        tiles = jnp.where(row == slot, align_ref[slot], tiles)
    out_ref[start:, :] = tiles.astype(jnp.float32).astype(jnp.bfloat16)
    for copy in copies:
        copy.wait()


def pack(state, align, arrays):
    rows = sum(array.shape[0] for array in arrays) + ALIGN_ROWS
    return call(
        pack_kernel,
        "pack",
        [SMEM, SMEM] + [HBM] * len(arrays),
        VMEM,
        shape(rows, arrays[0].shape[1] // 2),
        limit=PACK_VMEM_LIMIT,
        scratch_shapes=[pltpu.SemaphoreType.DMA((len(arrays),))],
    )(state, align, *arrays)


def pair_kernel(chunk, state_ref, gain_ref, key_ref, value_ref, mate_ref, *refs):
    pair_ref = refs[-1]
    rows = key_ref.shape[0]
    first = mate_ref.shape[0] - ALIGN_ROWS - 2 * rows
    own = chunk_of(key_ref, state_ref[0], chunk)
    cols = chunk_cols(chunk, pair_ref.shape[1])
    norm_columns(pair_ref, slice(0, rows), key_ref[:, own], gain_ref)
    pair_ref[rows : 2 * rows, :] = value_ref[:, own]
    norm_columns(
        pair_ref, slice(2 * rows, 3 * rows), mate_ref[first : first + rows, cols], gain_ref
    )
    pair_ref[3 * rows :, :] = mate_ref[first + rows : first + 2 * rows, cols]


def pair_lyrics(state, chunk, gains, lyric_key, lyric_value, mate, after):
    rows, width = lyric_key.shape
    return call(
        functools.partial(pair_kernel, chunk),
        "pair_lyrics",
        [SMEM] + [VMEM] * 4 + [ANY] * len(after),
        VMEM,
        shape(4 * rows, width // 2 // CHUNKS),
    )(state, gains, lyric_key, lyric_value, mate, *after)


def edge_kernel(
    chunk, touching, leading, state_ref, gain_ref, key_ref, value_ref, mate_ref, *refs
):
    out_ref = refs[-1]
    frames = key_ref.shape[0]
    first = out_ref.shape[0] - 2 * frames
    if leading:
        out_ref[0:first, :] = refs[0][...]
    mine = state_ref[1] == touching
    own = chunk_of(key_ref, state_ref[0], chunk)
    cols = chunk_cols(chunk, out_ref.shape[1])
    keys = jnp.where(mine, key_ref[:, own], mate_ref[2 * frames : 3 * frames, cols])
    norm_columns(out_ref, slice(first, first + frames), keys, gain_ref)
    out_ref[first + frames :, :] = jnp.where(
        mine, value_ref[:, own], mate_ref[3 * frames : 4 * frames, cols]
    )


def edge(state, chunk, touching, gains, key, value, mate, lead, after):
    frames, width = key.shape
    rows = sum(array.shape[0] for array in lead) + 2 * frames
    return call(
        functools.partial(edge_kernel, chunk, touching, bool(lead)),
        "edge",
        [SMEM] + [VMEM] * (4 + len(lead)) + [ANY] * len(after),
        VMEM,
        shape(rows, width // 2 // CHUNKS),
    )(state, gains, key, value, mate, *lead, *after)


def prepare_kernel(state_ref, gain_ref, key_ref, mate_ref, *refs):
    out_ref = refs[-1]
    frames = key_ref.shape[0]
    own = half_of(key_ref, state_ref[0])
    norm_columns(out_ref, slice(0, frames), key_ref[:, own], gain_ref)
    norm_columns(
        out_ref, slice(frames, 2 * frames), mate_ref[2 * frames : 3 * frames, :], gain_ref
    )


def prepare_keys(state, gains, key, mate, after):
    frames, width = key.shape
    return call(
        prepare_kernel,
        "prepare_keys",
        [SMEM] + [VMEM] * 3 + [ANY] * len(after),
        VMEM,
        shape(2 * frames, width // 2),
    )(state, gains, key, mate, *after)


def attention_kernel(
    chunk, groups, head_size, score_scale, meta_ref, gain_ref, query_ref, grad_ref, value_ref, key_ref,
    mate_ref, one_ref, mid_ref, *refs
):
    frames = query_ref.shape[0]
    exchanged = len(groups) == 4
    inputs = 3 if exchanged else 1
    lyric_in, refs = refs[:inputs], refs[inputs:]
    earlier, refs = refs[: 3 * chunk], refs[3 * chunk + (chunk if exchanged else 0) :]
    window = one_ref.shape[0] - 2 * frames
    out_ref, grad_query_ref, to_mate_ref, key_grad_ref, value_grad_ref = refs[:5]
    to_one_ref, to_mid_ref, gain_grad_ref = refs[5:8]
    lyric_out, mask_ref = refs[8:-1], refs[-1]
    runs = [(index, run) for index, group in enumerate(groups) for run in group]
    main = 2 * frames + sum(run[2] for _, run in runs)
    lanes = 2 * frames
    align = mate_ref.shape[0] - ALIGN_ROWS
    touching = meta_ref[1] == 1

    size = out_ref.shape[1]
    for index in range(chunk):
        for ref, part_ref in zip((to_one_ref, to_mid_ref), earlier[3 * index :]):
            if ref.shape[1] > size:
                ref[:, chunk_cols(index, size)] = part_ref[...]
    gain_grad_ref[...] = earlier[-1][...] if chunk else jnp.zeros_like(gain_grad_ref)
    mate_tiles = mate_ref[align:, 0:frames].astype(jnp.float32).astype(jnp.int32)
    start = 0
    for number, (_, (_, _, rows)) in enumerate(runs):
        row = lax.broadcasted_iota(jnp.int32, (rows, lanes), 0) + meta_ref[7 + number]
        keep = jnp.zeros((rows, lanes), jnp.float32)
        for slot in range(TILES):
            tile = jnp.concatenate(
                [
                    jnp.full((1, frames), meta_ref[2 + slot], jnp.int32),
                    mate_tiles[slot : slot + 1],
                ],
                axis=1,
            )
            lower = tile * BLK
            upper = jnp.minimum(lower + BLK, meta_ref[4])
            inside = (row >= lower) & (row < upper) & (lower >= 0)
            keep = jnp.where(inside, 1.0, keep)
        mask_ref[start : start + rows, :] = keep
        start += rows
    lane = lax.broadcasted_iota(jnp.int32, (frames, lanes), 1)
    mask_ref[start : start + frames, :] = jnp.where(
        lane < frames, meta_ref[5], meta_ref[6]
    ).astype(jnp.float32)

    q_gain = gain_ref[0:1, :]
    k_gain = gain_ref[1:2, :]
    heads = size // head_size
    sent = to_one_ref.shape[1] // size > 1

    def one_head(head):
        cols = pl.ds(pl.multiple_of(head * head_size, head_size), head_size)
        half_cols = pl.ds(
            pl.multiple_of((chunk * heads + head) * head_size, head_size), head_size
        )
        own_cols = pl.ds(
            pl.multiple_of(
                ((meta_ref[0] * CHUNKS + chunk) * heads + head) * head_size, head_size
            ),
            head_size,
        )
        sent_cols = half_cols if sent else cols
        lyric = [ref[:, cols if exchanged else own_cols] for ref in lyric_in]
        if exchanged:
            lyric = [lyric[0], lyric[1], one_ref[0:window, cols], lyric[2]]
        one_rows, mid_rows = one_ref[window:, cols], mid_ref[:, cols]
        near_rows = jnp.where(touching, one_rows, mid_rows)
        far_rows = jnp.where(touching, mid_rows, one_rows)

        def from_mate(number):
            return mate_ref[number * frames : (number + 1) * frames, half_cols]

        query = jnp.concatenate([query_ref[:, own_cols], from_mate(0)], axis=0)
        query = query.astype(jnp.float32)
        cot = jnp.concatenate([grad_ref[:, own_cols], from_mate(1)], axis=0)
        key_low = jnp.concatenate(
            [key_ref[:, half_cols]]
            + [lyric[index][run[0] : run[0] + run[2]] for index, run in runs]
            + [near_rows[:frames], far_rows[:frames]],
            axis=0,
        )
        value = jnp.concatenate(
            [value_ref[:, own_cols], from_mate(3)]
            + [lyric[index][run[1] : run[1] + run[2]] for index, run in runs]
            + [near_rows[frames:], far_rows[frames:]],
            axis=0,
        )
        query_inv = lax.rsqrt(jnp.mean(query * query, axis=1, keepdims=True) + NORM_EPS)
        query_hat = query * query_inv
        query_low = (query_hat * (q_gain * score_scale)).astype(jnp.bfloat16)

        near, far = slice(main, main + frames), slice(main + frames, main + 2 * frames)

        def against(rows, columns):
            return jnp.concatenate(
                [
                    dot(rows[:main], columns, 1, 1),
                    jnp.concatenate(
                        [
                            dot(rows[near], columns[:frames], 1, 1),
                            dot(rows[far], columns[frames:], 1, 1),
                        ],
                        axis=1,
                    ),
                ],
                axis=0,
            )

        def over_keys(weights, rows):
            return dot(weights[:main], rows[:main], 0, 0) + jnp.concatenate(
                [
                    dot(weights[main:, :frames], rows[near], 0, 0),
                    dot(weights[main:, frames:], rows[far], 0, 0),
                ],
                axis=0,
            )

        def over_queries(weights, columns):
            return jnp.concatenate(
                [
                    dot(weights[:main], columns, 1, 0),
                    dot(weights[main:, :frames], columns[:frames], 1, 0),
                    dot(weights[main:, frames:], columns[frames:], 1, 0),
                ],
                axis=0,
            )

        exp_scores = jnp.exp(against(key_low, query_low))
        exp_scores = jnp.concatenate(
            [exp_scores[: 2 * frames], exp_scores[2 * frames :] * mask_ref[...]], axis=0
        )
        grad_prob = against(value, cot)
        prob = exp_scores * (1.0 / jnp.sum(exp_scores, axis=0, keepdims=True))
        prob_low = prob.astype(jnp.bfloat16)
        weighted = prob * grad_prob
        delta = jnp.sum(weighted, axis=0, keepdims=True)
        grad_score = (weighted - prob * delta).astype(jnp.bfloat16)
        output = over_keys(prob_low, value).astype(jnp.bfloat16)
        grad_low = over_keys(grad_score, key_low)
        grad_qn = grad_low * score_scale
        grad_keys = over_queries(grad_score, query_low)
        grad_values = over_queries(prob_low, cot)
        scaled = grad_qn * q_gain
        grad_query = (
            query_inv * scaled
            - query_hat
            * (query_inv * query_inv)
            * jnp.mean(scaled * query, axis=1, keepdims=True)
        ).astype(jnp.bfloat16)
        gain_grad_ref[0:1, :] += jnp.sum(grad_qn * query_hat, axis=0, keepdims=True)
        gain_grad_ref[1:2, :] += (
            jnp.sum(grad_low * query_low.astype(jnp.float32), axis=0, keepdims=True) / k_gain
        )

        out_ref[:, cols] = output[:frames]
        grad_query_ref[:, cols] = grad_query[:frames]
        to_mate_ref[0:frames, cols] = output[frames:]
        to_mate_ref[frames:, cols] = grad_query[frames:]
        key_grad_ref[:, cols] = grad_keys[: 2 * frames]
        value_grad_ref[:, cols] = grad_values[: 2 * frames]
        for grads, part in (
            (grad_keys.astype(jnp.bfloat16), 0),
            (grad_values.astype(jnp.bfloat16), frames),
        ):
            to_one_ref[window + part : window + part + frames, sent_cols] = jnp.where(
                touching, grads[near], grads[far]
            )
            to_mid_ref[part : part + frames, sent_cols] = jnp.where(touching, grads[far], grads[near])
        if exchanged:
            held_ref, two_ref, to_two_ref = lyric_out
            outs = (held_ref, two_ref, to_one_ref, to_two_ref)
        else:
            outs = lyric_out
        start = 2 * frames
        for index, (key_row, value_row, rows) in runs:
            part = slice(start, start + rows)
            put = sent_cols if outs[index] is to_one_ref else cols
            outs[index][key_row : key_row + rows, put] = grad_keys[part].astype(jnp.bfloat16)
            outs[index][value_row : value_row + rows, put] = grad_values[part].astype(
                jnp.bfloat16
            )
            start += rows

    @pl.loop(0, heads // HEADS_PER_STEP)
    def _(step):
        for number in range(HEADS_PER_STEP):
            one_head(step * HEADS_PER_STEP + number)

    if exchanged and sent:
        to_two_ref = lyric_out[2]
        to_two_ref[window:, :] = split_rows(gain_grad_ref[...], size)


def attention(
    chunk, meta, gains, query, cot, value, key, mate, one, mid, lyrics, groups, earlier, after
):
    frames, width = query.shape
    head_size = gains.shape[1]
    size = width // 2 // CHUNKS
    sent = size if chunk < CHUNKS - 1 else width // 2
    lyric_rows = sum(run[2] for group in groups for run in group)
    key_rows = 3 * frames + lyric_rows
    bf16, f32 = jnp.bfloat16, jnp.float32
    slot = sum(2 * run[2] for run in groups[0])
    out_shape = [shape(frames, size)] * 2
    out_shape += [shape(2 * frames, size, dtype) for dtype in (bf16, f32, f32)]
    out_shape += [shape(one.shape[0], sent), shape(2 * frames, sent), shape(8, head_size, f32)]
    out_shape += [shape(slot, size)] * len(lyrics)
    if len(lyrics) > 1 and chunk == CHUNKS - 1:
        out_shape[-1] = shape(slot + GAIN_ROWS, size)
    return call(
        functools.partial(attention_kernel, chunk, groups, head_size, head_size ** (-0.5)),
        "attention",
        [SMEM] + [VMEM] * (8 + len(lyrics) + len(earlier)) + [ANY] * len(after),
        [VMEM] * len(out_shape),
        out_shape,
        limit=ATTENTION_VMEM_LIMIT,
        cost=pl.CostEstimate(
            flops=24 * key_rows * frames * size,
            bytes_accessed=8 * 1024 * 1024,
            transcendentals=2 * key_rows * frames * (size // head_size),
        ),
        scratch_shapes=[pltpu.VMEM((frames + lyric_rows, 2 * frames), f32)],
    )(meta, gains, query, cot, value, key, mate, one, mid, *lyrics, *earlier, *after)


def finish_audio_kernel(
    state_ref, gain_ref, raw_ref, mate_ref, one_ref, mid_ref, *refs
):
    chunk_refs, refs = refs[: 5 * CHUNKS], refs[5 * CHUNKS :]
    *lyric, out, query_out, key_out, value_out, to_mate_ref, key_ref, value_ref, sems = refs
    head_size = gain_ref.shape[1]
    k_gain = gain_ref[1:2, :]
    frames, half = key_ref.shape
    size = half // CHUNKS
    own, mate = slice(0, frames), slice(frames, 2 * frames)
    first = one_ref.shape[0] - 2 * frames
    touching = state_ref[1] == 1
    copies = []
    for chunk in range(CHUNKS):
        out_own_ref, query_own_ref, ready_ref = chunk_refs[5 * chunk : 5 * chunk + 3]
        for source, target in ((out_own_ref, out), (query_own_ref, query_out)):
            copies.append(
                pltpu.make_async_copy(
                    source,
                    target.at[:, chunk_of(target, state_ref[0], chunk)],
                    sems.at[len(copies)],
                )
            )
            copies[-1].start()
        to_mate_ref[0 : 2 * frames, chunk_cols(chunk, size)] = ready_ref[...]
    for ref in lyric:
        to_mate_ref[4 * frames :, :] = ref[...]
    raw_keys = raw_ref[:, half_of(raw_ref, state_ref[0])]
    for head in range(half // head_size):
        cols = slice(head * head_size, (head + 1) * head_size)
        chunk = head * head_size // size
        part = slice(head * head_size - chunk * size, (head + 1) * head_size - chunk * size)
        key_grad_ref, value_grad_ref = chunk_refs[5 * chunk + 3 : 5 * chunk + 5]
        one = one_ref[first:, cols].astype(jnp.float32)
        mid = mid_ref[:, cols].astype(jnp.float32)
        for_own = jnp.where(touching, one, mid)
        for_mate = jnp.where(touching, mid, one)
        key_ref[:, cols] = through_norm(
            raw_keys[:, cols], key_grad_ref[own, part] + for_own[:frames], k_gain
        )
        value_ref[:, cols] = (value_grad_ref[own, part] + for_own[frames:]).astype(jnp.bfloat16)
        to_mate_ref[2 * frames : 3 * frames, cols] = through_norm(
            mate_ref[2 * frames : 3 * frames, cols],
            key_grad_ref[mate, part] + for_mate[:frames],
            k_gain,
        )
        to_mate_ref[3 * frames : 4 * frames, cols] = (
            value_grad_ref[mate, part] + for_mate[frames:]
        ).astype(jnp.bfloat16)
    for source, target in ((key_ref, key_out), (value_ref, value_out)):
        copies.append(
            pltpu.make_async_copy(
                source, target.at[:, half_of(target, state_ref[0])], sems.at[len(copies)]
            )
        )
        copies[-1].start()
    for copy in copies:
        copy.wait()


def finish_audio(state, gains, raw, mate, one, mid, chunks, lyric):
    frames, width = raw.shape
    half = width // 2
    rows = 4 * frames + sum(array.shape[0] for array in lyric)
    return call(
        finish_audio_kernel,
        "finish_audio",
        [SMEM] + [VMEM] * (5 + len(chunks) + len(lyric)),
        [HBM] * 4 + [VMEM],
        [shape(frames, width)] * 4 + [shape(rows, half)],
        scratch_shapes=[pltpu.VMEM((frames, half), jnp.bfloat16)] * 2
        + [pltpu.SemaphoreType.DMA((2 * CHUNKS + 2,))],
    )(state, gains, raw, mate, one, mid, *chunks, *lyric)


def relay_kernel(gain_ref, later_ref, *refs):
    parts, arrived, (out_ref, _, total_ref) = (
        refs[:CHUNKS],
        refs[CHUNKS : 2 * CHUNKS],
        refs[2 * CHUNKS :],
    )
    rows, size = parts[0].shape
    for chunk, (part_ref, arrived_ref) in enumerate(zip(parts, arrived)):
        out_ref[:, chunk_cols(chunk, size)] = (
            part_ref[...].astype(jnp.float32) + arrived_ref[0:rows, :].astype(jnp.float32)
        ).astype(jnp.bfloat16)
    total_ref[...] = gain_ref[...] + joined_rows(arrived[-1][rows:, :], gain_ref.shape[1])


def relay(parts, arrived, gain, later):
    rows, size = parts[0].shape
    return call(
        relay_kernel,
        "relay",
        [VMEM, ANY] + [VMEM] * (2 * CHUNKS),
        [VMEM, ANY, VMEM],
        [
            shape(rows, CHUNKS * size),
            shape(*later.shape),
            shape(*gain.shape, jnp.float32),
        ],
        input_output_aliases={1: 1},
    )(gain, later, *parts, *arrived)


def finish_lyric_kernel(
    state_ref, gain_ref, raw_ref, mate_ref, one_ref, two_ref, sum_ref, *refs
):
    held_refs, (own_ref, to_mate_ref) = refs[:CHUNKS], refs[CHUNKS:]
    rows = raw_ref.shape[0]
    head_size = gain_ref.shape[1]
    k_gain = gain_ref[1:2, :]
    size = held_refs[0].shape[1]
    first = mate_ref.shape[0] - ALIGN_ROWS - 2 * rows
    to_mate_ref[2 * rows :, :] = split_rows(sum_ref[...], to_mate_ref.shape[1])
    raw_keys = raw_ref[:, half_of(raw_ref, state_ref[0])]
    for head in range(own_ref.shape[1] // head_size):
        cols = slice(head * head_size, (head + 1) * head_size)
        chunk = head * head_size // size
        part = slice(head * head_size - chunk * size, (head + 1) * head_size - chunk * size)
        total = held_refs[chunk][:, part].astype(jnp.float32)
        for ref in (one_ref, two_ref):
            total = total + ref[0 : 4 * rows, cols].astype(jnp.float32)
        mate_keys = mate_ref[first : first + rows, cols]
        for ref, base, raw in (
            (own_ref, 0, raw_keys[:, cols]),
            (to_mate_ref, 2 * rows, mate_keys),
        ):
            ref[0:rows, cols] = through_norm(raw, total[base : base + rows], k_gain)
            ref[rows : 2 * rows, cols] = total[base + rows : base + 2 * rows].astype(jnp.bfloat16)


def finish_lyric(state, gains, raw, mate, held, one, two, total):
    rows, width = raw.shape
    half = width // 2
    return call(
        finish_lyric_kernel,
        "finish_lyric",
        [SMEM] + [VMEM] * (6 + len(held)),
        [VMEM] * 2,
        [shape(2 * rows, half), shape(2 * rows + GAIN_ROWS, half)],
    )(state, gains, raw, mate, one, two, total, *held)


def join_kernel(count, state_ref, gain_ref, own_ref, mate_ref, *refs):
    outs, (q_total_ref, k_total_ref, sems) = refs[count:-3], refs[-3:]
    frames = outs[0].shape[0]
    rows = own_ref.shape[0] // 2
    pieces = [
        (mate_ref.at[index * frames : (index + 1) * frames, :], out, 1 - state_ref[0])
        for index, out in enumerate(outs[:count])
    ]
    for ref, first, core in ((own_ref, 0, state_ref[0]), (mate_ref, count * frames, 1 - state_ref[0])):
        for index, out in enumerate(outs[count:]):
            start = first + index * rows
            pieces.append((ref.at[start : start + rows, :], out, core))
    copies = [
        pltpu.make_async_copy(source, out.at[:, half_of(out, core)], sems.at[index])
        for index, (source, out, core) in enumerate(pieces)
    ]
    for copy in copies:
        copy.start()
    sums = mate_ref[mate_ref.shape[0] - GAIN_ROWS :, :]
    total = gain_ref[...] + joined_rows(sums, gain_ref.shape[1])
    q_total_ref[...] = total[0:1]
    k_total_ref[...] = total[1:2]
    for copy in copies:
        copy.wait()


def join(state, gain, arrays, own, mate):
    rows, half = own.shape
    count = len(arrays)
    return call(
        functools.partial(join_kernel, count),
        "join",
        [SMEM] + [VMEM] * 3 + [HBM] * count,
        [HBM] * (count + 2) + [VMEM] * 2,
        [shape(*array.shape) for array in arrays]
        + [shape(rows // 2, 2 * half)] * 2
        + [shape(1, gain.shape[1], jnp.float32)] * 2,
        input_output_aliases={4 + i: i for i in range(count)},
        scratch_shapes=[pltpu.SemaphoreType.DMA((count + 4,))],
    )(state, gain, own, mate, *arrays)


def fill_kernel(count, state_ref, mate_ref, *refs):
    outs, sems = refs[count:-1], refs[-1]
    frames = outs[0].shape[0]
    copies = [
        pltpu.make_async_copy(
            mate_ref.at[index * frames : (index + 1) * frames, :],
            out.at[:, half_of(out, 1 - state_ref[0])],
            sems.at[index],
        )
        for index, out in enumerate(outs)
    ]
    for copy in copies:
        copy.start()
    for copy in copies:
        copy.wait()


def fill_other(state, arrays, mate):
    count = len(arrays)
    return call(
        functools.partial(fill_kernel, count),
        "fill_other",
        [SMEM, VMEM] + [HBM] * count,
        [HBM] * count,
        [shape(*array.shape) for array in arrays],
        input_output_aliases={2 + i: i for i in range(count)},
        scratch_shapes=[pltpu.SemaphoreType.DMA((count,))],
    )(state, mate, *arrays)


def norm_rows_kernel(gain_ref, raw_ref, out_ref):
    norm_columns(out_ref, slice(0, raw_ref.shape[0]), raw_ref[...], gain_ref)


def norm_rows(gains, raw):
    return pl.pallas_call(
        norm_rows_kernel,
        out_shape=jax.ShapeDtypeStruct(raw.shape, raw.dtype),
        name="norm_rows",
    )(gains, raw)


def norm_lyric_kernel(head_size, gain_ref, raw_ref, grad_ref, out_ref):
    for head in range(raw_ref.shape[1] // head_size):
        cols = slice(head * head_size, (head + 1) * head_size)
        out_ref[:, cols] = through_norm(raw_ref[:, cols], grad_ref[:, cols], gain_ref[1:2, :])


def norm_lyric(gains, raw, grad):
    return pl.pallas_call(
        functools.partial(norm_lyric_kernel, gains.shape[1]),
        out_shape=jax.ShapeDtypeStruct(raw.shape, jnp.bfloat16),
        name="norm_lyric",
    )(gains, raw, grad)


def sum_over(total, axis, bits):
    count = lax.axis_size(axis)
    for bit in bits:
        total = total + lax.ppermute(total, axis, [(i, i ^ bit) for i in range(count)])
    return total


def bits_of(count):
    return [1 << bit for bit in range(count.bit_length() - 1)]


def body(
    queries, keys, values, lyric_keys, lyric_values, q_gain, k_gain, cotangent, alignment, lyric_len
):
    frames = queries.shape[1]
    lyric_local, width = lyric_keys.shape[1:]
    count = lax.axis_size("seq")
    songs = lax.axis_size("song")
    me = lax.axis_index("seq")
    core = me % 2
    chips = count // 2
    chip = me // 2
    touching = (chip % 2) ^ core
    state = jnp.stack([core, touching]).astype(jnp.int32)
    gains = jnp.stack([q_gain, k_gain])

    swap = [(i, i ^ 1) for i in range(count)]
    partners = [(a, a ^ 1) for a in range(chips)]
    across = [(a, a ^ 2) for a in range(chips)]
    between = [(a, a + 1) for a in range(1, chips - 1, 2)]
    between += [(b, a) for a, b in between]

    def hop(block, moves):
        pairs = [(2 * a + c, 2 * b + c) for a, b in moves for c in (0, 1)]
        return lax.ppermute(block, "seq", pairs)

    hops = chips == 4 and lyric_local % 16 == 0
    total_rows = lyric_local * count
    if hops:
        run = ((0, lyric_local, lyric_local), (2 * lyric_local, 3 * lyric_local, lyric_local))
        groups = (run,) * 4
        owners = [chip, chip ^ 2, chip ^ 1, chip ^ 3]
        first_rows = []
        for owner in owners:
            first_rows += [
                (2 * owner + core) * lyric_local,
                (2 * owner + 1 - core) * lyric_local,
            ]
    else:
        gathered = jnp.concatenate(
            [
                lax.all_gather(
                    norm_rows(gains, lyric_keys[0]), "seq", axis=0, tiled=True
                ),
                lax.all_gather(lyric_values[0], "seq", axis=0, tiled=True),
            ],
            axis=0,
        )
        groups = (((0, total_rows, total_rows),),)
        first_rows = [0]
    has_left, has_right = chip > 0, chip < chips - 1
    has_near = jnp.where(core == 0, has_left, has_right)
    has_far = jnp.where(core == 0, has_right, has_left)
    meta = jnp.stack(
        [
            jnp.asarray(value, jnp.int32)
            for value in [core, touching]
            + [alignment[0, 0, slot] for slot in range(TILES)]
            + [lyric_len[0], has_near, has_far]
            + first_rows
        ]
    )

    to_mate = pack(
        state,
        alignment[0, 0],
        [queries[0], cotangent[0], keys[0], values[0]]
        + ([lyric_keys[0], lyric_values[0]] if hops else []),
    )
    mate = lax.ppermute(to_mate, "seq", swap)
    chunks, parts, earlier, arrived = [], [], [], []
    after = []
    for chunk in range(CHUNKS):
        before, one_before = after, lyrics[2:] if chunk else []
        if hops:
            pair = pair_lyrics(state, chunk, gains, lyric_keys[0], lyric_values[0], mate, before)
            two = hop(pair, across)
            lyrics = [pair, two, hop(two, partners)]
            lead, after = [pair], [two]
        else:
            lyrics, lead = [gathered], []
        one = hop(edge(state, chunk, 1, gains, keys[0], values[0], mate, lead, one_before), partners)
        mid = hop(edge(state, chunk, 0, gains, keys[0], values[0], mate, [], after), between)
        if not chunk:
            key_low = prepare_keys(state, gains, keys[0], mate, after)
        results = attention(
            chunk, meta, gains, queries[0], cotangent[0], values[0], key_low, mate, one, mid,
            lyrics, groups, earlier, arrived,
        )
        chunks += results[:5]
        earlier = [*earlier, *results[5:8]]
        parts.append(results[8:])
        if hops:
            arrived.append(hop(results[-1], partners))
    to_one, to_mid, gain_part = earlier[-3:]

    mid = hop(to_mid, between)
    to_mate = []
    if hops:
        to_two, to_one, gain_total = relay(
            [part[1] for part in parts], arrived, gain_part, to_one
        )
        gain_total = sum_over(sum_over(gain_total, "song", bits_of(songs)), "seq", [4])
        two, one = hop(to_two, across), hop(to_one, partners)
        own_half, part_to_mate = finish_lyric(
            state, gains, lyric_keys[0], mate, [part[0] for part in parts], one, two, gain_total
        )
        to_mate = [part_to_mate]
    else:
        one = hop(to_one, partners)
    *filled, to_mate = finish_audio(state, gains, keys[0], mate, one, mid, chunks, to_mate)
    from_mate = lax.ppermute(to_mate, "seq", swap)
    if hops:
        *filled, grad_lyric_keys, grad_lyric_values, q_total, k_total = join(
            state, gain_total, filled, own_half, from_mate
        )
    else:
        filled = fill_other(state, filled, from_mate)
        gain_total = lax.psum(gain_part, ("song", "seq"))
        q_total, k_total = gain_total[0:1], gain_total[1:2]
        spread = lax.dynamic_update_slice(
            jnp.zeros((2 * total_rows, width), jnp.float32),
            jnp.concatenate([part[0] for part in parts], axis=1).astype(jnp.float32),
            (0, core * (width // 2)),
        )
        lyric_key_sum, grad_lyric_values = [
            lax.psum_scatter(part, "seq", scatter_dimension=0, tiled=True)
            for part in (spread[:total_rows], spread[total_rows:])
        ]
        grad_lyric_keys = norm_lyric(gains, lyric_keys[0], lyric_key_sum)
        grad_lyric_values = grad_lyric_values.astype(jnp.bfloat16)
    output, grad_queries, grad_keys, grad_values = filled
    return (
        output[None],
        grad_queries[None],
        grad_keys[None],
        grad_values[None],
        grad_lyric_keys[None],
        grad_lyric_values[None],
        q_total[0],
        k_total[0],
    )


def solution(mesh):
    split = P("song", "seq", None)
    return jax.shard_map(
        body,
        mesh=mesh,
        in_specs=(split, split, split, split, split, P(), P(), split, split, P("song")),
        out_specs=(split, split, split, split, split, split, P(), P()),
        check_vma=False,
    )
```

```python
import functools

import jax
import jax.numpy as jnp
from jax import lax
from jax.experimental import pallas as pl
from jax.experimental.pallas import tpu as pltpu
from jax.sharding import PartitionSpec as P

BLK = 128
TILES = 2
NORM_EPS = 1e-06
VMEM_LIMIT = 8 * 1024 * 1024
ATTENTION_VMEM_LIMIT = 24 * 1024 * 1024
PACK_VMEM_LIMIT = 60 * 1024 * 1024
VMEM = pl.BlockSpec(memory_space=pltpu.VMEM)
SMEM = pl.BlockSpec(memory_space=pltpu.SMEM)
HBM = pl.BlockSpec(memory_space=pltpu.HBM)
ANY = pl.BlockSpec(memory_space=pl.ANY)
GAIN_ROWS = 16
HEADS_PER_STEP = 2
CHUNKS = 2
ALIGN_ROWS = 32
SMALL = pl.CostEstimate(flops=1, bytes_accessed=1, transcendentals=0)


def dot(lhs, rhs, lhs_dim, rhs_dim):
    return lax.dot_general(
        lhs, rhs, (((lhs_dim,), (rhs_dim,)), ((), ())), preferred_element_type=jnp.float32
    )


def call(kernel, name, in_specs, out_specs, out_shape, limit=VMEM_LIMIT, cost=SMALL, **options):
    return pl.pallas_call(
        kernel,
        in_specs=in_specs,
        out_specs=out_specs,
        out_shape=out_shape,
        compiler_params=pltpu.CompilerParams(vmem_limit_bytes=limit),
        cost_estimate=cost,
        name=name,
        **options,
    )


def shape(rows, cols, dtype=jnp.bfloat16):
    return jax.ShapeDtypeStruct((rows, cols), dtype)


def half_of(ref, core):
    half = ref.shape[1] // 2
    return pl.ds(pl.multiple_of(core * half, half), half)


def chunk_of(ref, core, chunk):
    size = ref.shape[1] // 2 // CHUNKS
    return pl.ds(pl.multiple_of((core * CHUNKS + chunk) * size, size), size)


def chunk_cols(chunk, size):
    return slice(chunk * size, (chunk + 1) * size)


def split_rows(sums, cols):
    high = sums.astype(jnp.bfloat16).astype(jnp.float32)
    rest = sums - high
    middle = rest.astype(jnp.bfloat16).astype(jnp.float32)
    low = rest - middle
    empty = jnp.zeros((sums.shape[0], cols - 3 * sums.shape[1]), jnp.float32)
    rows = jnp.concatenate([high, middle, low, empty], axis=1)
    return jnp.concatenate([rows, jnp.zeros_like(rows)], axis=0).astype(jnp.bfloat16)


def joined_rows(rows, size):
    rows = rows.astype(jnp.float32)[0:8]
    return (rows[:, 2 * size : 3 * size] + rows[:, size : 2 * size]) + rows[:, 0:size]


def normed(raw, k_gain):
    raw = raw.astype(jnp.float32)
    inverse = lax.rsqrt(jnp.mean(raw * raw, axis=1, keepdims=True) + NORM_EPS)
    return (raw * inverse * k_gain).astype(jnp.bfloat16)


def norm_columns(out_ref, rows, raw, gain_ref):
    head_size = gain_ref.shape[1]
    for head in range(raw.shape[1] // head_size):
        cols = slice(head * head_size, (head + 1) * head_size)
        out_ref[rows, cols] = normed(raw[:, cols], gain_ref[1:2, :])


def through_norm(raw, grad, k_gain):
    raw = raw.astype(jnp.float32)
    inverse = lax.rsqrt(jnp.mean(raw * raw, axis=1, keepdims=True) + NORM_EPS)
    scaled = grad * k_gain
    return (
        inverse * scaled
        - raw * (inverse * inverse * inverse) * jnp.mean(scaled * raw, axis=1, keepdims=True)
    ).astype(jnp.bfloat16)


def pack_kernel(state_ref, align_ref, *refs):
    ins, (out_ref, sems) = refs[:-2], refs[-2:]
    start = 0
    copies = []
    for index, ref in enumerate(ins):
        rows = ref.shape[0]
        copies.append(
            pltpu.make_async_copy(
                ref.at[:, half_of(ref, 1 - state_ref[0])],
                out_ref.at[start : start + rows, :],
                sems.at[index],
            )
        )
        copies[-1].start()
        start += rows
    row = lax.broadcasted_iota(jnp.int32, (ALIGN_ROWS, out_ref.shape[1]), 0)
    tiles = jnp.zeros(row.shape, jnp.int32)
    for slot in range(TILES):
        tiles = jnp.where(row == slot, align_ref[slot], tiles)
    out_ref[start:, :] = tiles.astype(jnp.float32).astype(jnp.bfloat16)
    for copy in copies:
        copy.wait()


def pack(state, align, arrays):
    rows = sum(array.shape[0] for array in arrays) + ALIGN_ROWS
    return call(
        pack_kernel,
        "pack",
        [SMEM, SMEM] + [HBM] * len(arrays),
        VMEM,
        shape(rows, arrays[0].shape[1] // 2),
        limit=PACK_VMEM_LIMIT,
        scratch_shapes=[pltpu.SemaphoreType.DMA((len(arrays),))],
    )(state, align, *arrays)


def pair_kernel(chunk, state_ref, gain_ref, key_ref, value_ref, mate_ref, *refs):
    pair_ref = refs[-1]
    rows = key_ref.shape[0]
    first = mate_ref.shape[0] - ALIGN_ROWS - 2 * rows
    own = chunk_of(key_ref, state_ref[0], chunk)
    cols = chunk_cols(chunk, pair_ref.shape[1])
    norm_columns(pair_ref, slice(0, rows), key_ref[:, own], gain_ref)
    pair_ref[rows : 2 * rows, :] = value_ref[:, own]
    norm_columns(
        pair_ref, slice(2 * rows, 3 * rows), mate_ref[first : first + rows, cols], gain_ref
    )
    pair_ref[3 * rows :, :] = mate_ref[first + rows : first + 2 * rows, cols]


def pair_lyrics(state, chunk, gains, lyric_key, lyric_value, mate, after):
    rows, width = lyric_key.shape
    return call(
        functools.partial(pair_kernel, chunk),
        "pair_lyrics",
        [SMEM] + [VMEM] * 4 + [ANY] * len(after),
        VMEM,
        shape(4 * rows, width // 2 // CHUNKS),
    )(state, gains, lyric_key, lyric_value, mate, *after)


def edge_kernel(
    chunk, touching, leading, state_ref, gain_ref, key_ref, value_ref, mate_ref, *refs
):
    out_ref = refs[-1]
    frames = key_ref.shape[0]
    first = out_ref.shape[0] - 2 * frames
    if leading:
        out_ref[0:first, :] = refs[0][...]
    mine = state_ref[1] == touching
    own = chunk_of(key_ref, state_ref[0], chunk)
    cols = chunk_cols(chunk, out_ref.shape[1])
    keys = jnp.where(mine, key_ref[:, own], mate_ref[2 * frames : 3 * frames, cols])
    norm_columns(out_ref, slice(first, first + frames), keys, gain_ref)
    out_ref[first + frames :, :] = jnp.where(
        mine, value_ref[:, own], mate_ref[3 * frames : 4 * frames, cols]
    )


def edge(state, chunk, touching, gains, key, value, mate, lead, after):
    frames, width = key.shape
    rows = sum(array.shape[0] for array in lead) + 2 * frames
    return call(
        functools.partial(edge_kernel, chunk, touching, bool(lead)),
        "edge",
        [SMEM] + [VMEM] * (4 + len(lead)) + [ANY] * len(after),
        VMEM,
        shape(rows, width // 2 // CHUNKS),
    )(state, gains, key, value, mate, *lead, *after)


def prepare_kernel(state_ref, gain_ref, key_ref, mate_ref, *refs):
    out_ref = refs[-1]
    frames = key_ref.shape[0]
    own = half_of(key_ref, state_ref[0])
    norm_columns(out_ref, slice(0, frames), key_ref[:, own], gain_ref)
    norm_columns(
        out_ref, slice(frames, 2 * frames), mate_ref[2 * frames : 3 * frames, :], gain_ref
    )


def prepare_keys(state, gains, key, mate, after):
    frames, width = key.shape
    return call(
        prepare_kernel,
        "prepare_keys",
        [SMEM] + [VMEM] * 3 + [ANY] * len(after),
        VMEM,
        shape(2 * frames, width // 2),
    )(state, gains, key, mate, *after)


def attention_kernel(
    chunk, chained, waits, groups, head_size, score_scale, meta_ref, gain_ref, query_ref, grad_ref, value_ref, key_ref,
    mate_ref, one_ref, mid_ref, *refs
):
    frames = query_ref.shape[0]
    exchanged = len(groups) == 4
    inputs = 3 if exchanged else 1
    lyric_in, refs = refs[:inputs], refs[inputs:]
    earlier, refs = refs[:chained], refs[chained + waits :]
    window = one_ref.shape[0] - 2 * frames
    out_ref, grad_query_ref, to_mate_ref, key_grad_ref, value_grad_ref = refs[:5]
    to_one_ref, to_mid_ref, gain_grad_ref = refs[5:8]
    lyric_out, mask_ref = refs[8:-1], refs[-1]
    runs = [(index, run) for index, group in enumerate(groups) for run in group]
    main = 2 * frames + sum(run[2] for _, run in runs)
    lanes = 2 * frames
    align = mate_ref.shape[0] - ALIGN_ROWS
    touching = meta_ref[1] == 1

    size = out_ref.shape[1]
    gain_grad_ref[...] = earlier[0][...] if chained else jnp.zeros_like(gain_grad_ref)
    mate_tiles = mate_ref[align:, 0:frames].astype(jnp.float32).astype(jnp.int32)
    start = 0
    for number, (_, (_, _, rows)) in enumerate(runs):
        row = lax.broadcasted_iota(jnp.int32, (rows, lanes), 0) + meta_ref[7 + number]
        keep = jnp.zeros((rows, lanes), jnp.float32)
        for slot in range(TILES):
            tile = jnp.concatenate(
                [
                    jnp.full((1, frames), meta_ref[2 + slot], jnp.int32),
                    mate_tiles[slot : slot + 1],
                ],
                axis=1,
            )
            lower = tile * BLK
            upper = jnp.minimum(lower + BLK, meta_ref[4])
            inside = (row >= lower) & (row < upper) & (lower >= 0)
            keep = jnp.where(inside, 1.0, keep)
        mask_ref[start : start + rows, :] = keep
        start += rows
    lane = lax.broadcasted_iota(jnp.int32, (frames, lanes), 1)
    mask_ref[start : start + frames, :] = jnp.where(
        lane < frames, meta_ref[5], meta_ref[6]
    ).astype(jnp.float32)

    q_gain = gain_ref[0:1, :]
    k_gain = gain_ref[1:2, :]
    heads = size // head_size

    def one_head(head):
        cols = pl.ds(pl.multiple_of(head * head_size, head_size), head_size)
        half_cols = pl.ds(
            pl.multiple_of((chunk * heads + head) * head_size, head_size), head_size
        )
        own_cols = pl.ds(
            pl.multiple_of(
                ((meta_ref[0] * CHUNKS + chunk) * heads + head) * head_size, head_size
            ),
            head_size,
        )
        lyric = [ref[:, cols if exchanged else own_cols] for ref in lyric_in]
        if exchanged:
            lyric = [lyric[0], lyric[1], one_ref[0:window, cols], lyric[2]]
        one_rows, mid_rows = one_ref[window:, cols], mid_ref[:, cols]
        near_rows = jnp.where(touching, one_rows, mid_rows)
        far_rows = jnp.where(touching, mid_rows, one_rows)

        def from_mate(number):
            return mate_ref[number * frames : (number + 1) * frames, half_cols]

        query = jnp.concatenate([query_ref[:, own_cols], from_mate(0)], axis=0)
        query = query.astype(jnp.float32)
        cot = jnp.concatenate([grad_ref[:, own_cols], from_mate(1)], axis=0)
        key_low = jnp.concatenate(
            [key_ref[:, half_cols]]
            + [lyric[index][run[0] : run[0] + run[2]] for index, run in runs]
            + [near_rows[:frames], far_rows[:frames]],
            axis=0,
        )
        value = jnp.concatenate(
            [value_ref[:, own_cols], from_mate(3)]
            + [lyric[index][run[1] : run[1] + run[2]] for index, run in runs]
            + [near_rows[frames:], far_rows[frames:]],
            axis=0,
        )
        query_inv = lax.rsqrt(jnp.mean(query * query, axis=1, keepdims=True) + NORM_EPS)
        query_hat = query * query_inv
        query_low = (query_hat * (q_gain * score_scale)).astype(jnp.bfloat16)

        near, far = slice(main, main + frames), slice(main + frames, main + 2 * frames)

        def against(rows, columns):
            return jnp.concatenate(
                [
                    dot(rows[:main], columns, 1, 1),
                    jnp.concatenate(
                        [
                            dot(rows[near], columns[:frames], 1, 1),
                            dot(rows[far], columns[frames:], 1, 1),
                        ],
                        axis=1,
                    ),
                ],
                axis=0,
            )

        def over_keys(weights, rows):
            return dot(weights[:main], rows[:main], 0, 0) + jnp.concatenate(
                [
                    dot(weights[main:, :frames], rows[near], 0, 0),
                    dot(weights[main:, frames:], rows[far], 0, 0),
                ],
                axis=0,
            )

        def over_queries(weights, columns):
            return jnp.concatenate(
                [
                    dot(weights[:main], columns, 1, 0),
                    dot(weights[main:, :frames], columns[:frames], 1, 0),
                    dot(weights[main:, frames:], columns[frames:], 1, 0),
                ],
                axis=0,
            )

        exp_scores = jnp.exp(against(key_low, query_low))
        exp_scores = jnp.concatenate(
            [exp_scores[: 2 * frames], exp_scores[2 * frames :] * mask_ref[...]], axis=0
        )
        grad_prob = against(value, cot)
        prob = exp_scores * (1.0 / jnp.sum(exp_scores, axis=0, keepdims=True))
        prob_low = prob.astype(jnp.bfloat16)
        weighted = prob * grad_prob
        delta = jnp.sum(weighted, axis=0, keepdims=True)
        grad_score = (weighted - prob * delta).astype(jnp.bfloat16)
        output = over_keys(prob_low, value).astype(jnp.bfloat16)
        grad_low = over_keys(grad_score, key_low)
        grad_qn = grad_low * score_scale
        grad_keys = over_queries(grad_score, query_low)
        grad_values = over_queries(prob_low, cot)
        scaled = grad_qn * q_gain
        grad_query = (
            query_inv * scaled
            - query_hat
            * (query_inv * query_inv)
            * jnp.mean(scaled * query, axis=1, keepdims=True)
        ).astype(jnp.bfloat16)
        gain_grad_ref[0:1, :] += jnp.sum(grad_qn * query_hat, axis=0, keepdims=True)
        gain_grad_ref[1:2, :] += (
            jnp.sum(grad_low * query_low.astype(jnp.float32), axis=0, keepdims=True) / k_gain
        )

        out_ref[:, cols] = output[:frames]
        grad_query_ref[:, cols] = grad_query[:frames]
        to_mate_ref[0:frames, cols] = output[frames:]
        to_mate_ref[frames:, cols] = grad_query[frames:]
        key_grad_ref[:, cols] = grad_keys[: 2 * frames]
        value_grad_ref[:, cols] = grad_values[: 2 * frames]
        for grads, part in (
            (grad_keys.astype(jnp.bfloat16), 0),
            (grad_values.astype(jnp.bfloat16), frames),
        ):
            to_one_ref[window + part : window + part + frames, cols] = jnp.where(
                touching, grads[near], grads[far]
            )
            to_mid_ref[part : part + frames, cols] = jnp.where(touching, grads[far], grads[near])
        if exchanged:
            held_ref, two_ref, to_two_ref = lyric_out
            outs = (held_ref, two_ref, to_one_ref, to_two_ref)
        else:
            outs = lyric_out
        start = 2 * frames
        for index, (key_row, value_row, rows) in runs:
            part = slice(start, start + rows)
            outs[index][key_row : key_row + rows, cols] = grad_keys[part].astype(jnp.bfloat16)
            outs[index][value_row : value_row + rows, cols] = grad_values[part].astype(
                jnp.bfloat16
            )
            start += rows

    @pl.loop(0, heads // HEADS_PER_STEP)
    def _(step):
        for number in range(HEADS_PER_STEP):
            one_head(step * HEADS_PER_STEP + number)

    if exchanged and chunk == CHUNKS - 1:
        to_two_ref = lyric_out[2]
        to_two_ref[window:, :] = split_rows(gain_grad_ref[...], size)


def attention(
    chunk, meta, gains, query, cot, value, key, mate, one, mid, lyrics, groups, earlier, after
):
    frames, width = query.shape
    head_size = gains.shape[1]
    size = width // 2 // CHUNKS
    lyric_rows = sum(run[2] for group in groups for run in group)
    key_rows = 3 * frames + lyric_rows
    bf16, f32 = jnp.bfloat16, jnp.float32
    slot = sum(2 * run[2] for run in groups[0])
    out_shape = [shape(frames, size)] * 2
    out_shape += [shape(2 * frames, size, dtype) for dtype in (bf16, f32, f32)]
    out_shape += [shape(one.shape[0], size), shape(2 * frames, size), shape(8, head_size, f32)]
    out_shape += [shape(slot, size)] * len(lyrics)
    if len(lyrics) > 1 and chunk == CHUNKS - 1:
        out_shape[-1] = shape(slot + GAIN_ROWS, size)
    return call(
        functools.partial(
            attention_kernel, chunk, len(earlier), len(after), groups, head_size, head_size ** (-0.5)
        ),
        "attention",
        [SMEM] + [VMEM] * (8 + len(lyrics) + len(earlier)) + [ANY] * len(after),
        [VMEM] * len(out_shape),
        out_shape,
        limit=ATTENTION_VMEM_LIMIT,
        cost=pl.CostEstimate(
            flops=24 * key_rows * frames * size,
            bytes_accessed=8 * 1024 * 1024,
            transcendentals=2 * key_rows * frames * (size // head_size),
        ),
        scratch_shapes=[pltpu.VMEM((frames + lyric_rows, 2 * frames), f32)],
    )(meta, gains, query, cot, value, key, mate, one, mid, *lyrics, *earlier, *after)


def finish_audio_kernel(state_ref, gain_ref, raw_ref, mate_ref, *refs):
    chunk_refs, refs = refs[: 7 * CHUNKS], refs[7 * CHUNKS :]
    *lyric, out, query_out, key_out, value_out, to_mate_ref, key_ref, value_ref, sems = refs
    head_size = gain_ref.shape[1]
    k_gain = gain_ref[1:2, :]
    frames, half = key_ref.shape
    size = half // CHUNKS
    own, mate = slice(0, frames), slice(frames, 2 * frames)
    touching = state_ref[1] == 1
    copies = []
    for chunk in range(CHUNKS):
        out_own_ref, query_own_ref, ready_ref = chunk_refs[7 * chunk : 7 * chunk + 3]
        for source, target in ((out_own_ref, out), (query_own_ref, query_out)):
            copies.append(
                pltpu.make_async_copy(
                    source,
                    target.at[:, chunk_of(target, state_ref[0], chunk)],
                    sems.at[len(copies)],
                )
            )
            copies[-1].start()
        to_mate_ref[0 : 2 * frames, chunk_cols(chunk, size)] = ready_ref[...]
    for ref in lyric:
        to_mate_ref[4 * frames :, :] = ref[...]
    raw_keys = raw_ref[:, half_of(raw_ref, state_ref[0])]
    for head in range(half // head_size):
        cols = slice(head * head_size, (head + 1) * head_size)
        chunk = head * head_size // size
        part = slice(head * head_size - chunk * size, (head + 1) * head_size - chunk * size)
        key_grad_ref, value_grad_ref, one_ref, mid_ref = chunk_refs[7 * chunk + 3 : 7 * chunk + 7]
        one = one_ref[one_ref.shape[0] - 2 * frames :, part].astype(jnp.float32)
        mid = mid_ref[:, part].astype(jnp.float32)
        for_own = jnp.where(touching, one, mid)
        for_mate = jnp.where(touching, mid, one)
        key_ref[:, cols] = through_norm(
            raw_keys[:, cols], key_grad_ref[own, part] + for_own[:frames], k_gain
        )
        value_ref[:, cols] = (value_grad_ref[own, part] + for_own[frames:]).astype(jnp.bfloat16)
        to_mate_ref[2 * frames : 3 * frames, cols] = through_norm(
            mate_ref[2 * frames : 3 * frames, cols],
            key_grad_ref[mate, part] + for_mate[:frames],
            k_gain,
        )
        to_mate_ref[3 * frames : 4 * frames, cols] = (
            value_grad_ref[mate, part] + for_mate[frames:]
        ).astype(jnp.bfloat16)
    for source, target in ((key_ref, key_out), (value_ref, value_out)):
        copies.append(
            pltpu.make_async_copy(
                source, target.at[:, half_of(target, state_ref[0])], sems.at[len(copies)]
            )
        )
        copies[-1].start()
    for copy in copies:
        copy.wait()


def finish_audio(state, gains, raw, mate, chunks, lyric):
    frames, width = raw.shape
    half = width // 2
    rows = 4 * frames + sum(array.shape[0] for array in lyric)
    return call(
        finish_audio_kernel,
        "finish_audio",
        [SMEM] + [VMEM] * (3 + len(chunks) + len(lyric)),
        [HBM] * 4 + [VMEM],
        [shape(frames, width)] * 4 + [shape(rows, half)],
        scratch_shapes=[pltpu.VMEM((frames, half), jnp.bfloat16)] * 2
        + [pltpu.SemaphoreType.DMA((2 * CHUNKS + 2,))],
    )(state, gains, raw, mate, *chunks, *lyric)


def relay_kernel(part_ref, arrived_ref, *refs):
    rows = part_ref.shape[0]
    total = part_ref[...].astype(jnp.float32) + arrived_ref[0:rows, :].astype(jnp.float32)
    if arrived_ref.shape[0] == rows:
        refs[0][...] = total.astype(jnp.bfloat16)
        return
    gain_ref, (out_ref, total_ref, _) = refs[0], refs[-3:]
    out_ref[...] = total.astype(jnp.bfloat16)
    total_ref[...] = gain_ref[...] + joined_rows(arrived_ref[rows:, :], gain_ref.shape[1])


def relay(part, arrived):
    return call(relay_kernel, "relay", [VMEM] * 2, VMEM, shape(*part.shape))(part, arrived)


def last_relay(part, arrived, gain, later, after):
    return call(
        relay_kernel,
        "relay",
        [VMEM] * 3 + [ANY] * (1 + len(after)),
        [VMEM, VMEM, ANY],
        [shape(*part.shape), shape(*gain.shape, jnp.float32), shape(*later.shape)],
        input_output_aliases={3: 2},
    )(part, arrived, gain, later, *after)


def finish_lyric_kernel(
    state_ref, gain_ref, raw_ref, mate_ref, sum_ref, *refs
):
    chunk_refs, (own_ref, to_mate_ref) = refs[:-2], refs[-2:]
    rows = raw_ref.shape[0]
    head_size = gain_ref.shape[1]
    k_gain = gain_ref[1:2, :]
    size = chunk_refs[0].shape[1]
    first = mate_ref.shape[0] - ALIGN_ROWS - 2 * rows
    to_mate_ref[2 * rows :, :] = split_rows(sum_ref[...], to_mate_ref.shape[1])
    raw_keys = raw_ref[:, half_of(raw_ref, state_ref[0])]
    for head in range(own_ref.shape[1] // head_size):
        cols = slice(head * head_size, (head + 1) * head_size)
        chunk = head * head_size // size
        part = slice(head * head_size - chunk * size, (head + 1) * head_size - chunk * size)
        total = chunk_refs[3 * chunk][:, part].astype(jnp.float32)
        for ref in chunk_refs[3 * chunk + 1 : 3 * chunk + 3]:
            total = total + ref[0 : 4 * rows, part].astype(jnp.float32)
        mate_keys = mate_ref[first : first + rows, cols]
        for ref, base, raw in (
            (own_ref, 0, raw_keys[:, cols]),
            (to_mate_ref, 2 * rows, mate_keys),
        ):
            ref[0:rows, cols] = through_norm(raw, total[base : base + rows], k_gain)
            ref[rows : 2 * rows, cols] = total[base + rows : base + 2 * rows].astype(jnp.bfloat16)


def finish_lyric(state, gains, raw, mate, total, chunks):
    rows, width = raw.shape
    half = width // 2
    return call(
        finish_lyric_kernel,
        "finish_lyric",
        [SMEM] + [VMEM] * (4 + len(chunks)),
        [VMEM] * 2,
        [shape(2 * rows, half), shape(2 * rows + GAIN_ROWS, half)],
    )(state, gains, raw, mate, total, *chunks)


def join_kernel(count, state_ref, gain_ref, own_ref, mate_ref, *refs):
    outs, (q_total_ref, k_total_ref, sems) = refs[count:-3], refs[-3:]
    frames = outs[0].shape[0]
    rows = own_ref.shape[0] // 2
    pieces = [
        (mate_ref.at[index * frames : (index + 1) * frames, :], out, 1 - state_ref[0])
        for index, out in enumerate(outs[:count])
    ]
    for ref, first, core in ((own_ref, 0, state_ref[0]), (mate_ref, count * frames, 1 - state_ref[0])):
        for index, out in enumerate(outs[count:]):
            start = first + index * rows
            pieces.append((ref.at[start : start + rows, :], out, core))
    copies = [
        pltpu.make_async_copy(source, out.at[:, half_of(out, core)], sems.at[index])
        for index, (source, out, core) in enumerate(pieces)
    ]
    for copy in copies:
        copy.start()
    sums = mate_ref[mate_ref.shape[0] - GAIN_ROWS :, :]
    total = gain_ref[...] + joined_rows(sums, gain_ref.shape[1])
    q_total_ref[...] = total[0:1]
    k_total_ref[...] = total[1:2]
    for copy in copies:
        copy.wait()


def join(state, gain, arrays, own, mate):
    rows, half = own.shape
    count = len(arrays)
    return call(
        functools.partial(join_kernel, count),
        "join",
        [SMEM] + [VMEM] * 3 + [HBM] * count,
        [HBM] * (count + 2) + [VMEM] * 2,
        [shape(*array.shape) for array in arrays]
        + [shape(rows // 2, 2 * half)] * 2
        + [shape(1, gain.shape[1], jnp.float32)] * 2,
        input_output_aliases={4 + i: i for i in range(count)},
        scratch_shapes=[pltpu.SemaphoreType.DMA((count + 4,))],
    )(state, gain, own, mate, *arrays)


def fill_kernel(count, state_ref, mate_ref, *refs):
    outs, sems = refs[count:-1], refs[-1]
    frames = outs[0].shape[0]
    copies = [
        pltpu.make_async_copy(
            mate_ref.at[index * frames : (index + 1) * frames, :],
            out.at[:, half_of(out, 1 - state_ref[0])],
            sems.at[index],
        )
        for index, out in enumerate(outs)
    ]
    for copy in copies:
        copy.start()
    for copy in copies:
        copy.wait()


def fill_other(state, arrays, mate):
    count = len(arrays)
    return call(
        functools.partial(fill_kernel, count),
        "fill_other",
        [SMEM, VMEM] + [HBM] * count,
        [HBM] * count,
        [shape(*array.shape) for array in arrays],
        input_output_aliases={2 + i: i for i in range(count)},
        scratch_shapes=[pltpu.SemaphoreType.DMA((count,))],
    )(state, mate, *arrays)


def norm_rows_kernel(gain_ref, raw_ref, out_ref):
    norm_columns(out_ref, slice(0, raw_ref.shape[0]), raw_ref[...], gain_ref)


def norm_rows(gains, raw):
    return pl.pallas_call(
        norm_rows_kernel,
        out_shape=jax.ShapeDtypeStruct(raw.shape, raw.dtype),
        name="norm_rows",
    )(gains, raw)


def norm_lyric_kernel(head_size, gain_ref, raw_ref, grad_ref, out_ref):
    for head in range(raw_ref.shape[1] // head_size):
        cols = slice(head * head_size, (head + 1) * head_size)
        out_ref[:, cols] = through_norm(raw_ref[:, cols], grad_ref[:, cols], gain_ref[1:2, :])


def norm_lyric(gains, raw, grad):
    return pl.pallas_call(
        functools.partial(norm_lyric_kernel, gains.shape[1]),
        out_shape=jax.ShapeDtypeStruct(raw.shape, jnp.bfloat16),
        name="norm_lyric",
    )(gains, raw, grad)


def sum_over(total, axis, bits):
    count = lax.axis_size(axis)
    for bit in bits:
        total = total + lax.ppermute(total, axis, [(i, i ^ bit) for i in range(count)])
    return total


def bits_of(count):
    return [1 << bit for bit in range(count.bit_length() - 1)]


def body(
    queries, keys, values, lyric_keys, lyric_values, q_gain, k_gain, cotangent, alignment, lyric_len
):
    frames = queries.shape[1]
    lyric_local, width = lyric_keys.shape[1:]
    count = lax.axis_size("seq")
    songs = lax.axis_size("song")
    me = lax.axis_index("seq")
    core = me % 2
    chips = count // 2
    chip = me // 2
    touching = (chip % 2) ^ core
    state = jnp.stack([core, touching]).astype(jnp.int32)
    gains = jnp.stack([q_gain, k_gain])

    swap = [(i, i ^ 1) for i in range(count)]
    partners = [(a, a ^ 1) for a in range(chips)]
    across = [(a, a ^ 2) for a in range(chips)]
    between = [(a, a + 1) for a in range(1, chips - 1, 2)]
    between += [(b, a) for a, b in between]

    def hop(block, moves):
        pairs = [(2 * a + c, 2 * b + c) for a, b in moves for c in (0, 1)]
        return lax.ppermute(block, "seq", pairs)

    hops = chips == 4 and lyric_local % 16 == 0
    total_rows = lyric_local * count
    if hops:
        run = ((0, lyric_local, lyric_local), (2 * lyric_local, 3 * lyric_local, lyric_local))
        groups = (run,) * 4
        owners = [chip, chip ^ 2, chip ^ 1, chip ^ 3]
        first_rows = []
        for owner in owners:
            first_rows += [
                (2 * owner + core) * lyric_local,
                (2 * owner + 1 - core) * lyric_local,
            ]
    else:
        gathered = jnp.concatenate(
            [
                lax.all_gather(
                    norm_rows(gains, lyric_keys[0]), "seq", axis=0, tiled=True
                ),
                lax.all_gather(lyric_values[0], "seq", axis=0, tiled=True),
            ],
            axis=0,
        )
        groups = (((0, total_rows, total_rows),),)
        first_rows = [0]
    has_left, has_right = chip > 0, chip < chips - 1
    has_near = jnp.where(core == 0, has_left, has_right)
    has_far = jnp.where(core == 0, has_right, has_left)
    meta = jnp.stack(
        [
            jnp.asarray(value, jnp.int32)
            for value in [core, touching]
            + [alignment[0, 0, slot] for slot in range(TILES)]
            + [lyric_len[0], has_near, has_far]
            + first_rows
        ]
    )

    to_mate = pack(
        state,
        alignment[0, 0],
        [queries[0], cotangent[0], keys[0], values[0]]
        + ([lyric_keys[0], lyric_values[0]] if hops else []),
    )
    mate = lax.ppermute(to_mate, "seq", swap)
    chunks, lyric_chunks, earlier, relayed, sent = [], [], [], [], []
    after = []
    for chunk in range(CHUNKS):
        before, one_before = after, lyrics[2:] if chunk else []
        if hops:
            pair = pair_lyrics(state, chunk, gains, lyric_keys[0], lyric_values[0], mate, before)
            two = hop(pair, across)
            lyrics = [pair, two, hop(two, partners)]
            lead, after = [pair], [two]
        else:
            lyrics, lead = [gathered], []
        one = hop(edge(state, chunk, 1, gains, keys[0], values[0], mate, lead, one_before), partners)
        mid = hop(edge(state, chunk, 0, gains, keys[0], values[0], mate, [], after), between)
        if not chunk:
            key_low = prepare_keys(state, gains, keys[0], mate, after)
        results = attention(
            chunk, meta, gains, queries[0], cotangent[0], values[0], key_low, mate, one, mid,
            lyrics, groups, earlier, relayed,
        )
        to_one, to_mid, gain_part, *parts = results[5:]
        earlier = [gain_part]
        mid_back = hop(to_mid, between)
        if hops:
            held, for_two, to_two = parts
            arrived = hop(to_two, partners)
            if chunk < CHUNKS - 1:
                relayed = [relay(for_two, arrived)]
                to_two = relayed[0]
            else:
                to_two, gain_total, to_one = last_relay(
                    for_two, arrived, gain_part, to_one, sent
                )
            two_back, one_back = hop(to_two, across), hop(to_one, partners)
            lyric_chunks += [held, one_back, two_back]
            sent = [*sent, mid_back, one_back, two_back]
        else:
            one_back = hop(to_one, partners)
            lyric_chunks += parts
        chunks += [*results[:5], one_back, mid_back]

    to_mate = []
    if hops:
        gain_total = sum_over(sum_over(gain_total, "song", bits_of(songs)), "seq", [4])
        own_half, part_to_mate = finish_lyric(
            state, gains, lyric_keys[0], mate, gain_total, lyric_chunks
        )
        to_mate = [part_to_mate]
    *filled, to_mate = finish_audio(state, gains, keys[0], mate, chunks, to_mate)
    from_mate = lax.ppermute(to_mate, "seq", swap)
    if hops:
        *filled, grad_lyric_keys, grad_lyric_values, q_total, k_total = join(
            state, gain_total, filled, own_half, from_mate
        )
    else:
        filled = fill_other(state, filled, from_mate)
        gain_total = lax.psum(gain_part, ("song", "seq"))
        q_total, k_total = gain_total[0:1], gain_total[1:2]
        spread = lax.dynamic_update_slice(
            jnp.zeros((2 * total_rows, width), jnp.float32),
            jnp.concatenate(lyric_chunks, axis=1).astype(jnp.float32),
            (0, core * (width // 2)),
        )
        lyric_key_sum, grad_lyric_values = [
            lax.psum_scatter(part, "seq", scatter_dimension=0, tiled=True)
            for part in (spread[:total_rows], spread[total_rows:])
        ]
        grad_lyric_keys = norm_lyric(gains, lyric_keys[0], lyric_key_sum)
        grad_lyric_values = grad_lyric_values.astype(jnp.bfloat16)
    output, grad_queries, grad_keys, grad_values = filled
    return (
        output[None],
        grad_queries[None],
        grad_keys[None],
        grad_values[None],
        grad_lyric_keys[None],
        grad_lyric_values[None],
        q_total[0],
        k_total[0],
    )


def solution(mesh):
    split = P("song", "seq", None)
    return jax.shard_map(
        body,
        mesh=mesh,
        in_specs=(split, split, split, split, split, P(), P(), split, split, P("song")),
        out_specs=(split, split, split, split, split, split, P(), P()),
        check_vma=False,
    )
```

```python
import functools

import jax
import jax.numpy as jnp
from jax import lax
from jax.experimental import pallas as pl
from jax.experimental.pallas import tpu as pltpu
from jax.sharding import PartitionSpec as P

BLK = 128
TILES = 2
NORM_EPS = 1e-06
VMEM_LIMIT = 8 * 1024 * 1024
ATTENTION_VMEM_LIMIT = 24 * 1024 * 1024
PACK_VMEM_LIMIT = 60 * 1024 * 1024
VMEM = pl.BlockSpec(memory_space=pltpu.VMEM)
SMEM = pl.BlockSpec(memory_space=pltpu.SMEM)
HBM = pl.BlockSpec(memory_space=pltpu.HBM)
ANY = pl.BlockSpec(memory_space=pl.ANY)
GAIN_ROWS = 16
HEADS_PER_STEP = 2
CHUNKS = 2
ALIGN_ROWS = 32
SMALL = pl.CostEstimate(flops=1, bytes_accessed=1, transcendentals=0)


def dot(lhs, rhs, lhs_dim, rhs_dim):
    return lax.dot_general(
        lhs, rhs, (((lhs_dim,), (rhs_dim,)), ((), ())), preferred_element_type=jnp.float32
    )


def call(kernel, name, in_specs, out_specs, out_shape, limit=VMEM_LIMIT, cost=SMALL, **options):
    return pl.pallas_call(
        kernel,
        in_specs=in_specs,
        out_specs=out_specs,
        out_shape=out_shape,
        compiler_params=pltpu.CompilerParams(vmem_limit_bytes=limit),
        cost_estimate=cost,
        name=name,
        **options,
    )


def shape(rows, cols, dtype=jnp.bfloat16):
    return jax.ShapeDtypeStruct((rows, cols), dtype)


def half_of(ref, core):
    half = ref.shape[1] // 2
    return pl.ds(pl.multiple_of(core * half, half), half)


def chunk_of(ref, core, chunk):
    size = ref.shape[1] // 2 // CHUNKS
    return pl.ds(pl.multiple_of((core * CHUNKS + chunk) * size, size), size)


def chunk_cols(chunk, size):
    return slice(chunk * size, (chunk + 1) * size)


def split_rows(sums, cols):
    high = sums.astype(jnp.bfloat16).astype(jnp.float32)
    rest = sums - high
    middle = rest.astype(jnp.bfloat16).astype(jnp.float32)
    low = rest - middle
    empty = jnp.zeros((sums.shape[0], cols - 3 * sums.shape[1]), jnp.float32)
    rows = jnp.concatenate([high, middle, low, empty], axis=1)
    return jnp.concatenate([rows, jnp.zeros_like(rows)], axis=0).astype(jnp.bfloat16)


def joined_rows(rows, size):
    rows = rows.astype(jnp.float32)[0:8]
    return (rows[:, 2 * size : 3 * size] + rows[:, size : 2 * size]) + rows[:, 0:size]


def normed(raw, k_gain):
    raw = raw.astype(jnp.float32)
    inverse = lax.rsqrt(jnp.mean(raw * raw, axis=1, keepdims=True) + NORM_EPS)
    return (raw * inverse * k_gain).astype(jnp.bfloat16)


def norm_columns(out_ref, rows, raw, gain_ref):
    head_size = gain_ref.shape[1]
    for head in range(raw.shape[1] // head_size):
        cols = slice(head * head_size, (head + 1) * head_size)
        out_ref[rows, cols] = normed(raw[:, cols], gain_ref[1:2, :])


def through_norm(raw, grad, k_gain):
    raw = raw.astype(jnp.float32)
    inverse = lax.rsqrt(jnp.mean(raw * raw, axis=1, keepdims=True) + NORM_EPS)
    scaled = grad * k_gain
    return (
        inverse * scaled
        - raw * (inverse * inverse * inverse) * jnp.mean(scaled * raw, axis=1, keepdims=True)
    ).astype(jnp.bfloat16)


def pack_kernel(state_ref, align_ref, *refs):
    ins, (out_ref, sems) = refs[:-2], refs[-2:]
    start = 0
    copies = []
    for index, ref in enumerate(ins):
        rows = ref.shape[0]
        copies.append(
            pltpu.make_async_copy(
                ref.at[:, half_of(ref, 1 - state_ref[0])],
                out_ref.at[start : start + rows, :],
                sems.at[index],
            )
        )
        copies[-1].start()
        start += rows
    if out_ref.shape[0] > start:
        row = lax.broadcasted_iota(jnp.int32, (ALIGN_ROWS, out_ref.shape[1]), 0)
        tiles = jnp.zeros(row.shape, jnp.int32)
        for slot in range(TILES):
            tiles = jnp.where(row == slot, align_ref[slot], tiles)
        out_ref[start:, :] = tiles.astype(jnp.float32).astype(jnp.bfloat16)
    for copy in copies:
        copy.wait()


def pack(state, align, arrays, extra_rows):
    rows = sum(array.shape[0] for array in arrays) + extra_rows
    return call(
        pack_kernel,
        "pack",
        [SMEM, SMEM] + [HBM] * len(arrays),
        VMEM,
        shape(rows, arrays[0].shape[1] // 2),
        limit=PACK_VMEM_LIMIT,
        scratch_shapes=[pltpu.SemaphoreType.DMA((len(arrays),))],
    )(state, align, *arrays)


def pair_kernel(chunk, state_ref, gain_ref, key_ref, value_ref, mate_ref, *refs):
    pair_ref = refs[-1]
    rows = key_ref.shape[0]
    first = mate_ref.shape[0] - ALIGN_ROWS - 2 * rows
    own = chunk_of(key_ref, state_ref[0], chunk)
    cols = chunk_cols(chunk, pair_ref.shape[1])
    norm_columns(pair_ref, slice(0, rows), key_ref[:, own], gain_ref)
    pair_ref[rows : 2 * rows, :] = value_ref[:, own]
    norm_columns(
        pair_ref, slice(2 * rows, 3 * rows), mate_ref[first : first + rows, cols], gain_ref
    )
    pair_ref[3 * rows :, :] = mate_ref[first + rows : first + 2 * rows, cols]


def pair_lyrics(state, chunk, gains, lyric_key, lyric_value, mate, after):
    rows, width = lyric_key.shape
    return call(
        functools.partial(pair_kernel, chunk),
        "pair_lyrics",
        [SMEM] + [VMEM] * 4 + [ANY] * len(after),
        VMEM,
        shape(4 * rows, width // 2 // CHUNKS),
    )(state, gains, lyric_key, lyric_value, mate, *after)


def edge_kernel(
    chunk, touching, leading, state_ref, gain_ref, key_ref, value_ref, mate_ref, *refs
):
    out_ref = refs[-1]
    frames = key_ref.shape[0]
    first = out_ref.shape[0] - 2 * frames
    if leading:
        out_ref[0:first, :] = refs[0][...]
    mine = state_ref[1] == touching
    own = chunk_of(key_ref, state_ref[0], chunk)
    cols = chunk_cols(chunk, out_ref.shape[1])
    keys = jnp.where(mine, key_ref[:, own], mate_ref[0:frames, cols])
    norm_columns(out_ref, slice(first, first + frames), keys, gain_ref)
    out_ref[first + frames :, :] = jnp.where(
        mine, value_ref[:, own], mate_ref[frames : 2 * frames, cols]
    )


def edge(state, chunk, touching, gains, key, value, mate, lead, after):
    frames, width = key.shape
    rows = sum(array.shape[0] for array in lead) + 2 * frames
    return call(
        functools.partial(edge_kernel, chunk, touching, bool(lead)),
        "edge",
        [SMEM] + [VMEM] * (4 + len(lead)) + [ANY] * len(after),
        VMEM,
        shape(rows, width // 2 // CHUNKS),
    )(state, gains, key, value, mate, *lead, *after)


def prepare_kernel(state_ref, gain_ref, key_ref, mate_ref, *refs):
    out_ref = refs[-1]
    frames = key_ref.shape[0]
    own = half_of(key_ref, state_ref[0])
    norm_columns(out_ref, slice(0, frames), key_ref[:, own], gain_ref)
    norm_columns(out_ref, slice(frames, 2 * frames), mate_ref[0:frames, :], gain_ref)


def prepare_keys(state, gains, key, mate, after):
    frames, width = key.shape
    return call(
        prepare_kernel,
        "prepare_keys",
        [SMEM] + [VMEM] * 3 + [ANY] * len(after),
        VMEM,
        shape(2 * frames, width // 2),
    )(state, gains, key, mate, *after)


def attention_kernel(
    chunk, chained, waits, groups, head_size, score_scale, meta_ref, gain_ref, query_ref, grad_ref, value_ref, key_ref,
    mate_ref, asked_ref, one_ref, mid_ref, *refs
):
    frames = query_ref.shape[0]
    exchanged = len(groups) == 4
    inputs = 3 if exchanged else 1
    lyric_in, refs = refs[:inputs], refs[inputs:]
    earlier, refs = refs[:chained], refs[chained + waits :]
    window = one_ref.shape[0] - 2 * frames
    out_ref, grad_query_ref, to_mate_ref, key_grad_ref, value_grad_ref = refs[:5]
    to_one_ref, to_mid_ref, gain_grad_ref = refs[5:8]
    lyric_out, mask_ref = refs[8:-1], refs[-1]
    runs = [(index, run) for index, group in enumerate(groups) for run in group]
    main = 2 * frames + sum(run[2] for _, run in runs)
    lanes = 2 * frames
    align = mate_ref.shape[0] - ALIGN_ROWS
    touching = meta_ref[1] == 1

    size = out_ref.shape[1]
    gain_grad_ref[...] = earlier[0][...] if chained else jnp.zeros_like(gain_grad_ref)
    mate_tiles = mate_ref[align:, 0:frames].astype(jnp.float32).astype(jnp.int32)
    start = 0
    for number, (_, (_, _, rows)) in enumerate(runs):
        row = lax.broadcasted_iota(jnp.int32, (rows, lanes), 0) + meta_ref[7 + number]
        keep = jnp.zeros((rows, lanes), jnp.float32)
        for slot in range(TILES):
            tile = jnp.concatenate(
                [
                    jnp.full((1, frames), meta_ref[2 + slot], jnp.int32),
                    mate_tiles[slot : slot + 1],
                ],
                axis=1,
            )
            lower = tile * BLK
            upper = jnp.minimum(lower + BLK, meta_ref[4])
            inside = (row >= lower) & (row < upper) & (lower >= 0)
            keep = jnp.where(inside, 1.0, keep)
        mask_ref[start : start + rows, :] = keep
        start += rows
    lane = lax.broadcasted_iota(jnp.int32, (frames, lanes), 1)
    mask_ref[start : start + frames, :] = jnp.where(
        lane < frames, meta_ref[5], meta_ref[6]
    ).astype(jnp.float32)

    q_gain = gain_ref[0:1, :]
    k_gain = gain_ref[1:2, :]
    heads = size // head_size

    def one_head(head):
        cols = pl.ds(pl.multiple_of(head * head_size, head_size), head_size)
        half_cols = pl.ds(
            pl.multiple_of((chunk * heads + head) * head_size, head_size), head_size
        )
        own_cols = pl.ds(
            pl.multiple_of(
                ((meta_ref[0] * CHUNKS + chunk) * heads + head) * head_size, head_size
            ),
            head_size,
        )
        lyric = [ref[:, cols if exchanged else own_cols] for ref in lyric_in]
        if exchanged:
            lyric = [lyric[0], lyric[1], one_ref[0:window, cols], lyric[2]]
        one_rows, mid_rows = one_ref[window:, cols], mid_ref[:, cols]
        near_rows = jnp.where(touching, one_rows, mid_rows)
        far_rows = jnp.where(touching, mid_rows, one_rows)

        query = jnp.concatenate([query_ref[:, own_cols], asked_ref[0:frames, half_cols]], axis=0)
        query = query.astype(jnp.float32)
        cot = jnp.concatenate([grad_ref[:, own_cols], asked_ref[frames:, half_cols]], axis=0)
        key_low = jnp.concatenate(
            [key_ref[:, half_cols]]
            + [lyric[index][run[0] : run[0] + run[2]] for index, run in runs]
            + [near_rows[:frames], far_rows[:frames]],
            axis=0,
        )
        value = jnp.concatenate(
            [value_ref[:, own_cols], mate_ref[frames : 2 * frames, half_cols]]
            + [lyric[index][run[1] : run[1] + run[2]] for index, run in runs]
            + [near_rows[frames:], far_rows[frames:]],
            axis=0,
        )
        query_inv = lax.rsqrt(jnp.mean(query * query, axis=1, keepdims=True) + NORM_EPS)
        query_hat = query * query_inv
        query_low = (query_hat * (q_gain * score_scale)).astype(jnp.bfloat16)

        near, far = slice(main, main + frames), slice(main + frames, main + 2 * frames)

        def against(rows, columns):
            return jnp.concatenate(
                [
                    dot(rows[:main], columns, 1, 1),
                    jnp.concatenate(
                        [
                            dot(rows[near], columns[:frames], 1, 1),
                            dot(rows[far], columns[frames:], 1, 1),
                        ],
                        axis=1,
                    ),
                ],
                axis=0,
            )

        def over_keys(weights, rows):
            return dot(weights[:main], rows[:main], 0, 0) + jnp.concatenate(
                [
                    dot(weights[main:, :frames], rows[near], 0, 0),
                    dot(weights[main:, frames:], rows[far], 0, 0),
                ],
                axis=0,
            )

        def over_queries(weights, columns):
            return jnp.concatenate(
                [
                    dot(weights[:main], columns, 1, 0),
                    dot(weights[main:, :frames], columns[:frames], 1, 0),
                    dot(weights[main:, frames:], columns[frames:], 1, 0),
                ],
                axis=0,
            )

        exp_scores = jnp.exp(against(key_low, query_low))
        exp_scores = jnp.concatenate(
            [exp_scores[: 2 * frames], exp_scores[2 * frames :] * mask_ref[...]], axis=0
        )
        grad_prob = against(value, cot)
        prob = exp_scores * (1.0 / jnp.sum(exp_scores, axis=0, keepdims=True))
        prob_low = prob.astype(jnp.bfloat16)
        weighted = prob * grad_prob
        delta = jnp.sum(weighted, axis=0, keepdims=True)
        grad_score = (weighted - prob * delta).astype(jnp.bfloat16)
        output = over_keys(prob_low, value).astype(jnp.bfloat16)
        grad_low = over_keys(grad_score, key_low)
        grad_qn = grad_low * score_scale
        grad_keys = over_queries(grad_score, query_low)
        grad_values = over_queries(prob_low, cot)
        scaled = grad_qn * q_gain
        grad_query = (
            query_inv * scaled
            - query_hat
            * (query_inv * query_inv)
            * jnp.mean(scaled * query, axis=1, keepdims=True)
        ).astype(jnp.bfloat16)
        gain_grad_ref[0:1, :] += jnp.sum(grad_qn * query_hat, axis=0, keepdims=True)
        gain_grad_ref[1:2, :] += (
            jnp.sum(grad_low * query_low.astype(jnp.float32), axis=0, keepdims=True) / k_gain
        )

        out_ref[:, cols] = output[:frames]
        grad_query_ref[:, cols] = grad_query[:frames]
        to_mate_ref[0:frames, cols] = output[frames:]
        to_mate_ref[frames:, cols] = grad_query[frames:]
        key_grad_ref[:, cols] = grad_keys[: 2 * frames]
        value_grad_ref[:, cols] = grad_values[: 2 * frames]
        for grads, part in (
            (grad_keys.astype(jnp.bfloat16), 0),
            (grad_values.astype(jnp.bfloat16), frames),
        ):
            to_one_ref[window + part : window + part + frames, cols] = jnp.where(
                touching, grads[near], grads[far]
            )
            to_mid_ref[part : part + frames, cols] = jnp.where(touching, grads[far], grads[near])
        if exchanged:
            held_ref, two_ref, to_two_ref = lyric_out
            outs = (held_ref, two_ref, to_one_ref, to_two_ref)
        else:
            outs = lyric_out
        start = 2 * frames
        for index, (key_row, value_row, rows) in runs:
            part = slice(start, start + rows)
            outs[index][key_row : key_row + rows, cols] = grad_keys[part].astype(jnp.bfloat16)
            outs[index][value_row : value_row + rows, cols] = grad_values[part].astype(
                jnp.bfloat16
            )
            start += rows

    @pl.loop(0, heads // HEADS_PER_STEP)
    def _(step):
        for number in range(HEADS_PER_STEP):
            one_head(step * HEADS_PER_STEP + number)

    if exchanged and chunk == CHUNKS - 1:
        to_two_ref = lyric_out[2]
        to_two_ref[window:, :] = split_rows(gain_grad_ref[...], size)


def attention(
    chunk, meta, gains, query, cot, value, key, mate, asked, one, mid, lyrics, groups, earlier,
    after,
):
    frames, width = query.shape
    head_size = gains.shape[1]
    size = width // 2 // CHUNKS
    lyric_rows = sum(run[2] for group in groups for run in group)
    key_rows = 3 * frames + lyric_rows
    bf16, f32 = jnp.bfloat16, jnp.float32
    slot = sum(2 * run[2] for run in groups[0])
    out_shape = [shape(frames, size)] * 2
    out_shape += [shape(2 * frames, size, dtype) for dtype in (bf16, f32, f32)]
    out_shape += [shape(one.shape[0], size), shape(2 * frames, size), shape(8, head_size, f32)]
    out_shape += [shape(slot, size)] * len(lyrics)
    if len(lyrics) > 1 and chunk == CHUNKS - 1:
        out_shape[-1] = shape(slot + GAIN_ROWS, size)
    return call(
        functools.partial(
            attention_kernel, chunk, len(earlier), len(after), groups, head_size, head_size ** (-0.5)
        ),
        "attention",
        [SMEM] + [VMEM] * (9 + len(lyrics) + len(earlier)) + [ANY] * len(after),
        [VMEM] * len(out_shape),
        out_shape,
        limit=ATTENTION_VMEM_LIMIT,
        cost=pl.CostEstimate(
            flops=24 * key_rows * frames * size,
            bytes_accessed=8 * 1024 * 1024,
            transcendentals=2 * key_rows * frames * (size // head_size),
        ),
        scratch_shapes=[pltpu.VMEM((frames + lyric_rows, 2 * frames), f32)],
    )(meta, gains, query, cot, value, key, mate, asked, one, mid, *lyrics, *earlier, *after)


def finish_audio_kernel(
    chunk, filled, state_ref, gain_ref, raw_ref, mate_ref, lyric_ref, out_own_ref, query_own_ref,
    ready_ref, key_grad_ref, value_grad_ref, one_ref, mid_ref, *refs,
):
    out, query_out, key_out, value_out, to_mate_ref, key_ref, value_ref, sems = refs[filled:]
    head_size = gain_ref.shape[1]
    k_gain = gain_ref[1:2, :]
    frames, size = key_ref.shape
    own, mate = slice(0, frames), slice(frames, 2 * frames)
    touching = state_ref[1] == 1
    copies = [
        pltpu.make_async_copy(
            source, target.at[:, chunk_of(target, state_ref[0], chunk)], sems.at[index]
        )
        for index, (source, target) in enumerate(
            (
                (out_own_ref, out),
                (query_own_ref, query_out),
                (key_ref, key_out),
                (value_ref, value_out),
            )
        )
    ]
    copies[0].start()
    copies[1].start()
    to_mate_ref[0 : 2 * frames, :] = ready_ref[...]
    if to_mate_ref.shape[0] > 4 * frames:
        to_mate_ref[4 * frames :, :] = lyric_ref[...]
    raw_keys = raw_ref[:, chunk_of(raw_ref, state_ref[0], chunk)]
    mate_keys = mate_ref[0:frames, chunk_cols(chunk, size)]
    first = one_ref.shape[0] - 2 * frames
    for head in range(size // head_size):
        cols = slice(head * head_size, (head + 1) * head_size)
        one = one_ref[first:, cols].astype(jnp.float32)
        mid = mid_ref[:, cols].astype(jnp.float32)
        for_own = jnp.where(touching, one, mid)
        for_mate = jnp.where(touching, mid, one)
        key_ref[:, cols] = through_norm(
            raw_keys[:, cols], key_grad_ref[own, cols] + for_own[:frames], k_gain
        )
        value_ref[:, cols] = (value_grad_ref[own, cols] + for_own[frames:]).astype(jnp.bfloat16)
        to_mate_ref[2 * frames : 3 * frames, cols] = through_norm(
            mate_keys[:, cols], key_grad_ref[mate, cols] + for_mate[:frames], k_gain
        )
        to_mate_ref[3 * frames : 4 * frames, cols] = (
            value_grad_ref[mate, cols] + for_mate[frames:]
        ).astype(jnp.bfloat16)
    copies[2].start()
    copies[3].start()
    for copy in copies:
        copy.wait()


def finish_audio(state, chunk, gains, raw, mate, lyric, arrays, filled):
    frames, width = raw.shape
    size = width // 2 // CHUNKS
    rows = 4 * frames + (lyric.shape[0] if lyric.shape[1] == size else 0)
    return call(
        functools.partial(finish_audio_kernel, chunk, len(filled)),
        "finish_audio",
        [SMEM] + [VMEM] * 11 + [HBM] * len(filled),
        [HBM] * 4 + [VMEM],
        [shape(frames, width)] * 4 + [shape(rows, size)],
        input_output_aliases={12 + i: i for i in range(len(filled))},
        scratch_shapes=[pltpu.VMEM((frames, size), jnp.bfloat16)] * 2
        + [pltpu.SemaphoreType.DMA((4,))],
    )(state, gains, raw, mate, lyric, *arrays, *filled)


def relay_kernel(part_ref, arrived_ref, *refs):
    rows = part_ref.shape[0]
    total = part_ref[...].astype(jnp.float32) + arrived_ref[0:rows, :].astype(jnp.float32)
    if arrived_ref.shape[0] == rows:
        refs[0][...] = total.astype(jnp.bfloat16)
        return
    gain_ref, (out_ref, total_ref, _) = refs[0], refs[-3:]
    out_ref[...] = total.astype(jnp.bfloat16)
    total_ref[...] = gain_ref[...] + joined_rows(arrived_ref[rows:, :], gain_ref.shape[1])


def relay(part, arrived):
    return call(relay_kernel, "relay", [VMEM] * 2, VMEM, shape(*part.shape))(part, arrived)


def last_relay(part, arrived, gain, later, after):
    return call(
        relay_kernel,
        "relay",
        [VMEM] * 3 + [ANY] * (1 + len(after)),
        [VMEM, VMEM, ANY],
        [shape(*part.shape), shape(*gain.shape, jnp.float32), shape(*later.shape)],
        input_output_aliases={3: 2},
    )(part, arrived, gain, later, *after)


def finish_lyric_kernel(
    chunk, summed, state_ref, gain_ref, raw_ref, mate_ref, held_ref, one_ref, two_ref, *refs
):
    own_ref, to_mate_ref = refs[-2:]
    rows = raw_ref.shape[0]
    head_size = gain_ref.shape[1]
    k_gain = gain_ref[1:2, :]
    size = held_ref.shape[1]
    first = mate_ref.shape[0] - ALIGN_ROWS - 2 * rows
    if summed:
        to_mate_ref[2 * rows :, :] = split_rows(refs[0][...], size)
    raw_keys = raw_ref[:, chunk_of(raw_ref, state_ref[0], chunk)]
    mate_keys = mate_ref[first : first + rows, chunk_cols(chunk, size)]
    for head in range(size // head_size):
        cols = slice(head * head_size, (head + 1) * head_size)
        total = held_ref[:, cols].astype(jnp.float32)
        for ref in (one_ref, two_ref):
            total = total + ref[0 : 4 * rows, cols].astype(jnp.float32)
        for ref, base, raw in (
            (own_ref, 0, raw_keys[:, cols]),
            (to_mate_ref, 2 * rows, mate_keys[:, cols]),
        ):
            ref[0:rows, cols] = through_norm(raw, total[base : base + rows], k_gain)
            ref[rows : 2 * rows, cols] = total[base + rows : base + 2 * rows].astype(jnp.bfloat16)


def finish_lyric(state, chunk, gains, raw, mate, parts, sums, after):
    rows, width = raw.shape
    size = width // 2 // CHUNKS
    return call(
        functools.partial(finish_lyric_kernel, chunk, bool(sums)),
        "finish_lyric",
        [SMEM] + [VMEM] * (6 + len(sums)) + [ANY] * len(after),
        [VMEM] * 2,
        [shape(2 * rows, size), shape(2 * rows + GAIN_ROWS * len(sums), size)],
    )(state, gains, raw, mate, *parts, *sums, *after)


def join_kernel(chunk, count, filled, state_ref, own_ref, mate_ref, *refs):
    outs, rest = refs[filled : filled + count], refs[filled + count :]
    sems = rest[-1]
    frames = outs[0].shape[0]
    rows = own_ref.shape[0] // 2
    pieces = [
        (mate_ref.at[index * frames : (index + 1) * frames, :], out, 1 - state_ref[0])
        for index, out in enumerate(outs[:4])
    ]
    for ref, first, core in ((own_ref, 0, state_ref[0]), (mate_ref, 4 * frames, 1 - state_ref[0])):
        for index, out in enumerate(outs[4:]):
            start = first + index * rows
            pieces.append((ref.at[start : start + rows, :], out, core))
    copies = [
        pltpu.make_async_copy(source, out.at[:, chunk_of(out, core, chunk)], sems.at[index])
        for index, (source, out, core) in enumerate(pieces)
    ]
    for copy in copies:
        copy.start()
    if len(rest) > 1:
        gain_ref, (q_total_ref, k_total_ref) = refs[0], rest[:2]
        sums = mate_ref[mate_ref.shape[0] - GAIN_ROWS :, :]
        total = gain_ref[...] + joined_rows(sums, gain_ref.shape[1])
        q_total_ref[...] = total[0:1]
        k_total_ref[...] = total[1:2]
    for copy in copies:
        copy.wait()


def join(state, chunk, own, mate, sums, filled, lyric_shape):
    shapes = [shape(*array.shape) for array in filled[:4]] + [shape(*lyric_shape)] * 2
    first = len(sums)
    return call(
        functools.partial(join_kernel, chunk, 6, first + len(filled)),
        "join",
        [SMEM] + [VMEM] * (2 + first) + [HBM] * len(filled),
        [HBM] * 6 + [VMEM] * (2 * first),
        shapes + [shape(1, total.shape[1], jnp.float32) for total in sums for _ in range(2)],
        input_output_aliases={3 + first + i: i for i in range(len(filled))},
        scratch_shapes=[pltpu.SemaphoreType.DMA((8,))],
    )(state, own, mate, *sums, *filled)


def tie(block, after):
    return call(
        lambda *refs: None,
        "tie",
        [ANY] * (1 + len(after)),
        ANY,
        shape(*block.shape, block.dtype),
        input_output_aliases={0: 0},
    )(block, *after)


def fill_kernel(chunk, state_ref, mate_ref, *refs):
    outs, sems = refs[4:-1], refs[-1]
    frames = outs[0].shape[0]
    copies = [
        pltpu.make_async_copy(
            mate_ref.at[index * frames : (index + 1) * frames, :],
            out.at[:, chunk_of(out, 1 - state_ref[0], chunk)],
            sems.at[index],
        )
        for index, out in enumerate(outs)
    ]
    for copy in copies:
        copy.start()
    for copy in copies:
        copy.wait()


def fill_other(state, chunk, arrays, mate):
    return call(
        functools.partial(fill_kernel, chunk),
        "fill_other",
        [SMEM, VMEM] + [HBM] * 4,
        [HBM] * 4,
        [shape(*array.shape) for array in arrays],
        input_output_aliases={2 + i: i for i in range(4)},
        scratch_shapes=[pltpu.SemaphoreType.DMA((4,))],
    )(state, mate, *arrays)


def norm_rows_kernel(gain_ref, raw_ref, out_ref):
    norm_columns(out_ref, slice(0, raw_ref.shape[0]), raw_ref[...], gain_ref)


def norm_rows(gains, raw):
    return pl.pallas_call(
        norm_rows_kernel,
        out_shape=jax.ShapeDtypeStruct(raw.shape, raw.dtype),
        name="norm_rows",
    )(gains, raw)


def norm_lyric_kernel(head_size, gain_ref, raw_ref, grad_ref, out_ref):
    for head in range(raw_ref.shape[1] // head_size):
        cols = slice(head * head_size, (head + 1) * head_size)
        out_ref[:, cols] = through_norm(raw_ref[:, cols], grad_ref[:, cols], gain_ref[1:2, :])


def norm_lyric(gains, raw, grad):
    return pl.pallas_call(
        functools.partial(norm_lyric_kernel, gains.shape[1]),
        out_shape=jax.ShapeDtypeStruct(raw.shape, jnp.bfloat16),
        name="norm_lyric",
    )(gains, raw, grad)


def sum_over(total, axis, bits):
    count = lax.axis_size(axis)
    for bit in bits:
        total = total + lax.ppermute(total, axis, [(i, i ^ bit) for i in range(count)])
    return total


def bits_of(count):
    return [1 << bit for bit in range(count.bit_length() - 1)]


def body(
    queries, keys, values, lyric_keys, lyric_values, q_gain, k_gain, cotangent, alignment, lyric_len
):
    frames = queries.shape[1]
    lyric_local, width = lyric_keys.shape[1:]
    count = lax.axis_size("seq")
    songs = lax.axis_size("song")
    me = lax.axis_index("seq")
    core = me % 2
    chips = count // 2
    chip = me // 2
    touching = (chip % 2) ^ core
    state = jnp.stack([core, touching]).astype(jnp.int32)
    gains = jnp.stack([q_gain, k_gain])

    swap = [(i, i ^ 1) for i in range(count)]
    partners = [(a, a ^ 1) for a in range(chips)]
    across = [(a, a ^ 2) for a in range(chips)]
    between = [(a, a + 1) for a in range(1, chips - 1, 2)]
    between += [(b, a) for a, b in between]

    def hop(block, moves):
        pairs = [(2 * a + c, 2 * b + c) for a, b in moves for c in (0, 1)]
        return lax.ppermute(block, "seq", pairs)

    hops = chips == 4 and lyric_local % 16 == 0
    total_rows = lyric_local * count
    if hops:
        run = ((0, lyric_local, lyric_local), (2 * lyric_local, 3 * lyric_local, lyric_local))
        groups = (run,) * 4
        owners = [chip, chip ^ 2, chip ^ 1, chip ^ 3]
        first_rows = []
        for owner in owners:
            first_rows += [
                (2 * owner + core) * lyric_local,
                (2 * owner + 1 - core) * lyric_local,
            ]
    else:
        gathered = jnp.concatenate(
            [
                lax.all_gather(
                    norm_rows(gains, lyric_keys[0]), "seq", axis=0, tiled=True
                ),
                lax.all_gather(lyric_values[0], "seq", axis=0, tiled=True),
            ],
            axis=0,
        )
        groups = (((0, total_rows, total_rows),),)
        first_rows = [0]
    has_left, has_right = chip > 0, chip < chips - 1
    has_near = jnp.where(core == 0, has_left, has_right)
    has_far = jnp.where(core == 0, has_right, has_left)
    meta = jnp.stack(
        [
            jnp.asarray(value, jnp.int32)
            for value in [core, touching]
            + [alignment[0, 0, slot] for slot in range(TILES)]
            + [lyric_len[0], has_near, has_far]
            + first_rows
        ]
    )

    lyric_rows = [lyric_keys[0], lyric_values[0]] if hops else []
    to_mate = pack(state, alignment[0, 0], [keys[0], values[0], *lyric_rows], ALIGN_ROWS)
    mate = lax.ppermute(to_mate, "seq", swap)
    asked = pack(state, alignment[0, 0], [queries[0], cotangent[0]], 0)
    asked = lax.ppermute(asked, "seq", swap)
    chunks, lyric_chunks, earlier, relayed, sent = [], [], [], [], []
    after = []
    for chunk in range(CHUNKS):
        before, one_before = after, lyrics[2:] if chunk else []
        if hops:
            pair = pair_lyrics(state, chunk, gains, lyric_keys[0], lyric_values[0], mate, before)
            two = hop(pair, across)
            lyrics = [pair, two, hop(two, partners)]
            lead, after = [pair], [two]
        else:
            lyrics, lead = [gathered], []
        one = hop(edge(state, chunk, 1, gains, keys[0], values[0], mate, lead, one_before), partners)
        mid = hop(edge(state, chunk, 0, gains, keys[0], values[0], mate, [], after), between)
        if not chunk:
            key_low = prepare_keys(state, gains, keys[0], mate, after)
        results = attention(
            chunk, meta, gains, queries[0], cotangent[0], values[0], key_low, mate, asked, one,
            mid, lyrics, groups, earlier, relayed,
        )
        to_one, to_mid, gain_part, *parts = results[5:]
        earlier = [gain_part]
        mid_back = hop(to_mid, between)
        if hops:
            held, for_two, to_two = parts
            arrived = hop(to_two, partners)
            if chunk < CHUNKS - 1:
                relayed = [relay(for_two, arrived)]
                to_two = relayed[0]
            else:
                to_two, gain_total, to_one = last_relay(
                    for_two, arrived, gain_part, to_one, sent
                )
            two_back, one_back = hop(to_two, across), hop(to_one, partners)
            lyric_chunks += [held, one_back, two_back]
            sent = [*sent, mid_back, one_back, two_back]
        else:
            one_back = hop(to_one, partners)
            lyric_chunks += parts
        chunks += [*results[:5], one_back, mid_back]

    filled, lyric_grads, totals = [], [], []
    for chunk in range(CHUNKS):
        sums = []
        if hops and chunk == CHUNKS - 1:
            gain_total = tie(sum_over(gain_total, "song", bits_of(songs)), lyric_grads)
            sums = [sum_over(gain_total, "seq", [4])]
        if hops:
            own_lyric, lyric = finish_lyric(
                state, chunk, gains, lyric_keys[0], mate, lyric_chunks[3 * chunk : 3 * chunk + 3],
                sums, [to_two],
            )
        else:
            lyric = gains
        *filled, to_mate = finish_audio(
            state, chunk, gains, keys[0], mate, lyric, chunks[7 * chunk : 7 * chunk + 7], filled
        )
        from_mate = lax.ppermute(to_mate, "seq", swap)
        if hops:
            results = join(
                state, chunk, own_lyric, from_mate, sums, [*filled, *lyric_grads],
                (lyric_local, width),
            )
            filled, lyric_grads, totals = results[:4], results[4:6], results[6:]
        else:
            filled = fill_other(state, chunk, filled, from_mate)
    if hops:
        (grad_lyric_keys, grad_lyric_values), (q_total, k_total) = lyric_grads, totals
    else:
        gain_total = lax.psum(gain_part, ("song", "seq"))
        q_total, k_total = gain_total[0:1], gain_total[1:2]
        spread = lax.dynamic_update_slice(
            jnp.zeros((2 * total_rows, width), jnp.float32),
            jnp.concatenate(lyric_chunks, axis=1).astype(jnp.float32),
            (0, core * (width // 2)),
        )
        lyric_key_sum, grad_lyric_values = [
            lax.psum_scatter(part, "seq", scatter_dimension=0, tiled=True)
            for part in (spread[:total_rows], spread[total_rows:])
        ]
        grad_lyric_keys = norm_lyric(gains, lyric_keys[0], lyric_key_sum)
        grad_lyric_values = grad_lyric_values.astype(jnp.bfloat16)
    output, grad_queries, grad_keys, grad_values = filled
    return (
        output[None],
        grad_queries[None],
        grad_keys[None],
        grad_values[None],
        grad_lyric_keys[None],
        grad_lyric_values[None],
        q_total[0],
        k_total[0],
    )


def solution(mesh):
    split = P("song", "seq", None)
    return jax.shard_map(
        body,
        mesh=mesh,
        in_specs=(split, split, split, split, split, P(), P(), split, split, P("song")),
        out_specs=(split, split, split, split, split, split, P(), P()),
        check_vma=False,
    )
```

```python
import functools

import jax
import jax.numpy as jnp
from jax import lax
from jax.experimental import pallas as pl
from jax.experimental.pallas import tpu as pltpu
from jax.sharding import PartitionSpec as P

BLK = 128
TILES = 2
NORM_EPS = 1e-06
VMEM_LIMIT = 8 * 1024 * 1024
ATTENTION_VMEM_LIMIT = 24 * 1024 * 1024
PACK_VMEM_LIMIT = 60 * 1024 * 1024
VMEM = pl.BlockSpec(memory_space=pltpu.VMEM)
SMEM = pl.BlockSpec(memory_space=pltpu.SMEM)
HBM = pl.BlockSpec(memory_space=pltpu.HBM)
ANY = pl.BlockSpec(memory_space=pl.ANY)
GAIN_ROWS = 16
HEADS_PER_STEP = 2
CHUNKS = 2
ALIGN_ROWS = 32
SMALL = pl.CostEstimate(flops=1, bytes_accessed=1, transcendentals=0)


def dot(lhs, rhs, lhs_dim, rhs_dim):
    return lax.dot_general(
        lhs, rhs, (((lhs_dim,), (rhs_dim,)), ((), ())), preferred_element_type=jnp.float32
    )


def call(kernel, name, in_specs, out_specs, out_shape, limit=VMEM_LIMIT, cost=SMALL, **options):
    return pl.pallas_call(
        kernel,
        in_specs=in_specs,
        out_specs=out_specs,
        out_shape=out_shape,
        compiler_params=pltpu.CompilerParams(vmem_limit_bytes=limit),
        cost_estimate=cost,
        name=name,
        **options,
    )


def shape(rows, cols, dtype=jnp.bfloat16):
    return jax.ShapeDtypeStruct((rows, cols), dtype)


def half_of(ref, core):
    half = ref.shape[1] // 2
    return pl.ds(pl.multiple_of(core * half, half), half)


def chunk_of(ref, core, chunk):
    size = ref.shape[1] // 2 // CHUNKS
    return pl.ds(pl.multiple_of((core * CHUNKS + chunk) * size, size), size)


def chunk_cols(chunk, size):
    return slice(chunk * size, (chunk + 1) * size)


def split_rows(sums, cols):
    high = sums.astype(jnp.bfloat16).astype(jnp.float32)
    rest = sums - high
    middle = rest.astype(jnp.bfloat16).astype(jnp.float32)
    low = rest - middle
    empty = jnp.zeros((sums.shape[0], cols - 3 * sums.shape[1]), jnp.float32)
    rows = jnp.concatenate([high, middle, low, empty], axis=1)
    return jnp.concatenate([rows, jnp.zeros_like(rows)], axis=0).astype(jnp.bfloat16)


def joined_rows(rows, size):
    rows = rows.astype(jnp.float32)[0:8]
    return (rows[:, 2 * size : 3 * size] + rows[:, size : 2 * size]) + rows[:, 0:size]


def normed(raw, k_gain):
    raw = raw.astype(jnp.float32)
    inverse = lax.rsqrt(jnp.mean(raw * raw, axis=1, keepdims=True) + NORM_EPS)
    return (raw * inverse * k_gain).astype(jnp.bfloat16)


def norm_columns(out_ref, rows, raw, gain_ref):
    head_size = gain_ref.shape[1]
    for head in range(raw.shape[1] // head_size):
        cols = slice(head * head_size, (head + 1) * head_size)
        out_ref[rows, cols] = normed(raw[:, cols], gain_ref[1:2, :])


def through_norm(raw, grad, k_gain):
    raw = raw.astype(jnp.float32)
    inverse = lax.rsqrt(jnp.mean(raw * raw, axis=1, keepdims=True) + NORM_EPS)
    scaled = grad * k_gain
    return (
        inverse * scaled
        - raw * (inverse * inverse * inverse) * jnp.mean(scaled * raw, axis=1, keepdims=True)
    ).astype(jnp.bfloat16)


def pack_kernel(state_ref, align_ref, *refs):
    ins, (out_ref, sems) = refs[:-2], refs[-2:]
    start = 0
    copies = []
    for index, ref in enumerate(ins):
        rows = ref.shape[0]
        copies.append(
            pltpu.make_async_copy(
                ref.at[:, half_of(ref, 1 - state_ref[0])],
                out_ref.at[start : start + rows, :],
                sems.at[index],
            )
        )
        copies[-1].start()
        start += rows
    row = lax.broadcasted_iota(jnp.int32, (ALIGN_ROWS, out_ref.shape[1]), 0)
    tiles = jnp.zeros(row.shape, jnp.int32)
    for slot in range(TILES):
        tiles = jnp.where(row == slot, align_ref[slot], tiles)
    out_ref[start:, :] = tiles.astype(jnp.float32).astype(jnp.bfloat16)
    for copy in copies:
        copy.wait()


def pack(state, align, arrays):
    rows = sum(array.shape[0] for array in arrays) + ALIGN_ROWS
    return call(
        pack_kernel,
        "pack",
        [SMEM, SMEM] + [HBM] * len(arrays),
        VMEM,
        shape(rows, arrays[0].shape[1] // 2),
        limit=PACK_VMEM_LIMIT,
        scratch_shapes=[pltpu.SemaphoreType.DMA((len(arrays),))],
    )(state, align, *arrays)


def pair_kernel(chunk, state_ref, gain_ref, key_ref, value_ref, mate_ref, *refs):
    pair_ref = refs[-1]
    rows = key_ref.shape[0]
    first = mate_ref.shape[0] - ALIGN_ROWS - 2 * rows
    own = chunk_of(key_ref, state_ref[0], chunk)
    cols = chunk_cols(chunk, pair_ref.shape[1])
    norm_columns(pair_ref, slice(0, rows), key_ref[:, own], gain_ref)
    pair_ref[rows : 2 * rows, :] = value_ref[:, own]
    norm_columns(
        pair_ref, slice(2 * rows, 3 * rows), mate_ref[first : first + rows, cols], gain_ref
    )
    pair_ref[3 * rows :, :] = mate_ref[first + rows : first + 2 * rows, cols]


def pair_lyrics(state, chunk, gains, lyric_key, lyric_value, mate, after):
    rows, width = lyric_key.shape
    return call(
        functools.partial(pair_kernel, chunk),
        "pair_lyrics",
        [SMEM] + [VMEM] * 4 + [ANY] * len(after),
        VMEM,
        shape(4 * rows, width // 2 // CHUNKS),
    )(state, gains, lyric_key, lyric_value, mate, *after)


def edge_kernel(
    chunk, touching, leading, state_ref, gain_ref, key_ref, value_ref, mate_ref, *refs
):
    out_ref = refs[-1]
    frames = key_ref.shape[0]
    first = out_ref.shape[0] - 2 * frames
    if leading:
        out_ref[0:first, :] = refs[0][...]
    mine = state_ref[1] == touching
    own = chunk_of(key_ref, state_ref[0], chunk)
    cols = chunk_cols(chunk, out_ref.shape[1])
    keys = jnp.where(mine, key_ref[:, own], mate_ref[2 * frames : 3 * frames, cols])
    norm_columns(out_ref, slice(first, first + frames), keys, gain_ref)
    out_ref[first + frames :, :] = jnp.where(
        mine, value_ref[:, own], mate_ref[3 * frames : 4 * frames, cols]
    )


def edge(state, chunk, touching, gains, key, value, mate, lead, after):
    frames, width = key.shape
    rows = sum(array.shape[0] for array in lead) + 2 * frames
    return call(
        functools.partial(edge_kernel, chunk, touching, bool(lead)),
        "edge",
        [SMEM] + [VMEM] * (4 + len(lead)) + [ANY] * len(after),
        VMEM,
        shape(rows, width // 2 // CHUNKS),
    )(state, gains, key, value, mate, *lead, *after)


def prepare_kernel(state_ref, gain_ref, key_ref, mate_ref, *refs):
    out_ref = refs[-1]
    frames = key_ref.shape[0]
    own = half_of(key_ref, state_ref[0])
    norm_columns(out_ref, slice(0, frames), key_ref[:, own], gain_ref)
    norm_columns(
        out_ref, slice(frames, 2 * frames), mate_ref[2 * frames : 3 * frames, :], gain_ref
    )


def prepare_keys(state, gains, key, mate, after):
    frames, width = key.shape
    return call(
        prepare_kernel,
        "prepare_keys",
        [SMEM] + [VMEM] * 3 + [ANY] * len(after),
        VMEM,
        shape(2 * frames, width // 2),
    )(state, gains, key, mate, *after)


def attention_kernel(
    chunk, chained, waits, groups, head_size, score_scale, meta_ref, gain_ref, query_ref, grad_ref, value_ref, key_ref,
    mate_ref, one_ref, mid_ref, *refs
):
    frames = query_ref.shape[0]
    exchanged = len(groups) == 4
    inputs = 3 if exchanged else 1
    lyric_in, refs = refs[:inputs], refs[inputs:]
    earlier, refs = refs[:chained], refs[chained + waits :]
    window = one_ref.shape[0] - 2 * frames
    out_ref, grad_query_ref, to_mate_ref, key_grad_ref, value_grad_ref = refs[:5]
    to_one_ref, to_mid_ref, gain_grad_ref = refs[5:8]
    lyric_out, mask_ref = refs[8:-1], refs[-1]
    runs = [(index, run) for index, group in enumerate(groups) for run in group]
    main = 2 * frames + sum(run[2] for _, run in runs)
    lanes = 2 * frames
    align = mate_ref.shape[0] - ALIGN_ROWS
    touching = meta_ref[1] == 1

    size = out_ref.shape[1]
    gain_grad_ref[...] = earlier[0][...] if chained else jnp.zeros_like(gain_grad_ref)
    mate_tiles = mate_ref[align:, 0:frames].astype(jnp.float32).astype(jnp.int32)
    start = 0
    for number, (_, (_, _, rows)) in enumerate(runs):
        row = lax.broadcasted_iota(jnp.int32, (rows, lanes), 0) + meta_ref[7 + number]
        keep = jnp.zeros((rows, lanes), jnp.float32)
        for slot in range(TILES):
            tile = jnp.concatenate(
                [
                    jnp.full((1, frames), meta_ref[2 + slot], jnp.int32),
                    mate_tiles[slot : slot + 1],
                ],
                axis=1,
            )
            lower = tile * BLK
            upper = jnp.minimum(lower + BLK, meta_ref[4])
            inside = (row >= lower) & (row < upper) & (lower >= 0)
            keep = jnp.where(inside, 1.0, keep)
        mask_ref[start : start + rows, :] = keep
        start += rows
    lane = lax.broadcasted_iota(jnp.int32, (frames, lanes), 1)
    mask_ref[start : start + frames, :] = jnp.where(
        lane < frames, meta_ref[5], meta_ref[6]
    ).astype(jnp.float32)

    q_gain = gain_ref[0:1, :]
    k_gain = gain_ref[1:2, :]
    heads = size // head_size

    def one_head(head):
        cols = pl.ds(pl.multiple_of(head * head_size, head_size), head_size)
        half_cols = pl.ds(
            pl.multiple_of((chunk * heads + head) * head_size, head_size), head_size
        )
        own_cols = pl.ds(
            pl.multiple_of(
                ((meta_ref[0] * CHUNKS + chunk) * heads + head) * head_size, head_size
            ),
            head_size,
        )
        lyric = [ref[:, cols if exchanged else own_cols] for ref in lyric_in]
        if exchanged:
            lyric = [lyric[0], lyric[1], one_ref[0:window, cols], lyric[2]]
        one_rows, mid_rows = one_ref[window:, cols], mid_ref[:, cols]
        near_rows = jnp.where(touching, one_rows, mid_rows)
        far_rows = jnp.where(touching, mid_rows, one_rows)

        def from_mate(number):
            return mate_ref[number * frames : (number + 1) * frames, half_cols]

        query = jnp.concatenate([query_ref[:, own_cols], from_mate(0)], axis=0)
        query = query.astype(jnp.float32)
        cot = jnp.concatenate([grad_ref[:, own_cols], from_mate(1)], axis=0)
        key_low = jnp.concatenate(
            [key_ref[:, half_cols]]
            + [lyric[index][run[0] : run[0] + run[2]] for index, run in runs]
            + [near_rows[:frames], far_rows[:frames]],
            axis=0,
        )
        value = jnp.concatenate(
            [value_ref[:, own_cols], from_mate(3)]
            + [lyric[index][run[1] : run[1] + run[2]] for index, run in runs]
            + [near_rows[frames:], far_rows[frames:]],
            axis=0,
        )
        query_inv = lax.rsqrt(jnp.mean(query * query, axis=1, keepdims=True) + NORM_EPS)
        query_hat = query * query_inv
        query_low = (query_hat * (q_gain * score_scale)).astype(jnp.bfloat16)

        near, far = slice(main, main + frames), slice(main + frames, main + 2 * frames)

        def against(rows, columns):
            return jnp.concatenate(
                [
                    dot(rows[:main], columns, 1, 1),
                    jnp.concatenate(
                        [
                            dot(rows[near], columns[:frames], 1, 1),
                            dot(rows[far], columns[frames:], 1, 1),
                        ],
                        axis=1,
                    ),
                ],
                axis=0,
            )

        def over_keys(weights, rows):
            return dot(weights[:main], rows[:main], 0, 0) + jnp.concatenate(
                [
                    dot(weights[main:, :frames], rows[near], 0, 0),
                    dot(weights[main:, frames:], rows[far], 0, 0),
                ],
                axis=0,
            )

        def over_queries(weights, columns):
            return jnp.concatenate(
                [
                    dot(weights[:main], columns, 1, 0),
                    dot(weights[main:, :frames], columns[:frames], 1, 0),
                    dot(weights[main:, frames:], columns[frames:], 1, 0),
                ],
                axis=0,
            )

        exp_scores = jnp.exp(against(key_low, query_low))
        exp_scores = jnp.concatenate(
            [exp_scores[: 2 * frames], exp_scores[2 * frames :] * mask_ref[...]], axis=0
        )
        grad_prob = against(value, cot)
        prob = exp_scores * (1.0 / jnp.sum(exp_scores, axis=0, keepdims=True))
        prob_low = prob.astype(jnp.bfloat16)
        weighted = prob * grad_prob
        delta = jnp.sum(weighted, axis=0, keepdims=True)
        grad_score = (weighted - prob * delta).astype(jnp.bfloat16)
        output = over_keys(prob_low, value).astype(jnp.bfloat16)
        grad_low = over_keys(grad_score, key_low)
        grad_qn = grad_low * score_scale
        grad_keys = over_queries(grad_score, query_low)
        grad_values = over_queries(prob_low, cot)
        scaled = grad_qn * q_gain
        grad_query = (
            query_inv * scaled
            - query_hat
            * (query_inv * query_inv)
            * jnp.mean(scaled * query, axis=1, keepdims=True)
        ).astype(jnp.bfloat16)
        gain_grad_ref[0:1, :] += jnp.sum(grad_qn * query_hat, axis=0, keepdims=True)
        gain_grad_ref[1:2, :] += (
            jnp.sum(grad_low * query_low.astype(jnp.float32), axis=0, keepdims=True) / k_gain
        )

        out_ref[:, cols] = output[:frames]
        grad_query_ref[:, cols] = grad_query[:frames]
        to_mate_ref[0:frames, cols] = output[frames:]
        to_mate_ref[frames:, cols] = grad_query[frames:]
        key_grad_ref[:, cols] = grad_keys[: 2 * frames]
        value_grad_ref[:, cols] = grad_values[: 2 * frames]
        for grads, part in (
            (grad_keys.astype(jnp.bfloat16), 0),
            (grad_values.astype(jnp.bfloat16), frames),
        ):
            to_one_ref[window + part : window + part + frames, cols] = jnp.where(
                touching, grads[near], grads[far]
            )
            to_mid_ref[part : part + frames, cols] = jnp.where(touching, grads[far], grads[near])
        if exchanged:
            held_ref, two_ref, to_two_ref = lyric_out
            outs = (held_ref, two_ref, to_one_ref, to_two_ref)
        else:
            outs = lyric_out
        start = 2 * frames
        for index, (key_row, value_row, rows) in runs:
            part = slice(start, start + rows)
            outs[index][key_row : key_row + rows, cols] = grad_keys[part].astype(jnp.bfloat16)
            outs[index][value_row : value_row + rows, cols] = grad_values[part].astype(
                jnp.bfloat16
            )
            start += rows

    @pl.loop(0, heads // HEADS_PER_STEP)
    def _(step):
        for number in range(HEADS_PER_STEP):
            one_head(step * HEADS_PER_STEP + number)


def attention(
    chunk, meta, gains, query, cot, value, key, mate, one, mid, lyrics, groups, earlier, after
):
    frames, width = query.shape
    head_size = gains.shape[1]
    size = width // 2 // CHUNKS
    lyric_rows = sum(run[2] for group in groups for run in group)
    key_rows = 3 * frames + lyric_rows
    bf16, f32 = jnp.bfloat16, jnp.float32
    slot = sum(2 * run[2] for run in groups[0])
    out_shape = [shape(frames, size)] * 2
    out_shape += [shape(2 * frames, size, dtype) for dtype in (bf16, f32, f32)]
    out_shape += [shape(one.shape[0], size), shape(2 * frames, size), shape(8, head_size, f32)]
    out_shape += [shape(slot, size)] * len(lyrics)
    return call(
        functools.partial(
            attention_kernel, chunk, len(earlier), len(after), groups, head_size, head_size ** (-0.5)
        ),
        "attention",
        [SMEM] + [VMEM] * (8 + len(lyrics) + len(earlier)) + [ANY] * len(after),
        [VMEM] * len(out_shape),
        out_shape,
        limit=ATTENTION_VMEM_LIMIT,
        cost=pl.CostEstimate(
            flops=24 * key_rows * frames * size,
            bytes_accessed=8 * 1024 * 1024,
            transcendentals=2 * key_rows * frames * (size // head_size),
        ),
        scratch_shapes=[pltpu.VMEM((frames + lyric_rows, 2 * frames), f32)],
    )(meta, gains, query, cot, value, key, mate, one, mid, *lyrics, *earlier, *after)


def finish_audio_kernel(state_ref, gain_ref, raw_ref, mate_ref, *refs):
    chunk_refs, refs = refs[: 7 * CHUNKS], refs[7 * CHUNKS :]
    *lyric, out, query_out, key_out, value_out, to_mate_ref, key_ref, value_ref, sems = refs
    head_size = gain_ref.shape[1]
    k_gain = gain_ref[1:2, :]
    frames, half = key_ref.shape
    size = half // CHUNKS
    own, mate = slice(0, frames), slice(frames, 2 * frames)
    touching = state_ref[1] == 1
    copies = []
    for chunk in range(CHUNKS):
        out_own_ref, query_own_ref, ready_ref = chunk_refs[7 * chunk : 7 * chunk + 3]
        for source, target in ((out_own_ref, out), (query_own_ref, query_out)):
            copies.append(
                pltpu.make_async_copy(
                    source,
                    target.at[:, chunk_of(target, state_ref[0], chunk)],
                    sems.at[len(copies)],
                )
            )
            copies[-1].start()
        to_mate_ref[0 : 2 * frames, chunk_cols(chunk, size)] = ready_ref[...]
    for ref in lyric:
        to_mate_ref[4 * frames :, :] = ref[...]
    raw_keys = raw_ref[:, half_of(raw_ref, state_ref[0])]
    for head in range(half // head_size):
        cols = slice(head * head_size, (head + 1) * head_size)
        chunk = head * head_size // size
        part = slice(head * head_size - chunk * size, (head + 1) * head_size - chunk * size)
        key_grad_ref, value_grad_ref, one_ref, mid_ref = chunk_refs[7 * chunk + 3 : 7 * chunk + 7]
        one = one_ref[one_ref.shape[0] - 2 * frames :, part].astype(jnp.float32)
        mid = mid_ref[:, part].astype(jnp.float32)
        for_own = jnp.where(touching, one, mid)
        for_mate = jnp.where(touching, mid, one)
        key_ref[:, cols] = through_norm(
            raw_keys[:, cols], key_grad_ref[own, part] + for_own[:frames], k_gain
        )
        value_ref[:, cols] = (value_grad_ref[own, part] + for_own[frames:]).astype(jnp.bfloat16)
        to_mate_ref[2 * frames : 3 * frames, cols] = through_norm(
            mate_ref[2 * frames : 3 * frames, cols],
            key_grad_ref[mate, part] + for_mate[:frames],
            k_gain,
        )
        to_mate_ref[3 * frames : 4 * frames, cols] = (
            value_grad_ref[mate, part] + for_mate[frames:]
        ).astype(jnp.bfloat16)
    for source, target in ((key_ref, key_out), (value_ref, value_out)):
        copies.append(
            pltpu.make_async_copy(
                source, target.at[:, half_of(target, state_ref[0])], sems.at[len(copies)]
            )
        )
        copies[-1].start()
    for copy in copies:
        copy.wait()


def finish_audio(state, gains, raw, mate, chunks, lyric):
    frames, width = raw.shape
    half = width // 2
    rows = 4 * frames + sum(array.shape[0] for array in lyric)
    return call(
        finish_audio_kernel,
        "finish_audio",
        [SMEM] + [VMEM] * (3 + len(chunks) + len(lyric)),
        [HBM] * 4 + [VMEM],
        [shape(frames, width)] * 4 + [shape(rows, half)],
        scratch_shapes=[pltpu.VMEM((frames, half), jnp.bfloat16)] * 2
        + [pltpu.SemaphoreType.DMA((2 * CHUNKS + 2,))],
    )(state, gains, raw, mate, *chunks, *lyric)


def relay_kernel(part_ref, arrived_ref, *refs):
    out_ref = refs[0] if len(refs) == 1 else refs[-2]
    out_ref[...] = (
        part_ref[...].astype(jnp.float32) + arrived_ref[...].astype(jnp.float32)
    ).astype(jnp.bfloat16)


def relay(part, arrived):
    return call(relay_kernel, "relay", [VMEM] * 2, VMEM, shape(*part.shape))(part, arrived)


def last_relay(part, arrived, later, after):
    return call(
        relay_kernel,
        "relay",
        [VMEM] * 2 + [ANY] * (1 + len(after)),
        [VMEM, ANY],
        [shape(*part.shape), shape(*later.shape)],
        input_output_aliases={2: 1},
    )(part, arrived, later, *after)


def finish_lyric_kernel(
    state_ref, gain_ref, raw_ref, mate_ref, sum_ref, *refs
):
    chunk_refs, (own_ref, to_mate_ref) = refs[:-2], refs[-2:]
    rows = raw_ref.shape[0]
    head_size = gain_ref.shape[1]
    k_gain = gain_ref[1:2, :]
    size = chunk_refs[0].shape[1]
    first = mate_ref.shape[0] - ALIGN_ROWS - 2 * rows
    to_mate_ref[2 * rows :, :] = split_rows(sum_ref[...], to_mate_ref.shape[1])
    raw_keys = raw_ref[:, half_of(raw_ref, state_ref[0])]
    for head in range(own_ref.shape[1] // head_size):
        cols = slice(head * head_size, (head + 1) * head_size)
        chunk = head * head_size // size
        part = slice(head * head_size - chunk * size, (head + 1) * head_size - chunk * size)
        total = chunk_refs[3 * chunk][:, part].astype(jnp.float32)
        for ref in chunk_refs[3 * chunk + 1 : 3 * chunk + 3]:
            total = total + ref[0 : 4 * rows, part].astype(jnp.float32)
        mate_keys = mate_ref[first : first + rows, cols]
        for ref, base, raw in (
            (own_ref, 0, raw_keys[:, cols]),
            (to_mate_ref, 2 * rows, mate_keys),
        ):
            ref[0:rows, cols] = through_norm(raw, total[base : base + rows], k_gain)
            ref[rows : 2 * rows, cols] = total[base + rows : base + 2 * rows].astype(jnp.bfloat16)


def finish_lyric(state, gains, raw, mate, total, chunks):
    rows, width = raw.shape
    half = width // 2
    return call(
        finish_lyric_kernel,
        "finish_lyric",
        [SMEM] + [VMEM] * (4 + len(chunks)),
        [VMEM] * 2,
        [shape(2 * rows, half), shape(2 * rows + GAIN_ROWS, half)],
    )(state, gains, raw, mate, total, *chunks)


def join_kernel(count, state_ref, gain_ref, own_ref, mate_ref, *refs):
    outs, (q_total_ref, k_total_ref, sems) = refs[count:-3], refs[-3:]
    frames = outs[0].shape[0]
    rows = own_ref.shape[0] // 2
    pieces = [
        (mate_ref.at[index * frames : (index + 1) * frames, :], out, 1 - state_ref[0])
        for index, out in enumerate(outs[:count])
    ]
    for ref, first, core in ((own_ref, 0, state_ref[0]), (mate_ref, count * frames, 1 - state_ref[0])):
        for index, out in enumerate(outs[count:]):
            start = first + index * rows
            pieces.append((ref.at[start : start + rows, :], out, core))
    copies = [
        pltpu.make_async_copy(source, out.at[:, half_of(out, core)], sems.at[index])
        for index, (source, out, core) in enumerate(pieces)
    ]
    for copy in copies:
        copy.start()
    sums = mate_ref[mate_ref.shape[0] - GAIN_ROWS :, :]
    total = gain_ref[...] + joined_rows(sums, gain_ref.shape[1])
    q_total_ref[...] = total[0:1]
    k_total_ref[...] = total[1:2]
    for copy in copies:
        copy.wait()


def join(state, gain, arrays, own, mate):
    rows, half = own.shape
    count = len(arrays)
    return call(
        functools.partial(join_kernel, count),
        "join",
        [SMEM] + [VMEM] * 3 + [HBM] * count,
        [HBM] * (count + 2) + [VMEM] * 2,
        [shape(*array.shape) for array in arrays]
        + [shape(rows // 2, 2 * half)] * 2
        + [shape(1, gain.shape[1], jnp.float32)] * 2,
        input_output_aliases={4 + i: i for i in range(count)},
        scratch_shapes=[pltpu.SemaphoreType.DMA((count + 4,))],
    )(state, gain, own, mate, *arrays)


def fill_kernel(count, state_ref, mate_ref, *refs):
    outs, sems = refs[count:-1], refs[-1]
    frames = outs[0].shape[0]
    copies = [
        pltpu.make_async_copy(
            mate_ref.at[index * frames : (index + 1) * frames, :],
            out.at[:, half_of(out, 1 - state_ref[0])],
            sems.at[index],
        )
        for index, out in enumerate(outs)
    ]
    for copy in copies:
        copy.start()
    for copy in copies:
        copy.wait()


def fill_other(state, arrays, mate):
    count = len(arrays)
    return call(
        functools.partial(fill_kernel, count),
        "fill_other",
        [SMEM, VMEM] + [HBM] * count,
        [HBM] * count,
        [shape(*array.shape) for array in arrays],
        input_output_aliases={2 + i: i for i in range(count)},
        scratch_shapes=[pltpu.SemaphoreType.DMA((count,))],
    )(state, mate, *arrays)


def norm_rows_kernel(gain_ref, raw_ref, out_ref):
    norm_columns(out_ref, slice(0, raw_ref.shape[0]), raw_ref[...], gain_ref)


def norm_rows(gains, raw):
    return pl.pallas_call(
        norm_rows_kernel,
        out_shape=jax.ShapeDtypeStruct(raw.shape, raw.dtype),
        name="norm_rows",
    )(gains, raw)


def norm_lyric_kernel(head_size, gain_ref, raw_ref, grad_ref, out_ref):
    for head in range(raw_ref.shape[1] // head_size):
        cols = slice(head * head_size, (head + 1) * head_size)
        out_ref[:, cols] = through_norm(raw_ref[:, cols], grad_ref[:, cols], gain_ref[1:2, :])


def norm_lyric(gains, raw, grad):
    return pl.pallas_call(
        functools.partial(norm_lyric_kernel, gains.shape[1]),
        out_shape=jax.ShapeDtypeStruct(raw.shape, jnp.bfloat16),
        name="norm_lyric",
    )(gains, raw, grad)


def sum_over(total, axis, bits):
    count = lax.axis_size(axis)
    for bit in bits:
        total = total + lax.ppermute(total, axis, [(i, i ^ bit) for i in range(count)])
    return total


def bits_of(count):
    return [1 << bit for bit in range(count.bit_length() - 1)]


def body(
    queries, keys, values, lyric_keys, lyric_values, q_gain, k_gain, cotangent, alignment, lyric_len
):
    frames = queries.shape[1]
    lyric_local, width = lyric_keys.shape[1:]
    count = lax.axis_size("seq")
    songs = lax.axis_size("song")
    me = lax.axis_index("seq")
    core = me % 2
    chips = count // 2
    chip = me // 2
    touching = (chip % 2) ^ core
    state = jnp.stack([core, touching]).astype(jnp.int32)
    gains = jnp.stack([q_gain, k_gain])

    swap = [(i, i ^ 1) for i in range(count)]
    partners = [(a, a ^ 1) for a in range(chips)]
    across = [(a, a ^ 2) for a in range(chips)]
    between = [(a, a + 1) for a in range(1, chips - 1, 2)]
    between += [(b, a) for a, b in between]

    def hop(block, moves):
        pairs = [(2 * a + c, 2 * b + c) for a, b in moves for c in (0, 1)]
        return lax.ppermute(block, "seq", pairs)

    hops = chips == 4 and lyric_local % 16 == 0
    total_rows = lyric_local * count
    if hops:
        run = ((0, lyric_local, lyric_local), (2 * lyric_local, 3 * lyric_local, lyric_local))
        groups = (run,) * 4
        owners = [chip, chip ^ 2, chip ^ 1, chip ^ 3]
        first_rows = []
        for owner in owners:
            first_rows += [
                (2 * owner + core) * lyric_local,
                (2 * owner + 1 - core) * lyric_local,
            ]
    else:
        gathered = jnp.concatenate(
            [
                lax.all_gather(
                    norm_rows(gains, lyric_keys[0]), "seq", axis=0, tiled=True
                ),
                lax.all_gather(lyric_values[0], "seq", axis=0, tiled=True),
            ],
            axis=0,
        )
        groups = (((0, total_rows, total_rows),),)
        first_rows = [0]
    has_left, has_right = chip > 0, chip < chips - 1
    has_near = jnp.where(core == 0, has_left, has_right)
    has_far = jnp.where(core == 0, has_right, has_left)
    meta = jnp.stack(
        [
            jnp.asarray(value, jnp.int32)
            for value in [core, touching]
            + [alignment[0, 0, slot] for slot in range(TILES)]
            + [lyric_len[0], has_near, has_far]
            + first_rows
        ]
    )

    to_mate = pack(
        state,
        alignment[0, 0],
        [queries[0], cotangent[0], keys[0], values[0]]
        + ([lyric_keys[0], lyric_values[0]] if hops else []),
    )
    mate = lax.ppermute(to_mate, "seq", swap)
    chunks, lyric_chunks, earlier, relayed, sent = [], [], [], [], []
    after = []
    for chunk in range(CHUNKS):
        before, one_before = after, lyrics[2:] if chunk else []
        if hops:
            pair = pair_lyrics(state, chunk, gains, lyric_keys[0], lyric_values[0], mate, before)
            two = hop(pair, across)
            lyrics = [pair, two, hop(two, partners)]
            lead, after = [pair], [two]
        else:
            lyrics, lead = [gathered], []
        one = hop(edge(state, chunk, 1, gains, keys[0], values[0], mate, lead, one_before), partners)
        mid = hop(edge(state, chunk, 0, gains, keys[0], values[0], mate, [], after), between)
        if not chunk:
            key_low = prepare_keys(state, gains, keys[0], mate, after)
        results = attention(
            chunk, meta, gains, queries[0], cotangent[0], values[0], key_low, mate, one, mid,
            lyrics, groups, earlier, relayed,
        )
        to_one, to_mid, gain_part, *parts = results[5:]
        earlier = [gain_part]
        mid_back = hop(to_mid, between)
        if hops:
            held, for_two, to_two = parts
            arrived = hop(to_two, partners)
            if chunk < CHUNKS - 1:
                relayed = [relay(for_two, arrived)]
                to_two = relayed[0]
            else:
                gain_total = sum_over(gain_part, "song", bits_of(songs))
                to_two, to_one = last_relay(for_two, arrived, to_one, [*sent, gain_total])
            two_back, one_back = hop(to_two, across), hop(to_one, partners)
            lyric_chunks += [held, one_back, two_back]
            sent = [*sent, mid_back, one_back, two_back]
        else:
            one_back = hop(to_one, partners)
            lyric_chunks += parts
        chunks += [*results[:5], one_back, mid_back]

    to_mate = []
    if hops:
        gain_total = sum_over(gain_total, "seq", [2, 4])
        own_half, part_to_mate = finish_lyric(
            state, gains, lyric_keys[0], mate, gain_total, lyric_chunks
        )
        to_mate = [part_to_mate]
    *filled, to_mate = finish_audio(state, gains, keys[0], mate, chunks, to_mate)
    from_mate = lax.ppermute(to_mate, "seq", swap)
    if hops:
        *filled, grad_lyric_keys, grad_lyric_values, q_total, k_total = join(
            state, gain_total, filled, own_half, from_mate
        )
    else:
        filled = fill_other(state, filled, from_mate)
        gain_total = lax.psum(gain_part, ("song", "seq"))
        q_total, k_total = gain_total[0:1], gain_total[1:2]
        spread = lax.dynamic_update_slice(
            jnp.zeros((2 * total_rows, width), jnp.float32),
            jnp.concatenate(lyric_chunks, axis=1).astype(jnp.float32),
            (0, core * (width // 2)),
        )
        lyric_key_sum, grad_lyric_values = [
            lax.psum_scatter(part, "seq", scatter_dimension=0, tiled=True)
            for part in (spread[:total_rows], spread[total_rows:])
        ]
        grad_lyric_keys = norm_lyric(gains, lyric_keys[0], lyric_key_sum)
        grad_lyric_values = grad_lyric_values.astype(jnp.bfloat16)
    output, grad_queries, grad_keys, grad_values = filled
    return (
        output[None],
        grad_queries[None],
        grad_keys[None],
        grad_values[None],
        grad_lyric_keys[None],
        grad_lyric_values[None],
        q_total[0],
        k_total[0],
    )


def solution(mesh):
    split = P("song", "seq", None)
    return jax.shard_map(
        body,
        mesh=mesh,
        in_specs=(split, split, split, split, split, P(), P(), split, split, P("song")),
        out_specs=(split, split, split, split, split, split, P(), P()),
        check_vma=False,
    )
```

```python
import functools

import jax
import jax.numpy as jnp
from jax import lax
from jax.experimental import pallas as pl
from jax.experimental.pallas import tpu as pltpu
from jax.sharding import PartitionSpec as P

BLK = 128
TILES = 2
NORM_EPS = 1e-06
VMEM_LIMIT = 8 * 1024 * 1024
ATTENTION_VMEM_LIMIT = 24 * 1024 * 1024
PACK_VMEM_LIMIT = 60 * 1024 * 1024
VMEM = pl.BlockSpec(memory_space=pltpu.VMEM)
SMEM = pl.BlockSpec(memory_space=pltpu.SMEM)
HBM = pl.BlockSpec(memory_space=pltpu.HBM)
ANY = pl.BlockSpec(memory_space=pl.ANY)
GAIN_ROWS = 16
HEADS_PER_STEP = 4
CHUNKS = 2
ALIGN_ROWS = 32
SMALL = pl.CostEstimate(flops=1, bytes_accessed=1, transcendentals=0)


def dot(lhs, rhs, lhs_dim, rhs_dim):
    return lax.dot_general(
        lhs, rhs, (((lhs_dim,), (rhs_dim,)), ((), ())), preferred_element_type=jnp.float32
    )


def call(kernel, name, in_specs, out_specs, out_shape, limit=VMEM_LIMIT, cost=SMALL, **options):
    return pl.pallas_call(
        kernel,
        in_specs=in_specs,
        out_specs=out_specs,
        out_shape=out_shape,
        compiler_params=pltpu.CompilerParams(vmem_limit_bytes=limit),
        cost_estimate=cost,
        name=name,
        **options,
    )


def shape(rows, cols, dtype=jnp.bfloat16):
    return jax.ShapeDtypeStruct((rows, cols), dtype)


def half_of(ref, core):
    half = ref.shape[1] // 2
    return pl.ds(pl.multiple_of(core * half, half), half)


def chunk_of(ref, core, chunk):
    size = ref.shape[1] // 2 // CHUNKS
    return pl.ds(pl.multiple_of((core * CHUNKS + chunk) * size, size), size)


def chunk_cols(chunk, size):
    return slice(chunk * size, (chunk + 1) * size)


def split_rows(sums, cols):
    high = sums.astype(jnp.bfloat16).astype(jnp.float32)
    rest = sums - high
    middle = rest.astype(jnp.bfloat16).astype(jnp.float32)
    low = rest - middle
    empty = jnp.zeros((sums.shape[0], cols - 3 * sums.shape[1]), jnp.float32)
    rows = jnp.concatenate([high, middle, low, empty], axis=1)
    return jnp.concatenate([rows, jnp.zeros_like(rows)], axis=0).astype(jnp.bfloat16)


def joined_rows(rows, size):
    rows = rows.astype(jnp.float32)[0:8]
    return (rows[:, 2 * size : 3 * size] + rows[:, size : 2 * size]) + rows[:, 0:size]


def normed(raw, k_gain):
    raw = raw.astype(jnp.float32)
    inverse = lax.rsqrt(jnp.mean(raw * raw, axis=1, keepdims=True) + NORM_EPS)
    return (raw * inverse * k_gain).astype(jnp.bfloat16)


def norm_columns(out_ref, rows, raw, gain_ref):
    head_size = gain_ref.shape[1]
    for head in range(raw.shape[1] // head_size):
        cols = slice(head * head_size, (head + 1) * head_size)
        out_ref[rows, cols] = normed(raw[:, cols], gain_ref[1:2, :])


def through_norm(raw, grad, k_gain):
    raw = raw.astype(jnp.float32)
    inverse = lax.rsqrt(jnp.mean(raw * raw, axis=1, keepdims=True) + NORM_EPS)
    scaled = grad * k_gain
    return (
        inverse * scaled
        - raw * (inverse * inverse * inverse) * jnp.mean(scaled * raw, axis=1, keepdims=True)
    ).astype(jnp.bfloat16)


def pack_kernel(state_ref, align_ref, *refs):
    ins, (out_ref, sems) = refs[:-2], refs[-2:]
    start = 0
    copies = []
    for index, ref in enumerate(ins):
        rows = ref.shape[0]
        copies.append(
            pltpu.make_async_copy(
                ref.at[:, half_of(ref, 1 - state_ref[0])],
                out_ref.at[start : start + rows, :],
                sems.at[index],
            )
        )
        copies[-1].start()
        start += rows
    row = lax.broadcasted_iota(jnp.int32, (ALIGN_ROWS, out_ref.shape[1]), 0)
    tiles = jnp.zeros(row.shape, jnp.int32)
    for slot in range(TILES):
        tiles = jnp.where(row == slot, align_ref[slot], tiles)
    out_ref[start:, :] = tiles.astype(jnp.float32).astype(jnp.bfloat16)
    for copy in copies:
        copy.wait()


def pack(state, align, arrays):
    rows = sum(array.shape[0] for array in arrays) + ALIGN_ROWS
    return call(
        pack_kernel,
        "pack",
        [SMEM, SMEM] + [HBM] * len(arrays),
        VMEM,
        shape(rows, arrays[0].shape[1] // 2),
        limit=PACK_VMEM_LIMIT,
        scratch_shapes=[pltpu.SemaphoreType.DMA((len(arrays),))],
    )(state, align, *arrays)


def pair_kernel(chunk, state_ref, gain_ref, key_ref, value_ref, mate_ref, *refs):
    pair_ref = refs[-1]
    rows = key_ref.shape[0]
    first = mate_ref.shape[0] - ALIGN_ROWS - 2 * rows
    own = chunk_of(key_ref, state_ref[0], chunk)
    cols = chunk_cols(chunk, pair_ref.shape[1])
    norm_columns(pair_ref, slice(0, rows), key_ref[:, own], gain_ref)
    pair_ref[rows : 2 * rows, :] = value_ref[:, own]
    norm_columns(
        pair_ref, slice(2 * rows, 3 * rows), mate_ref[first : first + rows, cols], gain_ref
    )
    pair_ref[3 * rows :, :] = mate_ref[first + rows : first + 2 * rows, cols]


def pair_lyrics(state, chunk, gains, lyric_key, lyric_value, mate, after):
    rows, width = lyric_key.shape
    return call(
        functools.partial(pair_kernel, chunk),
        "pair_lyrics",
        [SMEM] + [VMEM] * 4 + [ANY] * len(after),
        VMEM,
        shape(4 * rows, width // 2 // CHUNKS),
    )(state, gains, lyric_key, lyric_value, mate, *after)


def edge_kernel(
    chunk, touching, leading, state_ref, gain_ref, key_ref, value_ref, mate_ref, *refs
):
    out_ref = refs[-1]
    frames = key_ref.shape[0]
    first = out_ref.shape[0] - 2 * frames
    if leading:
        out_ref[0:first, :] = refs[0][...]
    mine = state_ref[1] == touching
    own = chunk_of(key_ref, state_ref[0], chunk)
    cols = chunk_cols(chunk, out_ref.shape[1])
    keys = jnp.where(mine, key_ref[:, own], mate_ref[2 * frames : 3 * frames, cols])
    norm_columns(out_ref, slice(first, first + frames), keys, gain_ref)
    out_ref[first + frames :, :] = jnp.where(
        mine, value_ref[:, own], mate_ref[3 * frames : 4 * frames, cols]
    )


def edge(state, chunk, touching, gains, key, value, mate, lead, after):
    frames, width = key.shape
    rows = sum(array.shape[0] for array in lead) + 2 * frames
    return call(
        functools.partial(edge_kernel, chunk, touching, bool(lead)),
        "edge",
        [SMEM] + [VMEM] * (4 + len(lead)) + [ANY] * len(after),
        VMEM,
        shape(rows, width // 2 // CHUNKS),
    )(state, gains, key, value, mate, *lead, *after)


def prepare_kernel(state_ref, gain_ref, key_ref, mate_ref, *refs):
    out_ref = refs[-1]
    frames = key_ref.shape[0]
    own = half_of(key_ref, state_ref[0])
    norm_columns(out_ref, slice(0, frames), key_ref[:, own], gain_ref)
    norm_columns(
        out_ref, slice(frames, 2 * frames), mate_ref[2 * frames : 3 * frames, :], gain_ref
    )


def prepare_keys(state, gains, key, mate, after):
    frames, width = key.shape
    return call(
        prepare_kernel,
        "prepare_keys",
        [SMEM] + [VMEM] * 3 + [ANY] * len(after),
        VMEM,
        shape(2 * frames, width // 2),
    )(state, gains, key, mate, *after)


def attention_kernel(
    chunk, chained, waits, groups, head_size, score_scale, meta_ref, gain_ref, query_ref, grad_ref, value_ref, key_ref,
    mate_ref, one_ref, mid_ref, *refs
):
    frames = query_ref.shape[0]
    exchanged = len(groups) == 4
    inputs = 3 if exchanged else 1
    lyric_in, refs = refs[:inputs], refs[inputs:]
    earlier, refs = refs[:chained], refs[chained + waits :]
    window = one_ref.shape[0] - 2 * frames
    out_ref, grad_query_ref, to_mate_ref, key_grad_ref, value_grad_ref = refs[:5]
    to_one_ref, to_mid_ref, gain_grad_ref = refs[5:8]
    lyric_out, mask_ref = refs[8:-1], refs[-1]
    runs = [(index, run) for index, group in enumerate(groups) for run in group]
    main = 2 * frames + sum(run[2] for _, run in runs)
    lanes = 2 * frames
    align = mate_ref.shape[0] - ALIGN_ROWS
    touching = meta_ref[1] == 1

    size = out_ref.shape[1]
    gain_grad_ref[...] = earlier[0][...] if chained else jnp.zeros_like(gain_grad_ref)
    mate_tiles = mate_ref[align:, 0:frames].astype(jnp.float32).astype(jnp.int32)
    start = 0
    for number, (_, (_, _, rows)) in enumerate(runs):
        row = lax.broadcasted_iota(jnp.int32, (rows, lanes), 0) + meta_ref[7 + number]
        keep = jnp.zeros((rows, lanes), jnp.float32)
        for slot in range(TILES):
            tile = jnp.concatenate(
                [
                    jnp.full((1, frames), meta_ref[2 + slot], jnp.int32),
                    mate_tiles[slot : slot + 1],
                ],
                axis=1,
            )
            lower = tile * BLK
            upper = jnp.minimum(lower + BLK, meta_ref[4])
            inside = (row >= lower) & (row < upper) & (lower >= 0)
            keep = jnp.where(inside, 1.0, keep)
        mask_ref[start : start + rows, :] = keep
        start += rows
    lane = lax.broadcasted_iota(jnp.int32, (frames, lanes), 1)
    mask_ref[start : start + frames, :] = jnp.where(
        lane < frames, meta_ref[5], meta_ref[6]
    ).astype(jnp.float32)

    q_gain = gain_ref[0:1, :]
    k_gain = gain_ref[1:2, :]
    heads = size // head_size

    def one_head(head):
        cols = pl.ds(pl.multiple_of(head * head_size, head_size), head_size)
        half_cols = pl.ds(
            pl.multiple_of((chunk * heads + head) * head_size, head_size), head_size
        )
        own_cols = pl.ds(
            pl.multiple_of(
                ((meta_ref[0] * CHUNKS + chunk) * heads + head) * head_size, head_size
            ),
            head_size,
        )
        lyric = [ref[:, cols if exchanged else own_cols] for ref in lyric_in]
        if exchanged:
            lyric = [lyric[0], lyric[1], one_ref[0:window, cols], lyric[2]]
        one_rows, mid_rows = one_ref[window:, cols], mid_ref[:, cols]
        near_rows = jnp.where(touching, one_rows, mid_rows)
        far_rows = jnp.where(touching, mid_rows, one_rows)

        def from_mate(number):
            return mate_ref[number * frames : (number + 1) * frames, half_cols]

        query = jnp.concatenate([query_ref[:, own_cols], from_mate(0)], axis=0)
        query = query.astype(jnp.float32)
        cot = jnp.concatenate([grad_ref[:, own_cols], from_mate(1)], axis=0)
        key_low = jnp.concatenate(
            [key_ref[:, half_cols]]
            + [lyric[index][run[0] : run[0] + run[2]] for index, run in runs]
            + [near_rows[:frames], far_rows[:frames]],
            axis=0,
        )
        value = jnp.concatenate(
            [value_ref[:, own_cols], from_mate(3)]
            + [lyric[index][run[1] : run[1] + run[2]] for index, run in runs]
            + [near_rows[frames:], far_rows[frames:]],
            axis=0,
        )
        query_inv = lax.rsqrt(jnp.mean(query * query, axis=1, keepdims=True) + NORM_EPS)
        query_hat = query * query_inv
        query_low = (query_hat * (q_gain * score_scale)).astype(jnp.bfloat16)

        near, far = slice(main, main + frames), slice(main + frames, main + 2 * frames)

        def against(rows, columns):
            return jnp.concatenate(
                [
                    dot(rows[:main], columns, 1, 1),
                    jnp.concatenate(
                        [
                            dot(rows[near], columns[:frames], 1, 1),
                            dot(rows[far], columns[frames:], 1, 1),
                        ],
                        axis=1,
                    ),
                ],
                axis=0,
            )

        def over_keys(weights, rows):
            return dot(weights[:main], rows[:main], 0, 0) + jnp.concatenate(
                [
                    dot(weights[main:, :frames], rows[near], 0, 0),
                    dot(weights[main:, frames:], rows[far], 0, 0),
                ],
                axis=0,
            )

        def over_queries(weights, columns):
            return jnp.concatenate(
                [
                    dot(weights[:main], columns, 1, 0),
                    dot(weights[main:, :frames], columns[:frames], 1, 0),
                    dot(weights[main:, frames:], columns[frames:], 1, 0),
                ],
                axis=0,
            )

        exp_scores = jnp.exp(against(key_low, query_low))
        exp_scores = jnp.concatenate(
            [exp_scores[: 2 * frames], exp_scores[2 * frames :] * mask_ref[...]], axis=0
        )
        grad_prob = against(value, cot)
        prob = exp_scores * (1.0 / jnp.sum(exp_scores, axis=0, keepdims=True))
        prob_low = prob.astype(jnp.bfloat16)
        weighted = prob * grad_prob
        delta = jnp.sum(weighted, axis=0, keepdims=True)
        grad_score = (weighted - prob * delta).astype(jnp.bfloat16)
        output = over_keys(prob_low, value).astype(jnp.bfloat16)
        grad_low = over_keys(grad_score, key_low)
        grad_qn = grad_low * score_scale
        grad_keys = over_queries(grad_score, query_low)
        grad_values = over_queries(prob_low, cot)
        scaled = grad_qn * q_gain
        grad_query = (
            query_inv * scaled
            - query_hat
            * (query_inv * query_inv)
            * jnp.mean(scaled * query, axis=1, keepdims=True)
        ).astype(jnp.bfloat16)
        gain_grad_ref[0:1, :] += jnp.sum(grad_qn * query_hat, axis=0, keepdims=True)
        gain_grad_ref[1:2, :] += (
            jnp.sum(grad_low * query_low.astype(jnp.float32), axis=0, keepdims=True) / k_gain
        )

        out_ref[:, cols] = output[:frames]
        grad_query_ref[:, cols] = grad_query[:frames]
        to_mate_ref[0:frames, cols] = output[frames:]
        to_mate_ref[frames:, cols] = grad_query[frames:]
        key_grad_ref[:, cols] = grad_keys[: 2 * frames]
        value_grad_ref[:, cols] = grad_values[: 2 * frames]
        for grads, part in (
            (grad_keys.astype(jnp.bfloat16), 0),
            (grad_values.astype(jnp.bfloat16), frames),
        ):
            to_one_ref[window + part : window + part + frames, cols] = jnp.where(
                touching, grads[near], grads[far]
            )
            to_mid_ref[part : part + frames, cols] = jnp.where(touching, grads[far], grads[near])
        if exchanged:
            held_ref, two_ref, to_two_ref = lyric_out
            outs = (held_ref, two_ref, to_one_ref, to_two_ref)
        else:
            outs = lyric_out
        start = 2 * frames
        for index, (key_row, value_row, rows) in runs:
            part = slice(start, start + rows)
            outs[index][key_row : key_row + rows, cols] = grad_keys[part].astype(jnp.bfloat16)
            outs[index][value_row : value_row + rows, cols] = grad_values[part].astype(
                jnp.bfloat16
            )
            start += rows

    @pl.loop(0, heads // HEADS_PER_STEP)
    def _(step):
        for number in range(HEADS_PER_STEP):
            one_head(step * HEADS_PER_STEP + number)


def attention(
    chunk, meta, gains, query, cot, value, key, mate, one, mid, lyrics, groups, earlier, after
):
    frames, width = query.shape
    head_size = gains.shape[1]
    size = width // 2 // CHUNKS
    lyric_rows = sum(run[2] for group in groups for run in group)
    key_rows = 3 * frames + lyric_rows
    bf16, f32 = jnp.bfloat16, jnp.float32
    slot = sum(2 * run[2] for run in groups[0])
    out_shape = [shape(frames, size)] * 2
    out_shape += [shape(2 * frames, size, dtype) for dtype in (bf16, f32, f32)]
    out_shape += [shape(one.shape[0], size), shape(2 * frames, size), shape(8, head_size, f32)]
    out_shape += [shape(slot, size)] * len(lyrics)
    return call(
        functools.partial(
            attention_kernel, chunk, len(earlier), len(after), groups, head_size, head_size ** (-0.5)
        ),
        "attention",
        [SMEM] + [VMEM] * (8 + len(lyrics) + len(earlier)) + [ANY] * len(after),
        [VMEM] * len(out_shape),
        out_shape,
        limit=ATTENTION_VMEM_LIMIT,
        cost=pl.CostEstimate(
            flops=24 * key_rows * frames * size,
            bytes_accessed=8 * 1024 * 1024,
            transcendentals=2 * key_rows * frames * (size // head_size),
        ),
        scratch_shapes=[pltpu.VMEM((frames + lyric_rows, 2 * frames), f32)],
    )(meta, gains, query, cot, value, key, mate, one, mid, *lyrics, *earlier, *after)


def finish_audio_kernel(state_ref, gain_ref, raw_ref, mate_ref, *refs):
    chunk_refs, refs = refs[: 7 * CHUNKS], refs[7 * CHUNKS :]
    *lyric, out, query_out, key_out, value_out, to_mate_ref, key_ref, value_ref, sems = refs
    head_size = gain_ref.shape[1]
    k_gain = gain_ref[1:2, :]
    frames, half = key_ref.shape
    size = half // CHUNKS
    own, mate = slice(0, frames), slice(frames, 2 * frames)
    touching = state_ref[1] == 1
    copies = []
    for chunk in range(CHUNKS):
        out_own_ref, query_own_ref, ready_ref = chunk_refs[7 * chunk : 7 * chunk + 3]
        for source, target in ((out_own_ref, out), (query_own_ref, query_out)):
            copies.append(
                pltpu.make_async_copy(
                    source,
                    target.at[:, chunk_of(target, state_ref[0], chunk)],
                    sems.at[len(copies)],
                )
            )
            copies[-1].start()
        to_mate_ref[0 : 2 * frames, chunk_cols(chunk, size)] = ready_ref[...]
    for ref in lyric:
        to_mate_ref[4 * frames :, :] = ref[...]
    raw_keys = raw_ref[:, half_of(raw_ref, state_ref[0])]
    for head in range(half // head_size):
        cols = slice(head * head_size, (head + 1) * head_size)
        chunk = head * head_size // size
        part = slice(head * head_size - chunk * size, (head + 1) * head_size - chunk * size)
        key_grad_ref, value_grad_ref, one_ref, mid_ref = chunk_refs[7 * chunk + 3 : 7 * chunk + 7]
        one = one_ref[one_ref.shape[0] - 2 * frames :, part].astype(jnp.float32)
        mid = mid_ref[:, part].astype(jnp.float32)
        for_own = jnp.where(touching, one, mid)
        for_mate = jnp.where(touching, mid, one)
        key_ref[:, cols] = through_norm(
            raw_keys[:, cols], key_grad_ref[own, part] + for_own[:frames], k_gain
        )
        value_ref[:, cols] = (value_grad_ref[own, part] + for_own[frames:]).astype(jnp.bfloat16)
        to_mate_ref[2 * frames : 3 * frames, cols] = through_norm(
            mate_ref[2 * frames : 3 * frames, cols],
            key_grad_ref[mate, part] + for_mate[:frames],
            k_gain,
        )
        to_mate_ref[3 * frames : 4 * frames, cols] = (
            value_grad_ref[mate, part] + for_mate[frames:]
        ).astype(jnp.bfloat16)
    for source, target in ((key_ref, key_out), (value_ref, value_out)):
        copies.append(
            pltpu.make_async_copy(
                source, target.at[:, half_of(target, state_ref[0])], sems.at[len(copies)]
            )
        )
        copies[-1].start()
    for copy in copies:
        copy.wait()


def finish_audio(state, gains, raw, mate, chunks, lyric):
    frames, width = raw.shape
    half = width // 2
    rows = 4 * frames + sum(array.shape[0] for array in lyric)
    return call(
        finish_audio_kernel,
        "finish_audio",
        [SMEM] + [VMEM] * (3 + len(chunks) + len(lyric)),
        [HBM] * 4 + [VMEM],
        [shape(frames, width)] * 4 + [shape(rows, half)],
        scratch_shapes=[pltpu.VMEM((frames, half), jnp.bfloat16)] * 2
        + [pltpu.SemaphoreType.DMA((2 * CHUNKS + 2,))],
    )(state, gains, raw, mate, *chunks, *lyric)


def relay_kernel(part_ref, arrived_ref, *refs):
    out_ref = refs[0] if len(refs) == 1 else refs[-2]
    out_ref[...] = (
        part_ref[...].astype(jnp.float32) + arrived_ref[...].astype(jnp.float32)
    ).astype(jnp.bfloat16)


def relay(part, arrived):
    return call(relay_kernel, "relay", [VMEM] * 2, VMEM, shape(*part.shape))(part, arrived)


def last_relay(part, arrived, later, after):
    return call(
        relay_kernel,
        "relay",
        [VMEM] * 2 + [ANY] * (1 + len(after)),
        [VMEM, ANY],
        [shape(*part.shape), shape(*later.shape)],
        input_output_aliases={2: 1},
    )(part, arrived, later, *after)


def finish_lyric_kernel(
    state_ref, gain_ref, raw_ref, mate_ref, sum_ref, *refs
):
    chunk_refs, (own_ref, to_mate_ref) = refs[:-2], refs[-2:]
    rows = raw_ref.shape[0]
    head_size = gain_ref.shape[1]
    k_gain = gain_ref[1:2, :]
    size = chunk_refs[0].shape[1]
    first = mate_ref.shape[0] - ALIGN_ROWS - 2 * rows
    to_mate_ref[2 * rows :, :] = split_rows(sum_ref[...], to_mate_ref.shape[1])
    raw_keys = raw_ref[:, half_of(raw_ref, state_ref[0])]
    for head in range(own_ref.shape[1] // head_size):
        cols = slice(head * head_size, (head + 1) * head_size)
        chunk = head * head_size // size
        part = slice(head * head_size - chunk * size, (head + 1) * head_size - chunk * size)
        total = chunk_refs[3 * chunk][:, part].astype(jnp.float32)
        for ref in chunk_refs[3 * chunk + 1 : 3 * chunk + 3]:
            total = total + ref[0 : 4 * rows, part].astype(jnp.float32)
        mate_keys = mate_ref[first : first + rows, cols]
        for ref, base, raw in (
            (own_ref, 0, raw_keys[:, cols]),
            (to_mate_ref, 2 * rows, mate_keys),
        ):
            ref[0:rows, cols] = through_norm(raw, total[base : base + rows], k_gain)
            ref[rows : 2 * rows, cols] = total[base + rows : base + 2 * rows].astype(jnp.bfloat16)


def finish_lyric(state, gains, raw, mate, total, chunks):
    rows, width = raw.shape
    half = width // 2
    return call(
        finish_lyric_kernel,
        "finish_lyric",
        [SMEM] + [VMEM] * (4 + len(chunks)),
        [VMEM] * 2,
        [shape(2 * rows, half), shape(2 * rows + GAIN_ROWS, half)],
    )(state, gains, raw, mate, total, *chunks)


def join_kernel(count, state_ref, gain_ref, own_ref, mate_ref, *refs):
    outs, (q_total_ref, k_total_ref, sems) = refs[count:-3], refs[-3:]
    frames = outs[0].shape[0]
    rows = own_ref.shape[0] // 2
    pieces = [
        (mate_ref.at[index * frames : (index + 1) * frames, :], out, 1 - state_ref[0])
        for index, out in enumerate(outs[:count])
    ]
    for ref, first, core in ((own_ref, 0, state_ref[0]), (mate_ref, count * frames, 1 - state_ref[0])):
        for index, out in enumerate(outs[count:]):
            start = first + index * rows
            pieces.append((ref.at[start : start + rows, :], out, core))
    copies = [
        pltpu.make_async_copy(source, out.at[:, half_of(out, core)], sems.at[index])
        for index, (source, out, core) in enumerate(pieces)
    ]
    for copy in copies:
        copy.start()
    sums = mate_ref[mate_ref.shape[0] - GAIN_ROWS :, :]
    total = gain_ref[...] + joined_rows(sums, gain_ref.shape[1])
    q_total_ref[...] = total[0:1]
    k_total_ref[...] = total[1:2]
    for copy in copies:
        copy.wait()


def join(state, gain, arrays, own, mate):
    rows, half = own.shape
    count = len(arrays)
    return call(
        functools.partial(join_kernel, count),
        "join",
        [SMEM] + [VMEM] * 3 + [HBM] * count,
        [HBM] * (count + 2) + [VMEM] * 2,
        [shape(*array.shape) for array in arrays]
        + [shape(rows // 2, 2 * half)] * 2
        + [shape(1, gain.shape[1], jnp.float32)] * 2,
        input_output_aliases={4 + i: i for i in range(count)},
        scratch_shapes=[pltpu.SemaphoreType.DMA((count + 4,))],
    )(state, gain, own, mate, *arrays)


def fill_kernel(count, state_ref, mate_ref, *refs):
    outs, sems = refs[count:-1], refs[-1]
    frames = outs[0].shape[0]
    copies = [
        pltpu.make_async_copy(
            mate_ref.at[index * frames : (index + 1) * frames, :],
            out.at[:, half_of(out, 1 - state_ref[0])],
            sems.at[index],
        )
        for index, out in enumerate(outs)
    ]
    for copy in copies:
        copy.start()
    for copy in copies:
        copy.wait()


def fill_other(state, arrays, mate):
    count = len(arrays)
    return call(
        functools.partial(fill_kernel, count),
        "fill_other",
        [SMEM, VMEM] + [HBM] * count,
        [HBM] * count,
        [shape(*array.shape) for array in arrays],
        input_output_aliases={2 + i: i for i in range(count)},
        scratch_shapes=[pltpu.SemaphoreType.DMA((count,))],
    )(state, mate, *arrays)


def norm_rows_kernel(gain_ref, raw_ref, out_ref):
    norm_columns(out_ref, slice(0, raw_ref.shape[0]), raw_ref[...], gain_ref)


def norm_rows(gains, raw):
    return pl.pallas_call(
        norm_rows_kernel,
        out_shape=jax.ShapeDtypeStruct(raw.shape, raw.dtype),
        name="norm_rows",
    )(gains, raw)


def norm_lyric_kernel(head_size, gain_ref, raw_ref, grad_ref, out_ref):
    for head in range(raw_ref.shape[1] // head_size):
        cols = slice(head * head_size, (head + 1) * head_size)
        out_ref[:, cols] = through_norm(raw_ref[:, cols], grad_ref[:, cols], gain_ref[1:2, :])


def norm_lyric(gains, raw, grad):
    return pl.pallas_call(
        functools.partial(norm_lyric_kernel, gains.shape[1]),
        out_shape=jax.ShapeDtypeStruct(raw.shape, jnp.bfloat16),
        name="norm_lyric",
    )(gains, raw, grad)


def sum_over(total, axis, bits):
    count = lax.axis_size(axis)
    for bit in bits:
        total = total + lax.ppermute(total, axis, [(i, i ^ bit) for i in range(count)])
    return total


def bits_of(count):
    return [1 << bit for bit in range(count.bit_length() - 1)]


def body(
    queries, keys, values, lyric_keys, lyric_values, q_gain, k_gain, cotangent, alignment, lyric_len
):
    frames = queries.shape[1]
    lyric_local, width = lyric_keys.shape[1:]
    count = lax.axis_size("seq")
    songs = lax.axis_size("song")
    me = lax.axis_index("seq")
    core = me % 2
    chips = count // 2
    chip = me // 2
    touching = (chip % 2) ^ core
    state = jnp.stack([core, touching]).astype(jnp.int32)
    gains = jnp.stack([q_gain, k_gain])

    swap = [(i, i ^ 1) for i in range(count)]
    partners = [(a, a ^ 1) for a in range(chips)]
    across = [(a, a ^ 2) for a in range(chips)]
    between = [(a, a + 1) for a in range(1, chips - 1, 2)]
    between += [(b, a) for a, b in between]

    def hop(block, moves):
        pairs = [(2 * a + c, 2 * b + c) for a, b in moves for c in (0, 1)]
        return lax.ppermute(block, "seq", pairs)

    hops = chips == 4 and lyric_local % 16 == 0
    total_rows = lyric_local * count
    if hops:
        run = ((0, lyric_local, lyric_local), (2 * lyric_local, 3 * lyric_local, lyric_local))
        groups = (run,) * 4
        owners = [chip, chip ^ 2, chip ^ 1, chip ^ 3]
        first_rows = []
        for owner in owners:
            first_rows += [
                (2 * owner + core) * lyric_local,
                (2 * owner + 1 - core) * lyric_local,
            ]
    else:
        gathered = jnp.concatenate(
            [
                lax.all_gather(
                    norm_rows(gains, lyric_keys[0]), "seq", axis=0, tiled=True
                ),
                lax.all_gather(lyric_values[0], "seq", axis=0, tiled=True),
            ],
            axis=0,
        )
        groups = (((0, total_rows, total_rows),),)
        first_rows = [0]
    has_left, has_right = chip > 0, chip < chips - 1
    has_near = jnp.where(core == 0, has_left, has_right)
    has_far = jnp.where(core == 0, has_right, has_left)
    meta = jnp.stack(
        [
            jnp.asarray(value, jnp.int32)
            for value in [core, touching]
            + [alignment[0, 0, slot] for slot in range(TILES)]
            + [lyric_len[0], has_near, has_far]
            + first_rows
        ]
    )

    to_mate = pack(
        state,
        alignment[0, 0],
        [queries[0], cotangent[0], keys[0], values[0]]
        + ([lyric_keys[0], lyric_values[0]] if hops else []),
    )
    mate = lax.ppermute(to_mate, "seq", swap)
    chunks, lyric_chunks, earlier, relayed, sent = [], [], [], [], []
    after = []
    for chunk in range(CHUNKS):
        before, one_before = after, lyrics[2:] if chunk else []
        if hops:
            pair = pair_lyrics(state, chunk, gains, lyric_keys[0], lyric_values[0], mate, before)
            two = hop(pair, across)
            lyrics = [pair, two, hop(two, partners)]
            lead, after = [pair], [two]
        else:
            lyrics, lead = [gathered], []
        one = hop(edge(state, chunk, 1, gains, keys[0], values[0], mate, lead, one_before), partners)
        mid = hop(edge(state, chunk, 0, gains, keys[0], values[0], mate, [], after), between)
        if not chunk:
            key_low = prepare_keys(state, gains, keys[0], mate, after)
        results = attention(
            chunk, meta, gains, queries[0], cotangent[0], values[0], key_low, mate, one, mid,
            lyrics, groups, earlier, relayed,
        )
        to_one, to_mid, gain_part, *parts = results[5:]
        earlier = [gain_part]
        mid_back = hop(to_mid, between)
        if hops:
            held, for_two, to_two = parts
            arrived = hop(to_two, partners)
            if chunk < CHUNKS - 1:
                relayed = [relay(for_two, arrived)]
                to_two = relayed[0]
            else:
                gain_total = sum_over(gain_part, "song", bits_of(songs))
                to_two, to_one = last_relay(for_two, arrived, to_one, [*sent, gain_total])
            two_back, one_back = hop(to_two, across), hop(to_one, partners)
            lyric_chunks += [held, one_back, two_back]
            sent = [*sent, mid_back, one_back, two_back]
        else:
            one_back = hop(to_one, partners)
            lyric_chunks += parts
        chunks += [*results[:5], one_back, mid_back]

    to_mate = []
    if hops:
        gain_total = sum_over(gain_total, "seq", [2, 4])
        own_half, part_to_mate = finish_lyric(
            state, gains, lyric_keys[0], mate, gain_total, lyric_chunks
        )
        to_mate = [part_to_mate]
    *filled, to_mate = finish_audio(state, gains, keys[0], mate, chunks, to_mate)
    from_mate = lax.ppermute(to_mate, "seq", swap)
    if hops:
        *filled, grad_lyric_keys, grad_lyric_values, q_total, k_total = join(
            state, gain_total, filled, own_half, from_mate
        )
    else:
        filled = fill_other(state, filled, from_mate)
        gain_total = lax.psum(gain_part, ("song", "seq"))
        q_total, k_total = gain_total[0:1], gain_total[1:2]
        spread = lax.dynamic_update_slice(
            jnp.zeros((2 * total_rows, width), jnp.float32),
            jnp.concatenate(lyric_chunks, axis=1).astype(jnp.float32),
            (0, core * (width // 2)),
        )
        lyric_key_sum, grad_lyric_values = [
            lax.psum_scatter(part, "seq", scatter_dimension=0, tiled=True)
            for part in (spread[:total_rows], spread[total_rows:])
        ]
        grad_lyric_keys = norm_lyric(gains, lyric_keys[0], lyric_key_sum)
        grad_lyric_values = grad_lyric_values.astype(jnp.bfloat16)
    output, grad_queries, grad_keys, grad_values = filled
    return (
        output[None],
        grad_queries[None],
        grad_keys[None],
        grad_values[None],
        grad_lyric_keys[None],
        grad_lyric_values[None],
        q_total[0],
        k_total[0],
    )


def solution(mesh):
    split = P("song", "seq", None)
    return jax.shard_map(
        body,
        mesh=mesh,
        in_specs=(split, split, split, split, split, P(), P(), split, split, P("song")),
        out_specs=(split, split, split, split, split, split, P(), P()),
        check_vma=False,
    )
```

```python
import functools

import jax
import jax.numpy as jnp
from jax import lax
from jax.experimental import pallas as pl
from jax.experimental.pallas import tpu as pltpu
from jax.sharding import PartitionSpec as P

BLK = 128
TILES = 2
NORM_EPS = 1e-06
VMEM_LIMIT = 8 * 1024 * 1024
ATTENTION_VMEM_LIMIT = 24 * 1024 * 1024
PACK_VMEM_LIMIT = 60 * 1024 * 1024
VMEM = pl.BlockSpec(memory_space=pltpu.VMEM)
SMEM = pl.BlockSpec(memory_space=pltpu.SMEM)
HBM = pl.BlockSpec(memory_space=pltpu.HBM)
ANY = pl.BlockSpec(memory_space=pl.ANY)
GAIN_ROWS = 16
HEADS_PER_STEP = 4
CHUNKS = 2
ALIGN_ROWS = 32
SMALL = pl.CostEstimate(flops=1, bytes_accessed=1, transcendentals=0)


def dot(lhs, rhs, lhs_dim, rhs_dim):
    return lax.dot_general(
        lhs, rhs, (((lhs_dim,), (rhs_dim,)), ((), ())), preferred_element_type=jnp.float32
    )


def call(kernel, name, in_specs, out_specs, out_shape, limit=VMEM_LIMIT, cost=SMALL, **options):
    return pl.pallas_call(
        kernel,
        in_specs=in_specs,
        out_specs=out_specs,
        out_shape=out_shape,
        compiler_params=pltpu.CompilerParams(vmem_limit_bytes=limit),
        cost_estimate=cost,
        name=name,
        **options,
    )


def shape(rows, cols, dtype=jnp.bfloat16):
    return jax.ShapeDtypeStruct((rows, cols), dtype)


def half_of(ref, core):
    half = ref.shape[1] // 2
    return pl.ds(pl.multiple_of(core * half, half), half)


def chunk_of(ref, core, chunk):
    size = ref.shape[1] // 2 // CHUNKS
    return pl.ds(pl.multiple_of((core * CHUNKS + chunk) * size, size), size)


def chunk_cols(chunk, size):
    return slice(chunk * size, (chunk + 1) * size)


def split_rows(sums, cols):
    high = sums.astype(jnp.bfloat16).astype(jnp.float32)
    rest = sums - high
    middle = rest.astype(jnp.bfloat16).astype(jnp.float32)
    low = rest - middle
    empty = jnp.zeros((sums.shape[0], cols - 3 * sums.shape[1]), jnp.float32)
    rows = jnp.concatenate([high, middle, low, empty], axis=1)
    return jnp.concatenate([rows, jnp.zeros_like(rows)], axis=0).astype(jnp.bfloat16)


def joined_rows(rows, size):
    rows = rows.astype(jnp.float32)[0:8]
    return (rows[:, 2 * size : 3 * size] + rows[:, size : 2 * size]) + rows[:, 0:size]


def normed(raw, k_gain):
    raw = raw.astype(jnp.float32)
    inverse = lax.rsqrt(jnp.mean(raw * raw, axis=1, keepdims=True) + NORM_EPS)
    return (raw * inverse * k_gain).astype(jnp.bfloat16)


def norm_columns(out_ref, rows, raw, gain_ref):
    head_size = gain_ref.shape[1]
    for head in range(raw.shape[1] // head_size):
        cols = slice(head * head_size, (head + 1) * head_size)
        out_ref[rows, cols] = normed(raw[:, cols], gain_ref[1:2, :])


def through_norm(raw, grad, k_gain):
    raw = raw.astype(jnp.float32)
    inverse = lax.rsqrt(jnp.mean(raw * raw, axis=1, keepdims=True) + NORM_EPS)
    scaled = grad * k_gain
    return (
        inverse * scaled
        - raw * (inverse * inverse * inverse) * jnp.mean(scaled * raw, axis=1, keepdims=True)
    ).astype(jnp.bfloat16)


def pack_kernel(state_ref, align_ref, *refs):
    ins, (out_ref, sems) = refs[:-2], refs[-2:]
    start = 0
    copies = []
    for index, ref in enumerate(ins):
        rows = ref.shape[0]
        copies.append(
            pltpu.make_async_copy(
                ref.at[:, half_of(ref, 1 - state_ref[0])],
                out_ref.at[start : start + rows, :],
                sems.at[index],
            )
        )
        copies[-1].start()
        start += rows
    row = lax.broadcasted_iota(jnp.int32, (ALIGN_ROWS, out_ref.shape[1]), 0)
    tiles = jnp.zeros(row.shape, jnp.int32)
    for slot in range(TILES):
        tiles = jnp.where(row == slot, align_ref[slot], tiles)
    out_ref[start:, :] = tiles.astype(jnp.float32).astype(jnp.bfloat16)
    for copy in copies:
        copy.wait()


def pack(state, align, arrays):
    rows = sum(array.shape[0] for array in arrays) + ALIGN_ROWS
    return call(
        pack_kernel,
        "pack",
        [SMEM, SMEM] + [HBM] * len(arrays),
        VMEM,
        shape(rows, arrays[0].shape[1] // 2),
        limit=PACK_VMEM_LIMIT,
        scratch_shapes=[pltpu.SemaphoreType.DMA((len(arrays),))],
    )(state, align, *arrays)


def pair_kernel(chunk, state_ref, gain_ref, key_ref, value_ref, mate_ref, *refs):
    pair_ref = refs[-1]
    rows = key_ref.shape[0]
    first = mate_ref.shape[0] - ALIGN_ROWS - 2 * rows
    own = chunk_of(key_ref, state_ref[0], chunk)
    cols = chunk_cols(chunk, pair_ref.shape[1])
    norm_columns(pair_ref, slice(0, rows), key_ref[:, own], gain_ref)
    pair_ref[rows : 2 * rows, :] = value_ref[:, own]
    norm_columns(
        pair_ref, slice(2 * rows, 3 * rows), mate_ref[first : first + rows, cols], gain_ref
    )
    pair_ref[3 * rows :, :] = mate_ref[first + rows : first + 2 * rows, cols]


def pair_lyrics(state, chunk, gains, lyric_key, lyric_value, mate, after):
    rows, width = lyric_key.shape
    return call(
        functools.partial(pair_kernel, chunk),
        "pair_lyrics",
        [SMEM] + [VMEM] * 4 + [ANY] * len(after),
        VMEM,
        shape(4 * rows, width // 2 // CHUNKS),
    )(state, gains, lyric_key, lyric_value, mate, *after)


def edge_kernel(
    chunk, touching, leading, state_ref, gain_ref, key_ref, value_ref, mate_ref, *refs
):
    out_ref = refs[-1]
    frames = key_ref.shape[0]
    first = out_ref.shape[0] - 2 * frames
    if leading:
        out_ref[0:first, :] = refs[0][...]
    mine = state_ref[1] == touching
    own = chunk_of(key_ref, state_ref[0], chunk)
    cols = chunk_cols(chunk, out_ref.shape[1])
    keys = jnp.where(mine, key_ref[:, own], mate_ref[2 * frames : 3 * frames, cols])
    norm_columns(out_ref, slice(first, first + frames), keys, gain_ref)
    out_ref[first + frames :, :] = jnp.where(
        mine, value_ref[:, own], mate_ref[3 * frames : 4 * frames, cols]
    )


def edge(state, chunk, touching, gains, key, value, mate, lead, after):
    frames, width = key.shape
    rows = sum(array.shape[0] for array in lead) + 2 * frames
    return call(
        functools.partial(edge_kernel, chunk, touching, bool(lead)),
        "edge",
        [SMEM] + [VMEM] * (4 + len(lead)) + [ANY] * len(after),
        VMEM,
        shape(rows, width // 2 // CHUNKS),
    )(state, gains, key, value, mate, *lead, *after)


def prepare_kernel(state_ref, gain_ref, key_ref, mate_ref, *refs):
    out_ref = refs[-1]
    frames = key_ref.shape[0]
    own = half_of(key_ref, state_ref[0])
    norm_columns(out_ref, slice(0, frames), key_ref[:, own], gain_ref)
    norm_columns(
        out_ref, slice(frames, 2 * frames), mate_ref[2 * frames : 3 * frames, :], gain_ref
    )


def prepare_keys(state, gains, key, mate, after):
    frames, width = key.shape
    return call(
        prepare_kernel,
        "prepare_keys",
        [SMEM] + [VMEM] * 3 + [ANY] * len(after),
        VMEM,
        shape(2 * frames, width // 2),
    )(state, gains, key, mate, *after)


def attention_kernel(
    chunk, chained, waits, groups, head_size, score_scale, meta_ref, gain_ref, query_ref, grad_ref, value_ref, key_ref,
    mate_ref, one_ref, mid_ref, *refs
):
    frames = query_ref.shape[0]
    exchanged = len(groups) == 4
    inputs = 3 if exchanged else 1
    lyric_in, refs = refs[:inputs], refs[inputs:]
    earlier, refs = refs[:chained], refs[chained + waits :]
    window = one_ref.shape[0] - 2 * frames
    out_ref, grad_query_ref, to_mate_ref, key_grad_ref, value_grad_ref = refs[:5]
    to_one_ref, to_mid_ref, gain_grad_ref = refs[5:8]
    lyric_out, mask_ref = refs[8:-1], refs[-1]
    runs = [(index, run) for index, group in enumerate(groups) for run in group]
    main = 2 * frames + sum(run[2] for _, run in runs)
    lanes = 2 * frames
    align = mate_ref.shape[0] - ALIGN_ROWS
    touching = meta_ref[1] == 1

    size = out_ref.shape[1]
    gain_grad_ref[...] = earlier[0][...] if chained else jnp.zeros_like(gain_grad_ref)
    mate_tiles = mate_ref[align:, 0:frames].astype(jnp.float32).astype(jnp.int32)
    start = 0
    for number, (_, (_, _, rows)) in enumerate(runs):
        row = lax.broadcasted_iota(jnp.int32, (rows, lanes), 0) + meta_ref[7 + number]
        keep = jnp.zeros((rows, lanes), jnp.float32)
        for slot in range(TILES):
            tile = jnp.concatenate(
                [
                    jnp.full((1, frames), meta_ref[2 + slot], jnp.int32),
                    mate_tiles[slot : slot + 1],
                ],
                axis=1,
            )
            lower = tile * BLK
            upper = jnp.minimum(lower + BLK, meta_ref[4])
            inside = (row >= lower) & (row < upper) & (lower >= 0)
            keep = jnp.where(inside, 1.0, keep)
        mask_ref[start : start + rows, :] = keep
        start += rows
    lane = lax.broadcasted_iota(jnp.int32, (frames, lanes), 1)
    mask_ref[start : start + frames, :] = jnp.where(
        lane < frames, meta_ref[5], meta_ref[6]
    ).astype(jnp.float32)

    q_gain = gain_ref[0:1, :]
    k_gain = gain_ref[1:2, :]
    heads = size // head_size

    def one_head(head):
        cols = pl.ds(pl.multiple_of(head * head_size, head_size), head_size)
        half_cols = pl.ds(
            pl.multiple_of((chunk * heads + head) * head_size, head_size), head_size
        )
        own_cols = pl.ds(
            pl.multiple_of(
                ((meta_ref[0] * CHUNKS + chunk) * heads + head) * head_size, head_size
            ),
            head_size,
        )
        lyric = [ref[:, cols if exchanged else own_cols] for ref in lyric_in]
        if exchanged:
            lyric = [lyric[0], lyric[1], one_ref[0:window, cols], lyric[2]]
        one_rows, mid_rows = one_ref[window:, cols], mid_ref[:, cols]
        near_rows = jnp.where(touching, one_rows, mid_rows)
        far_rows = jnp.where(touching, mid_rows, one_rows)

        def from_mate(number):
            return mate_ref[number * frames : (number + 1) * frames, half_cols]

        query = jnp.concatenate([query_ref[:, own_cols], from_mate(0)], axis=0)
        query = query.astype(jnp.float32)
        cot = jnp.concatenate([grad_ref[:, own_cols], from_mate(1)], axis=0)
        key_low = jnp.concatenate(
            [key_ref[:, half_cols]]
            + [lyric[index][run[0] : run[0] + run[2]] for index, run in runs]
            + [near_rows[:frames], far_rows[:frames]],
            axis=0,
        )
        value = jnp.concatenate(
            [value_ref[:, own_cols], from_mate(3)]
            + [lyric[index][run[1] : run[1] + run[2]] for index, run in runs]
            + [near_rows[frames:], far_rows[frames:]],
            axis=0,
        )
        query_inv = lax.rsqrt(jnp.mean(query * query, axis=1, keepdims=True) + NORM_EPS)
        query_hat = query * query_inv
        query_low = (query_hat * (q_gain * score_scale)).astype(jnp.bfloat16)

        near, far = slice(main, main + frames), slice(main + frames, main + 2 * frames)

        def against(rows, columns):
            return jnp.concatenate(
                [
                    dot(rows[:main], columns, 1, 1),
                    jnp.concatenate(
                        [
                            dot(rows[near], columns[:frames], 1, 1),
                            dot(rows[far], columns[frames:], 1, 1),
                        ],
                        axis=1,
                    ),
                ],
                axis=0,
            )

        def over_keys(weights, rows):
            return dot(weights[:main], rows[:main], 0, 0) + jnp.concatenate(
                [
                    dot(weights[main:, :frames], rows[near], 0, 0),
                    dot(weights[main:, frames:], rows[far], 0, 0),
                ],
                axis=0,
            )

        def over_queries(weights, columns):
            return jnp.concatenate(
                [
                    dot(weights[:main], columns, 1, 0),
                    dot(weights[main:, :frames], columns[:frames], 1, 0),
                    dot(weights[main:, frames:], columns[frames:], 1, 0),
                ],
                axis=0,
            )

        exp_scores = jnp.exp(against(key_low, query_low))
        exp_scores = jnp.concatenate(
            [exp_scores[: 2 * frames], exp_scores[2 * frames :] * mask_ref[...]], axis=0
        )
        grad_prob = against(value, cot)
        prob = exp_scores * (1.0 / jnp.sum(exp_scores, axis=0, keepdims=True))
        prob_low = prob.astype(jnp.bfloat16)
        weighted = prob * grad_prob
        delta = jnp.sum(weighted, axis=0, keepdims=True)
        grad_score = (weighted - prob * delta).astype(jnp.bfloat16)
        output = over_keys(prob_low, value).astype(jnp.bfloat16)
        grad_low = over_keys(grad_score, key_low)
        grad_qn = grad_low * score_scale
        grad_keys = over_queries(grad_score, query_low)
        grad_values = over_queries(prob_low, cot)
        scaled = grad_qn * q_gain
        grad_query = (
            query_inv * scaled
            - query_hat
            * (query_inv * query_inv)
            * jnp.mean(scaled * query, axis=1, keepdims=True)
        ).astype(jnp.bfloat16)
        gain_grad_ref[0:1, :] += jnp.sum(grad_qn * query_hat, axis=0, keepdims=True)
        gain_grad_ref[1:2, :] += (
            jnp.sum(grad_low * query_low.astype(jnp.float32), axis=0, keepdims=True) / k_gain
        )

        out_ref[:, cols] = output[:frames]
        grad_query_ref[:, cols] = grad_query[:frames]
        to_mate_ref[0:frames, cols] = output[frames:]
        to_mate_ref[frames:, cols] = grad_query[frames:]
        key_grad_ref[:, cols] = grad_keys[: 2 * frames]
        value_grad_ref[:, cols] = grad_values[: 2 * frames]
        for grads, part in (
            (grad_keys.astype(jnp.bfloat16), 0),
            (grad_values.astype(jnp.bfloat16), frames),
        ):
            to_one_ref[window + part : window + part + frames, cols] = jnp.where(
                touching, grads[near], grads[far]
            )
            to_mid_ref[part : part + frames, cols] = jnp.where(touching, grads[far], grads[near])
        if exchanged:
            held_ref, two_ref, to_two_ref = lyric_out
            outs = (held_ref, two_ref, to_one_ref, to_two_ref)
        else:
            outs = lyric_out
        start = 2 * frames
        for index, (key_row, value_row, rows) in runs:
            part = slice(start, start + rows)
            outs[index][key_row : key_row + rows, cols] = grad_keys[part].astype(jnp.bfloat16)
            outs[index][value_row : value_row + rows, cols] = grad_values[part].astype(
                jnp.bfloat16
            )
            start += rows

    @pl.loop(0, heads // HEADS_PER_STEP)
    def _(step):
        for number in range(HEADS_PER_STEP):
            one_head(step * HEADS_PER_STEP + number)


def attention(
    chunk, meta, gains, query, cot, value, key, mate, one, mid, lyrics, groups, earlier, after
):
    frames, width = query.shape
    head_size = gains.shape[1]
    size = width // 2 // CHUNKS
    lyric_rows = sum(run[2] for group in groups for run in group)
    key_rows = 3 * frames + lyric_rows
    bf16, f32 = jnp.bfloat16, jnp.float32
    slot = sum(2 * run[2] for run in groups[0])
    out_shape = [shape(frames, size)] * 2
    out_shape += [shape(2 * frames, size, dtype) for dtype in (bf16, f32, f32)]
    out_shape += [shape(one.shape[0], size), shape(2 * frames, size), shape(8, head_size, f32)]
    out_shape += [shape(slot, size)] * len(lyrics)
    return call(
        functools.partial(
            attention_kernel, chunk, len(earlier), len(after), groups, head_size, head_size ** (-0.5)
        ),
        "attention",
        [SMEM] + [VMEM] * (8 + len(lyrics) + len(earlier)) + [ANY] * len(after),
        [VMEM] * len(out_shape),
        out_shape,
        limit=ATTENTION_VMEM_LIMIT,
        cost=pl.CostEstimate(
            flops=24 * key_rows * frames * size,
            bytes_accessed=8 * 1024 * 1024,
            transcendentals=2 * key_rows * frames * (size // head_size),
        ),
        scratch_shapes=[pltpu.VMEM((frames + lyric_rows, 2 * frames), f32)],
    )(meta, gains, query, cot, value, key, mate, one, mid, *lyrics, *earlier, *after)


def finish_audio_kernel(state_ref, gain_ref, raw_ref, mate_ref, *refs):
    chunk_refs, refs = refs[: 7 * CHUNKS], refs[7 * CHUNKS :]
    *lyric, out, query_out, key_out, value_out, to_mate_ref, key_ref, value_ref, sems = refs
    head_size = gain_ref.shape[1]
    k_gain = gain_ref[1:2, :]
    frames, half = key_ref.shape
    size = half // CHUNKS
    own, mate = slice(0, frames), slice(frames, 2 * frames)
    touching = state_ref[1] == 1
    copies = []
    for chunk in range(CHUNKS):
        out_own_ref, query_own_ref, ready_ref = chunk_refs[7 * chunk : 7 * chunk + 3]
        for source, target in ((out_own_ref, out), (query_own_ref, query_out)):
            copies.append(
                pltpu.make_async_copy(
                    source,
                    target.at[:, chunk_of(target, state_ref[0], chunk)],
                    sems.at[len(copies)],
                )
            )
            copies[-1].start()
        to_mate_ref[0 : 2 * frames, chunk_cols(chunk, size)] = ready_ref[...]
    for ref in lyric:
        to_mate_ref[4 * frames :, :] = ref[...]
    raw_keys = raw_ref[:, half_of(raw_ref, state_ref[0])]
    for head in range(half // head_size):
        cols = slice(head * head_size, (head + 1) * head_size)
        chunk = head * head_size // size
        part = slice(head * head_size - chunk * size, (head + 1) * head_size - chunk * size)
        key_grad_ref, value_grad_ref, one_ref, mid_ref = chunk_refs[7 * chunk + 3 : 7 * chunk + 7]
        one = one_ref[one_ref.shape[0] - 2 * frames :, part].astype(jnp.float32)
        mid = mid_ref[:, part].astype(jnp.float32)
        for_own = jnp.where(touching, one, mid)
        for_mate = jnp.where(touching, mid, one)
        key_ref[:, cols] = through_norm(
            raw_keys[:, cols], key_grad_ref[own, part] + for_own[:frames], k_gain
        )
        value_ref[:, cols] = (value_grad_ref[own, part] + for_own[frames:]).astype(jnp.bfloat16)
        to_mate_ref[2 * frames : 3 * frames, cols] = through_norm(
            mate_ref[2 * frames : 3 * frames, cols],
            key_grad_ref[mate, part] + for_mate[:frames],
            k_gain,
        )
        to_mate_ref[3 * frames : 4 * frames, cols] = (
            value_grad_ref[mate, part] + for_mate[frames:]
        ).astype(jnp.bfloat16)
    for source, target in ((key_ref, key_out), (value_ref, value_out)):
        copies.append(
            pltpu.make_async_copy(
                source, target.at[:, half_of(target, state_ref[0])], sems.at[len(copies)]
            )
        )
        copies[-1].start()
    for copy in copies:
        copy.wait()


def finish_audio(state, gains, raw, mate, chunks, lyric):
    frames, width = raw.shape
    half = width // 2
    rows = 4 * frames + sum(array.shape[0] for array in lyric)
    return call(
        finish_audio_kernel,
        "finish_audio",
        [SMEM] + [VMEM] * (3 + len(chunks) + len(lyric)),
        [HBM] * 4 + [VMEM],
        [shape(frames, width)] * 4 + [shape(rows, half)],
        scratch_shapes=[pltpu.VMEM((frames, half), jnp.bfloat16)] * 2
        + [pltpu.SemaphoreType.DMA((2 * CHUNKS + 2,))],
    )(state, gains, raw, mate, *chunks, *lyric)


def relay_kernel(part_ref, arrived_ref, *refs):
    out_ref = refs[0] if len(refs) == 1 else refs[-2]
    out_ref[...] = (
        part_ref[...].astype(jnp.float32) + arrived_ref[...].astype(jnp.float32)
    ).astype(jnp.bfloat16)


def relay(part, arrived):
    return call(relay_kernel, "relay", [VMEM] * 2, VMEM, shape(*part.shape))(part, arrived)


def last_relay(part, arrived, later, after):
    return call(
        relay_kernel,
        "relay",
        [VMEM] * 2 + [ANY] * (1 + len(after)),
        [VMEM, ANY],
        [shape(*part.shape), shape(*later.shape)],
        input_output_aliases={2: 1},
    )(part, arrived, later, *after)


def finish_lyric_kernel(
    state_ref, gain_ref, raw_ref, mate_ref, sum_ref, *refs
):
    chunk_refs, (own_ref, to_mate_ref) = refs[:-2], refs[-2:]
    rows = raw_ref.shape[0]
    head_size = gain_ref.shape[1]
    k_gain = gain_ref[1:2, :]
    size = chunk_refs[0].shape[1]
    first = mate_ref.shape[0] - ALIGN_ROWS - 2 * rows
    to_mate_ref[2 * rows :, :] = split_rows(sum_ref[...], to_mate_ref.shape[1])
    raw_keys = raw_ref[:, half_of(raw_ref, state_ref[0])]
    for head in range(own_ref.shape[1] // head_size):
        cols = slice(head * head_size, (head + 1) * head_size)
        chunk = head * head_size // size
        part = slice(head * head_size - chunk * size, (head + 1) * head_size - chunk * size)
        total = chunk_refs[3 * chunk][:, part].astype(jnp.float32)
        for ref in chunk_refs[3 * chunk + 1 : 3 * chunk + 3]:
            total = total + ref[0 : 4 * rows, part].astype(jnp.float32)
        mate_keys = mate_ref[first : first + rows, cols]
        for ref, base, raw in (
            (own_ref, 0, raw_keys[:, cols]),
            (to_mate_ref, 2 * rows, mate_keys),
        ):
            ref[0:rows, cols] = through_norm(raw, total[base : base + rows], k_gain)
            ref[rows : 2 * rows, cols] = total[base + rows : base + 2 * rows].astype(jnp.bfloat16)


def finish_lyric(state, gains, raw, mate, total, chunks):
    rows, width = raw.shape
    half = width // 2
    return call(
        finish_lyric_kernel,
        "finish_lyric",
        [SMEM] + [VMEM] * (4 + len(chunks)),
        [VMEM] * 2,
        [shape(2 * rows, half), shape(2 * rows + GAIN_ROWS, half)],
    )(state, gains, raw, mate, total, *chunks)


def join_kernel(count, state_ref, gain_ref, own_ref, mate_ref, *refs):
    outs, (q_total_ref, k_total_ref, sems) = refs[count:-3], refs[-3:]
    frames = outs[0].shape[0]
    rows = own_ref.shape[0] // 2
    pieces = [
        (mate_ref.at[index * frames : (index + 1) * frames, :], out, 1 - state_ref[0])
        for index, out in enumerate(outs[:count])
    ]
    for ref, first, core in ((own_ref, 0, state_ref[0]), (mate_ref, count * frames, 1 - state_ref[0])):
        for index, out in enumerate(outs[count:]):
            start = first + index * rows
            pieces.append((ref.at[start : start + rows, :], out, core))
    copies = [
        pltpu.make_async_copy(source, out.at[:, half_of(out, core)], sems.at[index])
        for index, (source, out, core) in enumerate(pieces)
    ]
    for copy in copies:
        copy.start()
    sums = mate_ref[mate_ref.shape[0] - GAIN_ROWS :, :]
    total = gain_ref[...] + joined_rows(sums, gain_ref.shape[1])
    q_total_ref[...] = total[0:1]
    k_total_ref[...] = total[1:2]
    for copy in copies:
        copy.wait()


def join(state, gain, arrays, own, mate):
    rows, half = own.shape
    count = len(arrays)
    return call(
        functools.partial(join_kernel, count),
        "join",
        [SMEM] + [VMEM] * 3 + [HBM] * count,
        [HBM] * (count + 2) + [VMEM] * 2,
        [shape(*array.shape) for array in arrays]
        + [shape(rows // 2, 2 * half)] * 2
        + [shape(1, gain.shape[1], jnp.float32)] * 2,
        input_output_aliases={4 + i: i for i in range(count)},
        scratch_shapes=[pltpu.SemaphoreType.DMA((count + 4,))],
    )(state, gain, own, mate, *arrays)


def fill_kernel(count, state_ref, mate_ref, *refs):
    outs, sems = refs[count:-1], refs[-1]
    frames = outs[0].shape[0]
    copies = [
        pltpu.make_async_copy(
            mate_ref.at[index * frames : (index + 1) * frames, :],
            out.at[:, half_of(out, 1 - state_ref[0])],
            sems.at[index],
        )
        for index, out in enumerate(outs)
    ]
    for copy in copies:
        copy.start()
    for copy in copies:
        copy.wait()


def fill_other(state, arrays, mate):
    count = len(arrays)
    return call(
        functools.partial(fill_kernel, count),
        "fill_other",
        [SMEM, VMEM] + [HBM] * count,
        [HBM] * count,
        [shape(*array.shape) for array in arrays],
        input_output_aliases={2 + i: i for i in range(count)},
        scratch_shapes=[pltpu.SemaphoreType.DMA((count,))],
    )(state, mate, *arrays)


def norm_rows_kernel(gain_ref, raw_ref, out_ref):
    norm_columns(out_ref, slice(0, raw_ref.shape[0]), raw_ref[...], gain_ref)


def norm_rows(gains, raw):
    return pl.pallas_call(
        norm_rows_kernel,
        out_shape=jax.ShapeDtypeStruct(raw.shape, raw.dtype),
        name="norm_rows",
    )(gains, raw)


def norm_lyric_kernel(head_size, gain_ref, raw_ref, grad_ref, out_ref):
    for head in range(raw_ref.shape[1] // head_size):
        cols = slice(head * head_size, (head + 1) * head_size)
        out_ref[:, cols] = through_norm(raw_ref[:, cols], grad_ref[:, cols], gain_ref[1:2, :])


def norm_lyric(gains, raw, grad):
    return pl.pallas_call(
        functools.partial(norm_lyric_kernel, gains.shape[1]),
        out_shape=jax.ShapeDtypeStruct(raw.shape, jnp.bfloat16),
        name="norm_lyric",
    )(gains, raw, grad)


def sum_over(total, axis, bits):
    count = lax.axis_size(axis)
    for bit in bits:
        total = total + lax.ppermute(total, axis, [(i, i ^ bit) for i in range(count)])
    return total


def bits_of(count):
    return [1 << bit for bit in range(count.bit_length() - 1)]


def body(
    queries, keys, values, lyric_keys, lyric_values, q_gain, k_gain, cotangent, alignment, lyric_len
):
    frames = queries.shape[1]
    lyric_local, width = lyric_keys.shape[1:]
    count = lax.axis_size("seq")
    songs = lax.axis_size("song")
    me = lax.axis_index("seq")
    core = me % 2
    chips = count // 2
    chip = me // 2
    touching = (chip % 2) ^ core
    state = jnp.stack([core, touching]).astype(jnp.int32)
    gains = jnp.stack([q_gain, k_gain])

    swap = [(i, i ^ 1) for i in range(count)]
    partners = [(a, a ^ 1) for a in range(chips)]
    across = [(a, a ^ 2) for a in range(chips)]
    between = [(a, a + 1) for a in range(1, chips - 1, 2)]
    between += [(b, a) for a, b in between]

    def hop(block, moves):
        pairs = [(2 * a + c, 2 * b + c) for a, b in moves for c in (0, 1)]
        return lax.ppermute(block, "seq", pairs)

    hops = chips == 4 and lyric_local % 16 == 0
    total_rows = lyric_local * count
    if hops:
        run = ((0, lyric_local, lyric_local), (2 * lyric_local, 3 * lyric_local, lyric_local))
        groups = (run,) * 4
        owners = [chip, chip ^ 2, chip ^ 1, chip ^ 3]
        first_rows = []
        for owner in owners:
            first_rows += [
                (2 * owner + core) * lyric_local,
                (2 * owner + 1 - core) * lyric_local,
            ]
    else:
        gathered = jnp.concatenate(
            [
                lax.all_gather(
                    norm_rows(gains, lyric_keys[0]), "seq", axis=0, tiled=True
                ),
                lax.all_gather(lyric_values[0], "seq", axis=0, tiled=True),
            ],
            axis=0,
        )
        groups = (((0, total_rows, total_rows),),)
        first_rows = [0]
    has_left, has_right = chip > 0, chip < chips - 1
    has_near = jnp.where(core == 0, has_left, has_right)
    has_far = jnp.where(core == 0, has_right, has_left)
    meta = jnp.stack(
        [
            jnp.asarray(value, jnp.int32)
            for value in [core, touching]
            + [alignment[0, 0, slot] for slot in range(TILES)]
            + [lyric_len[0], has_near, has_far]
            + first_rows
        ]
    )

    to_mate = pack(
        state,
        alignment[0, 0],
        [queries[0], cotangent[0], keys[0], values[0]]
        + ([lyric_keys[0], lyric_values[0]] if hops else []),
    )
    mate = lax.ppermute(to_mate, "seq", swap)
    chunks, lyric_chunks, earlier, relayed, sent = [], [], [], [], []
    after = []
    for chunk in range(CHUNKS):
        before, one_before = after, lyrics[2:] if chunk else []
        if hops:
            pair = pair_lyrics(state, chunk, gains, lyric_keys[0], lyric_values[0], mate, before)
            two = hop(pair, across)
            lyrics = [pair, two, hop(two, partners)]
            lead, after = [pair], [two]
        else:
            lyrics, lead = [gathered], []
        one = hop(edge(state, chunk, 1, gains, keys[0], values[0], mate, lead, one_before), partners)
        mid = hop(edge(state, chunk, 0, gains, keys[0], values[0], mate, [], after), between)
        if not chunk:
            key_low = prepare_keys(state, gains, keys[0], mate, after)
        results = attention(
            chunk, meta, gains, queries[0], cotangent[0], values[0], key_low, mate, one, mid,
            lyrics, groups, earlier, relayed,
        )
        to_one, to_mid, gain_part, *parts = results[5:]
        earlier = [gain_part]
        mid_back = hop(to_mid, between)
        if hops:
            held, for_two, to_two = parts
            arrived = hop(to_two, partners)
            if chunk < CHUNKS - 1:
                relayed = [relay(for_two, arrived)]
                to_two = relayed[0]
            else:
                gain_total = sum_over(gain_part, "song", bits_of(songs)[:1])
                to_two, to_one = last_relay(for_two, arrived, to_one, [*sent, gain_total])
            two_back, one_back = hop(to_two, across), hop(to_one, partners)
            lyric_chunks += [held, one_back, two_back]
            sent = [*sent, mid_back, one_back, two_back]
        else:
            one_back = hop(to_one, partners)
            lyric_chunks += parts
        chunks += [*results[:5], one_back, mid_back]

    to_mate = []
    if hops:
        gain_total = sum_over(gain_total, "song", bits_of(songs)[1:])
        gain_total = sum_over(gain_total, "seq", [2, 4])
        own_half, part_to_mate = finish_lyric(
            state, gains, lyric_keys[0], mate, gain_total, lyric_chunks
        )
        to_mate = [part_to_mate]
    *filled, to_mate = finish_audio(state, gains, keys[0], mate, chunks, to_mate)
    from_mate = lax.ppermute(to_mate, "seq", swap)
    if hops:
        *filled, grad_lyric_keys, grad_lyric_values, q_total, k_total = join(
            state, gain_total, filled, own_half, from_mate
        )
    else:
        filled = fill_other(state, filled, from_mate)
        gain_total = lax.psum(gain_part, ("song", "seq"))
        q_total, k_total = gain_total[0:1], gain_total[1:2]
        spread = lax.dynamic_update_slice(
            jnp.zeros((2 * total_rows, width), jnp.float32),
            jnp.concatenate(lyric_chunks, axis=1).astype(jnp.float32),
            (0, core * (width // 2)),
        )
        lyric_key_sum, grad_lyric_values = [
            lax.psum_scatter(part, "seq", scatter_dimension=0, tiled=True)
            for part in (spread[:total_rows], spread[total_rows:])
        ]
        grad_lyric_keys = norm_lyric(gains, lyric_keys[0], lyric_key_sum)
        grad_lyric_values = grad_lyric_values.astype(jnp.bfloat16)
    output, grad_queries, grad_keys, grad_values = filled
    return (
        output[None],
        grad_queries[None],
        grad_keys[None],
        grad_values[None],
        grad_lyric_keys[None],
        grad_lyric_values[None],
        q_total[0],
        k_total[0],
    )


def solution(mesh):
    split = P("song", "seq", None)
    return jax.shard_map(
        body,
        mesh=mesh,
        in_specs=(split, split, split, split, split, P(), P(), split, split, P("song")),
        out_specs=(split, split, split, split, split, split, P(), P()),
        check_vma=False,
    )
```
